32 devices in a mesh: blk: 8 (over y, x, core), uly: 4 (over z).
Axes of the slice: x: 2, y: 2, z: 4, core: 2. Of those that a mesh axis runs over, the one named last changes fastest.
Arguments:
- tokens: bfloat16 [2, 4096, 2048], P(None, ('blk', 'uly')), may hold values from -6 to 6
- retain_gain: bfloat16 [2048], P('blk'), may hold values from 0.5 to 1.5
- query_weight: bfloat16 [2048, 2048], P('blk', 'uly'), may hold values from -0.125 to 0.125
- key_weight: bfloat16 [2048, 2048], P('blk', 'uly'), may hold values from -0.125 to 0.125
- value_weight: bfloat16 [2048, 4096], P('blk', 'uly'), may hold values from -0.125 to 0.125
- gate_matrix: bfloat16 [2048, 4096], P('blk', 'uly'), may hold values from -0.125 to 0.125
- output_weight: bfloat16 [4096, 2048], P('uly', 'blk'), may hold values from -0.125 to 0.125
- feed_gain: bfloat16 [2048], P('blk'), may hold values from 0.5 to 1.5
- up_weight: bfloat16 [2048, 4096], P('blk', 'uly'), may hold values from -0.125 to 0.125
- down_weight: bfloat16 [4096, 2048], P('uly', 'blk'), may hold values from -0.125 to 0.125
- decay_rate: float32 [8], replicated, may hold values from 0.00025 to 0.04
- lengths: int32 [2, 2], replicated, may hold values from 1024 to 3072, as said below
- out_grad: bfloat16 [2, 4096, 2048], P(None, ('blk', 'uly')), may hold values from -6 to 6
Outputs:
- block_out: bfloat16 [2, 4096, 2048], P(None, ('blk', 'uly'))
- input_grad: float32 [2, 4096, 2048], P(None, ('blk', 'uly'))
- retain_gain_grad: float32 [2048], P('blk')
- query_grad: float32 [2048, 2048], P('blk', 'uly')
- key_grad: float32 [2048, 2048], P('blk', 'uly')
- value_grad: float32 [2048, 4096], P('blk', 'uly')
- gate_grad: float32 [2048, 4096], P('blk', 'uly')
- output_grad: float32 [4096, 2048], P('uly', 'blk')
- feed_gain_grad: float32 [2048], P('blk')
- up_grad: float32 [2048, 4096], P('blk', 'uly')
- down_grad: float32 [4096, 2048], P('uly', 'blk')
The draws below stay inside these ranges and needn't reach their ends.
Inputs may be any that keep to these rules, and one draw needn't show every extreme that they name: Each row holds 2 sequence lengths that sum to 4096; every one is at least 1024 and the longest of each row is exactly 3072.
All inputs are finite; a program needn't handle non-finite values.
Results may differ from the reference program's by a relative error of at most 0.015.
The reference program's roundings to bfloat16 on the way count: a program that leaves them out, or rounds other values in their place, can miss the bound.
Values may be sent and summed in bfloat16 or wider, within the bound.
A program may use at most 320 MiB of HBM per device.

```python
import math
import jax
import jax.numpy as jnp
from jax import lax

D = 2048
HEADS = 8
FF = 4096
MB = 2
LENGTH_FLOOR = 1024
TOK_MB = 4096
NSEQ = 2
LEN_MAX = 3072


def draw_lengths(key, part):
    remain = NSEQ - 1
    base_len = (TOK_MB - LEN_MAX) // remain
    surplus = (TOK_MB - LEN_MAX) % remain
    reach_len = base_len - LENGTH_FLOOR
    pair_count = remain // 2
    rows_out = []
    for micro_step in range(MB):
        row_key = jax.random.fold_in(key, micro_step)
        shift_key, order_key = jax.random.split(row_key)
        shifts = jax.random.randint(shift_key, (pair_count,), -reach_len, reach_len + 1, dtype=jnp.int32)
        others = base_len + (jnp.arange(remain) < surplus).astype(jnp.int32)
        move_set = jnp.zeros((remain,), jnp.int32).at[0:2 * pair_count:2].add(shifts).at[1:2 * pair_count:2].add(-shifts)
        all_lengths = jnp.concatenate([jnp.full((1,), LEN_MAX, jnp.int32), others + move_set])
        rows_out.append(jax.random.permutation(order_key, all_lengths))
    return jnp.stack(rows_out)


def block_levels(own_key, shape, shards, low, largest):
    def one(axis_at, parts):
        steps = jax.random.uniform(jax.random.fold_in(jax.random.fold_in(own_key, 6), axis_at), (parts,), jnp.float32, low / len(shards), largest / len(shards))
        return jnp.repeat(jnp.exp(steps), shape[axis_at] // parts).reshape((-1,) + (1,) * (len(shape) - axis_at - 1))

    loudness = one(*shards[0])
    for cut in shards[1:]:
        loudness = loudness * one(*cut)
    return loudness


def scatter_about(key, dims, width, reach, cuts=(), held_as=jnp.bfloat16):
    array = width * jax.random.normal(key, dims, jnp.float32)
    if cuts:
        array = array * block_levels(key, dims, cuts, -0.22, 0.18)
    return jnp.clip(array, -reach, reach).astype(held_as)


def setup_inputs(seed: int = 0) -> dict:
    seeds = jax.random.split(jax.random.key(seed), 14)
    tokens = scatter_about(seeds[0], (MB, TOK_MB, D), 1.0, 6.0, ((1, 32),))
    retain_gain = jnp.clip(1.0 + 0.1 * jax.random.normal(seeds[1], (D,), jnp.float32), 0.5, 1.5).astype(jnp.bfloat16)
    query_weight = scatter_about(seeds[2], (D, D), D ** -0.5, 0.125, ((0, 8), (1, 4)))
    key_weight = scatter_about(seeds[3], (D, D), D ** -0.5, 0.125, ((0, 8), (1, 4)))
    value_weight = scatter_about(seeds[4], (D, 2 * D), D ** -0.5, 0.125, ((0, 8), (1, 4)))
    gate_matrix = scatter_about(seeds[5], (D, 2 * D), D ** -0.5, 0.125, ((0, 8), (1, 4)))
    output_weight = scatter_about(seeds[6], (2 * D, D), D ** -0.5, 0.125, ((0, 4), (1, 8)))
    feed_gain = jnp.clip(1.0 + 0.1 * jax.random.normal(seeds[7], (D,), jnp.float32), 0.5, 1.5).astype(jnp.bfloat16)
    up_weight = scatter_about(seeds[8], (D, FF), D ** -0.5, 0.125, ((0, 8), (1, 4)))
    down_weight = scatter_about(seeds[9], (FF, D), (FF // 2) ** -0.5, 0.125, ((0, 4), (1, 8)))
    decay_rate = jnp.clip(jnp.exp(jax.random.uniform(seeds[10], (HEADS,), jnp.float32, math.log(0.00025), math.log(0.04))), 0.00025, 0.04)
    lengths = draw_lengths(jax.random.fold_in(seeds[13], 71), 0)
    out_grad = scatter_about(seeds[12], (MB, TOK_MB, D), 1.0, 6.0, ((1, 32),))
    return {"tokens": tokens, "retain_gain": retain_gain, "query_weight": query_weight, "key_weight": key_weight, "value_weight": value_weight, "gate_matrix": gate_matrix, "output_weight": output_weight, "feed_gain": feed_gain, "up_weight": up_weight, "down_weight": down_weight, "decay_rate": decay_rate, "lengths": lengths, "out_grad": out_grad}


EPSILON = 1e-05
TOP_PRECISION = lax.Precision.HIGHEST

@jax.custom_vjp
def low(v):
    return lax.optimization_barrier(v.astype(jnp.bfloat16)).astype(jnp.float32)

@jax.custom_vjp
def low_back(v):
    return v

def low_keep(v):
    return (low(v), None)

def low_pass(kept, grad):
    return (grad,)

def back_keep(v):
    return (v, None)

def back_low(kept, grad):
    return (low(grad),)
low.defvjp(low_keep, low_pass)
low_back.defvjp(back_keep, back_low)

def layer_norm(values, gain_row):
    center = values - lax.optimization_barrier(jnp.mean(values, axis=-1, keepdims=True))
    spread = lax.optimization_barrier(jnp.mean(center * center, axis=-1, keepdims=True))
    return center * lax.rsqrt(spread + EPSILON) * gain_row

def group_norm(values):
    center = values - lax.optimization_barrier(jnp.mean(values, axis=-1, keepdims=True))
    spread = lax.optimization_barrier(jnp.mean(center * center, axis=-1, keepdims=True))
    return center * lax.rsqrt(spread + EPSILON)

def swish(values):
    return values * jax.nn.sigmoid(values)

def gelu_tanh(values):
    return jax.nn.gelu(values, approximate=True)

def segment_ids(positions, lengths_row):
    bounds = jnp.cumsum(lengths_row) - lengths_row
    return lax.optimization_barrier(jnp.sum((bounds[None, :] <= positions[:, None]).astype(jnp.int32), axis=1))

def retention_parts(rate_row, seg_local, seg_prev, length):
    places = jnp.arange(length).astype(rate_row.dtype)
    offset = places[:, None] - places[None, :]
    causal = (offset >= 0) & (seg_local[:, None] == seg_local[None, :])
    decay_table = jnp.exp(-rate_row[:, None, None] * jnp.maximum(offset, 0.0)[None])
    inner_width = jnp.where(causal[None], decay_table, 0.0)
    carry_in = (seg_local == seg_prev).astype(rate_row.dtype)
    entry = carry_in[None, :] * jnp.exp(-rate_row[:, None] * (places[None, :] + 1.0))
    carry_out = (seg_local == seg_local[length - 1]).astype(rate_row.dtype)
    leave = carry_out[None, :] * jnp.exp(-rate_row[:, None] * (length - 1.0 - places[None, :]))
    through = (seg_local[length - 1] == seg_prev).astype(rate_row.dtype) * jnp.exp(-rate_row * length)
    return (inner_width, entry, leave, through)

def state_local(leave, head_keys, value_heads):
    return jnp.einsum('hld,hle->hde', head_keys * leave[:, :, None], value_heads, precision=TOP_PRECISION)

def read_out(inner_width, entry, head_queries, head_keys, value_heads, state_in):
    score_matrix = jnp.einsum('eng,ekg->enk', head_queries, head_keys, precision=TOP_PRECISION) * inner_width
    local_part = jnp.einsum('hlm,hme->hle', score_matrix, value_heads, precision=TOP_PRECISION)
    carried = jnp.einsum('hld,hde->hle', head_queries, state_in, precision=TOP_PRECISION)
    return local_part + entry[:, :, None] * carried

def matmul(left_side, right_side):
    return jnp.dot(left_side, right_side, precision=TOP_PRECISION)

def retention(query_rows, key_rows, value_rows, rate_row, lengths_row):
    stream_len = query_rows.shape[0]
    head_count = rate_row.shape[0]
    block_size = min(512, stream_len)
    block_count = stream_len // block_size

    def split(row_block):
        return row_block.reshape(block_count, block_size, head_count, -1).transpose(0, 2, 1, 3)
    positions = jnp.arange(stream_len, dtype=jnp.int32)
    seg_all = segment_ids(positions, lengths_row).reshape(block_count, block_size)
    seg_first = segment_ids(positions[::block_size] - 1, lengths_row)

    @jax.checkpoint
    def advance(state, pieces):
        query_block, key_block, value_block, seg_local, seg_prev = pieces
        inner_width, entry, leave, through = retention_parts(rate_row, seg_local, seg_prev, block_size)
        output = read_out(inner_width, entry, query_block, key_block, value_block, state)
        state_next = through[:, None, None] * state + state_local(leave, key_block, value_block)
        return (state_next, output)
    state_zero = jnp.zeros((head_count, query_rows.shape[1] // head_count, value_rows.shape[1] // head_count), jnp.float32)
    final_state, outputs = lax.scan(advance, state_zero, (split(query_rows), split(key_rows), split(value_rows), seg_all, seg_first))
    return outputs.transpose(0, 2, 1, 3).reshape(stream_len, -1)

def block(inputs, weights, rate_row, lengths_row):
    gain_one, query_full, key_full, value_full, gate_full, output_full, gain_two, up_full, down_full = weights
    head_count = rate_row.shape[0]
    norm_one = low(layer_norm(inputs, gain_one))
    query_rows = low(low_back(matmul(norm_one, query_full)))
    key_rows = low(low_back(matmul(norm_one, key_full)))
    value_rows = low(low_back(matmul(norm_one, value_full)))
    gate_rows = low_back(matmul(norm_one, gate_full))
    retained = retention(query_rows, key_rows, value_rows, rate_row, lengths_row)
    stream_len = inputs.shape[0]
    normed_heads = group_norm(retained.reshape(stream_len, head_count, -1)).reshape(stream_len, -1)
    mixed_rows = low(swish(gate_rows) * normed_heads)
    hidden = inputs + low_back(matmul(mixed_rows, output_full))
    norm_two = low(layer_norm(hidden, gain_two))
    upward = low_back(matmul(norm_two, up_full))
    activated = low(gelu_tanh(upward))
    return hidden + low_back(matmul(activated, down_full))

def reference(tokens, retain_gain, query_weight, key_weight, value_weight, gate_matrix, output_weight, feed_gain, up_weight, down_weight, decay_rate, lengths, out_grad):
    params = tuple((weight.astype(jnp.float32) for weight in (retain_gain, query_weight, key_weight, value_weight, gate_matrix, output_weight, feed_gain, up_weight, down_weight)))
    rate_row = decay_rate.astype(jnp.float32)
    outputs = []
    input_grads = []
    totals = None
    for micro_step in range(tokens.shape[0]):
        lengths_row = lengths[micro_step]

        def forward(inputs, weights):
            return block(inputs, weights, rate_row, lengths_row)
        result, pullback = jax.vjp(forward, tokens[micro_step].astype(jnp.float32), params)
        input_part, grad_set = pullback(out_grad[micro_step].astype(jnp.float32))
        outputs.append(result.astype(jnp.bfloat16))
        input_grads.append(input_part)
        totals = grad_set if totals is None else jax.tree.map(jnp.add, totals, grad_set)
    return (jnp.stack(outputs), jnp.stack(input_grads), totals[0], totals[1], totals[2], totals[3], totals[4], totals[5], totals[6], totals[7], totals[8])
```

```python
import jax
import jax.numpy as jnp
from jax import lax
from jax.sharding import PartitionSpec as P

EPSILON = 1e-05
BF = jnp.bfloat16
F32 = jnp.float32


def dot_nn(left, right, kind=F32):
    return jnp.dot(left, right, preferred_element_type=F32).astype(kind)


def dot_tn(left, right, kind=F32):
    return lax.dot_general(
        left, right, (((0,), (0,)), ((), ())), preferred_element_type=F32
    ).astype(kind)


def dot_nt(left, right, kind=F32):
    return lax.dot_general(
        left, right, (((1,), (1,)), ((), ())), preferred_element_type=F32
    ).astype(kind)


def swap(array, mask):
    count = lax.axis_size("blk")
    return lax.ppermute(array, "blk", [(b, b ^ mask) for b in range(count)])


def shift(array, step):
    count = lax.axis_size("uly")
    return lax.ppermute(array, "uly", [(z, (z + step) % count) for z in range(count)])


def is_cube():
    return lax.axis_size("blk") == 8


def masks():
    return [2 * k + j for j in range(2) for k in range(4)]


def arrange(array):
    if not is_cube():
        return array
    me = lax.axis_index("blk")
    width = array.shape[-1] // 8
    parts = [
        lax.dynamic_slice_in_dim(array, (me ^ m) * width, width, array.ndim - 1) for m in masks()
    ]
    return jnp.concatenate(parts, axis=-1)


def restore(array):
    if not is_cube():
        return array
    me = lax.axis_index("blk")
    width = array.shape[-1] // 8
    parts = []
    for b in range(8):
        m = me ^ b
        place = (m & 1) * 4 + (m >> 1)
        parts.append(lax.dynamic_slice_in_dim(array, place * width, width, array.ndim - 1))
    return jnp.concatenate(parts, axis=-1)


def mirror(array):
    if not is_cube():
        return array
    half = array.shape[-1] // 2
    return jnp.concatenate([array[..., half:], array[..., :half]], axis=-1)


def plane_gather(first, second):
    first_x = swap(first, 2)
    second_y = swap(second, 4)
    first_y, first_xy = swap(first, 4), swap(first_x, 4)
    second_x, second_xy = swap(second, 2), swap(second_y, 2)
    return [first, first_x, first_y, first_xy], [second, second_x, second_y, second_xy]


def block_gather(first, second, dim):
    if not is_cube():
        return (
            lax.all_gather(first, "blk", axis=dim, tiled=True),
            lax.all_gather(second, "blk", axis=dim, tiled=True),
        )
    out = []
    for pieces in plane_gather(first, second):
        out.append(jnp.concatenate(pieces + [swap(p, 1) for p in pieces], axis=dim))
    return out


def both(own, came):
    return (own.astype(F32) + came.astype(F32)).astype(BF)


def plane_reduce(first, second):
    first = [both(first[k], swap(first[k + 2], 4)) for k in range(2)]
    second = [both(second[k], swap(second[k + 1], 2)) for k in (0, 2)]
    return both(first[0], swap(first[1], 2)), both(second[0], swap(second[1], 4))


def block_reduce(first, second, dim):
    if not is_cube():
        return (
            lax.psum_scatter(first.astype(BF), "blk", scatter_dimension=dim, tiled=True),
            lax.psum_scatter(second.astype(BF), "blk", scatter_dimension=dim, tiled=True),
        )
    sums = []
    for array in (first, second):
        parts = jnp.split(array.astype(BF), 8, axis=dim)
        sums.append([both(parts[k], swap(parts[4 + k], 1)) for k in range(4)])
    return plane_reduce(*sums)


def cube_all(array):
    if not is_cube():
        return lax.all_gather(array, "blk")
    array = array[None]
    for mask in (2, 4, 1):
        array = jnp.concatenate([array, swap(array, mask)], axis=0)
    return array


def cube_sum(array):
    if not is_cube():
        return lax.psum_scatter(array, "blk", scatter_dimension=array.ndim - 1, tiled=True)
    for mask in (1, 4, 2):
        half = array.shape[-1] // 2
        array = array[..., :half] + swap(array[..., half:], mask)
    return array


def spread(rows):
    count = lax.axis_size("uly")
    place = lax.axis_index("uly")
    came = [rows] + [shift(rows, s) for s in range(1, count)]
    window = came[:0:-1] + came[:1] + came[:0:-1]
    length = rows.shape[0]
    return lax.dynamic_slice_in_dim(
        jnp.concatenate(window, axis=0), (count - 1 - place) * length, count * length, 0
    )


def collect(partial):
    count = lax.axis_size("uly")
    place = lax.axis_index("uly")
    length = partial.shape[0] // count

    def rows_of(step):
        return lax.dynamic_slice_in_dim(partial, ((place + step) % count) * length, length, 0)

    total = rows_of(0)
    for s in range(1, count):
        total = total + shift(rows_of(s).astype(BF), s).astype(F32)
    return total


def normed(values):
    center = values - jnp.mean(values, axis=-1, keepdims=True)
    scale = lax.rsqrt(jnp.mean(center * center, axis=-1, keepdims=True) + EPSILON)
    return center * scale, scale


def norm_back(grad, hat, scale):
    return scale * (
        grad
        - jnp.mean(grad, axis=-1, keepdims=True)
        - hat * jnp.mean(grad * hat, axis=-1, keepdims=True)
    )


GELU_A = 0.7978845608028654
GELU_B = 0.044715


def gelu_pair(u):
    square = u * u
    tanh = jnp.tanh(GELU_A * u * (1.0 + GELU_B * square))
    slope = 0.5 * (1.0 + tanh) + 0.5 * u * (1.0 - tanh * tanh) * GELU_A * (
        1.0 + 3.0 * GELU_B * square
    )
    return 0.5 * u * (1.0 + tanh), slope


def segment_ids(positions, lengths_row):
    count = lengths_row.shape[0]
    before = jnp.arange(count)[None, :] < jnp.arange(count)[:, None]
    bounds = jnp.sum(jnp.where(before, lengths_row[None, :], 0), axis=1)
    return jnp.sum((bounds[None, :] <= positions[:, None]).astype(jnp.int32), axis=1)


def decay_parts(rates, lengths_row, length):
    me = lax.axis_index("blk")
    count = lax.axis_size("blk")
    places = jnp.arange(length, dtype=jnp.int32)
    seg = segment_ids(me * length + places, lengths_row)
    ends = segment_ids((jnp.arange(count, dtype=jnp.int32) + 1) * length - 1, lengths_row)
    seg_prev = segment_ids(jnp.reshape(me * length - 1, (1,)), lengths_row)[0]
    offset = places[:, None] - places[None, :]
    causal = (offset >= 0) & (seg[:, None] == seg[None, :])
    far = jnp.maximum(offset, 0).astype(F32)
    inner = jnp.where(causal[None], jnp.exp(-rates[:, None, None] * far[None]), 0.0)
    at = places.astype(F32)
    entry = jnp.where(seg == seg_prev, jnp.exp(-rates[:, None] * (at + 1.0)), 0.0)
    leave = jnp.where(seg == seg[length - 1], jnp.exp(-rates[:, None] * (length - 1.0 - at)), 0.0)
    if is_cube():
        source = me ^ jnp.asarray(masks(), jnp.int32)
    else:
        source = jnp.arange(count, dtype=jnp.int32)
    end_of = ends[source]
    end_before = jnp.where(source > 0, ends[jnp.maximum(source - 1, 0)], 0)
    past = jnp.maximum(me - 1 - source, 0).astype(F32)
    ahead = jnp.maximum(source - 1 - me, 0).astype(F32)
    from_past = jnp.where(
        (source < me) & (end_of == seg_prev), jnp.exp(-rates[:, None] * (length * past)), 0.0
    )
    from_ahead = jnp.where(
        (source > me) & (end_before == ends[me]), jnp.exp(-rates[:, None] * (length * ahead)), 0.0
    )
    return inner, entry[:, :, None], leave[:, :, None], from_past, from_ahead


def state_sum(weights, states):
    return jnp.einsum("hb,bhde->hde", weights, states.astype(F32))


def retention_state(heads, leave):
    return jnp.stack(
        [
            dot_tn((k.astype(F32) * leave[h]).astype(BF), v, BF)
            for h, (q, k, v) in enumerate(heads)
        ]
    )


def retention(heads, parts, state):
    inner, entry = parts[0], parts[1]
    out = []
    for h, (q, k, v) in enumerate(heads):
        scores = (dot_nt(q, k) * inner[h]).astype(BF)
        out.append(dot_nn(scores, v) + entry[h] * dot_nn(q, state[h].astype(BF)))
    return out


def mix(gate, retained):
    out = []
    for h, r in enumerate(retained):
        g = gate[:, h * r.shape[1] : (h + 1) * r.shape[1]]
        out.append((g * jax.nn.sigmoid(g) * normed(r)[0]).astype(BF))
    return jnp.concatenate(out, axis=1)


def mix_back(gate, retained, grad_mixed):
    grad_gate, grad_retained = [], []
    for h, r in enumerate(retained):
        cols = slice(h * r.shape[1], (h + 1) * r.shape[1])
        g, gm = gate[:, cols], grad_mixed[:, cols]
        sigma = jax.nn.sigmoid(g)
        hat, scale = normed(r)
        grad_gate.append((gm * hat * (sigma + g * sigma * (1.0 - sigma))).astype(BF))
        grad_retained.append(norm_back(gm * g * sigma, hat, scale).astype(BF))
    return jnp.concatenate(grad_gate, axis=1), grad_retained


def retention_back(heads, parts, state, grad_retained, grad_state):
    inner, entry, leave = parts[0], parts[1], parts[2]
    grads = []
    for h, (q, k, v) in enumerate(heads):
        gr = grad_retained[h]
        scores = (dot_nt(q, k) * inner[h]).astype(BF)
        pulls = (dot_nt(gr, v) * inner[h]).astype(BF)
        gs, st = grad_state[h].astype(BF), state[h].astype(BF)
        gq = dot_nn(pulls, k) + entry[h] * dot_nt(gr, st)
        gk = dot_tn(pulls, q) + leave[h] * dot_nt(v, gs)
        gv = dot_tn(scores, gr) + leave[h] * dot_nn(k, gs)
        grads.append((gq.astype(BF), gk.astype(BF), gv.astype(BF)))
    return grads


def core_cut(array, dim):
    core = lax.axis_index("blk") % 2
    half = array.shape[dim] // 2
    own = lax.dynamic_slice_in_dim(array, core * half, half, dim)
    other = lax.dynamic_slice_in_dim(array, (1 - core) * half, half, dim)
    return own, other


def core_order(own, other, dim):
    if is_cube():
        return jnp.concatenate([own, other], axis=dim)
    return core_join(own, other, dim)


def core_join(own, other, dim):
    first = lax.axis_index("blk") % 2 == 0
    return jnp.concatenate([jnp.where(first, own, other), jnp.where(first, other, own)], axis=dim)


def core_groups():
    count = lax.axis_size("blk")
    return [list(range(0, count, 2)), list(range(1, count, 2))]


def feed_weights(up_shard, down_shard):
    own, other = core_cut(up_shard, 1)
    up = core_order(own, swap(other, 1), 0)
    own, other = core_cut(down_shard, 0)
    down = core_order(own, swap(other, 1), 1)
    ups, downs = [], []
    for s in range(lax.axis_size("uly")):
        up_s = up if s == 0 else shift(up, s)
        down_s = down if s == 0 else shift(down, s)
        if is_cube():
            up_k, down_k = plane_gather(up_s, down_s)
            half = up.shape[0] // 2
            ups.append(
                jnp.concatenate([u[:half] for u in up_k] + [u[half:] for u in up_k], axis=0)
            )
            downs.append(
                jnp.concatenate([d[:, :half] for d in down_k] + [d[:, half:] for d in down_k], axis=1)
            )
        else:
            groups = core_groups()
            ups.append(lax.all_gather(up_s, "blk", axis=0, tiled=True, axis_index_groups=groups))
            downs.append(lax.all_gather(down_s, "blk", axis=1, tiled=True, axis_index_groups=groups))
    return jnp.concatenate(ups, axis=1), jnp.concatenate(downs, axis=0)


def feed_reduce(up_grad, down_grad):
    count = lax.axis_size("uly")
    depth = up_grad.shape[0]
    wide = up_grad.shape[1] // count
    up_sum, down_sum = None, None
    for s in range(count):
        up_s = up_grad[:, s * wide : (s + 1) * wide]
        down_s = down_grad[s * wide : (s + 1) * wide]
        if is_cube():
            c = depth // 8
            up_k = [
                jnp.concatenate(
                    [up_s[k * c : (k + 1) * c], up_s[(4 + k) * c : (5 + k) * c]], axis=0
                )
                for k in range(4)
            ]
            down_k = [
                jnp.concatenate(
                    [down_s[:, k * c : (k + 1) * c], down_s[:, (4 + k) * c : (5 + k) * c]], axis=1
                )
                for k in range(4)
            ]
            up_s, down_s = plane_reduce(up_k, down_k)
        else:
            groups = core_groups()
            up_s = lax.psum_scatter(
                up_s, "blk", scatter_dimension=0, tiled=True, axis_index_groups=groups
            )
            down_s = lax.psum_scatter(
                down_s, "blk", scatter_dimension=1, tiled=True, axis_index_groups=groups
            )
        if s:
            up_s, down_s = shift(up_s, -s), shift(down_s, -s)
        up_s, down_s = up_s.astype(F32), down_s.astype(F32)
        up_sum = up_s if up_sum is None else up_sum + up_s
        down_sum = down_s if down_sum is None else down_sum + down_s
    half = up_sum.shape[0] // 2
    core = lax.axis_index("blk") % 2
    first = 0 if is_cube() else core * half
    second = half if is_cube() else (1 - core) * half
    up_own = lax.dynamic_slice_in_dim(up_sum, first, half, 0)
    up_other = lax.dynamic_slice_in_dim(up_sum, second, half, 0)
    down_own = lax.dynamic_slice_in_dim(down_sum, first, half, 1)
    down_other = lax.dynamic_slice_in_dim(down_sum, second, half, 1)
    return (
        core_join(up_own, swap(up_other.astype(BF), 1).astype(F32), 1),
        core_join(down_own, swap(down_other.astype(BF), 1).astype(F32), 0),
    )


def feed(norm_two, out_rows, up, down):
    upward = dot_nn(norm_two, up)
    act, slope = gelu_pair(upward)
    act = act.astype(BF)
    grad_act = dot_nt(out_rows, down)
    grad_up = (grad_act * slope).astype(BF)
    return (
        dot_nn(act, down),
        dot_nt(grad_up, up),
        dot_tn(norm_two, grad_up, BF),
        dot_tn(act, out_rows, BF),
    )


def body(
    tokens,
    retain_gain,
    query_weight,
    key_weight,
    value_weight,
    gate_matrix,
    output_weight,
    feed_gain,
    up_weight,
    down_weight,
    decay_rate,
    lengths,
    out_grad,
):
    micro, rows, width = tokens.shape
    heads_here = decay_rate.shape[0] // lax.axis_size("uly")
    rates = lax.dynamic_slice_in_dim(decay_rate, lax.axis_index("uly") * heads_here, heads_here)
    hd = query_weight.shape[1] // heads_here
    vd = value_weight.shape[1] // heads_here
    cut_v = value_weight.shape[1] // 2
    cut_o = output_weight.shape[0] // 2

    tokens = arrange(tokens)
    wide_tokens = [spread(tokens[m]) for m in range(micro)]
    gains = cube_all(jnp.stack([retain_gain, feed_gain]))
    gain_one = gains[:, 0].reshape(-1).astype(F32)
    gain_two = gains[:, 1].reshape(-1).astype(F32)

    first = jnp.concatenate([query_weight, key_weight, value_weight[:, :cut_v]], axis=1)
    second = jnp.concatenate([value_weight[:, cut_v:], gate_matrix], axis=1)
    w_first, w_second = block_gather(first, second, 0)
    w_out = jnp.concatenate(
        block_gather(output_weight[:cut_o], output_weight[cut_o:], 1), axis=0
    )
    up, down = feed_weights(up_weight, down_weight)

    outs = arrange(out_grad)
    outs_other = swap(mirror(outs), 1)

    length = wide_tokens[0].shape[0]
    qk = query_weight.shape[1]

    wide_hat, wide_one, sets, gates, parts, states = [], [], [], [], [], []
    for m in range(micro):
        hat, _ = normed(wide_tokens[m].astype(F32))
        one = (hat * gain_one).astype(BF)
        a = dot_nn(one, w_first, BF)
        v_high = dot_nn(one, w_second[:, :cut_v], BF)
        gate = dot_nn(one, w_second[:, cut_v:])
        values = jnp.concatenate([a[:, 2 * qk :], v_high], axis=1)
        heads = [
            (
                a[:, h * hd : (h + 1) * hd],
                a[:, qk + h * hd : qk + (h + 1) * hd],
                values[:, h * vd : (h + 1) * vd],
            )
            for h in range(heads_here)
        ]
        part = decay_parts(rates, lengths[m], length)
        states.append(retention_state(heads, part[2]))
        wide_one.append(one)
        sets.append(heads)
        gates.append(gate)
        parts.append(part)

    def exchange(pieces):
        if not is_cube():
            return [lax.all_gather(p, "blk") for p in pieces]
        half = len(pieces) // 2
        a, b = plane_gather(jnp.stack(pieces[:half]), jnp.stack(pieces[half:]))
        got = []
        for four in (a, b):
            full = jnp.stack(four + [swap(p, 1) for p in four])
            got += [full[:, i] for i in range(full.shape[1])]
        return got

    all_states = exchange(states)
    state_in, retained, mixed, hidden, hats, scales, norm_two = [], [], [], [], [], [], []
    for m in range(micro):
        state = state_sum(parts[m][3], all_states[m])
        kept = retention(sets[m], parts[m], state)
        mx = mix(gates[m], kept)
        hid = tokens[m].astype(F32) + collect(dot_nn(mx, w_out))
        hat, scale = normed(hid)
        state_in.append(state)
        retained.append(kept)
        mixed.append(mx)
        hidden.append(hid)
        hats.append(hat)
        scales.append(scale)
        norm_two.append((hat * gain_two).astype(BF))

    two = jnp.concatenate(norm_two, axis=0)
    two_both = jnp.concatenate([two, swap(mirror(two), 1)], axis=0)
    flat = outs.reshape(micro * rows, width)
    out_both = jnp.concatenate([flat, outs_other.reshape(micro * rows, width)], axis=0)
    down_rows, grad_two, up_part, down_part = feed(two_both, out_both, up, down)
    own = micro * rows
    back_sum = swap(mirror(grad_two[own:].astype(BF)), 1)
    down_sum = swap(mirror(down_rows[own:].astype(BF)), 1)
    grad_two = grad_two[:own] + back_sum.astype(F32)
    down_rows = down_rows[:own] + down_sum.astype(F32)
    up_grad, down_grad = feed_reduce(up_part, down_part)

    block_out = restore(
        (jnp.stack(hidden) + down_rows.reshape(micro, rows, width)).astype(BF)
    )

    grad_hidden, wide_att = [], []
    gain_two_part = jnp.zeros((width,), F32)
    for m in range(micro):
        g2 = grad_two[m * rows : (m + 1) * rows]
        gain_two_part = gain_two_part + jnp.sum(g2 * hats[m], axis=0)
        gh = outs[m].astype(F32) + norm_back(g2 * gain_two, hats[m], scales[m])
        grad_hidden.append(gh)
        wide_att.append(spread(gh.astype(BF)))

    grad_gates, grad_rets, grad_states = [], [], []
    for m in range(micro):
        grad_mixed = dot_nt(wide_att[m], w_out)
        gg, gr = mix_back(gates[m], retained[m], grad_mixed)
        grad_gates.append(gg)
        grad_rets.append(gr)
        grad_states.append(
            jnp.stack(
                [
                    dot_tn((q.astype(F32) * parts[m][1][h]).astype(BF), gr[h], BF)
                    for h, (q, k, v) in enumerate(sets[m])
                ]
            )
        )
    all_back = exchange(grad_states)
    out_part = dot_tn(
        jnp.concatenate(mixed, axis=0), jnp.concatenate(wide_att, axis=0), BF
    )

    first_grads, second_grads, input_grads = [], [], []
    gain_one_part = jnp.zeros((width,), F32)
    for m in range(micro):
        back = state_sum(parts[m][4], all_back[m])
        grads = retention_back(sets[m], parts[m], state_in[m], grad_rets[m], back)
        gq = jnp.concatenate([g[0] for g in grads], axis=1)
        gk = jnp.concatenate([g[1] for g in grads], axis=1)
        gv = jnp.concatenate([g[2] for g in grads], axis=1)
        ga = jnp.concatenate([gq, gk, gv[:, :cut_v]], axis=1)
        gb = jnp.concatenate([gv[:, cut_v:], grad_gates[m]], axis=1)
        first_grads.append(ga)
        second_grads.append(gb)
        partial = dot_nt(ga, w_first) + dot_nt(gb, w_second)
        wide_hat, _ = normed(wide_tokens[m].astype(F32))
        gain_one_part = gain_one_part + jnp.sum(partial * wide_hat, axis=0)
        grad_one = collect(partial)
        hat, scale = normed(tokens[m].astype(F32))
        input_grads.append(grad_hidden[m] + norm_back(grad_one * gain_one, hat, scale))

    one_all = jnp.concatenate(wide_one, axis=0)
    first_part = dot_tn(one_all, jnp.concatenate(first_grads, axis=0), BF)
    second_part = dot_tn(one_all, jnp.concatenate(second_grads, axis=0), BF)
    out_first, out_second = block_reduce(out_part[:cut_o], out_part[cut_o:], 1)
    first_sum, second_sum = block_reduce(first_part, second_part, 0)
    first_sum, second_sum = first_sum.astype(F32), second_sum.astype(F32)
    output_grad = jnp.concatenate([out_first, out_second], axis=0).astype(F32)

    gain_pair = cube_sum(jnp.stack([gain_one_part, gain_two_part]))
    total = gain_pair
    for s in range(1, lax.axis_size("uly")):
        total = total + shift(gain_pair, s)

    return (
        block_out,
        restore(jnp.stack(input_grads)),
        total[0],
        first_sum[:, :qk],
        first_sum[:, qk : 2 * qk],
        jnp.concatenate([first_sum[:, 2 * qk :], second_sum[:, :cut_v]], axis=1),
        second_sum[:, cut_v:],
        output_grad,
        total[1],
        up_grad,
        down_grad,
    )


def solution(mesh):
    rows = P(None, ("blk", "uly"), None)
    gain, wide, tall = P("blk"), P("blk", "uly"), P("uly", "blk")
    return jax.shard_map(
        body,
        mesh=mesh,
        in_specs=(rows, gain, wide, wide, wide, wide, tall, gain, wide, tall, P(), P(), rows),
        out_specs=(rows, rows, gain, wide, wide, wide, wide, tall, gain, wide, tall),
        check_vma=False,
    )
```

```python
import functools

import jax
import jax.numpy as jnp
from jax import lax
from jax.experimental import pallas as pl
from jax.experimental.pallas import tpu as pltpu
from jax.sharding import Mesh
from jax.sharding import PartitionSpec as P

EPSILON = 1e-05
BF = jnp.bfloat16
F32 = jnp.float32
AXES = ("chip", "core", "uly")
BLK = ("chip", "core")
MESH = pl.DeviceIdType.MESH
VMEM_LIMIT = 60 * 1024 * 1024


def dot_nn(left, right, kind=F32):
    return jnp.dot(left, right, preferred_element_type=F32).astype(kind)


def dot_tn(left, right, kind=F32):
    return lax.dot_general(
        left, right, (((0,), (0,)), ((), ())), preferred_element_type=F32
    ).astype(kind)


def dot_nt(left, right, kind=F32):
    return lax.dot_general(
        left, right, (((1,), (1,)), ((), ())), preferred_element_type=F32
    ).astype(kind)


def block_index():
    return lax.axis_index("chip") * 2 + lax.axis_index("core")


def block_count():
    return lax.axis_size("chip") * 2


def swap(array, mask):
    if mask == 1:
        return lax.ppermute(array, "core", [(0, 1), (1, 0)])
    count = lax.axis_size("chip")
    return lax.ppermute(array, "chip", [(b, b ^ (mask // 2)) for b in range(count)])


def shift(array, step):
    count = lax.axis_size("uly")
    return lax.ppermute(array, "uly", [(z, (z + step) % count) for z in range(count)])


def is_cube():
    return lax.axis_size("chip") == 4 and lax.axis_size("uly") == 4


def masks():
    return [2 * k + j for j in range(2) for k in range(4)]


def plane_gather(first, second):
    first_x = swap(first, 2)
    second_y = swap(second, 4)
    first_y, first_xy = swap(first, 4), swap(first_x, 4)
    second_x, second_xy = swap(second, 2), swap(second_y, 2)
    return [first, first_x, first_y, first_xy], [second, second_x, second_y, second_xy]


def exchange(pieces):
    if not is_cube():
        return [lax.all_gather(p, BLK) for p in pieces]
    half = len(pieces) // 2
    a, b = plane_gather(jnp.stack(pieces[:half]), jnp.stack(pieces[half:]))
    got = []
    for four in (a, b):
        full = jnp.stack(four + [swap(p, 1) for p in four])
        got += [full[:, i] for i in range(full.shape[1])]
    return got


def spread(rows):
    return lax.all_gather(rows, "uly", axis=1, tiled=True)


def collect(partial):
    return lax.psum_scatter(partial.astype(BF), "uly", scatter_dimension=1, tiled=True).astype(F32)


def core_cut(array, dim):
    core = lax.axis_index("core")
    half = array.shape[dim] // 2
    own = lax.dynamic_slice_in_dim(array, core * half, half, dim)
    other = lax.dynamic_slice_in_dim(array, (1 - core) * half, half, dim)
    return own, other


def core_join(own, other, dim):
    first = lax.axis_index("core") == 0
    return jnp.concatenate([jnp.where(first, own, other), jnp.where(first, other, own)], axis=dim)


def feed_weights(up_shard, down_shard):
    own, other = core_cut(up_shard, 1)
    up = core_join(own, swap(other, 1), 0)
    own, other = core_cut(down_shard, 0)
    down = core_join(own, swap(other, 1), 1)
    pair = lax.all_gather(jnp.stack([up, down.T]), ("chip", "uly"), axis=0, tiled=False)
    chips, count = lax.axis_size("chip"), lax.axis_size("uly")
    rows, hidden = up.shape
    pair = pair.reshape(chips, count, 2, rows, hidden)
    return pair


def feed_reduce(up_grad, down_grad):
    pair = jnp.stack([up_grad, down_grad], axis=2)
    chips, count = pair.shape[:2]
    pair = pair.reshape(chips * count * 2, *pair.shape[3:])
    total = lax.psum_scatter(pair, ("chip", "uly"), scatter_dimension=0, tiled=True)
    half = total.shape[1] // 2
    own, other = core_cut(total, 1)
    both_halves = core_join(own, swap(other, 1), 2).astype(F32)
    return both_halves[0], both_halves[1].T


def normed(values):
    center = values - jnp.mean(values, axis=-1, keepdims=True)
    scale = lax.rsqrt(jnp.mean(center * center, axis=-1, keepdims=True) + EPSILON)
    return center * scale, scale


def norm_back(grad, hat, scale):
    return scale * (
        grad
        - jnp.mean(grad, axis=-1, keepdims=True)
        - hat * jnp.mean(grad * hat, axis=-1, keepdims=True)
    )


GELU_A = 0.7978845608028654
GELU_B = 0.044715


def gelu_pair(u):
    square = u * u
    tanh = jnp.tanh(GELU_A * u * (1.0 + GELU_B * square))
    slope = 0.5 * (1.0 + tanh) + 0.5 * u * (1.0 - tanh * tanh) * GELU_A * (
        1.0 + 3.0 * GELU_B * square
    )
    return 0.5 * u * (1.0 + tanh), slope


def segment_ids(positions, lengths_row):
    count = lengths_row.shape[0]
    before = jnp.arange(count)[None, :] < jnp.arange(count)[:, None]
    bounds = jnp.sum(jnp.where(before, lengths_row[None, :], 0), axis=1)
    return jnp.sum((bounds[None, :] <= positions[:, None]).astype(jnp.int32), axis=1)


def decay_parts(rates, lengths_row, length):
    me = block_index()
    count = block_count()
    places = jnp.arange(length, dtype=jnp.int32)
    seg = segment_ids(me * length + places, lengths_row)
    ends = segment_ids((jnp.arange(count, dtype=jnp.int32) + 1) * length - 1, lengths_row)
    seg_prev = segment_ids(jnp.reshape(me * length - 1, (1,)), lengths_row)[0]
    offset = places[:, None] - places[None, :]
    causal = (offset >= 0) & (seg[:, None] == seg[None, :])
    far = jnp.maximum(offset, 0).astype(F32)
    inner = jnp.where(causal[None], jnp.exp(-rates[:, None, None] * far[None]), 0.0)
    at = places.astype(F32)
    entry = jnp.where(seg == seg_prev, jnp.exp(-rates[:, None] * (at + 1.0)), 0.0)
    leave = jnp.where(seg == seg[length - 1], jnp.exp(-rates[:, None] * (length - 1.0 - at)), 0.0)
    if is_cube():
        source = me ^ jnp.asarray(masks(), jnp.int32)
    else:
        source = jnp.arange(count, dtype=jnp.int32)
    end_of = ends[source]
    end_before = jnp.where(source > 0, ends[jnp.maximum(source - 1, 0)], 0)
    past = jnp.maximum(me - 1 - source, 0).astype(F32)
    ahead = jnp.maximum(source - 1 - me, 0).astype(F32)
    from_past = jnp.where(
        (source < me) & (end_of == seg_prev), jnp.exp(-rates[:, None] * (length * past)), 0.0
    )
    from_ahead = jnp.where(
        (source > me) & (end_before == ends[me]), jnp.exp(-rates[:, None] * (length * ahead)), 0.0
    )
    return inner, entry[:, :, None], leave[:, :, None], from_past, from_ahead


def state_sum(weights, states):
    return jnp.einsum("hb,bhde->hde", weights, states.astype(F32))


def retention_state(heads, leave):
    return jnp.stack(
        [
            dot_tn((k.astype(F32) * leave[h]).astype(BF), v, BF)
            for h, (q, k, v) in enumerate(heads)
        ]
    )


def retention(heads, parts, state):
    inner, entry = parts[0], parts[1]
    out = []
    for h, (q, k, v) in enumerate(heads):
        scores = (dot_nt(q, k) * inner[h]).astype(BF)
        out.append(dot_nn(scores, v) + entry[h] * dot_nn(q, state[h].astype(BF)))
    return out


def mix(gate, retained):
    out = []
    for h, r in enumerate(retained):
        g = gate[:, h * r.shape[1] : (h + 1) * r.shape[1]]
        out.append((g * jax.nn.sigmoid(g) * normed(r)[0]).astype(BF))
    return jnp.concatenate(out, axis=1)


def mix_back(gate, retained, grad_mixed):
    grad_gate, grad_retained = [], []
    for h, r in enumerate(retained):
        cols = slice(h * r.shape[1], (h + 1) * r.shape[1])
        g, gm = gate[:, cols], grad_mixed[:, cols]
        sigma = jax.nn.sigmoid(g)
        hat, scale = normed(r)
        grad_gate.append((gm * hat * (sigma + g * sigma * (1.0 - sigma))).astype(BF))
        grad_retained.append(norm_back(gm * g * sigma, hat, scale).astype(BF))
    return jnp.concatenate(grad_gate, axis=1), grad_retained


def retention_back(heads, parts, state, grad_retained, grad_state):
    inner, entry, leave = parts[0], parts[1], parts[2]
    grads = []
    for h, (q, k, v) in enumerate(heads):
        gr = grad_retained[h]
        scores = (dot_nt(q, k) * inner[h]).astype(BF)
        pulls = (dot_nt(gr, v) * inner[h]).astype(BF)
        gs, st = grad_state[h].astype(BF), state[h].astype(BF)
        gq = dot_nn(pulls, k) + entry[h] * dot_nt(gr, st)
        gk = dot_tn(pulls, q) + leave[h] * dot_nt(v, gs)
        gv = dot_tn(scores, gr) + leave[h] * dot_nn(k, gs)
        grads.append((gq.astype(BF), gk.astype(BF), gv.astype(BF)))
    return grads


def vmem():
    return pl.BlockSpec(memory_space=pltpu.VMEM)


def anywhere():
    return pl.BlockSpec(memory_space=pl.ANY)


def greet(plane=False, line=False, cores=False, pair=False):
    barrier = pltpu.get_barrier_semaphore()
    chip, core, z = (lax.axis_index(a) for a in AXES)
    others = []
    if plane:
        others += [{"chip": chip ^ 1}, {"chip": chip ^ 2}]
    if cores:
        others.append({"core": 1 - core})
    if pair:
        others.append({"uly": z ^ 1})
    for to in others:
        pl.semaphore_signal(barrier, inc=1, device_id=to, device_id_type=MESH)
    count = len(others)
    if line:
        last = lax.axis_size("uly") - 1

        @pl.when(z > 0)
        def _():
            pl.semaphore_signal(barrier, inc=1, device_id={"uly": z - 1}, device_id_type=MESH)

        @pl.when(z < last)
        def _():
            pl.semaphore_signal(barrier, inc=1, device_id={"uly": z + 1}, device_id_type=MESH)

        count = count + jnp.where(z > 0, 1, 0) + jnp.where(z < last, 1, 0)
    pl.semaphore_wait(barrier, count)


class PlaneGather:
    def __init__(self, own, at, x_first, send, recv, cores=True):
        chip, core = lax.axis_index("chip"), lax.axis_index("core")
        x, y, other = {"chip": chip ^ 1}, {"chip": chip ^ 2}, {"core": 1 - core}

        def copy(i, src, place, to):
            return pltpu.make_async_remote_copy(
                src_ref=src,
                dst_ref=at(place),
                send_sem=send.at[i],
                recv_sem=recv.at[i],
                device_id=to,
                device_id_type=MESH,
            )

        self.x_first = x_first
        self.copies = [
            copy(0, own, 1, x),
            copy(1, own, 2, y),
            copy(2, at(1), 3, y) if x_first else copy(2, at(2), 3, x),
        ]
        self.cores = cores
        if cores:
            self.copies += [
                copy(3, own, 4, other),
                copy(4, at(1), 5, other),
                copy(5, at(2), 6, other),
                copy(6, at(3), 7, other),
            ]

    def start(self):
        for i in (0, 1) if self.x_first else (1, 0):
            self.copies[i].start()
        if self.cores:
            self.copies[3].start()

    def near(self):
        first = 0 if self.x_first else 1
        self.copies[first].wait_recv()
        self.copies[2].start()
        if self.cores:
            self.copies[4 + first].start()

    def far(self):
        second = 1 if self.x_first else 0
        self.copies[second].wait_recv()
        if self.cores:
            self.copies[4 + second].start()

    def corner(self):
        self.copies[2].wait_recv()
        if self.cores:
            self.copies[6].start()

    def finish(self):
        for c in self.copies[3:]:
            c.wait_recv()
        for c in self.copies:
            c.wait_send()


class LineGather:
    def __init__(self, slots, send, recv):
        self.z = lax.axis_index("uly")
        self.last = lax.axis_size("uly") - 1
        self.slots, self.send, self.recv = slots, send, recv

    def copy(self, right, d):
        z, last = self.z, self.last
        at = jnp.maximum(z - d, 0) if right else jnp.minimum(z + d, last)
        to = jnp.minimum(z + 1, last) if right else jnp.maximum(z - 1, 0)
        way = 0 if right else 1
        return pltpu.make_async_remote_copy(
            src_ref=self.slots.at[at],
            dst_ref=self.slots.at[at],
            send_sem=self.send.at[way, d],
            recv_sem=self.recv.at[way, d],
            device_id={"uly": to},
            device_id_type=MESH,
        )

    def pass_on(self, d):
        z, last = self.z, self.last

        @pl.when((z - d >= 0) & (z < last))
        def _():
            self.copy(True, d).start()

        @pl.when((z + d <= last) & (z > 0))
        def _():
            self.copy(False, d).start()

    def take(self, d, then):
        z, last = self.z, self.last

        @pl.when(z - d >= 0)
        def _():
            self.copy(True, d - 1).wait_recv()

        @pl.when(z + d <= last)
        def _():
            self.copy(False, d - 1).wait_recv()

        if d < last:
            self.pass_on(d)

        @pl.when(z - d >= 0)
        def _():
            then(jnp.maximum(z - d, 0))

        @pl.when(z + d <= last)
        def _():
            then(jnp.minimum(z + d, last))

    def finish(self):
        z, last = self.z, self.last
        for d in range(last):

            @pl.when((z - d >= 0) & (z < last))
            def _():
                self.copy(True, d).wait_send()

            @pl.when((z + d <= last) & (z > 0))
            def _():
                self.copy(False, d).wait_send()


class LineReduce:
    def __init__(self, make, out, held, came, send, recv):
        self.z = lax.axis_index("uly")
        self.last = lax.axis_size("uly") - 1
        self.make, self.out, self.held, self.came = make, out, held, came
        self.send, self.recv = send, recv

    def copy(self, right, d):
        z, last = self.z, self.last
        way = 0 if right else 1
        to = jnp.minimum(z + 1, last) if right else jnp.maximum(z - 1, 0)
        return pltpu.make_async_remote_copy(
            src_ref=self.held.at[way, d - 1],
            dst_ref=self.came.at[way, d - 1],
            send_sem=self.send.at[way, d - 1],
            recv_sem=self.recv.at[way, d - 1],
            device_id={"uly": to},
            device_id_type=MESH,
        )

    def step(self, d):
        z, last = self.z, self.last
        for right in (True, False):
            way = 0 if right else 1
            valid = (z + d <= last) if right else (z - d >= 0)
            more = (z > 0) if right else (z < last)
            to = jnp.minimum(z + d, last) if right else jnp.maximum(z - d, 0)

            @pl.when(valid)
            def _():
                self.make(to, self.held.at[way, d - 1])

                if d < last:

                    @pl.when(more)
                    def _():
                        self.copy(right, d + 1).wait_recv()
                        self.held[way, d - 1] = (
                            self.held[way, d - 1].astype(F32) + self.came[way, d].astype(F32)
                        ).astype(BF)

                self.copy(right, d).start()

    def close(self):
        z, last = self.z, self.last
        self.make(z, self.out)

        @pl.when(z > 0)
        def _():
            self.copy(True, 1).wait_recv()
            self.out[...] += self.came[0, 0].astype(F32)

        @pl.when(z < last)
        def _():
            self.copy(False, 1).wait_recv()
            self.out[...] += self.came[1, 0].astype(F32)

        for d in range(1, last + 1):

            @pl.when(z + d <= last)
            def _():
                self.copy(True, d).wait_send()

            @pl.when(z - d >= 0)
            def _():
                self.copy(False, d).wait_send()


def chunk_of(place, width):
    chip, core = lax.axis_index("chip"), lax.axis_index("core")
    block = (chip ^ (place % 4)) * 2 + (core ^ (place // 4))
    return pl.ds(pl.multiple_of(block * width, width), width)


def chip_order(place, width):
    core = lax.axis_index("core")
    return pl.ds(pl.multiple_of((place % 4) * (2 * width) + (core ^ (place // 4)) * width, width), width)


def project_kernel(
    tok_ref,
    gain_ref,
    first_hbm,
    second_hbm,
    out_hbm,
    one_ref,
    first_ref,
    high_ref,
    gate_ref,
    w_first_hbm,
    w_second_hbm,
    w_out_hbm,
    gains_ref,
    slots,
    wa,
    wb,
    gains,
    psend,
    precv,
    zsend,
    zrecv,
    lsem,
):
    z = lax.axis_index("uly")
    rows = tok_ref.shape[0] // 2
    width = tok_ref.shape[1]
    piece = width // 8
    greet(plane=True, line=True, cores=True)
    items = [
        PlaneGather(gain_ref, lambda p: gains.at[p], True, psend.at[0], precv.at[0]),
        PlaneGather(
            first_hbm,
            lambda p: wa.at[pl.ds(p * piece, piece)],
            True,
            psend.at[1],
            precv.at[1],
        ),
        PlaneGather(
            second_hbm,
            lambda p: wb.at[pl.ds(p * piece, piece)],
            False,
            psend.at[2],
            precv.at[2],
        ),
    ]
    half = out_hbm.shape[0] // 2
    for i in range(2):
        part = pl.ds(i * half, half)
        items.append(
            PlaneGather(
                out_hbm.at[part],
                lambda p, part=part: w_out_hbm.at[part, pl.ds(p * piece, piece)],
                i == 0,
                psend.at[3 + i],
                precv.at[3 + i],
            )
        )
    line = LineGather(slots, zsend, zrecv)
    slots[z] = tok_ref[...]
    line.pass_on(0)
    for item in items[:3]:
        item.start()
    local = [
        pltpu.make_async_copy(first_hbm, wa.at[pl.ds(0, piece)], lsem.at[0]),
        pltpu.make_async_copy(second_hbm, wb.at[pl.ds(0, piece)], lsem.at[1]),
        pltpu.make_async_copy(out_hbm, w_out_hbm.at[:, pl.ds(0, piece)], lsem.at[2]),
    ]
    for c in local:
        c.start()
    gains[0] = gain_ref[...]
    items[0].near()
    items[0].far()
    items[0].corner()
    items[0].finish()
    gains_ref[...] = gains[...]

    def normalize(slot):
        step = 32
        for m in range(2):

            @pl.loop(0, rows // step)
            def _(i):
                at = pl.multiple_of(i * step, step)
                v = slots[slot, pl.ds(m * rows + at, step), :].astype(F32)
                mean = jnp.mean(v, axis=-1, keepdims=True)
                center = v - mean
                scale = lax.rsqrt(jnp.mean(center * center, axis=-1, keepdims=True) + EPSILON)
                to = pl.ds(pl.multiple_of(slot * rows + at, step), step)
                for p in range(8):
                    src = slots[slot, pl.ds(m * rows + at, step), chunk_of(p, piece)].astype(F32)
                    one_ref[m, to, pl.ds(p * piece, piece)] = (
                        (src - mean) * scale * gains[p, 0:1, :].astype(F32)
                    ).astype(BF)

    normalize(z)
    line.take(1, normalize)
    items[1].near()
    items[2].near()
    for item in items[3:]:
        item.start()
    items[1].far()
    items[2].far()
    line.take(2, normalize)
    items[1].corner()
    items[2].corner()
    for item in items[3:]:
        item.near()
    line.take(3, normalize)
    for item in items[1:3]:
        item.finish()
    local[0].wait()
    local[1].wait()
    outs = [
        pltpu.make_async_copy(wa, w_first_hbm, lsem.at[3]),
        pltpu.make_async_copy(wb, w_second_hbm, lsem.at[4]),
    ]
    for c in outs:
        c.start()
    tile = 512
    for m in range(2):

        @pl.loop(0, wa.shape[1] // tile)
        def _(n):
            cols = pl.ds(pl.multiple_of(n * tile, tile), tile)
            first_ref[m, :, cols] = jnp.dot(
                one_ref[m], wa[:, cols], preferred_element_type=F32
            ).astype(BF)

        high = high_ref.shape[2]

        @pl.loop(0, high // tile)
        def _(n):
            cols = pl.ds(pl.multiple_of(n * tile, tile), tile)
            high_ref[m, :, cols] = jnp.dot(
                one_ref[m], wb[:, cols], preferred_element_type=F32
            ).astype(BF)

        @pl.loop(0, gate_ref.shape[2] // tile)
        def _(n):
            cols = pl.ds(pl.multiple_of(n * tile, tile), tile)
            from_ = pl.ds(pl.multiple_of(high + n * tile, tile), tile)
            gate_ref[m, :, cols] = jnp.dot(
                one_ref[m], wb[:, from_], preferred_element_type=F32
            )

    for item in items[3:]:
        item.far()
        item.corner()
        item.finish()
    line.finish()
    local[2].wait()
    for c in outs:
        c.wait()


def add_rows_kernel(
    x_ref,
    w_ref,
    up_hbm,
    down_hbm,
    out_ref,
    ups_hbm,
    downs_hbm,
    held,
    came,
    send,
    recv,
    psend,
    precv,
    lsem,
):
    rows = out_ref.shape[0] // 2
    width = out_ref.shape[1] // 8
    greet(plane=True, line=True)
    part = up_hbm.shape[0]

    def up_at(p):
        return ups_hbm.at[pl.ds(p * part, part)]

    def down_at(p):
        return downs_hbm.at[:, pl.ds(p * part, part)]

    items = [
        PlaneGather(up_hbm, up_at, True, psend.at[0], precv.at[0], False),
        PlaneGather(down_hbm, down_at, False, psend.at[1], precv.at[1], False),
    ]
    local = [
        pltpu.make_async_copy(up_hbm, up_at(0), lsem.at[0]),
        pltpu.make_async_copy(down_hbm, down_at(0), lsem.at[1]),
    ]

    def make(a, to):
        at = pl.ds(pl.multiple_of(a * rows, rows), rows)
        x = jnp.concatenate([x_ref[0, at, :], x_ref[1, at, :]], axis=0)

        @pl.loop(0, 8)
        def _(p):
            cols = w_ref[:, pl.ds(pl.multiple_of(p * width, width), width)]
            to[:, chip_order(p, width)] = jnp.dot(x, cols, preferred_element_type=F32).astype(
                to.dtype
            )

    line = LineReduce(make, out_ref, held, came, send, recv)
    for item in items:
        item.start()
    line.step(3)
    for c in local:
        c.start()
    for item in items:
        item.near()
    line.step(2)
    for item in items:
        item.far()
    line.step(1)
    line.close()
    for item in items:
        item.corner()
    for item in items:
        item.finish()
    for c in local:
        c.wait()


def fan_out_kernel(
    rows_ref,
    w_ref,
    up_hbm,
    down_hbm,
    wide_ref,
    grad_ref,
    up_ref,
    down_ref,
    slots,
    ordered,
    near_up,
    near_down,
    came_up,
    came_down,
    send,
    recv,
    psend,
    precv,
    lsem,
):
    z = lax.axis_index("uly")
    rows = rows_ref.shape[0] // 2
    width = rows_ref.shape[1] // 8
    greet(plane=True, line=True)
    line = LineGather(slots, send, recv)
    slots[z] = rows_ref[...]
    line.pass_on(0)
    local = [
        pltpu.make_async_copy(up_hbm, near_up, lsem.at[0]),
        pltpu.make_async_copy(down_hbm, near_down, lsem.at[1]),
    ]
    for c in local:
        c.start()
    groups = [
        PlaneReduce(None, near_up, came_up, True, psend.at[0], precv.at[0]),
        PlaneReduce(None, near_down, came_down, False, psend.at[1], precv.at[1]),
    ]
    for c in local:
        c.wait()
    for g in groups:
        g.start_first()

    def multiply(slot):
        at = pl.ds(pl.multiple_of(slot * rows, rows), rows)
        for m in range(2):
            wide_ref[m, at, :] = slots[slot, m * rows : (m + 1) * rows, :]
        for p in range(8):
            ordered[:, p * width : (p + 1) * width] = slots[slot, :, chip_order(p, width)]
        tile = 256

        @pl.loop(0, w_ref.shape[0] // tile)
        def _(n):
            part = pl.ds(pl.multiple_of(n * tile, tile), tile)
            product = dot_nt(ordered[...], w_ref[part, :])
            for m in range(2):
                grad_ref[m, at, part] = product[m * rows : (m + 1) * rows]

    multiply(z)
    line.take(1, multiply)
    for g in groups:
        g.first_sums(0)
    line.take(2, multiply)
    for g in groups:
        g.first_sums(1)
    line.take(3, multiply)
    groups[0].finish(up_ref)
    groups[1].finish(down_ref)
    line.finish()


def feed_kernel(
    hid_ref,
    douts_ref,
    gain_ref,
    ups_ref,
    downs_ref,
    out_ref,
    grad_ref,
    gain_grad_ref,
    up_grad_ref,
    down_grad_ref,
    two,
    act,
    gu,
    sums,
    held,
    came,
    send,
    recv,
):
    core, z = lax.axis_index("core"), lax.axis_index("uly")
    rows, width = hid_ref.shape
    hidden = ups_ref.shape[1]
    other, pair = {"core": 1 - core}, {"uly": z ^ 1}
    greet(cores=True, pair=True)

    def group(g):
        return pl.ds(g * rows, rows)

    def copy(i, src, dst, to):
        return pltpu.make_async_remote_copy(
            src_ref=src,
            dst_ref=dst,
            send_sem=send.at[i],
            recv_sem=recv.at[i],
            device_id=to,
            device_id_type=MESH,
        )

    step = 32

    @pl.loop(0, rows // step)
    def _(i):
        at = pl.ds(pl.multiple_of(i * step, step), step)
        hat, _scale = normed(hid_ref[at, :])
        two[at, :] = (hat * gain_ref[...]).astype(BF)

    to_pair = copy(0, two.at[group(0)], two.at[group(2)], pair)
    to_other = copy(1, two.at[group(0)], two.at[group(1)], other)
    through = copy(2, two.at[group(2)], two.at[group(3)], other)
    to_pair.start()
    to_other.start()

    def work(g):
        tile = 256

        @pl.loop(0, hidden // tile)
        def _(n):
            cols = pl.ds(pl.multiple_of(n * tile, tile), tile)
            upward = jnp.dot(two[group(g), :], ups_ref[:, cols], preferred_element_type=F32)
            value, slope = gelu_pair(upward)
            act[group(g), cols] = value.astype(BF)
            pulled = dot_nt(douts_ref[group(g), :], downs_ref[cols, :])
            gu[group(g), cols] = (pulled * slope).astype(BF)

        tile = 512

        @pl.loop(0, width // tile)
        def _(n):
            cols = pl.ds(pl.multiple_of(n * tile, tile), tile)
            back = dot_nt(gu[group(g), :], ups_ref[cols, :])
            down = jnp.dot(act[group(g), :], downs_ref[:, cols], preferred_element_type=F32)
            if g == 0:
                sums[0, :, cols] = back
                sums[1, :, cols] = down
            else:
                held[g - 1, 0, :, cols] = back.astype(BF)
                held[g - 1, 1, :, cols] = down.astype(BF)

    returns = [copy(3 + i, held.at[0, i], came.at[0, i], other) for i in range(2)]
    returns += [copy(5 + i, held.at[2, i], came.at[1, i], other) for i in range(2)]
    last = [copy(7 + i, held.at[1, i], came.at[2, i], pair) for i in range(2)]

    work(0)
    to_other.wait_recv()
    work(1)
    for c in returns[:2]:
        c.start()
    to_pair.wait_recv()
    through.start()
    work(2)
    through.wait_recv()
    work(3)
    for c in returns[2:]:
        c.start()
    for i in range(2):
        returns[2 + i].wait_recv()

        @pl.loop(0, rows // step)
        def _(r):
            at = pl.ds(pl.multiple_of(r * step, step), step)
            held[1, i, at, :] = (
                held[1, i, at, :].astype(F32) + came[1, i, at, :].astype(F32)
            ).astype(BF)

        last[i].start()
    tile = 512

    @pl.loop(0, width // tile)
    def _(n):
        cols = pl.ds(pl.multiple_of(n * tile, tile), tile)
        up_grad_ref[n] = dot_tn(two[:, cols], gu[...], BF)
        down_grad_ref[n] = dot_tn(act[...], douts_ref[:, cols], BF)

    for i in range(2):
        returns[i].wait_recv()
    last[0].wait_recv()
    gain_grad_ref[...] = jnp.zeros_like(gain_grad_ref)

    @pl.loop(0, rows // step)
    def _(r):
        at = pl.ds(pl.multiple_of(r * step, step), step)
        back = sums[0, at, :] + came[0, 0, at, :].astype(F32) + came[2, 0, at, :].astype(F32)
        hat, scale = normed(hid_ref[at, :])
        gain_grad_ref[...] += jnp.sum(back * hat, axis=0, keepdims=True)
        grad_ref[at, :] = douts_ref[at, :].astype(F32) + norm_back(
            back * gain_ref[...], hat, scale
        )

    last[1].wait_recv()

    @pl.loop(0, rows // step)
    def _(r):
        at = pl.ds(pl.multiple_of(r * step, step), step)
        out_ref[at, :] = (
            hid_ref[at, :]
            + sums[1, at, :]
            + came[0, 1, at, :].astype(F32)
            + came[2, 1, at, :].astype(F32)
        ).astype(BF)

    for c in [to_pair, to_other, through] + returns + last:
        c.wait_send()


class PlaneReduce:
    def __init__(self, far, near, came, x_first, send, recv):
        chip, core = lax.axis_index("chip"), lax.axis_index("core")
        x, y, other = {"chip": chip ^ 1}, {"chip": chip ^ 2}, {"core": 1 - core}
        self.near, self.came, self.x_first = near, came, x_first

        def copy(i, src, to):
            return pltpu.make_async_remote_copy(
                src_ref=src,
                dst_ref=came.at[i],
                send_sem=send.at[i],
                recv_sem=recv.at[i],
                device_id=to,
                device_id_type=MESH,
            )

        self.away = (1, 3) if x_first else (2, 3)
        self.stay = (0, 2) if x_first else (0, 1)
        one, two = (x, y) if x_first else (y, x)
        self.cores = 4 if far else 0
        self.copies = [copy(i, far(4 + i), other) for i in range(self.cores)]
        self.copies += [copy(self.cores + i, near.at[self.away[i]], one) for i in range(2)]
        self.copies.append(copy(self.cores + 2, near.at[self.stay[1]], two))

    def start(self):
        for i in (3, self.away[0], self.stay[1], 0):
            self.copies[i].start()

    def add(self, place, i):
        step = 64

        @pl.loop(0, self.near.shape[1] // step)
        def _(r):
            at = pl.ds(pl.multiple_of(r * step, step), step)
            self.near[place, at, :] = (
                self.near[place, at, :].astype(F32) + self.came[i, at, :].astype(F32)
            ).astype(BF)

    def core_sums(self):
        for i in (1, 0):
            p = self.away[i]
            self.copies[p].wait_recv()
            self.add(p, p)
            self.copies[4 + i].start()
        for p in (self.stay[1], self.stay[0]):
            self.copies[p].wait_recv()
            self.add(p, p)

    def start_first(self):
        for i in (1, 0):
            self.copies[self.cores + i].start()

    def first_sums(self, step):
        i = 1 - step
        self.copies[self.cores + i].wait_recv()
        self.add(self.stay[i], self.cores + i)
        if i == 1:
            self.copies[self.cores + 2].start()

    def finish(self, out_ref):
        self.copies[self.cores + 2].wait_recv()
        self.add(self.stay[0], self.cores + 2)
        out_ref[...] = self.near[0]
        for c in self.copies:
            c.wait_send()


def close_rows_kernel(
    xa_ref,
    xb_ref,
    wa_ref,
    wb_ref,
    ga_hbm,
    gb_hbm,
    go_hbm,
    out_ref,
    sum_a_ref,
    sum_b_ref,
    sum_o_ref,
    held,
    came,
    near_a,
    near_b,
    near_o,
    came_a,
    came_b,
    came_o,
    send,
    recv,
    psend,
    precv,
    lsem,
):
    rows = out_ref.shape[0] // 2
    width = out_ref.shape[1] // 8
    greet(plane=True, line=True, cores=True)
    groups = []
    local = []
    for i, (hbm, near, got, x_first) in enumerate(
        ((ga_hbm, near_a, came_a, True), (gb_hbm, near_b, came_b, False), (go_hbm, near_o, came_o, True))
    ):
        groups.append(
            PlaneReduce(
                lambda p, hbm=hbm: hbm.at[p], near, got, x_first, psend.at[i], precv.at[i]
            )
        )
        local.append(pltpu.make_async_copy(hbm.at[pl.ds(0, 4)], near, lsem.at[i]))
    for g in groups:
        g.start()
    for c in local:
        c.start()

    def make(a, to):
        at = pl.ds(pl.multiple_of(a * rows, rows), rows)
        xa = jnp.concatenate([xa_ref[0, at, :], xa_ref[1, at, :]], axis=0)
        xb = jnp.concatenate([xb_ref[0, at, :], xb_ref[1, at, :]], axis=0)

        @pl.loop(0, 8)
        def _(p):
            part = pl.ds(pl.multiple_of(p * width, width), width)
            to[:, chunk_of(p, width)] = (
                dot_nt(xa, wa_ref[part, :]) + dot_nt(xb, wb_ref[part, :])
            ).astype(to.dtype)

    line = LineReduce(make, out_ref, held, came, send, recv)
    line.step(3)
    for c in local:
        c.wait()
    for g in groups:
        g.core_sums()
    line.step(2)
    line.step(1)
    for g in groups:
        g.first_sums(0)
    for g in groups:
        g.first_sums(1)
    line.close()
    for g, out in zip(groups, (sum_a_ref, sum_b_ref, sum_o_ref)):
        g.finish(out)


def sems(*shape):
    return pltpu.SemaphoreType.DMA(shape)


def like(shape, kind):
    return jax.ShapeDtypeStruct(shape, kind)


def call(kernel, number, ins, outs, scratch, flops, *args):
    moved = sum(a.size * a.dtype.itemsize for a in args)
    return pl.pallas_call(
        kernel,
        out_shape=[like(s, t) for s, t, _ in outs],
        in_specs=ins,
        out_specs=[spec for _, _, spec in outs],
        scratch_shapes=scratch,
        compiler_params=pltpu.CompilerParams(
            collective_id=number, has_side_effects=True, vmem_limit_bytes=VMEM_LIMIT
        ),
        cost_estimate=pl.CostEstimate(flops=flops, bytes_accessed=moved, transcendentals=0),
    )(*args)


def project(tokens, gains, first, second, out_weight):
    micro, rows, width = tokens.shape
    count = lax.axis_size("uly")
    high = second.shape[1] - out_weight.shape[0]
    if not is_cube():
        full = lax.all_gather(gains, BLK, axis=1, tiled=True)
        w_first = lax.all_gather(first, BLK, axis=0, tiled=True)
        w_second = lax.all_gather(second, BLK, axis=0, tiled=True)
        w_out = lax.all_gather(out_weight, BLK, axis=1, tiled=True)
        one = (normed(spread(tokens).astype(F32))[0] * full[0].astype(F32)).astype(BF)
        return (
            one,
            dot_nn(one, w_first, BF),
            dot_nn(one, w_second[:, :high], BF),
            dot_nn(one, w_second[:, high:]),
            w_first,
            w_second,
            w_out,
            full,
        )
    wide = count * rows
    piece = width // 8
    padded = jnp.concatenate([gains, jnp.zeros((14, piece), BF)], axis=0)
    na, nb, no = first.shape[1], second.shape[1], out_weight.shape[0]
    out = call(
        project_kernel,
        0,
        [vmem(), vmem(), anywhere(), anywhere(), anywhere()],
        [
            ((micro, wide, width), BF, vmem()),
            ((micro, wide, na), BF, vmem()),
            ((micro, wide, high), BF, vmem()),
            ((micro, wide, nb - high), F32, vmem()),
            ((width, na), BF, anywhere()),
            ((width, nb), BF, anywhere()),
            ((no, width), BF, anywhere()),
            ((8, 16, piece), BF, vmem()),
        ],
        [
            pltpu.VMEM((count, micro * rows, width), BF),
            pltpu.VMEM((width, na), BF),
            pltpu.VMEM((width, nb), BF),
            pltpu.VMEM((8, 16, piece), BF),
            sems(5, 7),
            sems(5, 7),
            sems(2, count - 1),
            sems(2, count - 1),
            sems(5),
        ],
        2 * micro * wide * width * (na + nb),
        tokens.reshape(micro * rows, width),
        padded,
        first,
        second,
        out_weight,
    )
    got = out[7][:, :2]
    me = block_index()
    full = jnp.concatenate(
        [
            lax.dynamic_index_in_dim(got, ((me ^ b) & 1) * 4 + ((me ^ b) >> 1), 0, False)
            for b in range(8)
        ],
        axis=1,
    )
    return (*out[:7], full)


def line_scratch(count, rows, width):
    return [
        pltpu.VMEM((2, count - 1, rows, width), BF),
        pltpu.VMEM((2, count - 1, rows, width), BF),
    ]


def add_rows(mixed, w_out, up, down):
    micro, wide, hidden = mixed.shape
    count = lax.axis_size("uly")
    rows = wide // count
    width = w_out.shape[1]
    units = up.shape[1]
    out = call(
        add_rows_kernel,
        1,
        [vmem(), vmem(), anywhere(), anywhere()],
        [
            ((micro * rows, width), F32, vmem()),
            ((width, units), BF, anywhere()),
            ((units, width), BF, anywhere()),
        ],
        line_scratch(count, micro * rows, width)
        + [sems(2, count - 1)] * 2
        + [sems(2, 3), sems(2, 3), sems(2)],
        2 * micro * wide * hidden * width,
        mixed,
        w_out,
        up,
        down,
    )
    return out


def fan_out(rows_bf, w_out, up_grad, down_grad):
    own, width = rows_bf.shape
    micro, rows = 2, own // 2
    count = lax.axis_size("uly")
    hidden = w_out.shape[0]
    up_shape, down_shape = up_grad.shape[1:], down_grad.shape[1:]
    return call(
        fan_out_kernel,
        2,
        [vmem(), vmem(), anywhere(), anywhere()],
        [
            ((micro, count * rows, width), BF, vmem()),
            ((micro, count * rows, hidden), F32, vmem()),
            (up_shape, BF, vmem()),
            (down_shape, BF, vmem()),
        ],
        [
            pltpu.VMEM((count, own, width), BF),
            pltpu.VMEM((own, width), BF),
            pltpu.VMEM((4, *up_shape), BF),
            pltpu.VMEM((4, *down_shape), BF),
            pltpu.VMEM((3, *up_shape), BF),
            pltpu.VMEM((3, *down_shape), BF),
            sems(2, count - 1),
            sems(2, count - 1),
            sems(2, 3),
            sems(2, 3),
            sems(2),
        ],
        2 * micro * count * rows * hidden * width,
        rows_bf,
        w_out,
        up_grad,
        down_grad,
    )


def feed_all(hidden, douts, gain, ups, downs):
    own, width = hidden.shape
    units = ups.shape[1]
    return call(
        feed_kernel,
        4,
        [vmem()] * 5,
        [
            ((own, width), BF, vmem()),
            ((own, width), F32, vmem()),
            ((1, width), F32, vmem()),
            ((4, width // 4, units), BF, vmem()),
            ((4, units, width // 4), BF, vmem()),
        ],
        [
            pltpu.VMEM((4 * own, width), BF),
            pltpu.VMEM((4 * own, units), BF),
            pltpu.VMEM((4 * own, units), BF),
            pltpu.VMEM((2, own, width), F32),
            pltpu.VMEM((3, 2, own, width), BF),
            pltpu.VMEM((3, 2, own, width), BF),
            sems(9),
            sems(9),
        ],
        2 * 6 * 4 * own * units * width,
        hidden,
        douts,
        gain,
        ups,
        downs,
    )


def to_chips(array):
    if not is_cube():
        return array
    chip = lax.axis_index("chip")
    width = array.shape[-1] // 4
    return jnp.concatenate(
        [
            lax.dynamic_slice_in_dim(array, (chip ^ k) * width, width, array.ndim - 1)
            for k in range(4)
        ],
        axis=-1,
    )


def core_half(array, dim):
    own, other = core_cut(array, dim)
    return core_join(own, swap(other, 1), 1 - dim)


def feed_shards(up_shard, down_shard):
    up, down = core_half(up_shard, 1), core_half(down_shard, 0)
    return (
        jnp.concatenate([up, shift(up, 2)], axis=1),
        jnp.concatenate([down, shift(down, 2)], axis=0),
    )


def feed_gather(rows):
    count = lax.axis_size("uly")
    pair = lax.ppermute(rows, "uly", [(z, z ^ 1) for z in range(count)])
    return jnp.concatenate([rows, swap(rows, 1), pair, swap(pair, 1)], axis=0)


def feed_scatter(up_sum, down_sum):
    def settle(array, dim):
        half = array.shape[dim] // 2
        keep = lax.slice_in_dim(array, 0, half, axis=dim)
        away = lax.slice_in_dim(array, half, 2 * half, axis=dim)
        total = (keep.astype(F32) + shift(away, 2).astype(F32)).astype(BF)
        own, other = core_cut(total, 1 - dim)
        return core_join(own, swap(other, 1), dim).astype(F32)

    return settle(up_sum, 1), settle(down_sum, 0)


def middle(tokens, out_grad, gain_two, mixed, w_out, up_weight, down_weight):
    micro, rows, width = tokens.shape
    own = micro * rows
    if not is_cube():
        hidden = tokens.astype(F32) + collect(
            jnp.stack([dot_nn(mixed[m], w_out) for m in range(micro)])
        )
        pair = feed_weights(up_weight, down_weight)
        hat, scale = normed(hidden)
        two = (hat * gain_two).astype(BF)
        flat_two, flat_out = two.reshape(own, width), out_grad.reshape(own, width)
        two_both = jnp.concatenate([flat_two, swap(flat_two, 1)], axis=0)
        out_both = jnp.concatenate([flat_out, swap(flat_out, 1)], axis=0)
        down_rows, grad_two, up_part, down_part = feed(two_both, out_both, pair)
        grad_two = grad_two[:own] + swap(grad_two[own:].astype(BF), 1).astype(F32)
        down_rows = down_rows[:own] + swap(down_rows[own:].astype(BF), 1).astype(F32)
        up_grad, down_grad = feed_reduce(up_part, down_part)
        block_out = (hidden + down_rows.reshape(micro, rows, width)).astype(BF)
        grad_two = grad_two.reshape(micro, rows, width)
        gain_part = jnp.sum(grad_two * hat, axis=(0, 1))
        grad_hidden = out_grad.astype(F32) + norm_back(grad_two * gain_two, hat, scale)
        wide_att = spread(grad_hidden.astype(BF))
        grad_mixed = jnp.stack([dot_nt(wide_att[m], w_out) for m in range(micro)])
        return block_out, up_grad, down_grad, gain_part, grad_hidden, wide_att, grad_mixed
    up, down = feed_shards(up_weight, down_weight)
    douts = feed_gather(to_chips(out_grad).reshape(own, width))
    rows_sum, ups, downs = add_rows(mixed, w_out, up, down)
    hidden = to_chips(tokens).reshape(own, width).astype(F32) + rows_sum
    block_out, grad_hidden, gain_part, up_part, down_part = feed_all(
        hidden, douts, to_chips(gain_two[None]), ups, downs
    )
    wide_att, grad_mixed, up_sum, down_sum = fan_out(
        grad_hidden.astype(BF), w_out, up_part, down_part
    )
    up_grad, down_grad = feed_scatter(up_sum, down_sum)
    return (
        to_chips(block_out).reshape(micro, rows, width),
        up_grad,
        down_grad,
        to_chips(gain_part)[0],
        to_chips(grad_hidden).reshape(micro, rows, width),
        wide_att,
        grad_mixed,
    )


def close_rows(xa, xb, w_first, w_second, ga, gb, out_grad):
    micro, wide, na = xa.shape
    nb = xb.shape[2]
    width = w_first.shape[0]
    if not is_cube():
        partial = jnp.stack(
            [dot_nt(xa[m], w_first) + dot_nt(xb[m], w_second) for m in range(micro)]
        )
        return (
            collect(partial),
            lax.psum_scatter(ga, BLK, scatter_dimension=0, tiled=True),
            lax.psum_scatter(gb, BLK, scatter_dimension=0, tiled=True),
            lax.psum_scatter(out_grad, BLK, scatter_dimension=1, tiled=True),
        )
    count = lax.axis_size("uly")
    rows = wide // count
    piece = width // 8
    no = out_grad.shape[0]
    core = lax.axis_index("core")
    pieces_o = jnp.stack(
        [
            lax.dynamic_slice_in_dim(out_grad, (2 * k + (core ^ j)) * piece, piece, 1)
            for j in range(2)
            for k in range(4)
        ]
    )
    out = call(
        close_rows_kernel,
        3,
        [vmem()] * 4 + [anywhere()] * 3,
        [
            ((micro * rows, width), F32, vmem()),
            ((piece, na), BF, vmem()),
            ((piece, nb), BF, vmem()),
            ((no, piece), BF, vmem()),
        ],
        line_scratch(count, micro * rows, width)
        + [
            pltpu.VMEM((4, piece, na), BF),
            pltpu.VMEM((4, piece, nb), BF),
            pltpu.VMEM((4, no, piece), BF),
            pltpu.VMEM((7, piece, na), BF),
            pltpu.VMEM((7, piece, nb), BF),
            pltpu.VMEM((7, no, piece), BF),
            sems(2, count - 1),
            sems(2, count - 1),
            sems(3, 7),
            sems(3, 7),
            sems(3),
        ],
        2 * micro * wide * width * (na + nb),
        xa,
        xb,
        w_first,
        w_second,
        ga.reshape(8, piece, na),
        gb.reshape(8, piece, nb),
        pieces_o,
    )
    return out[0].reshape(micro, rows, width), out[1], out[2], out[3]


def feed(norm_two, out_rows, pair):
    chips, count, _, rows, hidden = pair.shape
    up = pair[:, :, 0].transpose(0, 2, 1, 3).reshape(chips * rows, count * hidden)
    down_t = pair[:, :, 1].transpose(0, 2, 1, 3).reshape(chips * rows, count * hidden)
    upward = dot_nn(norm_two, up)
    act, slope = gelu_pair(upward)
    act = act.astype(BF)
    grad_act = dot_nn(out_rows, down_t)
    grad_up = (grad_act * slope).astype(BF)

    def by_owner(grad):
        return grad.reshape(chips, rows, count, hidden).transpose(0, 2, 1, 3)

    return (
        dot_nt(act, down_t),
        dot_nt(grad_up, up),
        by_owner(dot_tn(norm_two, grad_up, BF)),
        by_owner(dot_tn(out_rows, act, BF)),
    )


def body(
    tokens,
    retain_gain,
    query_weight,
    key_weight,
    value_weight,
    gate_matrix,
    output_weight,
    feed_gain,
    up_weight,
    down_weight,
    decay_rate,
    lengths,
    out_grad,
):
    micro, rows, width = tokens.shape
    heads_here = decay_rate.shape[0] // lax.axis_size("uly")
    rates = lax.dynamic_slice_in_dim(decay_rate, lax.axis_index("uly") * heads_here, heads_here)
    qk = query_weight.shape[1]
    hd = qk // heads_here
    vd = value_weight.shape[1] // heads_here
    cut_v = value_weight.shape[1] // 2

    first = jnp.concatenate([query_weight, key_weight, value_weight[:, :cut_v]], axis=1)
    second = jnp.concatenate([value_weight[:, cut_v:], gate_matrix], axis=1)
    one, a, v_high, gate, w_first, w_second, w_out, gains = project(
        tokens, jnp.stack([retain_gain, feed_gain]), first, second, output_weight
    )
    gain_one, gain_two = gains[0].astype(F32), gains[1].astype(F32)
    length = one.shape[1]

    sets, parts, states = [], [], []
    for m in range(micro):
        values = jnp.concatenate([a[m, :, 2 * qk :], v_high[m]], axis=1)
        heads = [
            (
                a[m, :, h * hd : (h + 1) * hd],
                a[m, :, qk + h * hd : qk + (h + 1) * hd],
                values[:, h * vd : (h + 1) * vd],
            )
            for h in range(heads_here)
        ]
        part = decay_parts(rates, lengths[m], length)
        states.append(retention_state(heads, part[2]))
        sets.append(heads)
        parts.append(part)

    all_states = exchange(states)
    state_in, retained, mixed = [], [], []
    for m in range(micro):
        state = state_sum(parts[m][3], all_states[m])
        kept = retention(sets[m], parts[m], state)
        state_in.append(state)
        retained.append(kept)
        mixed.append(mix(gate[m], kept))
    mixed = jnp.stack(mixed)

    block_out, up_grad, down_grad, gain_two_part, grad_hidden, wide_att, grad_mixed = middle(
        tokens, out_grad, gain_two, mixed, w_out, up_weight, down_weight
    )

    grad_gates, grad_rets, grad_states = [], [], []
    for m in range(micro):
        gg, gr = mix_back(gate[m], retained[m], grad_mixed[m])
        grad_gates.append(gg)
        grad_rets.append(gr)
        grad_states.append(
            jnp.stack(
                [
                    dot_tn((q.astype(F32) * parts[m][1][h]).astype(BF), gr[h], BF)
                    for h, (q, k, v) in enumerate(sets[m])
                ]
            )
        )
    all_back = exchange(grad_states)

    def flat(array):
        return array.reshape(micro * length, array.shape[-1])

    out_part = dot_tn(flat(mixed), flat(wide_att), BF)

    xa, xb = [], []
    for m in range(micro):
        back = state_sum(parts[m][4], all_back[m])
        grads = retention_back(sets[m], parts[m], state_in[m], grad_rets[m], back)
        gq = jnp.concatenate([g[0] for g in grads], axis=1)
        gk = jnp.concatenate([g[1] for g in grads], axis=1)
        gv = jnp.concatenate([g[2] for g in grads], axis=1)
        xa.append(jnp.concatenate([gq, gk, gv[:, :cut_v]], axis=1))
        xb.append(jnp.concatenate([gv[:, cut_v:], grad_gates[m]], axis=1))
    xa, xb = jnp.stack(xa), jnp.stack(xb)
    grad_one, first_sum, second_sum, out_sum = close_rows(
        xa,
        xb,
        w_first,
        w_second,
        dot_tn(flat(one), flat(xa), BF),
        dot_tn(flat(one), flat(xb), BF),
        out_part,
    )
    hat, scale = normed(tokens.astype(F32))
    input_grad = grad_hidden + norm_back(grad_one * gain_one, hat, scale)
    gain_one_part = jnp.sum(grad_one * hat, axis=(0, 1))

    total = lax.psum_scatter(
        jnp.stack([gain_one_part, gain_two_part]), BLK, scatter_dimension=1, tiled=True
    )
    total = lax.psum(total, "uly")
    first_sum, second_sum = first_sum.astype(F32), second_sum.astype(F32)
    return (
        block_out,
        input_grad,
        total[0],
        first_sum[:, :qk],
        first_sum[:, qk : 2 * qk],
        jnp.concatenate([first_sum[:, 2 * qk :], second_sum[:, :cut_v]], axis=1),
        second_sum[:, cut_v:],
        out_sum.astype(F32),
        total[1],
        up_grad,
        down_grad,
    )


def solution(mesh):
    blocks, count = mesh.devices.shape
    split = Mesh(mesh.devices.reshape(blocks // 2, 2, count), AXES)
    rows = P(None, AXES, None)
    gain, wide, tall = P(BLK), P(BLK, "uly"), P("uly", BLK)
    return jax.shard_map(
        body,
        mesh=split,
        in_specs=(rows, gain, wide, wide, wide, wide, tall, gain, wide, tall, P(), P(), rows),
        out_specs=(rows, rows, gain, wide, wide, wide, wide, tall, gain, wide, tall),
        check_vma=False,
    )
```

```python
import functools

import jax
import jax.numpy as jnp
from jax import lax
from jax.experimental import pallas as pl
from jax.experimental.pallas import tpu as pltpu
from jax.sharding import Mesh
from jax.sharding import PartitionSpec as P

EPSILON = 1e-05
BF = jnp.bfloat16
F32 = jnp.float32
AXES = ("chip", "core", "uly")
BLK = ("chip", "core")
MESH = pl.DeviceIdType.MESH
VMEM_LIMIT = 62 * 1024 * 1024


def dot_nn(left, right, kind=F32):
    return jnp.dot(left, right, preferred_element_type=F32).astype(kind)


def dot_tn(left, right, kind=F32):
    return lax.dot_general(
        left, right, (((0,), (0,)), ((), ())), preferred_element_type=F32
    ).astype(kind)


def dot_nt(left, right, kind=F32):
    return lax.dot_general(
        left, right, (((1,), (1,)), ((), ())), preferred_element_type=F32
    ).astype(kind)


def block_index():
    return lax.axis_index("chip") * 2 + lax.axis_index("core")


def block_count():
    return lax.axis_size("chip") * 2


def swap(array, mask):
    if mask == 1:
        return lax.ppermute(array, "core", [(0, 1), (1, 0)])
    count = lax.axis_size("chip")
    return lax.ppermute(array, "chip", [(b, b ^ (mask // 2)) for b in range(count)])


def shift(array, step):
    count = lax.axis_size("uly")
    return lax.ppermute(array, "uly", [(z, (z + step) % count) for z in range(count)])


def is_cube():
    return lax.axis_size("chip") == 4 and lax.axis_size("uly") == 4


def masks():
    return [2 * k + j for j in range(2) for k in range(4)]


def plane_gather(first, second):
    first_x = swap(first, 2)
    second_y = swap(second, 4)
    first_y, first_xy = swap(first, 4), swap(first_x, 4)
    second_x, second_xy = swap(second, 2), swap(second_y, 2)
    return [first, first_x, first_y, first_xy], [second, second_x, second_y, second_xy]


def exchange(pieces):
    if not is_cube():
        return [lax.all_gather(p, BLK) for p in pieces]
    half = len(pieces) // 2
    a, b = plane_gather(jnp.stack(pieces[:half]), jnp.stack(pieces[half:]))
    got = []
    for four in (a, b):
        full = jnp.stack(four + [swap(p, 1) for p in four])
        got += [full[:, i] for i in range(full.shape[1])]
    return got


def spread(rows):
    return lax.all_gather(rows, "uly", axis=1, tiled=True)


def collect(partial):
    return lax.psum_scatter(partial.astype(BF), "uly", scatter_dimension=1, tiled=True).astype(F32)


def core_cut(array, dim):
    core = lax.axis_index("core")
    half = array.shape[dim] // 2
    own = lax.dynamic_slice_in_dim(array, core * half, half, dim)
    other = lax.dynamic_slice_in_dim(array, (1 - core) * half, half, dim)
    return own, other


def core_join(own, other, dim):
    first = lax.axis_index("core") == 0
    return jnp.concatenate([jnp.where(first, own, other), jnp.where(first, other, own)], axis=dim)


def feed_weights(up_shard, down_shard):
    own, other = core_cut(up_shard, 1)
    up = core_join(own, swap(other, 1), 0)
    own, other = core_cut(down_shard, 0)
    down = core_join(own, swap(other, 1), 1)
    pair = lax.all_gather(jnp.stack([up, down.T]), ("chip", "uly"), axis=0, tiled=False)
    chips, count = lax.axis_size("chip"), lax.axis_size("uly")
    rows, hidden = up.shape
    pair = pair.reshape(chips, count, 2, rows, hidden)
    return pair


def feed_reduce(up_grad, down_grad):
    pair = jnp.stack([up_grad, down_grad], axis=2)
    chips, count = pair.shape[:2]
    pair = pair.reshape(chips * count * 2, *pair.shape[3:])
    total = lax.psum_scatter(pair, ("chip", "uly"), scatter_dimension=0, tiled=True)
    half = total.shape[1] // 2
    own, other = core_cut(total, 1)
    both_halves = core_join(own, swap(other, 1), 2).astype(F32)
    return both_halves[0], both_halves[1].T


def normed(values):
    center = values - jnp.mean(values, axis=-1, keepdims=True)
    scale = lax.rsqrt(jnp.mean(center * center, axis=-1, keepdims=True) + EPSILON)
    return center * scale, scale


def norm_back(grad, hat, scale):
    return scale * (
        grad
        - jnp.mean(grad, axis=-1, keepdims=True)
        - hat * jnp.mean(grad * hat, axis=-1, keepdims=True)
    )


GELU_A = 0.7978845608028654
GELU_B = 0.044715


def gelu_pair(u):
    square = u * u
    tanh = jnp.tanh(GELU_A * u * (1.0 + GELU_B * square))
    slope = 0.5 * (1.0 + tanh) + 0.5 * u * (1.0 - tanh * tanh) * GELU_A * (
        1.0 + 3.0 * GELU_B * square
    )
    return 0.5 * u * (1.0 + tanh), slope


def segment_ids(positions, lengths_row):
    count = lengths_row.shape[0]
    before = jnp.arange(count)[None, :] < jnp.arange(count)[:, None]
    bounds = jnp.sum(jnp.where(before, lengths_row[None, :], 0), axis=1)
    return jnp.sum((bounds[None, :] <= positions[:, None]).astype(jnp.int32), axis=1)


def decay_parts(rates, lengths_row, length):
    me = block_index()
    count = block_count()
    places = jnp.arange(length, dtype=jnp.int32)
    seg = segment_ids(me * length + places, lengths_row)
    ends = segment_ids((jnp.arange(count, dtype=jnp.int32) + 1) * length - 1, lengths_row)
    seg_prev = segment_ids(jnp.reshape(me * length - 1, (1,)), lengths_row)[0]
    offset = places[:, None] - places[None, :]
    causal = (offset >= 0) & (seg[:, None] == seg[None, :])
    far = jnp.maximum(offset, 0).astype(F32)
    inner = jnp.where(causal[None], jnp.exp(-rates[:, None, None] * far[None]), 0.0)
    at = places.astype(F32)
    entry = jnp.where(seg == seg_prev, jnp.exp(-rates[:, None] * (at + 1.0)), 0.0)
    leave = jnp.where(seg == seg[length - 1], jnp.exp(-rates[:, None] * (length - 1.0 - at)), 0.0)
    if is_cube():
        source = me ^ jnp.asarray(masks(), jnp.int32)
    else:
        source = jnp.arange(count, dtype=jnp.int32)
    end_of = ends[source]
    end_before = jnp.where(source > 0, ends[jnp.maximum(source - 1, 0)], 0)
    past = jnp.maximum(me - 1 - source, 0).astype(F32)
    ahead = jnp.maximum(source - 1 - me, 0).astype(F32)
    from_past = jnp.where(
        (source < me) & (end_of == seg_prev), jnp.exp(-rates[:, None] * (length * past)), 0.0
    )
    from_ahead = jnp.where(
        (source > me) & (end_before == ends[me]), jnp.exp(-rates[:, None] * (length * ahead)), 0.0
    )
    return inner, entry[:, :, None], leave[:, :, None], from_past, from_ahead


def state_sum(weights, states):
    return jnp.einsum("hb,bhde->hde", weights, states.astype(F32))


def retention_state(heads, leave):
    return jnp.stack(
        [
            dot_tn((k.astype(F32) * leave[h]).astype(BF), v, BF)
            for h, (q, k, v) in enumerate(heads)
        ]
    )


def retention(heads, parts, state):
    inner, entry = parts[0], parts[1]
    out = []
    for h, (q, k, v) in enumerate(heads):
        scores = (dot_nt(q, k) * inner[h]).astype(BF)
        out.append(dot_nn(scores, v) + entry[h] * dot_nn(q, state[h].astype(BF)))
    return out


def mix(gate, retained):
    out = []
    for h, r in enumerate(retained):
        g = gate[:, h * r.shape[1] : (h + 1) * r.shape[1]]
        out.append((g * jax.nn.sigmoid(g) * normed(r)[0]).astype(BF))
    return jnp.concatenate(out, axis=1)


def mix_back(gate, retained, grad_mixed):
    grad_gate, grad_retained = [], []
    for h, r in enumerate(retained):
        cols = slice(h * r.shape[1], (h + 1) * r.shape[1])
        g, gm = gate[:, cols], grad_mixed[:, cols]
        sigma = jax.nn.sigmoid(g)
        hat, scale = normed(r)
        grad_gate.append((gm * hat * (sigma + g * sigma * (1.0 - sigma))).astype(BF))
        grad_retained.append(norm_back(gm * g * sigma, hat, scale).astype(BF))
    return jnp.concatenate(grad_gate, axis=1), grad_retained


def retention_back(heads, parts, state, grad_retained, grad_state):
    inner, entry, leave = parts[0], parts[1], parts[2]
    grads = []
    for h, (q, k, v) in enumerate(heads):
        gr = grad_retained[h]
        scores = (dot_nt(q, k) * inner[h]).astype(BF)
        pulls = (dot_nt(gr, v) * inner[h]).astype(BF)
        gs, st = grad_state[h].astype(BF), state[h].astype(BF)
        gq = dot_nn(pulls, k) + entry[h] * dot_nt(gr, st)
        gk = dot_tn(pulls, q) + leave[h] * dot_nt(v, gs)
        gv = dot_tn(scores, gr) + leave[h] * dot_nn(k, gs)
        grads.append((gq.astype(BF), gk.astype(BF), gv.astype(BF)))
    return grads


def vmem():
    return pl.BlockSpec(memory_space=pltpu.VMEM)


def anywhere():
    return pl.BlockSpec(memory_space=pl.ANY)


def greet(plane=False, line=False, cores=False, pair=False, across=False, whole=False):
    barrier = pltpu.get_barrier_semaphore()
    chip, core, z = (lax.axis_index(a) for a in AXES)
    others = []
    if plane:
        others += [{"chip": chip ^ 1}, {"chip": chip ^ 2}]
    if cores:
        others.append({"core": 1 - core})
    if pair:
        others.append({"uly": z ^ 1})
    if across:
        others.append({"uly": z ^ 2})
    if whole:
        others += [{"uly": z ^ k} for k in range(1, 4)]
    for to in others:
        pl.semaphore_signal(barrier, inc=1, device_id=to, device_id_type=MESH)
    count = len(others)
    if line:
        last = lax.axis_size("uly") - 1

        @pl.when(z > 0)
        def _():
            pl.semaphore_signal(barrier, inc=1, device_id={"uly": z - 1}, device_id_type=MESH)

        @pl.when(z < last)
        def _():
            pl.semaphore_signal(barrier, inc=1, device_id={"uly": z + 1}, device_id_type=MESH)

        count = count + jnp.where(z > 0, 1, 0) + jnp.where(z < last, 1, 0)
    pl.semaphore_wait(barrier, count)


class PlaneGather:
    def __init__(self, own, at, x_first, send, recv, cores=True):
        chip, core = lax.axis_index("chip"), lax.axis_index("core")
        x, y, other = {"chip": chip ^ 1}, {"chip": chip ^ 2}, {"core": 1 - core}

        def copy(i, src, place, to):
            return pltpu.make_async_remote_copy(
                src_ref=src,
                dst_ref=at(place),
                send_sem=send.at[i],
                recv_sem=recv.at[i],
                device_id=to,
                device_id_type=MESH,
            )

        self.x_first = x_first
        self.copies = [
            copy(0, own, 1, x),
            copy(1, own, 2, y),
            copy(2, at(1), 3, y) if x_first else copy(2, at(2), 3, x),
        ]
        self.cores = cores
        if cores:
            self.copies += [
                copy(3, own, 4, other),
                copy(4, at(1), 5, other),
                copy(5, at(2), 6, other),
                copy(6, at(3), 7, other),
            ]

    def start(self):
        for i in (0, 1) if self.x_first else (1, 0):
            self.copies[i].start()
        if self.cores:
            self.copies[3].start()

    def near(self):
        first = 0 if self.x_first else 1
        self.copies[first].wait_recv()
        self.copies[2].start()
        if self.cores:
            self.copies[4 + first].start()

    def far(self):
        second = 1 if self.x_first else 0
        self.copies[second].wait_recv()
        if self.cores:
            self.copies[4 + second].start()

    def corner(self):
        self.copies[2].wait_recv()
        if self.cores:
            self.copies[6].start()

    def finish(self):
        for c in self.copies[3:]:
            c.wait_recv()
        for c in self.copies:
            c.wait_send()


class LineGather:
    def __init__(self, slots, send, recv):
        self.z = lax.axis_index("uly")
        self.last = lax.axis_size("uly") - 1
        self.slots, self.send, self.recv = slots, send, recv

    def copy(self, right, d):
        z, last = self.z, self.last
        at = jnp.maximum(z - d, 0) if right else jnp.minimum(z + d, last)
        to = jnp.minimum(z + 1, last) if right else jnp.maximum(z - 1, 0)
        way = 0 if right else 1
        return pltpu.make_async_remote_copy(
            src_ref=self.slots.at[at],
            dst_ref=self.slots.at[at],
            send_sem=self.send.at[way, d],
            recv_sem=self.recv.at[way, d],
            device_id={"uly": to},
            device_id_type=MESH,
        )

    def pass_on(self, d):
        z, last = self.z, self.last

        @pl.when((z - d >= 0) & (z < last))
        def _():
            self.copy(True, d).start()

        @pl.when((z + d <= last) & (z > 0))
        def _():
            self.copy(False, d).start()

    def take(self, d, then):
        z, last = self.z, self.last

        @pl.when(z - d >= 0)
        def _():
            self.copy(True, d - 1).wait_recv()

        @pl.when(z + d <= last)
        def _():
            self.copy(False, d - 1).wait_recv()

        if d < last:
            self.pass_on(d)
        self.each(d, then)

    def each(self, d, then):
        z, last = self.z, self.last

        @pl.when(z - d >= 0)
        def _():
            then(jnp.maximum(z - d, 0))

        @pl.when(z + d <= last)
        def _():
            then(jnp.minimum(z + d, last))

    def finish(self):
        z, last = self.z, self.last
        for d in range(last):

            @pl.when((z - d >= 0) & (z < last))
            def _():
                self.copy(True, d).wait_send()

            @pl.when((z + d <= last) & (z > 0))
            def _():
                self.copy(False, d).wait_send()


class LineReduce:
    def __init__(self, make, out, held, came, send, recv):
        self.z = lax.axis_index("uly")
        self.last = lax.axis_size("uly") - 1
        self.make, self.out, self.held, self.came = make, out, held, came
        self.send, self.recv = send, recv

    def copy(self, right, d):
        z, last = self.z, self.last
        way = 0 if right else 1
        to = jnp.minimum(z + 1, last) if right else jnp.maximum(z - 1, 0)
        return pltpu.make_async_remote_copy(
            src_ref=self.held.at[self.place(right, d)],
            dst_ref=self.came.at[way, d - 1],
            send_sem=self.send.at[way, d - 1],
            recv_sem=self.recv.at[way, d - 1],
            device_id={"uly": to},
            device_id_type=MESH,
        )

    def place(self, right, d):
        return d - 1 if right else self.last - d

    def step(self, d):
        z, last = self.z, self.last
        for right in (True, False):
            way = 0 if right else 1
            held = self.held.at[self.place(right, d)]
            valid = (z + d <= last) if right else (z - d >= 0)
            more = (z > 0) if right else (z < last)
            to = jnp.minimum(z + d, last) if right else jnp.maximum(z - d, 0)

            @pl.when(valid)
            def _():
                self.make(to, held)

                if d < last:

                    @pl.when(more)
                    def _():
                        self.copy(right, d + 1).wait_recv()
                        held[...] = (held[...].astype(F32) + self.came[way, d].astype(F32)).astype(
                            BF
                        )

                self.copy(right, d).start()

    def close(self):
        z, last = self.z, self.last
        self.make(z, self.out)

        @pl.when(z > 0)
        def _():
            self.copy(True, 1).wait_recv()
            self.out[...] += self.came[0, 0].astype(F32)

        @pl.when(z < last)
        def _():
            self.copy(False, 1).wait_recv()
            self.out[...] += self.came[1, 0].astype(F32)

        for d in range(1, last + 1):

            @pl.when(z + d <= last)
            def _():
                self.copy(True, d).wait_send()

            @pl.when(z - d >= 0)
            def _():
                self.copy(False, d).wait_send()


def chunk_of(place, width):
    chip, core = lax.axis_index("chip"), lax.axis_index("core")
    block = (chip ^ (place % 4)) * 2 + (core ^ (place // 4))
    return pl.ds(pl.multiple_of(block * width, width), width)


def chip_chunk(k, width):
    return pl.ds(pl.multiple_of((lax.axis_index("chip") ^ k) * width, width), width)


def chip_order(place, width):
    core = lax.axis_index("core")
    return pl.ds(pl.multiple_of((place % 4) * (2 * width) + (core ^ (place // 4)) * width, width), width)


def project_kernel(
    tok_ref,
    gain_one_ref,
    gain_two_ref,
    q_hbm,
    k_hbm,
    v_hbm,
    g_hbm,
    out_hbm,
    up_hbm,
    down_hbm,
    one_ref,
    first_ref,
    high_ref,
    gate_ref,
    w_first_hbm,
    w_second_hbm,
    w_out_hbm,
    gains_ref,
    up_own_hbm,
    down_own_hbm,
    slots,
    wa,
    wb,
    gains,
    psend,
    precv,
    zsend,
    zrecv,
    fsend,
    frecv,
    lsem,
):
    core, z = lax.axis_index("core"), lax.axis_index("uly")
    rows = tok_ref.shape[0] // 2
    width = tok_ref.shape[1]
    piece = width // 8
    qk, high = q_hbm.shape[1], high_ref.shape[2]
    greet(plane=True, line=True, cores=True)
    line = LineGather(slots, zsend, zrecv)
    slots[z] = tok_ref[...]
    line.pass_on(0)
    own = pl.ds(0, piece)
    local = [
        pltpu.make_async_copy(src, dst, lsem.at[i])
        for i, (src, dst) in enumerate(
            (
                (q_hbm, wa.at[own, pl.ds(0, qk)]),
                (k_hbm, wa.at[own, pl.ds(qk, qk)]),
                (v_hbm.at[:, pl.ds(0, high)], wa.at[own, pl.ds(2 * qk, high)]),
                (v_hbm.at[:, pl.ds(high, high)], wb.at[own, pl.ds(0, high)]),
                (g_hbm, wb.at[own, pl.ds(high, g_hbm.shape[1])]),
                (out_hbm, w_out_hbm.at[:, own]),
            )
        )
    ]
    for c in local:
        c.start()
    gains[0] = jnp.zeros_like(gains[0])
    gains[0, 0:1, :] = gain_one_ref[...].astype(F32)
    gains[0, 1:2, :] = gain_two_ref[...].astype(F32)
    items = [
        PlaneGather(gains.at[0], lambda p: gains.at[p], True, psend.at[0], precv.at[0])
    ]
    for i, w in enumerate((wa, wb)):
        items.append(
            PlaneGather(
                w.at[own],
                lambda p, w=w: w.at[pl.ds(p * piece, piece)],
                i == 0,
                psend.at[1 + i],
                precv.at[1 + i],
            )
        )
    half = out_hbm.shape[0] // 2
    for i in range(2):
        part = pl.ds(i * half, half)
        items.append(
            PlaneGather(
                out_hbm.at[part],
                lambda p, part=part: w_out_hbm.at[part, pl.ds(p * piece, piece)],
                i == 0,
                psend.at[3 + i],
                precv.at[3 + i],
            )
        )
    items[0].start()
    units, cols = up_hbm.shape[1] // 2, down_hbm.shape[1]
    first_half = pl.ds(0, units)
    mine, theirs = (pl.ds(pl.multiple_of(c * units, units), units) for c in (core, 1 - core))
    here = pl.ds(pl.multiple_of(core * cols, cols), cols)

    def remote(i, src, dst, to):
        return pltpu.make_async_remote_copy(
            src_ref=src,
            dst_ref=dst,
            send_sem=fsend.at[i],
            recv_sem=frecv.at[i],
            device_id=to,
            device_id_type=MESH,
        )

    cut = [
        pltpu.make_async_copy(up_hbm.at[:, mine], up_own_hbm.at[here, first_half], lsem.at[6]),
        pltpu.make_async_copy(down_hbm.at[mine], down_own_hbm.at[first_half, here], lsem.at[7]),
    ]
    give = [
        remote(0, up_hbm.at[:, theirs], up_own_hbm.at[here, first_half], {"core": 1 - core}),
        remote(1, down_hbm.at[theirs], down_own_hbm.at[first_half, here], {"core": 1 - core}),
    ]
    for c in cut:
        c.start()
    for c in local[:5]:
        c.wait()
    for item in items[1:3]:
        item.start()
    for c in give:
        c.start()
    items[0].near()
    items[0].far()
    items[0].corner()
    items[0].finish()
    gains_ref[...] = jnp.zeros_like(gains_ref)
    for p in range(8):
        gains_ref[0:1, chunk_of(p, piece)] = gains[p, 0:1, :]
        gains_ref[1:2, chip_order(p, piece)] = gains[p, 1:2, :]

    def normalize(slot):
        step = 32
        for m in range(2):

            @pl.loop(0, rows // step)
            def _(i):
                at = pl.multiple_of(i * step, step)
                v = slots[slot, pl.ds(m * rows + at, step), :].astype(F32)
                mean = jnp.mean(v, axis=-1, keepdims=True)
                center = v - mean
                scale = lax.rsqrt(jnp.mean(center * center, axis=-1, keepdims=True) + EPSILON)
                to = pl.ds(pl.multiple_of(slot * rows + at, step), step)
                for p in range(8):
                    src = slots[slot, pl.ds(m * rows + at, step), chunk_of(p, piece)].astype(F32)
                    one_ref[m, to, pl.ds(p * piece, piece)] = (
                        (src - mean) * scale * gains[p, 0:1, :]
                    ).astype(BF)

    normalize(z)
    line.take(1, normalize)
    for item in items[1:3]:
        item.near()
    for item in items[1:3]:
        item.far()
    for item in items[3:]:
        item.start()
    line.take(2, normalize)
    for item in items[1:3]:
        item.corner()
    for item in items[1:3]:
        item.finish()
    outs = [
        pltpu.make_async_copy(wa, w_first_hbm, lsem.at[8]),
        pltpu.make_async_copy(wb, w_second_hbm, lsem.at[9]),
    ]
    for c in outs:
        c.start()
    tile = 512

    def multiply(slot):
        at = pl.ds(pl.multiple_of(slot * rows, rows), rows)
        x = jnp.concatenate([one_ref[0, at, :], one_ref[1, at, :]], axis=0)

        def tiles(w, start, to_ref):
            @pl.loop(0, to_ref.shape[2] // tile)
            def _(n):
                cols = pl.ds(pl.multiple_of(n * tile, tile), tile)
                from_ = pl.ds(pl.multiple_of(start + n * tile, tile), tile)
                r = jnp.dot(x, w[:, from_], preferred_element_type=F32).astype(to_ref.dtype)
                for m in range(2):
                    to_ref[m, at, cols] = r[m * rows : (m + 1) * rows]

        tiles(wa, 0, first_ref)
        tiles(wb, 0, high_ref)
        tiles(wb, high, gate_ref)

    multiply(z)
    line.each(1, multiply)
    for item in items[3:]:
        item.near()
    for item in items[3:]:
        item.far()
    line.each(2, multiply)

    def both_steps(slot):
        normalize(slot)
        multiply(slot)

    line.take(3, both_steps)
    for item in items[3:]:
        item.corner()
    for item in items[3:]:
        item.finish()
    line.finish()
    local[5].wait()
    for c in outs + cut:
        c.wait()
    for c in give:
        c.wait()


def add_rows_kernel(
    x_ref,
    w_ref,
    tok_ref,
    up_hbm,
    down_hbm,
    out_ref,
    ups_hbm,
    downs_hbm,
    held,
    came,
    send,
    recv,
    psend,
    precv,
    lsem,
):
    rows = out_ref.shape[0] // 2
    width = out_ref.shape[1] // 8
    greet(plane=True, line=True)
    part = up_hbm.shape[0]

    def up_at(p):
        return ups_hbm.at[pl.ds(p * part, part)]

    def down_at(p):
        return downs_hbm.at[:, pl.ds(p * part, part)]

    items = [
        PlaneGather(up_hbm, up_at, True, psend.at[0], precv.at[0], False),
        PlaneGather(down_hbm, down_at, False, psend.at[1], precv.at[1], False),
    ]
    local = [
        pltpu.make_async_copy(up_hbm, up_at(0), lsem.at[0]),
        pltpu.make_async_copy(down_hbm, down_at(0), lsem.at[1]),
    ]

    def make(a, to):
        at = pl.ds(pl.multiple_of(a * rows, rows), rows)
        x = jnp.concatenate([x_ref[0, at, :], x_ref[1, at, :]], axis=0)

        @pl.loop(0, 8)
        def _(p):
            cols = w_ref[:, pl.ds(pl.multiple_of(p * width, width), width)]
            to[:, chip_order(p, width)] = jnp.dot(x, cols, preferred_element_type=F32).astype(
                to.dtype
            )

    line = LineReduce(make, out_ref, held, came, send, recv)
    for item in items:
        item.start()
    line.step(3)
    for c in local:
        c.start()
    line.step(2)
    for item in items:
        item.near()
    for item in items:
        item.far()
    line.step(1)
    line.close()
    for k in range(4):
        cols = pl.ds(k * 2 * width, 2 * width)
        out_ref[:, cols] += tok_ref[:, chip_chunk(k, 2 * width)].astype(F32)
    for item in items:
        item.corner()
    for item in items:
        item.finish()
    for c in local:
        c.wait()


def fan_out_kernel(
    rows_ref,
    w_ref,
    mixed_ref,
    up_hbm,
    down_hbm,
    grad_ref,
    part_ref,
    up_ref,
    down_ref,
    slots,
    ordered,
    total,
    near_up,
    near_down,
    came_up,
    came_down,
    send,
    recv,
    psend,
    precv,
    lsem,
):
    z = lax.axis_index("uly")
    rows = rows_ref.shape[0] // 2
    width = rows_ref.shape[1] // 8
    greet(plane=True, line=True)
    line = LineGather(slots, send, recv)
    slots[z] = rows_ref[...]
    line.pass_on(0)
    local = [
        pltpu.make_async_copy(up_hbm, near_up, lsem.at[0]),
        pltpu.make_async_copy(down_hbm, near_down, lsem.at[1]),
    ]
    for c in local:
        c.start()
    groups = [
        PlaneReduce(None, near_up, came_up, True, psend.at[0], precv.at[0]),
        PlaneReduce(None, near_down, came_down, False, psend.at[1], precv.at[1]),
    ]
    for c in local:
        c.wait()
    for g in groups:
        g.start_first()

    def multiply(slot):
        at = pl.ds(pl.multiple_of(slot * rows, rows), rows)
        for p in range(8):
            ordered[:, p * width : (p + 1) * width] = slots[slot, :, chip_order(p, width)]
        tile = 256

        @pl.loop(0, w_ref.shape[0] // tile)
        def _(n):
            part = pl.ds(pl.multiple_of(n * tile, tile), tile)
            product = dot_nt(ordered[...], w_ref[part, :])
            for m in range(2):
                grad_ref[m, at, part] = product[m * rows : (m + 1) * rows]

        mixed = jnp.concatenate([mixed_ref[0, at, :], mixed_ref[1, at, :]], axis=0)

        @pl.loop(0, 8)
        def _(p):
            cols = pl.ds(pl.multiple_of(p * width, width), width)
            total[p] += dot_tn(ordered[:, cols], mixed)

    total[...] = jnp.zeros_like(total)
    multiply(z)
    line.take(1, multiply)
    for g in groups:
        g.first_sums(0)
    line.take(2, multiply)
    for g in groups:
        g.first_sums(1)
    line.take(3, multiply)
    part_ref[...] = total[...].astype(BF)
    groups[0].finish(up_ref)
    groups[1].finish(down_ref)
    line.finish()


def feed_kernel(
    hid_ref,
    douts_ref,
    gain_ref,
    ups_ref,
    downs_ref,
    keep_ref,
    give_ref,
    grad_ref,
    rows_ref,
    gain_grad_ref,
    up_grad_ref,
    down_grad_ref,
    two,
    act,
    gu,
    sums,
    held,
    came,
    send,
    recv,
):
    core, z = lax.axis_index("core"), lax.axis_index("uly")
    rows, width = hid_ref.shape
    hidden = ups_ref.shape[1]
    other, pair = {"core": 1 - core}, {"uly": z ^ 1}
    greet(cores=True, pair=True)

    def group(g):
        return pl.ds(g * rows, rows)

    def copy(i, src, dst, to):
        return pltpu.make_async_remote_copy(
            src_ref=src,
            dst_ref=dst,
            send_sem=send.at[i],
            recv_sem=recv.at[i],
            device_id=to,
            device_id_type=MESH,
        )

    step = 32

    @pl.loop(0, rows // step)
    def _(i):
        at = pl.ds(pl.multiple_of(i * step, step), step)
        hat, _scale = normed(hid_ref[at, :])
        two[at, :] = (hat * gain_ref[1:2, :]).astype(BF)

    to_pair = copy(0, two.at[group(0)], two.at[group(2)], pair)
    to_other = copy(1, two.at[group(0)], two.at[group(1)], other)
    through = copy(2, two.at[group(2)], two.at[group(3)], other)
    to_pair.start()
    to_other.start()

    def work(g):
        tile = 256

        @pl.loop(0, hidden // tile)
        def _(n):
            cols = pl.ds(pl.multiple_of(n * tile, tile), tile)
            upward = jnp.dot(two[group(g), :], ups_ref[:, cols], preferred_element_type=F32)
            value, slope = gelu_pair(upward)
            act[group(g), cols] = value.astype(BF)
            pulled = dot_nt(douts_ref[group(g), :], downs_ref[cols, :])
            gu[group(g), cols] = (pulled * slope).astype(BF)

        tile = 512

        @pl.loop(0, width // tile)
        def _(n):
            cols = pl.ds(pl.multiple_of(n * tile, tile), tile)
            back = dot_nt(gu[group(g), :], ups_ref[cols, :])
            down = jnp.dot(act[group(g), :], downs_ref[:, cols], preferred_element_type=F32)
            if g == 0:
                sums[0, :, cols] = back
                sums[1, :, cols] = down
            else:
                held[g - 1, 0, :, cols] = back.astype(BF)
                held[g - 1, 1, :, cols] = down.astype(BF)

    returns = [copy(3 + i, held.at[0, i], came.at[3 * i], other) for i in range(2)]
    returns += [copy(5 + i, held.at[2, i], came.at[1 + 3 * i], other) for i in range(2)]
    last = copy(7, held.at[1, 0], came.at[2], pair)

    work(0)
    to_other.wait_recv()
    work(1)
    for c in returns[:2]:
        c.start()
    to_pair.wait_recv()
    through.start()
    work(2)
    through.wait_recv()
    work(3)
    for c in returns[2:]:
        c.start()
    for i in range(2):
        returns[2 + i].wait_recv()

        @pl.loop(0, rows // step)
        def _(r):
            at = pl.ds(pl.multiple_of(r * step, step), step)
            held[1, i, at, :] = (
                held[1, i, at, :].astype(F32) + came[1 + 3 * i, at, :].astype(F32)
            ).astype(BF)

        if i == 0:
            last.start()
    give_ref[...] = held[1, 1]
    tile = 512

    @pl.loop(0, width // tile)
    def _(n):
        cols = pl.ds(pl.multiple_of(n * tile, tile), tile)
        up_grad_ref[n] = dot_tn(two[:, cols], gu[...], BF)
        down_grad_ref[n] = dot_tn(act[...], douts_ref[:, cols], BF)

    for i in range(2):
        returns[i].wait_recv()
    last.wait_recv()
    gain_grad_ref[...] = jnp.zeros_like(gain_grad_ref)

    @pl.loop(0, rows // step)
    def _(r):
        at = pl.ds(pl.multiple_of(r * step, step), step)
        back = sums[0, at, :] + came[0, at, :].astype(F32) + came[2, at, :].astype(F32)
        hat, scale = normed(hid_ref[at, :])
        gain_grad_ref[...] += jnp.sum(back * hat, axis=0, keepdims=True)
        grad = douts_ref[at, :].astype(F32) + norm_back(back * gain_ref[1:2, :], hat, scale)
        grad_ref[at, :] = grad
        rows_ref[at, :] = grad.astype(BF)
        keep_ref[at, :] = hid_ref[at, :] + sums[1, at, :] + came[3, at, :].astype(F32)

    for c in [to_pair, to_other, through, last] + returns:
        c.wait_send()


class PlaneReduce:
    def __init__(self, far, near, came, x_first, send, recv):
        chip, core = lax.axis_index("chip"), lax.axis_index("core")
        x, y, other = {"chip": chip ^ 1}, {"chip": chip ^ 2}, {"core": 1 - core}
        self.near, self.came, self.x_first = near, came, x_first
        self.waited = ()

        def copy(i, src, to):
            return pltpu.make_async_remote_copy(
                src_ref=src,
                dst_ref=came.at[i],
                send_sem=send.at[i],
                recv_sem=recv.at[i],
                device_id=to,
                device_id_type=MESH,
            )

        self.away = (1, 3) if x_first else (2, 3)
        self.stay = (0, 2) if x_first else (0, 1)
        one, two = (x, y) if x_first else (y, x)
        self.cores = 4 if far else 0
        self.copies = [copy(i, far(4 + i), other) for i in range(self.cores)]
        self.copies += [copy(self.cores + i, near.at[self.away[i]], one) for i in range(2)]
        self.copies.append(copy(self.cores + 2, near.at[self.stay[1]], two))

    def start(self):
        for i in (3, self.away[0], self.stay[1], 0):
            self.copies[i].start()

    def add(self, place, i):
        step = 64

        @pl.loop(0, self.near.shape[1] // step)
        def _(r):
            at = pl.ds(pl.multiple_of(r * step, step), step)
            self.near[place, at, :] = (
                self.near[place, at, :].astype(F32) + self.came[i, at, :].astype(F32)
            ).astype(BF)

    def core_sums(self):
        for i in (1, 0):
            p = self.away[i]
            self.copies[p].wait_recv()
            self.add(p, p)
            self.copies[4 + i].start()
        for p in (self.stay[1], self.stay[0]):
            self.copies[p].wait_recv()
            self.add(p, p)

    def start_first(self):
        for i in (1, 0):
            self.copies[self.cores + i].start()

    def first_sums(self, step):
        i = 1 - step
        self.copies[self.cores + i].wait_recv()
        self.add(self.stay[i], self.cores + i)
        if i == 1:
            self.copies[self.cores + 2].start()

    def finish(self, out_ref):
        self.copies[self.cores + 2].wait_recv()
        self.add(self.stay[0], self.cores + 2)
        out_ref[...] = self.near[0]
        for i, c in enumerate(self.copies):
            if i not in self.waited:
                c.wait_send()


def far_slot(i, x_first):
    return ((3, 1, 2, 0) if x_first else (3, 2, 1, 0)).index(i) % 2


def close_rows_kernel(
    xa_ref,
    xb_ref,
    wa_ref,
    wb_ref,
    one_ref,
    tok_ref,
    hid_ref,
    gain_ref,
    gain_two_ref,
    out_ref,
    sum_a_ref,
    sum_b_ref,
    gains_ref,
    held,
    came,
    near_a,
    near_b,
    far_a,
    far_b,
    came_a,
    came_b,
    gain_sum,
    small,
    small_came,
    small_line,
    send,
    recv,
    psend,
    precv,
    ssend,
    srecv,
):
    chip, core, z = (lax.axis_index(a) for a in AXES)
    rows = out_ref.shape[0] // 2
    length = one_ref.shape[0] // 2
    width = out_ref.shape[1] // 8
    greet(plane=True, cores=True, whole=True)

    def make(a, to):
        at = [
            pl.ds(pl.multiple_of(m * length + a * rows, rows), rows) for m in range(2)
        ]
        xa = jnp.concatenate([xa_ref[i, :] for i in at], axis=0)
        xb = jnp.concatenate([xb_ref[i, :] for i in at], axis=0)

        @pl.loop(0, 8)
        def _(p):
            part = pl.ds(pl.multiple_of(p * width, width), width)
            to[:, chunk_of(p, width)] = (
                dot_nt(xa, wa_ref[part, :]) + dot_nt(xb, wb_ref[part, :])
            ).astype(to.dtype)

    line = LineReduce(make, out_ref, held, came, send, recv)
    sets = []
    for i, (x_ref, near, far, got, x_first) in enumerate(
        (
            (xa_ref, near_a, far_a, came_a, True),
            (xb_ref, near_b, far_b, came_b, False),
        )
    ):
        group = PlaneReduce(
            lambda p, far=far, x=x_first: far.at[far_slot(p - 4, x)],
            near,
            got,
            x_first,
            psend.at[i],
            precv.at[i],
        )
        group.waited = tuple((3, group.away[0]))
        sets.append((group, x_ref, near, far, got))

    tile = 512

    def product(x_ref, place, to, more=None):
        @pl.loop(0, x_ref.shape[1] // tile)
        def _(n):
            cols = pl.ds(pl.multiple_of(n * tile, tile), tile)
            r = dot_tn(one_ref[:, place * width : (place + 1) * width], x_ref[:, cols])
            if more is not None:
                r = r + more[:, cols].astype(F32)
            to[:, cols] = r.astype(BF)

    line.step(3)
    for n in range(4):
        for group, x_ref, near, far, got in sets:
            order = (3, group.away[0], group.stay[1], 0)
            if n >= 2:
                group.copies[order[n - 2]].wait_send()
            product(x_ref, 4 + order[n], far.at[n % 2])
            group.copies[order[n]].start()

    def add_near(n):
        for group, x_ref, near, far, got in sets:
            i = (3, group.away[0], group.stay[1], 0)[n]
            group.copies[i].wait_recv()
            product(x_ref, i, near.at[i], got.at[i])
            if n < 2:
                group.copies[4 + (1 - n)].start()

    add_near(0)
    add_near(1)
    line.step(2)
    add_near(2)
    add_near(3)
    line.step(1)
    for group, *_ in sets:
        group.first_sums(0)
    line.close()
    step = 32
    gain_sum[...] = jnp.zeros_like(gain_sum)

    @pl.loop(0, 2 * rows // step)
    def _(r):
        at = pl.ds(pl.multiple_of(r * step, step), step)
        hat, scale = normed(tok_ref[at, :].astype(F32))
        grad = out_ref[at, :]
        gain_sum[...] += jnp.sum(grad * hat, axis=0, keepdims=True)
        out_ref[at, :] = norm_back(grad * gain_ref[0:1, :], hat, scale)
        for k in range(4):
            out_ref[at, chip_chunk(k, 2 * width)] += hid_ref[
                at, k * 2 * width : (k + 1) * 2 * width
            ]

    small[...] = jnp.zeros_like(small)
    for p in range(8):
        small[p, 0:1, :] = gain_sum[:, chunk_of(p, width)]
        small[p, 1:2, :] = gain_two_ref[:, chip_order(p, width)]

    def pass_small(i, src, dst, to):
        return pltpu.make_async_remote_copy(
            src_ref=src,
            dst_ref=dst,
            send_sem=ssend.at[i],
            recv_sem=srecv.at[i],
            device_id=to,
            device_id_type=MESH,
        )

    sent = []
    for i, (count, to) in enumerate(
        ((4, {"core": 1 - core}), (2, {"chip": chip ^ 2}), (1, {"chip": chip ^ 1}))
    ):
        c = pass_small(
            i, small.at[pl.ds(count, count)], small_came.at[pl.ds(count, count)], to
        )
        c.start()
        if i == 0:
            for group, *_ in sets:
                group.first_sums(1)
        c.wait_recv()
        small[0:count] = small[0:count] + small_came[count : 2 * count]
        sent.append(c)
    last = [
        pass_small(2 + k, small.at[0], small_line.at[k], {"uly": z ^ k}) for k in range(1, 4)
    ]
    for c in last:
        c.start()
    for (group, *_), out in zip(sets, (sum_a_ref, sum_b_ref)):
        group.finish(out)
    total = small[0]
    for k in range(1, 4):
        last[k - 1].wait_recv()
        total = total + small_line[k]
    gains_ref[...] = total
    for c in sent + last:
        c.wait_send()


class StateExchange:
    def __init__(self, coef_ref, own, sib, chips, mine, came, final, send, recv):
        self.core = lax.axis_index("core")
        self.coef, self.own, self.sib, self.chips = coef_ref, own, sib, chips
        self.mine, self.came, self.final = mine, came, final

        def copy(i, src, dst):
            return pltpu.make_async_remote_copy(
                src_ref=src,
                dst_ref=dst,
                send_sem=send.at[2, i],
                recv_sem=recv.at[2, i],
                device_id={"core": 1 - self.core},
                device_id_type=MESH,
            )

        self.first = copy(0, own, sib)
        self.second = copy(1, mine, came)
        self.items = [
            PlaneGather(
                chips.at[0, h], lambda p, h=h: chips.at[p, h], h == 0, send.at[h], recv.at[h], False
            )
            for h in range(2)
        ]

    def start(self):
        self.first.start()

    def join(self):
        self.first.wait_recv()
        m = self.core
        for h in range(2):
            self.chips[0, h] = (
                self.coef[m, h, 0] * self.own[m, h].astype(F32)
                + self.coef[m, h, 1] * self.sib[m, h].astype(F32)
            ).astype(BF)
            self.items[h].start()

    def near(self):
        for item in self.items:
            item.near()

    def far(self):
        for item in self.items:
            item.far()

    def settle(self):
        for item in self.items:
            item.corner()
        m = self.core
        for h in range(2):
            total = self.coef[m, h, 5] * self.chips[1, h].astype(F32)
            for k in (2, 3):
                total = total + self.coef[m, h, 4 + k] * self.chips[k, h].astype(F32)
            self.mine[h] = total.astype(BF)
        self.second.start()
        self.last(m, self.mine)
        self.second.wait_recv()
        self.last(1 - m, self.came)

    def last(self, m, chip_state):
        for h in range(2):
            self.final[m, h] = (
                self.coef[m, h, 2] * chip_state[h].astype(F32)
                + self.coef[m, h, 3] * self.sib[m, h].astype(F32)
            ).astype(BF)

    def finish(self):
        self.first.wait_send()
        self.second.wait_send()
        for item in self.items:
            item.finish()


def state_scratch(shape):
    half = shape[1:]
    return [
        pltpu.VMEM(shape, BF),
        pltpu.VMEM(shape, BF),
        pltpu.VMEM((4, *half), BF),
        pltpu.VMEM(half, BF),
        pltpu.VMEM(half, BF),
        sems(3, 3),
        sems(3, 3),
    ]


class Places:
    def __init__(self, lengths_ref, m, length):
        self.length = length
        self.base = (lax.axis_index("chip") * 2 + lax.axis_index("core")) * length
        self.bounds = []
        total = 0
        for n in range(lengths_ref.shape[1]):
            self.bounds.append(total)
            total = total + lengths_ref[m, n]

    def segment(self, at):
        found = jnp.zeros_like(at)
        for b in self.bounds:
            found = found + jnp.where(self.base + at >= b, 1, 0)
        return found

    def table(self, rate, start, count, across):
        shape = (count, self.length)
        rows = start + lax.broadcasted_iota(jnp.int32, shape, 0)
        cols = lax.broadcasted_iota(jnp.int32, shape, 1)
        off = cols - rows if across else rows - cols
        seg_rows = self.segment(start + lax.broadcasted_iota(jnp.int32, (count, 1), 0))
        seg_cols = self.segment(lax.broadcasted_iota(jnp.int32, (1, self.length), 1))
        far = jnp.maximum(off, 0).astype(F32)
        return jnp.where((off >= 0) & (seg_rows == seg_cols), jnp.exp(-rate * far), 0.0)

    def entry(self, rate, start, count):
        at = start + lax.broadcasted_iota(jnp.int32, (count, 1), 0)
        same = self.segment(at) == self.segment(jnp.full((1, 1), -1, jnp.int32))
        return jnp.where(same, jnp.exp(-rate * (at + 1).astype(F32)), 0.0)

    def leave(self, rate, start, count):
        at = start + lax.broadcasted_iota(jnp.int32, (count, 1), 0)
        end = jnp.full((1, 1), self.length - 1, jnp.int32)
        same = self.segment(at) == self.segment(end)
        return jnp.where(same, jnp.exp(-rate * (self.length - 1 - at).astype(F32)), 0.0)


ROWS = 128


def retain_kernel(
    rates_ref,
    lengths_ref,
    coef_ref,
    a_ref,
    high_ref,
    gate_ref,
    dout_ref,
    up_hbm,
    down_hbm,
    mixed_ref,
    kept_ref,
    state_ref,
    douts_ref,
    up_own_hbm,
    down_own_hbm,
    own,
    sib,
    chips,
    mine,
    came,
    send,
    recv,
    ordered,
    others,
    dsend,
    drecv,
    fsend,
    frecv,
    lsem,
):
    _, length, vd = high_ref.shape
    qk = (a_ref.shape[2] - vd) // 2
    hd = qk // 2
    greet(plane=True, cores=True, pair=True, across=True)
    z = lax.axis_index("uly")
    units = up_hbm.shape[1]
    first_half, second_half = pl.ds(0, units), pl.ds(units, units)
    keep, away = [], []
    for i, (src, first, second) in enumerate(
        (
            (up_hbm, up_own_hbm.at[:, first_half], up_own_hbm.at[:, second_half]),
            (down_hbm, down_own_hbm.at[first_half], down_own_hbm.at[second_half]),
        )
    ):
        keep.append(pltpu.make_async_copy(src, first, lsem.at[i]))
        away.append(
            pltpu.make_async_remote_copy(
                src_ref=src,
                dst_ref=second,
                send_sem=fsend.at[i],
                recv_sem=frecv.at[i],
                device_id={"uly": z ^ 2},
                device_id_type=MESH,
            )
        )
    for c in away + keep:
        c.start()
    quarter = ordered.shape[1] // 4
    for k in range(4):
        ordered[:, k * quarter : (k + 1) * quarter] = dout_ref[:, chip_chunk(k, quarter)]

    def rows_to(i, src, to):
        return pltpu.make_async_remote_copy(
            src_ref=src,
            dst_ref=others.at[i],
            send_sem=dsend.at[i],
            recv_sem=drecv.at[i],
            device_id=to,
            device_id_type=MESH,
        )

    other = {"core": 1 - lax.axis_index("core")}
    to_pair = rows_to(1, ordered, {"uly": z ^ 1})
    to_other = rows_to(0, ordered, other)
    through = rows_to(2, others.at[1], other)
    to_pair.start()
    states = StateExchange(coef_ref, own, sib, chips, mine, came, state_ref, send, recv)

    def values(m, h):
        return high_ref[m] if h else a_ref[m, :, 2 * qk :]

    def keys(m, h):
        return a_ref[m, :, qk + h * hd : qk + (h + 1) * hd]

    for h in range(2):

        @pl.loop(0, 2)
        def _(m):
            leave = Places(lengths_ref, m, length).leave(rates_ref[h], 0, length)
            k = (keys(m, h).astype(F32) * leave).astype(BF)
            own[m, h] = dot_tn(k, values(m, h), BF)

    states.start()
    parts = length // ROWS

    def local(h):
        @pl.loop(0, 2 * parts)
        def _(i):
            m, r = i // parts, i % parts
            at = pl.ds(pl.multiple_of(r * ROWS, ROWS), ROWS)
            table = Places(lengths_ref, m, length).table(rates_ref[h], r * ROWS, ROWS, False)
            q = a_ref[m, at, h * hd : (h + 1) * hd]
            scores = (dot_nt(q, keys(m, h)) * table).astype(BF)
            kept_ref[m, at, h * vd : (h + 1) * vd] = jnp.dot(
                scores, values(m, h), preferred_element_type=F32
            )

    states.join()
    to_other.start()
    local(0)
    states.near()
    local(1)
    states.far()
    to_pair.wait_recv()
    through.start()
    states.settle()
    for h in range(2):

        @pl.loop(0, 2 * parts)
        def _(i):
            m, r = i // parts, i % parts
            at = pl.ds(pl.multiple_of(r * ROWS, ROWS), ROWS)
            cols = slice(h * vd, (h + 1) * vd)
            entry = Places(lengths_ref, m, length).entry(rates_ref[h], r * ROWS, ROWS)
            q = a_ref[m, at, h * hd : (h + 1) * hd]
            kept = kept_ref[m, at, cols] + entry * jnp.dot(
                q, state_ref[m, h], preferred_element_type=F32
            )
            kept_ref[m, at, cols] = kept
            g = gate_ref[m, at, cols]
            mixed_ref[m, at, cols] = (g * sigmoid(g) * normed(kept)[0]).astype(BF)

    states.finish()
    rows = ordered.shape[0]
    douts_ref[0:rows, :] = ordered[...]
    to_other.wait_recv()
    through.wait_recv()
    for i in range(3):
        douts_ref[(1 + i) * rows : (2 + i) * rows, :] = others[i]
    for c in (to_pair, to_other, through):
        c.wait_send()
    for c in keep + away:
        c.wait()


def sigmoid(v):
    return 0.5 * jnp.tanh(0.5 * v) + 0.5


def retain_back_kernel(
    rates_ref,
    lengths_ref,
    coef_ref,
    a_ref,
    high_ref,
    gate_ref,
    kept_ref,
    grad_ref,
    state_ref,
    part_hbm,
    keep_ref,
    give_hbm,
    xa_ref,
    xb_ref,
    sum_ref,
    out_ref,
    pulled,
    grad_k,
    grad_v,
    final,
    own,
    sib,
    chips,
    mine,
    came,
    send,
    recv,
    near,
    got,
    psend,
    precv,
    lsem,
    came_rows,
    rsend,
    rrecv,
):
    _, length, vd = high_ref.shape
    qk = (a_ref.shape[2] - vd) // 2
    hd = qk // 2
    greet(plane=True, cores=True, pair=True)
    give = pltpu.make_async_remote_copy(
        src_ref=give_hbm,
        dst_ref=came_rows,
        send_sem=rsend,
        recv_sem=rrecv,
        device_id={"uly": lax.axis_index("uly") ^ 1},
        device_id_type=MESH,
    )
    give.start()
    group = PlaneReduce(lambda p: part_hbm.at[p], near, got, True, psend, precv)
    local = pltpu.make_async_copy(part_hbm.at[pl.ds(0, 4)], near, lsem)
    local.start()
    group.start()
    states = StateExchange(coef_ref, own, sib, chips, mine, came, final, send, recv)
    parts = length // ROWS

    def values(m, h, at=slice(None)):
        return high_ref[m, at, :] if h else a_ref[m, at, 2 * qk :]

    def keys(m, h, at=slice(None)):
        return a_ref[m, at, qk + h * hd : qk + (h + 1) * hd]

    def queries(m, h, at=slice(None)):
        return a_ref[m, at, h * hd : (h + 1) * hd]

    for h in range(2):
        cols = slice(h * vd, (h + 1) * vd)

        @pl.loop(0, 2 * parts)
        def _(i):
            m, r = i // parts, i % parts
            at = pl.ds(pl.multiple_of(r * ROWS, ROWS), ROWS)
            g, gm = gate_ref[m, at, cols], grad_ref[m, at, cols]
            sigma = sigmoid(g)
            hat, scale = normed(kept_ref[m, at, cols])
            xb_ref[m, at, vd + h * vd : vd + (h + 1) * vd] = (
                gm * hat * (sigma + g * sigma * (1.0 - sigma))
            ).astype(BF)
            pulled[m, at, cols] = norm_back(gm * g * sigma, hat, scale).astype(BF)

        @pl.loop(0, 2)
        def _(m):
            entry = Places(lengths_ref, m, length).entry(rates_ref[h], 0, length)
            q = (queries(m, h).astype(F32) * entry).astype(BF)
            own[m, h] = dot_tn(q, pulled[m, :, cols], BF)

    states.start()

    def local_q(h):
        cols = slice(h * vd, (h + 1) * vd)

        @pl.loop(0, 2 * parts)
        def _(i):
            m, r = i // parts, i % parts
            at = pl.ds(pl.multiple_of(r * ROWS, ROWS), ROWS)
            places = Places(lengths_ref, m, length)
            table = places.table(rates_ref[h], r * ROWS, ROWS, False)
            gr = pulled[m, at, cols]
            p = (dot_nt(gr, values(m, h)) * table).astype(BF)
            entry = places.entry(rates_ref[h], r * ROWS, ROWS)
            xa_ref[m, at, h * hd : (h + 1) * hd] = (
                jnp.dot(p, keys(m, h), preferred_element_type=F32)
                + entry * dot_nt(gr, state_ref[m, h])
            ).astype(BF)

    def local_kv(h):
        cols = slice(h * vd, (h + 1) * vd)

        @pl.loop(0, 2 * parts)
        def _(i):
            m, r = i // parts, i % parts
            at = pl.ds(pl.multiple_of(r * ROWS, ROWS), ROWS)
            table = Places(lengths_ref, m, length).table(rates_ref[h], r * ROWS, ROWS, True)
            p = (dot_nt(values(m, h, at), pulled[m, :, cols]) * table).astype(BF)
            scores = (dot_nt(keys(m, h, at), queries(m, h)) * table).astype(BF)
            grad_k[m, at, h * hd : (h + 1) * hd] = jnp.dot(
                p, queries(m, h), preferred_element_type=F32
            )
            grad_v[m, at, cols] = jnp.dot(
                scores, pulled[m, :, cols], preferred_element_type=F32
            )

    states.join()
    local_q(0)
    states.near()
    states.far()
    local_q(1)
    states.settle()
    local.wait()
    group.core_sums()
    local_kv(0)
    local_kv(1)
    group.first_sums(0)
    group.first_sums(1)
    for h in range(2):

        @pl.loop(0, 2 * parts)
        def _(i):
            m, r = i // parts, i % parts
            at = pl.ds(pl.multiple_of(r * ROWS, ROWS), ROWS)
            leave = Places(lengths_ref, m, length).leave(rates_ref[h], r * ROWS, ROWS)
            xa_ref[m, at, qk + h * hd : qk + (h + 1) * hd] = (
                grad_k[m, at, h * hd : (h + 1) * hd]
                + leave * dot_nt(values(m, h, at), final[m, h])
            ).astype(BF)
            gv = (
                grad_v[m, at, h * vd : (h + 1) * vd]
                + leave * jnp.dot(keys(m, h, at), final[m, h], preferred_element_type=F32)
            ).astype(BF)
            if h:
                xb_ref[m, at, :vd] = gv
            else:
                xa_ref[m, at, 2 * qk :] = gv

    states.finish()
    give.wait()
    quarter = keep_ref.shape[1] // 4
    for k in range(4):
        cols = slice(k * quarter, (k + 1) * quarter)
        out_ref[:, chip_chunk(k, quarter)] = (
            keep_ref[:, cols] + came_rows[:, cols].astype(F32)
        ).astype(BF)
    group.finish(sum_ref)


def sems(*shape):
    return pltpu.SemaphoreType.DMA(shape)


def like(shape, kind):
    return jax.ShapeDtypeStruct(shape, kind)


def call(kernel, number, ins, outs, scratch, flops, *args):
    moved = sum(a.size * a.dtype.itemsize for a in args)
    return pl.pallas_call(
        kernel,
        out_shape=[like(s, t) for s, t, _ in outs],
        in_specs=ins,
        out_specs=[spec for _, _, spec in outs],
        scratch_shapes=scratch,
        compiler_params=pltpu.CompilerParams(
            collective_id=number, has_side_effects=True, vmem_limit_bytes=VMEM_LIMIT
        ),
        cost_estimate=pl.CostEstimate(flops=flops, bytes_accessed=moved, transcendentals=0),
    )(*args)


def smem():
    return pl.BlockSpec(memory_space=pltpu.SMEM)


def chip_weights(rates, lengths, block):
    chip, core = lax.axis_index("chip"), lax.axis_index("core")
    count = block_count()
    places = jnp.arange(count, dtype=jnp.int32)
    ahead, back = [], []
    others = chip ^ jnp.arange(4, dtype=jnp.int32)
    for m in range(lengths.shape[0]):
        ends = segment_ids((places + 1) * block - 1, lengths[m])

        def end(b):
            return jnp.where(b < 0, 0, ends[jnp.maximum(b, 0)])

        whole = jnp.exp(-rates * block)
        even = jnp.where(end(2 * chip) == end(2 * chip - 1), whole, 0.0)
        odd = jnp.where(end(2 * chip + 1) == end(2 * chip), whole, 0.0)
        one, zero = jnp.ones_like(whole), jnp.zeros_like(whole)
        first = core == 0

        def pick(a, b):
            return jnp.where(first, a, b)

        past = jnp.where(
            ((others < chip) & (end(2 * others + 1) == end(2 * chip - 1)))[None],
            jnp.exp(-rates[:, None] * (2.0 * block) * jnp.maximum(chip - 1 - others, 0)[None]),
            0.0,
        )
        later = jnp.where(
            ((others > chip) & (end(2 * chip + 1) == end(2 * others - 1)))[None],
            jnp.exp(-rates[:, None] * (2.0 * block) * jnp.maximum(others - 1 - chip, 0)[None]),
            0.0,
        )
        four = [pick(odd, one), pick(one, odd), pick(one, even), pick(zero, one)]
        ahead.append(jnp.concatenate([jnp.stack(four, axis=1), past], axis=1))
        four = [pick(one, even), pick(even, one), pick(odd, one), pick(one, zero)]
        back.append(jnp.concatenate([jnp.stack(four, axis=1), later], axis=1))
    return jnp.stack(ahead), jnp.stack(back)


def retain(rates, lengths, coef, a, high, gate, out_rows, up, down):
    micro, length, vd = high.shape
    hd = (a.shape[2] - vd) // 4
    state = (micro, 2, hd, vd)
    return call(
        retain_kernel,
        5,
        [smem()] * 3 + [vmem()] * 4 + [anywhere()] * 2,
        [
            ((micro, length, 2 * vd), BF, vmem()),
            ((micro, length, 2 * vd), F32, vmem()),
            (state, BF, vmem()),
            ((4 * out_rows.shape[0], out_rows.shape[1]), BF, vmem()),
            ((up.shape[0], 2 * up.shape[1]), BF, anywhere()),
            ((2 * down.shape[0], down.shape[1]), BF, anywhere()),
        ],
        state_scratch(state)
        + [
            pltpu.VMEM(out_rows.shape, BF),
            pltpu.VMEM((3, *out_rows.shape), BF),
            sems(3),
            sems(3),
            sems(2),
            sems(2),
            sems(2),
        ],
        4 * micro * length * length * (hd + vd),
        rates,
        lengths,
        coef,
        a,
        high,
        gate,
        out_rows,
        up,
        down,
    )


def retain_back(rates, lengths, coef, a, high, gate, kept, grad_mixed, state, part, keep, give):
    micro, length, vd = high.shape
    hd = (a.shape[2] - vd) // 4
    return call(
        retain_back_kernel,
        6,
        [smem()] * 3 + [vmem()] * 6 + [anywhere(), vmem(), anywhere()],
        [
            ((micro, length, a.shape[2]), BF, vmem()),
            ((micro, length, 3 * vd), BF, vmem()),
            (part.shape[1:], BF, vmem()),
            (give.shape, BF, vmem()),
        ],
        [
            pltpu.VMEM((micro, length, 2 * vd), BF),
            pltpu.VMEM((micro, length, 2 * hd), F32),
            pltpu.VMEM((micro, length, 2 * vd), F32),
            pltpu.VMEM(state.shape, BF),
        ]
        + state_scratch(state.shape)
        + [
            pltpu.VMEM((4, *part.shape[1:]), BF),
            pltpu.VMEM((7, *part.shape[1:]), BF),
            sems(7),
            sems(7),
            pltpu.SemaphoreType.DMA,
            pltpu.VMEM(give.shape, BF),
            pltpu.SemaphoreType.DMA,
            pltpu.SemaphoreType.DMA,
        ],
        12 * micro * length * length * (hd + vd),
        rates,
        lengths,
        coef,
        a,
        high,
        gate,
        kept,
        grad_mixed,
        state,
        part,
        keep,
        give,
    )


def project(tokens, gains, weights, out_weight, up_weight, down_weight):
    micro, rows, width = tokens.shape
    count = lax.axis_size("uly")
    query, key, value, gate = weights
    high = value.shape[1] // 2
    if not is_cube():
        first = jnp.concatenate([query, key, value[:, :high]], axis=1)
        second = jnp.concatenate([value[:, high:], gate], axis=1)
        full = lax.all_gather(jnp.stack(gains), BLK, axis=1, tiled=True)
        w_first = lax.all_gather(first, BLK, axis=0, tiled=True)
        w_second = lax.all_gather(second, BLK, axis=0, tiled=True)
        w_out = lax.all_gather(out_weight, BLK, axis=1, tiled=True)
        one = (normed(spread(tokens).astype(F32))[0] * full[0].astype(F32)).astype(BF)
        return (
            one,
            dot_nn(one, w_first, BF),
            dot_nn(one, w_second[:, :high], BF),
            dot_nn(one, w_second[:, high:]),
            w_first,
            w_second,
            w_out,
            full.astype(F32),
            up_weight,
            down_weight,
        )
    wide = count * rows
    piece = width // 8
    na, nb, no = 2 * query.shape[1] + high, high + gate.shape[1], out_weight.shape[0]
    units = up_weight.shape[1]
    return call(
        project_kernel,
        0,
        [vmem()] * 3 + [anywhere()] * 7,
        [
            ((micro, wide, width), BF, vmem()),
            ((micro, wide, na), BF, vmem()),
            ((micro, wide, high), BF, vmem()),
            ((micro, wide, nb - high), F32, vmem()),
            ((width, na), BF, anywhere()),
            ((width, nb), BF, anywhere()),
            ((no, width), BF, anywhere()),
            ((8, width), F32, vmem()),
            ((2 * piece, units // 2), BF, anywhere()),
            ((units // 2, 2 * piece), BF, anywhere()),
        ],
        [
            pltpu.VMEM((count, micro * rows, width), BF),
            pltpu.VMEM((width, na), BF),
            pltpu.VMEM((width, nb), BF),
            pltpu.VMEM((8, 8, piece), F32),
            sems(5, 7),
            sems(5, 7),
            sems(2, count - 1),
            sems(2, count - 1),
            sems(2),
            sems(2),
            sems(10),
        ],
        2 * micro * wide * width * (na + nb),
        tokens.reshape(micro * rows, width),
        gains[0][None],
        gains[1][None],
        query,
        key,
        value,
        gate,
        out_weight,
        up_weight,
        down_weight,
    )


def line_scratch(count, rows, width):
    return [
        pltpu.VMEM((count - 1, rows, width), BF),
        pltpu.VMEM((2, count - 1, rows, width), BF),
    ]


def add_rows(mixed, w_out, tokens, up, down):
    micro, wide, hidden = mixed.shape
    count = lax.axis_size("uly")
    rows = wide // count
    width = w_out.shape[1]
    units = up.shape[1]
    out = call(
        add_rows_kernel,
        1,
        [vmem()] * 3 + [anywhere()] * 2,
        [
            ((micro * rows, width), F32, vmem()),
            ((width, units), BF, anywhere()),
            ((units, width), BF, anywhere()),
        ],
        line_scratch(count, micro * rows, width)
        + [sems(2, count - 1)] * 2
        + [sems(2, 3), sems(2, 3), sems(2)],
        2 * micro * wide * hidden * width,
        mixed,
        w_out,
        tokens,
        up,
        down,
    )
    return out


def fan_out(rows_bf, w_out, mixed, up_grad, down_grad):
    own, width = rows_bf.shape
    micro, rows = 2, own // 2
    count = lax.axis_size("uly")
    hidden = w_out.shape[0]
    up_shape, down_shape = up_grad.shape[1:], down_grad.shape[1:]
    return call(
        fan_out_kernel,
        2,
        [vmem()] * 3 + [anywhere()] * 2,
        [
            ((micro, count * rows, hidden), F32, vmem()),
            ((8, width // 8, hidden), BF, vmem()),
            (up_shape, BF, vmem()),
            (down_shape, BF, vmem()),
        ],
        [
            pltpu.VMEM((count, own, width), BF),
            pltpu.VMEM((own, width), BF),
            pltpu.VMEM((8, width // 8, hidden), F32),
            pltpu.VMEM((4, *up_shape), BF),
            pltpu.VMEM((4, *down_shape), BF),
            pltpu.VMEM((3, *up_shape), BF),
            pltpu.VMEM((3, *down_shape), BF),
            sems(2, count - 1),
            sems(2, count - 1),
            sems(2, 3),
            sems(2, 3),
            sems(2),
        ],
        4 * micro * count * rows * hidden * width,
        rows_bf,
        w_out,
        mixed,
        up_grad,
        down_grad,
    )


def feed_all(hidden, douts, gain, ups, downs):
    own, width = hidden.shape
    units = ups.shape[1]
    return call(
        feed_kernel,
        4,
        [vmem()] * 5,
        [
            ((own, width), F32, vmem()),
            ((own, width), BF, vmem()),
            ((own, width), F32, vmem()),
            ((own, width), BF, vmem()),
            ((1, width), F32, vmem()),
            ((4, width // 4, units), BF, vmem()),
            ((4, units, width // 4), BF, vmem()),
        ],
        [
            pltpu.VMEM((4 * own, width), BF),
            pltpu.VMEM((4 * own, units), BF),
            pltpu.VMEM((4 * own, units), BF),
            pltpu.VMEM((2, own, width), F32),
            pltpu.VMEM((3, 2, own, width), BF),
            pltpu.VMEM((5, own, width), BF),
            sems(8),
            sems(8),
        ],
        2 * 6 * 4 * own * units * width,
        hidden,
        douts,
        gain,
        ups,
        downs,
    )


def feed_scatter(up_sum, down_sum):
    def settle(array, dim):
        half = array.shape[dim] // 2
        keep = lax.slice_in_dim(array, 0, half, axis=dim)
        away = lax.slice_in_dim(array, half, 2 * half, axis=dim)
        total = (keep.astype(F32) + shift(away, 2).astype(F32)).astype(BF)
        own, other = core_cut(total, 1 - dim)
        return core_join(own, swap(other, 1), dim).astype(F32)

    return settle(up_sum, 1), settle(down_sum, 0)


def middle(tokens, out_grad, douts, gains, mixed, w_out, up_weight, down_weight):
    micro, rows, width = tokens.shape
    own = micro * rows
    if not is_cube():
        gain_two = gains[1]
        hidden = tokens.astype(F32) + collect(
            jnp.stack([dot_nn(mixed[m], w_out) for m in range(micro)])
        )
        pair = feed_weights(up_weight, down_weight)
        hat, scale = normed(hidden)
        two = (hat * gain_two).astype(BF)
        flat_two, flat_out = two.reshape(own, width), out_grad.reshape(own, width)
        two_both = jnp.concatenate([flat_two, swap(flat_two, 1)], axis=0)
        out_both = jnp.concatenate([flat_out, swap(flat_out, 1)], axis=0)
        down_rows, grad_two, up_part, down_part = feed(two_both, out_both, pair)
        grad_two = grad_two[:own] + swap(grad_two[own:].astype(BF), 1).astype(F32)
        down_rows = down_rows[:own] + swap(down_rows[own:].astype(BF), 1).astype(F32)
        up_grad, down_grad = feed_reduce(up_part, down_part)
        block_out = (hidden + down_rows.reshape(micro, rows, width)).astype(BF)
        grad_two = grad_two.reshape(micro, rows, width)
        gain_part = jnp.sum(grad_two * hat, axis=(0, 1))
        grad_hidden = out_grad.astype(F32) + norm_back(grad_two * gain_two, hat, scale)
        wide_att = spread(grad_hidden.astype(BF))
        grad_mixed = jnp.stack([dot_nt(wide_att[m], w_out) for m in range(micro)])
        part = dot_tn(
            mixed.reshape(-1, mixed.shape[2]), wide_att.reshape(-1, wide_att.shape[2]), BF
        )
        return block_out, up_grad, down_grad, gain_part, grad_hidden, grad_mixed, part
    hidden, ups, downs = add_rows(mixed, w_out, tokens.reshape(own, width), up_weight, down_weight)
    keep, give, grad_hidden, rows_bf, gain_part, up_part, down_part = feed_all(
        hidden, douts, gains, ups, downs
    )
    grad_mixed, part, up_sum, down_sum = fan_out(rows_bf, w_out, mixed, up_part, down_part)
    up_grad, down_grad = feed_scatter(up_sum, down_sum)
    return (
        (keep, give),
        up_grad,
        down_grad,
        gain_part,
        grad_hidden,
        grad_mixed,
        part,
    )


def close_rows(xa, xb, w_first, w_second, one, tokens, grad_hidden, gains, gain_two):
    micro, wide, na = xa.shape
    nb = xb.shape[2]
    width = w_first.shape[0]
    flat_a, flat_b = xa.reshape(micro * wide, na), xb.reshape(micro * wide, nb)
    flat_one = one.reshape(micro * wide, width)
    if not is_cube():
        partial = jnp.stack(
            [dot_nt(xa[m], w_first) + dot_nt(xb[m], w_second) for m in range(micro)]
        )
        grad_one = collect(partial)
        hat, scale = normed(tokens.astype(F32))
        both_gains = jnp.stack([jnp.sum(grad_one * hat, axis=(0, 1)), gain_two])
        total = lax.psum_scatter(both_gains, BLK, scatter_dimension=1, tiled=True)
        return (
            grad_hidden + norm_back(grad_one * gains[0], hat, scale),
            lax.psum_scatter(dot_tn(flat_one, flat_a, BF), BLK, scatter_dimension=0, tiled=True),
            lax.psum_scatter(dot_tn(flat_one, flat_b, BF), BLK, scatter_dimension=0, tiled=True),
            lax.psum(total, "uly"),
        )
    count = lax.axis_size("uly")
    rows = wide // count
    piece = width // 8
    out = call(
        close_rows_kernel,
        3,
        [vmem()] * 9,
        [
            ((micro * rows, width), F32, vmem()),
            ((piece, na), BF, vmem()),
            ((piece, nb), BF, vmem()),
            ((8, piece), F32, vmem()),
        ],
        line_scratch(count, micro * rows, width)
        + [
            pltpu.VMEM((4, piece, na), BF),
            pltpu.VMEM((4, piece, nb), BF),
            pltpu.VMEM((2, piece, na), BF),
            pltpu.VMEM((2, piece, nb), BF),
            pltpu.VMEM((7, piece, na), BF),
            pltpu.VMEM((7, piece, nb), BF),
            pltpu.VMEM((1, width), F32),
            pltpu.VMEM((8, 8, piece), F32),
            pltpu.VMEM((8, 8, piece), F32),
            pltpu.VMEM((4, 8, piece), F32),
            sems(2, count - 1),
            sems(2, count - 1),
            sems(2, 7),
            sems(2, 7),
            sems(6),
            sems(6),
        ],
        4 * micro * wide * width * (na + nb),
        flat_a,
        flat_b,
        w_first,
        w_second,
        flat_one,
        tokens.reshape(micro * rows, width),
        grad_hidden,
        gains,
        gain_two,
    )
    return out[0].reshape(micro, rows, width), *out[1:]


def feed(norm_two, out_rows, pair):
    chips, count, _, rows, hidden = pair.shape
    up = pair[:, :, 0].transpose(0, 2, 1, 3).reshape(chips * rows, count * hidden)
    down_t = pair[:, :, 1].transpose(0, 2, 1, 3).reshape(chips * rows, count * hidden)
    upward = dot_nn(norm_two, up)
    act, slope = gelu_pair(upward)
    act = act.astype(BF)
    grad_act = dot_nn(out_rows, down_t)
    grad_up = (grad_act * slope).astype(BF)

    def by_owner(grad):
        return grad.reshape(chips, rows, count, hidden).transpose(0, 2, 1, 3)

    return (
        dot_nt(act, down_t),
        dot_nt(grad_up, up),
        by_owner(dot_tn(norm_two, grad_up, BF)),
        by_owner(dot_tn(out_rows, act, BF)),
    )


def plain_forward(rates, lengths, a, v_high, gate):
    micro, length = a.shape[:2]
    heads_here = rates.shape[0]
    cut_v = v_high.shape[2]
    qk = (a.shape[2] - cut_v) // 2
    hd, vd = qk // heads_here, 2 * cut_v // heads_here
    sets, parts, states = [], [], []
    for m in range(micro):
        values = jnp.concatenate([a[m, :, 2 * qk :], v_high[m]], axis=1)
        heads = [
            (
                a[m, :, h * hd : (h + 1) * hd],
                a[m, :, qk + h * hd : qk + (h + 1) * hd],
                values[:, h * vd : (h + 1) * vd],
            )
            for h in range(heads_here)
        ]
        part = decay_parts(rates, lengths[m], length)
        states.append(retention_state(heads, part[2]))
        sets.append(heads)
        parts.append(part)

    all_states = exchange(states)
    state_in, retained, mixed = [], [], []
    for m in range(micro):
        state = state_sum(parts[m][3], all_states[m])
        kept = retention(sets[m], parts[m], state)
        state_in.append(state)
        retained.append(kept)
        mixed.append(mix(gate[m], kept))
    mixed = jnp.stack(mixed)
    return mixed, (sets, parts, state_in, retained)


def plain_backward(gate, kept, grad_mixed):
    sets, parts, state_in, retained = kept
    micro, cut_v = len(sets), gate.shape[2] // 2
    grad_gates, grad_rets, grad_states = [], [], []
    for m in range(micro):
        gg, gr = mix_back(gate[m], retained[m], grad_mixed[m])
        grad_gates.append(gg)
        grad_rets.append(gr)
        grad_states.append(
            jnp.stack(
                [
                    dot_tn((q.astype(F32) * parts[m][1][h]).astype(BF), gr[h], BF)
                    for h, (q, k, v) in enumerate(sets[m])
                ]
            )
        )
    all_back = exchange(grad_states)
    xa, xb = [], []
    for m in range(micro):
        back = state_sum(parts[m][4], all_back[m])
        grads = retention_back(sets[m], parts[m], state_in[m], grad_rets[m], back)
        gq = jnp.concatenate([g[0] for g in grads], axis=1)
        gk = jnp.concatenate([g[1] for g in grads], axis=1)
        gv = jnp.concatenate([g[2] for g in grads], axis=1)
        xa.append(jnp.concatenate([gq, gk, gv[:, :cut_v]], axis=1))
        xb.append(jnp.concatenate([gv[:, cut_v:], grad_gates[m]], axis=1))
    xa, xb = jnp.stack(xa), jnp.stack(xb)
    return xa, xb


def body(
    tokens,
    retain_gain,
    query_weight,
    key_weight,
    value_weight,
    gate_matrix,
    output_weight,
    feed_gain,
    up_weight,
    down_weight,
    decay_rate,
    lengths,
    out_grad,
):
    micro, rows, width = tokens.shape
    heads_here = decay_rate.shape[0] // lax.axis_size("uly")
    rates = lax.dynamic_slice_in_dim(decay_rate, lax.axis_index("uly") * heads_here, heads_here)
    qk = query_weight.shape[1]
    cut_v = value_weight.shape[1] // 2

    one, a, v_high, gate, w_first, w_second, w_out, gains, up, down = project(
        tokens,
        (retain_gain, feed_gain),
        (query_weight, key_weight, value_weight, gate_matrix),
        output_weight,
        up_weight,
        down_weight,
    )
    if is_cube():
        coef, coef_back = chip_weights(rates, lengths, one.shape[1])
        mixed, kept, state, douts, up, down = retain(
            rates, lengths, coef, a, v_high, gate, out_grad.reshape(micro * rows, width), up, down
        )
    else:
        mixed, kept = plain_forward(rates, lengths, a, v_high, gate)
        douts = None

    block_out, up_grad, down_grad, gain_two, grad_hidden, grad_mixed, part = middle(
        tokens, out_grad, douts, gains, mixed, w_out, up, down
    )

    if is_cube():
        xa, xb, out_sum, block_out = retain_back(
            rates, lengths, coef_back, a, v_high, gate, kept, grad_mixed, state, part, *block_out
        )
        block_out = block_out.reshape(tokens.shape)
        out_sum = out_sum.T
    else:
        xa, xb = plain_backward(gate, kept, grad_mixed)
        out_sum = lax.psum_scatter(part, BLK, scatter_dimension=1, tiled=True)

    input_grad, first_sum, second_sum, gain_sums = close_rows(
        xa, xb, w_first, w_second, one, tokens, grad_hidden, gains, gain_two
    )
    first_sum, second_sum = first_sum.astype(F32), second_sum.astype(F32)
    return (
        block_out,
        input_grad,
        gain_sums[0],
        first_sum[:, :qk],
        first_sum[:, qk : 2 * qk],
        jnp.concatenate([first_sum[:, 2 * qk :], second_sum[:, :cut_v]], axis=1),
        second_sum[:, cut_v:],
        out_sum.astype(F32),
        gain_sums[1],
        up_grad,
        down_grad,
    )


def solution(mesh):
    blocks, count = mesh.devices.shape
    split = Mesh(mesh.devices.reshape(blocks // 2, 2, count), AXES)
    rows = P(None, AXES, None)
    gain, wide, tall = P(BLK), P(BLK, "uly"), P("uly", BLK)
    return jax.shard_map(
        body,
        mesh=split,
        in_specs=(rows, gain, wide, wide, wide, wide, tall, gain, wide, tall, P(), P(), rows),
        out_specs=(rows, rows, gain, wide, wide, wide, wide, tall, gain, wide, tall),
        check_vma=False,
    )
```

```python
import functools

import jax
import jax.numpy as jnp
from jax import lax
from jax.experimental import pallas as pl
from jax.experimental.pallas import tpu as pltpu
from jax.sharding import Mesh
from jax.sharding import PartitionSpec as P

EPSILON = 1e-05
BF = jnp.bfloat16
F32 = jnp.float32
AXES = ("chip", "core", "uly")
BLK = ("chip", "core")
MESH = pl.DeviceIdType.MESH
VMEM_LIMIT = 62 * 1024 * 1024


def dot_nn(left, right, kind=F32):
    return jnp.dot(left, right, preferred_element_type=F32).astype(kind)


def dot_tn(left, right, kind=F32):
    return lax.dot_general(
        left, right, (((0,), (0,)), ((), ())), preferred_element_type=F32
    ).astype(kind)


def dot_nt(left, right, kind=F32):
    return lax.dot_general(
        left, right, (((1,), (1,)), ((), ())), preferred_element_type=F32
    ).astype(kind)


def block_index():
    return lax.axis_index("chip") * 2 + lax.axis_index("core")


def block_count():
    return lax.axis_size("chip") * 2


def swap(array, mask):
    if mask == 1:
        return lax.ppermute(array, "core", [(0, 1), (1, 0)])
    count = lax.axis_size("chip")
    return lax.ppermute(array, "chip", [(b, b ^ (mask // 2)) for b in range(count)])


def shift(array, step):
    count = lax.axis_size("uly")
    return lax.ppermute(array, "uly", [(z, (z + step) % count) for z in range(count)])


def is_cube():
    return lax.axis_size("chip") == 4 and lax.axis_size("uly") == 4


def masks():
    return [2 * k + j for j in range(2) for k in range(4)]


def plane_gather(first, second):
    first_x = swap(first, 2)
    second_y = swap(second, 4)
    first_y, first_xy = swap(first, 4), swap(first_x, 4)
    second_x, second_xy = swap(second, 2), swap(second_y, 2)
    return [first, first_x, first_y, first_xy], [second, second_x, second_y, second_xy]


def exchange(pieces):
    if not is_cube():
        return [lax.all_gather(p, BLK) for p in pieces]
    half = len(pieces) // 2
    a, b = plane_gather(jnp.stack(pieces[:half]), jnp.stack(pieces[half:]))
    got = []
    for four in (a, b):
        full = jnp.stack(four + [swap(p, 1) for p in four])
        got += [full[:, i] for i in range(full.shape[1])]
    return got


def spread(rows):
    return lax.all_gather(rows, "uly", axis=1, tiled=True)


def collect(partial):
    return lax.psum_scatter(partial.astype(BF), "uly", scatter_dimension=1, tiled=True).astype(F32)


def core_cut(array, dim):
    core = lax.axis_index("core")
    half = array.shape[dim] // 2
    own = lax.dynamic_slice_in_dim(array, core * half, half, dim)
    other = lax.dynamic_slice_in_dim(array, (1 - core) * half, half, dim)
    return own, other


def core_join(own, other, dim):
    first = lax.axis_index("core") == 0
    return jnp.concatenate([jnp.where(first, own, other), jnp.where(first, other, own)], axis=dim)


def feed_weights(up_shard, down_shard):
    own, other = core_cut(up_shard, 1)
    up = core_join(own, swap(other, 1), 0)
    own, other = core_cut(down_shard, 0)
    down = core_join(own, swap(other, 1), 1)
    pair = lax.all_gather(jnp.stack([up, down.T]), ("chip", "uly"), axis=0, tiled=False)
    chips, count = lax.axis_size("chip"), lax.axis_size("uly")
    rows, hidden = up.shape
    pair = pair.reshape(chips, count, 2, rows, hidden)
    return pair


def feed_reduce(up_grad, down_grad):
    pair = jnp.stack([up_grad, down_grad], axis=2)
    chips, count = pair.shape[:2]
    pair = pair.reshape(chips * count * 2, *pair.shape[3:])
    total = lax.psum_scatter(pair, ("chip", "uly"), scatter_dimension=0, tiled=True)
    half = total.shape[1] // 2
    own, other = core_cut(total, 1)
    both_halves = core_join(own, swap(other, 1), 2).astype(F32)
    return both_halves[0], both_halves[1].T


def normed(values):
    center = values - jnp.mean(values, axis=-1, keepdims=True)
    scale = lax.rsqrt(jnp.mean(center * center, axis=-1, keepdims=True) + EPSILON)
    return center * scale, scale


def norm_back(grad, hat, scale):
    return scale * (
        grad
        - jnp.mean(grad, axis=-1, keepdims=True)
        - hat * jnp.mean(grad * hat, axis=-1, keepdims=True)
    )


GELU_A = 0.7978845608028654
GELU_B = 0.044715


def gelu_pair(u):
    square = u * u
    tanh = jnp.tanh(GELU_A * u * (1.0 + GELU_B * square))
    slope = 0.5 * (1.0 + tanh) + 0.5 * u * (1.0 - tanh * tanh) * GELU_A * (
        1.0 + 3.0 * GELU_B * square
    )
    return 0.5 * u * (1.0 + tanh), slope


def segment_ids(positions, lengths_row):
    count = lengths_row.shape[0]
    before = jnp.arange(count)[None, :] < jnp.arange(count)[:, None]
    bounds = jnp.sum(jnp.where(before, lengths_row[None, :], 0), axis=1)
    return jnp.sum((bounds[None, :] <= positions[:, None]).astype(jnp.int32), axis=1)


def decay_parts(rates, lengths_row, length):
    me = block_index()
    count = block_count()
    places = jnp.arange(length, dtype=jnp.int32)
    seg = segment_ids(me * length + places, lengths_row)
    ends = segment_ids((jnp.arange(count, dtype=jnp.int32) + 1) * length - 1, lengths_row)
    seg_prev = segment_ids(jnp.reshape(me * length - 1, (1,)), lengths_row)[0]
    offset = places[:, None] - places[None, :]
    causal = (offset >= 0) & (seg[:, None] == seg[None, :])
    far = jnp.maximum(offset, 0).astype(F32)
    inner = jnp.where(causal[None], jnp.exp(-rates[:, None, None] * far[None]), 0.0)
    at = places.astype(F32)
    entry = jnp.where(seg == seg_prev, jnp.exp(-rates[:, None] * (at + 1.0)), 0.0)
    leave = jnp.where(seg == seg[length - 1], jnp.exp(-rates[:, None] * (length - 1.0 - at)), 0.0)
    if is_cube():
        source = me ^ jnp.asarray(masks(), jnp.int32)
    else:
        source = jnp.arange(count, dtype=jnp.int32)
    end_of = ends[source]
    end_before = jnp.where(source > 0, ends[jnp.maximum(source - 1, 0)], 0)
    past = jnp.maximum(me - 1 - source, 0).astype(F32)
    ahead = jnp.maximum(source - 1 - me, 0).astype(F32)
    from_past = jnp.where(
        (source < me) & (end_of == seg_prev), jnp.exp(-rates[:, None] * (length * past)), 0.0
    )
    from_ahead = jnp.where(
        (source > me) & (end_before == ends[me]), jnp.exp(-rates[:, None] * (length * ahead)), 0.0
    )
    return inner, entry[:, :, None], leave[:, :, None], from_past, from_ahead


def state_sum(weights, states):
    return jnp.einsum("hb,bhde->hde", weights, states.astype(F32))


def retention_state(heads, leave):
    return jnp.stack(
        [
            dot_tn((k.astype(F32) * leave[h]).astype(BF), v, BF)
            for h, (q, k, v) in enumerate(heads)
        ]
    )


def retention(heads, parts, state):
    inner, entry = parts[0], parts[1]
    out = []
    for h, (q, k, v) in enumerate(heads):
        scores = (dot_nt(q, k) * inner[h]).astype(BF)
        out.append(dot_nn(scores, v) + entry[h] * dot_nn(q, state[h].astype(BF)))
    return out


def mix(gate, retained):
    out = []
    for h, r in enumerate(retained):
        g = gate[:, h * r.shape[1] : (h + 1) * r.shape[1]]
        out.append((g * jax.nn.sigmoid(g) * normed(r)[0]).astype(BF))
    return jnp.concatenate(out, axis=1)


def mix_back(gate, retained, grad_mixed):
    grad_gate, grad_retained = [], []
    for h, r in enumerate(retained):
        cols = slice(h * r.shape[1], (h + 1) * r.shape[1])
        g, gm = gate[:, cols], grad_mixed[:, cols]
        sigma = jax.nn.sigmoid(g)
        hat, scale = normed(r)
        grad_gate.append((gm * hat * (sigma + g * sigma * (1.0 - sigma))).astype(BF))
        grad_retained.append(norm_back(gm * g * sigma, hat, scale).astype(BF))
    return jnp.concatenate(grad_gate, axis=1), grad_retained


def retention_back(heads, parts, state, grad_retained, grad_state):
    inner, entry, leave = parts[0], parts[1], parts[2]
    grads = []
    for h, (q, k, v) in enumerate(heads):
        gr = grad_retained[h]
        scores = (dot_nt(q, k) * inner[h]).astype(BF)
        pulls = (dot_nt(gr, v) * inner[h]).astype(BF)
        gs, st = grad_state[h].astype(BF), state[h].astype(BF)
        gq = dot_nn(pulls, k) + entry[h] * dot_nt(gr, st)
        gk = dot_tn(pulls, q) + leave[h] * dot_nt(v, gs)
        gv = dot_tn(scores, gr) + leave[h] * dot_nn(k, gs)
        grads.append((gq.astype(BF), gk.astype(BF), gv.astype(BF)))
    return grads


def vmem():
    return pl.BlockSpec(memory_space=pltpu.VMEM)


def anywhere():
    return pl.BlockSpec(memory_space=pl.ANY)


def greet(plane=False, line=False, cores=False, pair=False, across=False, whole=False, every=False):
    barrier = pltpu.get_barrier_semaphore()
    chip, core, z = (lax.axis_index(a) for a in AXES)
    others = []
    if plane:
        others += [{"chip": chip ^ 1}, {"chip": chip ^ 2}]
    if cores:
        others.append({"core": 1 - core})
    if pair:
        others.append({"uly": z ^ 1})
    if across:
        others.append({"uly": z ^ 2})
    if whole:
        others += [{"uly": z ^ k} for k in range(1, 4)]
    if every:
        others += [{"chip": chip ^ (p % 4), "core": core ^ (p // 4)} for p in range(1, 8)]
    for to in others:
        pl.semaphore_signal(barrier, inc=1, device_id=to, device_id_type=MESH)
    count = len(others)
    if line:
        last = lax.axis_size("uly") - 1

        @pl.when(z > 0)
        def _():
            pl.semaphore_signal(barrier, inc=1, device_id={"uly": z - 1}, device_id_type=MESH)

        @pl.when(z < last)
        def _():
            pl.semaphore_signal(barrier, inc=1, device_id={"uly": z + 1}, device_id_type=MESH)

        count = count + jnp.where(z > 0, 1, 0) + jnp.where(z < last, 1, 0)
    pl.semaphore_wait(barrier, count)


class PlaneGather:
    def __init__(self, own, at, x_first, send, recv, cores=True):
        chip, core = lax.axis_index("chip"), lax.axis_index("core")
        x, y, other = {"chip": chip ^ 1}, {"chip": chip ^ 2}, {"core": 1 - core}

        def copy(i, src, place, to):
            return pltpu.make_async_remote_copy(
                src_ref=src,
                dst_ref=at(place),
                send_sem=send.at[i],
                recv_sem=recv.at[i],
                device_id=to,
                device_id_type=MESH,
            )

        self.x_first = x_first
        self.copies = [
            copy(0, own, 1, x),
            copy(1, own, 2, y),
            copy(2, at(1), 3, y) if x_first else copy(2, at(2), 3, x),
        ]
        self.cores = cores
        if cores:
            self.copies += [
                copy(3, own, 4, other),
                copy(4, at(1), 5, other),
                copy(5, at(2), 6, other),
                copy(6, at(3), 7, other),
            ]

    def start(self):
        for i in (0, 1) if self.x_first else (1, 0):
            self.copies[i].start()
        if self.cores:
            self.copies[3].start()

    def near(self):
        first = 0 if self.x_first else 1
        self.copies[first].wait_recv()
        self.copies[2].start()
        if self.cores:
            self.copies[4 + first].start()

    def far(self):
        second = 1 if self.x_first else 0
        self.copies[second].wait_recv()
        if self.cores:
            self.copies[4 + second].start()

    def corner(self):
        self.copies[2].wait_recv()
        if self.cores:
            self.copies[6].start()

    def finish(self):
        for c in self.copies[3:]:
            c.wait_recv()
        for c in self.copies:
            c.wait_send()


class LineGather:
    def __init__(self, slots, send, recv):
        self.z = lax.axis_index("uly")
        self.last = lax.axis_size("uly") - 1
        self.slots, self.send, self.recv = slots, send, recv

    def copy(self, right, d):
        z, last = self.z, self.last
        at = jnp.maximum(z - d, 0) if right else jnp.minimum(z + d, last)
        to = jnp.minimum(z + 1, last) if right else jnp.maximum(z - 1, 0)
        way = 0 if right else 1
        return pltpu.make_async_remote_copy(
            src_ref=self.slots.at[at],
            dst_ref=self.slots.at[at],
            send_sem=self.send.at[way, d],
            recv_sem=self.recv.at[way, d],
            device_id={"uly": to},
            device_id_type=MESH,
        )

    def pass_on(self, d):
        z, last = self.z, self.last

        @pl.when((z - d >= 0) & (z < last))
        def _():
            self.copy(True, d).start()

        @pl.when((z + d <= last) & (z > 0))
        def _():
            self.copy(False, d).start()

    def take(self, d, then):
        z, last = self.z, self.last

        @pl.when(z - d >= 0)
        def _():
            self.copy(True, d - 1).wait_recv()

        @pl.when(z + d <= last)
        def _():
            self.copy(False, d - 1).wait_recv()

        if d < last:
            self.pass_on(d)
        self.each(d, then)

    def each(self, d, then):
        z, last = self.z, self.last

        @pl.when(z - d >= 0)
        def _():
            then(jnp.maximum(z - d, 0))

        @pl.when(z + d <= last)
        def _():
            then(jnp.minimum(z + d, last))

    def finish(self):
        z, last = self.z, self.last
        for d in range(last):

            @pl.when((z - d >= 0) & (z < last))
            def _():
                self.copy(True, d).wait_send()

            @pl.when((z + d <= last) & (z > 0))
            def _():
                self.copy(False, d).wait_send()


class LineReduce:
    def __init__(self, make, out, held, came, send, recv):
        self.z = lax.axis_index("uly")
        self.last = lax.axis_size("uly") - 1
        self.make, self.out, self.held, self.came = make, out, held, came
        self.send, self.recv = send, recv

    def copy(self, right, d):
        z, last = self.z, self.last
        way = 0 if right else 1
        to = jnp.minimum(z + 1, last) if right else jnp.maximum(z - 1, 0)
        return pltpu.make_async_remote_copy(
            src_ref=self.held.at[self.place(right, d)],
            dst_ref=self.came.at[way, d - 1],
            send_sem=self.send.at[way, d - 1],
            recv_sem=self.recv.at[way, d - 1],
            device_id={"uly": to},
            device_id_type=MESH,
        )

    def place(self, right, d):
        return d - 1 if right else self.last - d

    def step(self, d):
        z, last = self.z, self.last
        for right in (True, False):
            way = 0 if right else 1
            held = self.held.at[self.place(right, d)]
            valid = (z + d <= last) if right else (z - d >= 0)
            more = (z > 0) if right else (z < last)
            to = jnp.minimum(z + d, last) if right else jnp.maximum(z - d, 0)

            @pl.when(valid)
            def _():
                self.make(to, held)

                if d < last:

                    @pl.when(more)
                    def _():
                        self.copy(right, d + 1).wait_recv()
                        held[...] = (held[...].astype(F32) + self.came[way, d].astype(F32)).astype(
                            BF
                        )

                self.copy(right, d).start()

    def close(self):
        z, last = self.z, self.last
        self.make(z, self.out)

        @pl.when(z > 0)
        def _():
            self.copy(True, 1).wait_recv()
            self.out[...] += self.came[0, 0].astype(F32)

        @pl.when(z < last)
        def _():
            self.copy(False, 1).wait_recv()
            self.out[...] += self.came[1, 0].astype(F32)

        for d in range(1, last + 1):

            @pl.when(z + d <= last)
            def _():
                self.copy(True, d).wait_send()

            @pl.when(z - d >= 0)
            def _():
                self.copy(False, d).wait_send()


def chunk_of(place, width):
    chip, core = lax.axis_index("chip"), lax.axis_index("core")
    block = (chip ^ (place % 4)) * 2 + (core ^ (place // 4))
    return pl.ds(pl.multiple_of(block * width, width), width)


def chip_chunk(k, width):
    return pl.ds(pl.multiple_of((lax.axis_index("chip") ^ k) * width, width), width)


def chip_order(place, width):
    core = lax.axis_index("core")
    return pl.ds(pl.multiple_of((place % 4) * (2 * width) + (core ^ (place // 4)) * width, width), width)


def front_kernel(
    rates_ref,
    lengths_ref,
    tok_ref,
    dout_ref,
    gain_ref,
    q_hbm,
    k_hbm,
    v_hbm,
    g_hbm,
    out_hbm,
    up_hbm,
    down_hbm,
    one_ref,
    first_ref,
    high_ref,
    gate_ref,
    w_first_hbm,
    w_second_hbm,
    w_out_hbm,
    gains_ref,
    up_own_hbm,
    down_own_hbm,
    mixed_ref,
    kept_ref,
    state_ref,
    douts_ref,
    slots,
    wa,
    wb,
    gains,
    psend,
    precv,
    zsend,
    zrecv,
    fsend,
    frecv,
    dsend,
    drecv,
    lsem,
    *state_refs,
):
    core, z = lax.axis_index("core"), lax.axis_index("uly")
    rows = tok_ref.shape[0] // 2
    width = tok_ref.shape[1]
    piece = width // 8
    qk, high = q_hbm.shape[1], high_ref.shape[2]
    greet(plane=True, line=True, cores=True, across=True)
    line = LineGather(slots, zsend, zrecv)
    slots[z] = tok_ref[...]
    line.pass_on(0)
    own = pl.ds(0, piece)
    local = [
        pltpu.make_async_copy(src, dst, lsem.at[i])
        for i, (src, dst) in enumerate(
            (
                (q_hbm, wa.at[own, pl.ds(0, qk)]),
                (k_hbm, wa.at[own, pl.ds(qk, qk)]),
                (v_hbm.at[:, pl.ds(0, high)], wa.at[own, pl.ds(2 * qk, high)]),
                (v_hbm.at[:, pl.ds(high, high)], wb.at[own, pl.ds(0, high)]),
                (g_hbm, wb.at[own, pl.ds(high, g_hbm.shape[1])]),
                (out_hbm, w_out_hbm.at[:, own]),
            )
        )
    ]
    for c in local:
        c.start()
    gains[0] = jnp.zeros_like(gains[0])
    gains[0, 0:2, :] = gain_ref[...]
    items = [
        PlaneGather(gains.at[0], lambda p: gains.at[p], True, psend.at[0], precv.at[0])
    ]
    for i, w in enumerate((wa, wb)):
        items.append(
            PlaneGather(
                w.at[own],
                lambda p, w=w: w.at[pl.ds(p * piece, piece)],
                i == 0,
                psend.at[1 + i],
                precv.at[1 + i],
            )
        )
    half = out_hbm.shape[0] // 2
    for i in range(2):
        part = pl.ds(i * half, half)
        items.append(
            PlaneGather(
                out_hbm.at[part],
                lambda p, part=part: w_out_hbm.at[part, pl.ds(p * piece, piece)],
                i == 0,
                psend.at[3 + i],
                precv.at[3 + i],
            )
        )
    items[0].start()
    units, cols = up_hbm.shape[1] // 2, down_hbm.shape[1]
    first_half = pl.ds(0, units)
    mine, theirs = (pl.ds(pl.multiple_of(c * units, units), units) for c in (core, 1 - core))
    here = pl.ds(pl.multiple_of(core * cols, cols), cols)

    def remote(i, src, dst, to):
        return pltpu.make_async_remote_copy(
            src_ref=src,
            dst_ref=dst,
            send_sem=fsend.at[i],
            recv_sem=frecv.at[i],
            device_id=to,
            device_id_type=MESH,
        )

    cut = [
        pltpu.make_async_copy(up_hbm.at[:, mine], up_own_hbm.at[here, first_half], lsem.at[6]),
        pltpu.make_async_copy(down_hbm.at[mine], down_own_hbm.at[first_half, here], lsem.at[7]),
    ]
    give = [
        remote(0, up_hbm.at[:, theirs], up_own_hbm.at[here, first_half], {"core": 1 - core}),
        remote(1, down_hbm.at[theirs], down_own_hbm.at[first_half, here], {"core": 1 - core}),
    ]
    first_wide, second_wide = up_own_hbm.at[:, first_half], up_own_hbm.at[:, pl.ds(units, units)]
    first_tall, second_tall = down_own_hbm.at[first_half], down_own_hbm.at[pl.ds(units, units)]
    away = [
        remote(2, first_wide, second_wide, {"uly": z ^ 2}),
        remote(3, first_tall, second_tall, {"uly": z ^ 2}),
    ]
    own_rows = 2 * rows

    def rows_to(i, src, dst, to):
        return pltpu.make_async_remote_copy(
            src_ref=douts_ref.at[pl.ds(src * own_rows, own_rows)],
            dst_ref=douts_ref.at[pl.ds(dst * own_rows, own_rows)],
            send_sem=dsend.at[i],
            recv_sem=drecv.at[i],
            device_id=to,
            device_id_type=MESH,
        )

    send_rows = [
        rows_to(0, 0, 2, {"uly": z ^ 1}),
        rows_to(1, 0, 1, {"core": 1 - core}),
        rows_to(2, 2, 3, {"core": 1 - core}),
    ]
    for c in cut:
        c.start()
    for c in local[:5]:
        c.wait()
    for item in items[1:3]:
        item.start()
    for c in give:
        c.start()
    items[0].near()
    items[0].far()
    items[0].corner()
    items[0].finish()
    gains_ref[...] = jnp.zeros_like(gains_ref)
    for p in range(8):
        gains_ref[0:1, chunk_of(p, piece)] = gains[p, 0:1, :]
        gains_ref[1:2, chip_order(p, piece)] = gains[p, 1:2, :]

    def normalize(slot):
        step = 32
        for m in range(2):

            @pl.loop(0, rows // step)
            def _(i):
                at = pl.multiple_of(i * step, step)
                v = slots[slot, pl.ds(m * rows + at, step), :].astype(F32)
                mean = jnp.mean(v, axis=-1, keepdims=True)
                center = v - mean
                scale = lax.rsqrt(jnp.mean(center * center, axis=-1, keepdims=True) + EPSILON)
                to = pl.ds(pl.multiple_of(slot * rows + at, step), step)
                for p in range(8):
                    src = slots[slot, pl.ds(m * rows + at, step), chunk_of(p, piece)].astype(F32)
                    one_ref[m, to, pl.ds(p * piece, piece)] = (
                        (src - mean) * scale * gains[p, 0:1, :]
                    ).astype(BF)

    for k in range(4):
        douts_ref[0:own_rows, k * 2 * piece : (k + 1) * 2 * piece] = dout_ref[
            :, chip_chunk(k, 2 * piece)
        ]
    normalize(z)
    line.take(1, normalize)
    for item in items[1:3]:
        item.near()
    for item in items[1:3]:
        item.far()
    for item in items[3:]:
        item.start()
    line.take(2, normalize)
    for item in items[1:3]:
        item.corner()
    for item in items[1:3]:
        item.finish()
    outs = [
        pltpu.make_async_copy(wa, w_first_hbm, lsem.at[8]),
        pltpu.make_async_copy(wb, w_second_hbm, lsem.at[9]),
    ]
    for c in outs:
        c.start()
    tile = 512

    def multiply(slot):
        at = pl.ds(pl.multiple_of(slot * rows, rows), rows)
        x = jnp.concatenate([one_ref[0, at, :], one_ref[1, at, :]], axis=0)

        def tiles(w, start, to_ref):
            @pl.loop(0, to_ref.shape[2] // tile)
            def _(n):
                cols = pl.ds(pl.multiple_of(n * tile, tile), tile)
                from_ = pl.ds(pl.multiple_of(start + n * tile, tile), tile)
                r = jnp.dot(x, w[:, from_], preferred_element_type=F32).astype(to_ref.dtype)
                for m in range(2):
                    to_ref[m, at, cols] = r[m * rows : (m + 1) * rows]

        tiles(wa, 0, first_ref)
        tiles(wb, 0, high_ref)
        tiles(wb, high, gate_ref)

    multiply(z)
    line.each(1, multiply)
    for item in items[3:]:
        item.near()
    for item in items[3:]:
        item.far()
    line.each(2, multiply)

    def both_steps(slot):
        normalize(slot)
        multiply(slot)

    line.take(3, lambda slot: None)
    for c in cut:
        c.wait()
    for c in give:
        c.wait()
    for c in away:
        c.start()
    send_rows[0].start()
    line.each(3, both_steps)
    for item in items[3:]:
        item.corner()
    for item in items[3:]:
        item.finish()
    line.finish()
    retain_part(
        rates_ref,
        lengths_ref,
        first_ref,
        high_ref,
        gate_ref,
        mixed_ref,
        kept_ref,
        state_ref,
        douts_ref,
        send_rows,
        *state_refs,
    )
    local[5].wait()
    for c in outs + away:
        c.wait()


def add_rows_kernel(
    x_ref,
    w_ref,
    tok_ref,
    up_hbm,
    down_hbm,
    out_ref,
    ups_hbm,
    downs_hbm,
    held,
    came,
    send,
    recv,
    psend,
    precv,
    lsem,
):
    rows = out_ref.shape[0] // 2
    width = out_ref.shape[1] // 8
    greet(plane=True, line=True)
    part = up_hbm.shape[0]

    def up_at(p):
        return ups_hbm.at[pl.ds(p * part, part)]

    def down_at(p):
        return downs_hbm.at[:, pl.ds(p * part, part)]

    items = [
        PlaneGather(up_hbm, up_at, True, psend.at[0], precv.at[0], False),
        PlaneGather(down_hbm, down_at, False, psend.at[1], precv.at[1], False),
    ]
    local = [
        pltpu.make_async_copy(up_hbm, up_at(0), lsem.at[0]),
        pltpu.make_async_copy(down_hbm, down_at(0), lsem.at[1]),
    ]

    def make(a, to):
        at = pl.ds(pl.multiple_of(a * rows, rows), rows)
        x = jnp.concatenate([x_ref[0, at, :], x_ref[1, at, :]], axis=0)

        @pl.loop(0, 8)
        def _(p):
            cols = w_ref[:, pl.ds(pl.multiple_of(p * width, width), width)]
            to[:, chip_order(p, width)] = jnp.dot(x, cols, preferred_element_type=F32).astype(
                to.dtype
            )

    line = LineReduce(make, out_ref, held, came, send, recv)
    for item in items:
        item.start()
    line.step(3)
    for c in local:
        c.start()
    line.step(2)
    for item in items:
        item.near()
    for item in items:
        item.far()
    line.step(1)
    line.close()
    for k in range(4):
        cols = pl.ds(k * 2 * width, 2 * width)
        out_ref[:, cols] += tok_ref[:, chip_chunk(k, 2 * width)].astype(F32)
    for item in items:
        item.corner()
    for item in items:
        item.finish()
    for c in local:
        c.wait()


def fan_out_kernel(
    rows_ref,
    w_ref,
    mixed_ref,
    up_hbm,
    down_hbm,
    grad_ref,
    part_ref,
    up_ref,
    down_ref,
    slots,
    ordered,
    total,
    near_up,
    near_down,
    came_up,
    came_down,
    send,
    recv,
    psend,
    precv,
    lsem,
):
    z = lax.axis_index("uly")
    rows = rows_ref.shape[0] // 2
    width = rows_ref.shape[1] // 8
    greet(plane=True, line=True)
    line = LineGather(slots, send, recv)
    slots[z] = rows_ref[...]
    line.pass_on(0)
    local = [
        pltpu.make_async_copy(up_hbm, near_up, lsem.at[0]),
        pltpu.make_async_copy(down_hbm, near_down, lsem.at[1]),
    ]
    for c in local:
        c.start()
    groups = [
        PlaneReduce(None, near_up, came_up, True, psend.at[0], precv.at[0]),
        PlaneReduce(None, near_down, came_down, False, psend.at[1], precv.at[1]),
    ]
    for c in local:
        c.wait()
    for g in groups:
        g.start_first()

    def multiply(slot):
        at = pl.ds(pl.multiple_of(slot * rows, rows), rows)
        for p in range(8):
            ordered[:, p * width : (p + 1) * width] = slots[slot, :, chip_order(p, width)]
        tile = 256

        @pl.loop(0, w_ref.shape[0] // tile)
        def _(n):
            part = pl.ds(pl.multiple_of(n * tile, tile), tile)
            product = dot_nt(ordered[...], w_ref[part, :])
            for m in range(2):
                grad_ref[m, at, part] = product[m * rows : (m + 1) * rows]

        mixed = jnp.concatenate([mixed_ref[0, at, :], mixed_ref[1, at, :]], axis=0)

        @pl.loop(0, 8)
        def _(p):
            cols = pl.ds(pl.multiple_of(p * width, width), width)
            total[p] += dot_tn(ordered[:, cols], mixed)

    total[...] = jnp.zeros_like(total)
    multiply(z)
    line.take(1, multiply)
    for g in groups:
        g.first_sums(0)
    line.take(2, multiply)
    for g in groups:
        g.first_sums(1)
    line.take(3, multiply)
    half = part_ref.shape[3]
    for i in range(2):
        part_ref[i] = total[:, :, i * half : (i + 1) * half].astype(BF)
    groups[0].finish(up_ref)
    groups[1].finish(down_ref)
    line.finish()


def feed_kernel(
    hid_ref,
    douts_ref,
    gain_ref,
    ups_ref,
    downs_ref,
    keep_ref,
    give_ref,
    grad_ref,
    rows_ref,
    gain_grad_ref,
    up_grad_ref,
    down_grad_ref,
    two,
    act,
    gu,
    sums,
    held,
    came,
    send,
    recv,
):
    core, z = lax.axis_index("core"), lax.axis_index("uly")
    rows, width = hid_ref.shape
    hidden = ups_ref.shape[1]
    other, pair = {"core": 1 - core}, {"uly": z ^ 1}
    greet(cores=True, pair=True)

    def group(g):
        return pl.ds(g * rows, rows)

    def copy(i, src, dst, to):
        return pltpu.make_async_remote_copy(
            src_ref=src,
            dst_ref=dst,
            send_sem=send.at[i],
            recv_sem=recv.at[i],
            device_id=to,
            device_id_type=MESH,
        )

    step = 32

    @pl.loop(0, rows // step)
    def _(i):
        at = pl.ds(pl.multiple_of(i * step, step), step)
        hat, _scale = normed(hid_ref[at, :])
        two[at, :] = (hat * gain_ref[1:2, :]).astype(BF)

    to_pair = copy(0, two.at[group(0)], two.at[group(2)], pair)
    to_other = copy(1, two.at[group(0)], two.at[group(1)], other)
    through = copy(2, two.at[group(2)], two.at[group(3)], other)
    to_pair.start()
    to_other.start()

    def work(g):
        tile = 256

        @pl.loop(0, hidden // tile)
        def _(n):
            cols = pl.ds(pl.multiple_of(n * tile, tile), tile)
            upward = jnp.dot(two[group(g), :], ups_ref[:, cols], preferred_element_type=F32)
            value, slope = gelu_pair(upward)
            act[group(g), cols] = value.astype(BF)
            pulled = dot_nt(douts_ref[group(g), :], downs_ref[cols, :])
            gu[group(g), cols] = (pulled * slope).astype(BF)

        tile = 512

        @pl.loop(0, width // tile)
        def _(n):
            cols = pl.ds(pl.multiple_of(n * tile, tile), tile)
            back = dot_nt(gu[group(g), :], ups_ref[cols, :])
            down = jnp.dot(act[group(g), :], downs_ref[:, cols], preferred_element_type=F32)
            if g == 0:
                sums[0, :, cols] = back
                sums[1, :, cols] = down
            else:
                held[g - 1, 0, :, cols] = back.astype(BF)
                held[g - 1, 1, :, cols] = down.astype(BF)

    returns = [copy(3 + i, held.at[0, i], came.at[3 * i], other) for i in range(2)]
    returns += [copy(5 + i, held.at[2, i], came.at[1 + 3 * i], other) for i in range(2)]
    last = copy(7, held.at[1, 0], came.at[2], pair)

    work(0)
    to_other.wait_recv()
    work(1)
    for c in returns[:2]:
        c.start()
    to_pair.wait_recv()
    through.start()
    work(2)
    through.wait_recv()
    work(3)
    for c in returns[2:]:
        c.start()
    for i in range(2):
        returns[2 + i].wait_recv()

        @pl.loop(0, rows // step)
        def _(r):
            at = pl.ds(pl.multiple_of(r * step, step), step)
            held[1, i, at, :] = (
                held[1, i, at, :].astype(F32) + came[1 + 3 * i, at, :].astype(F32)
            ).astype(BF)

        if i == 0:
            last.start()
    give_ref[...] = held[1, 1]
    tile = 512

    @pl.loop(0, width // tile)
    def _(n):
        cols = pl.ds(pl.multiple_of(n * tile, tile), tile)
        up_grad_ref[n] = dot_tn(two[:, cols], gu[...], BF)
        down_grad_ref[n] = dot_tn(act[...], douts_ref[:, cols], BF)

    for i in range(2):
        returns[i].wait_recv()
    last.wait_recv()
    gain_grad_ref[...] = jnp.zeros_like(gain_grad_ref)

    @pl.loop(0, rows // step)
    def _(r):
        at = pl.ds(pl.multiple_of(r * step, step), step)
        back = sums[0, at, :] + came[0, at, :].astype(F32) + came[2, at, :].astype(F32)
        hat, scale = normed(hid_ref[at, :])
        gain_grad_ref[...] += jnp.sum(back * hat, axis=0, keepdims=True)
        grad = douts_ref[at, :].astype(F32) + norm_back(back * gain_ref[1:2, :], hat, scale)
        grad_ref[at, :] = grad
        rows_ref[at, :] = grad.astype(BF)
        keep_ref[at, :] = hid_ref[at, :] + sums[1, at, :] + came[3, at, :].astype(F32)

    for c in [to_pair, to_other, through, last] + returns:
        c.wait_send()


class PlaneReduce:
    def __init__(self, far, near, came, x_first, send, recv):
        chip, core = lax.axis_index("chip"), lax.axis_index("core")
        x, y, other = {"chip": chip ^ 1}, {"chip": chip ^ 2}, {"core": 1 - core}
        self.near, self.came, self.x_first = near, came, x_first
        self.waited = ()

        def copy(i, src, to):
            return pltpu.make_async_remote_copy(
                src_ref=src,
                dst_ref=came.at[i],
                send_sem=send.at[i],
                recv_sem=recv.at[i],
                device_id=to,
                device_id_type=MESH,
            )

        self.away = (1, 3) if x_first else (2, 3)
        self.stay = (0, 2) if x_first else (0, 1)
        one, two = (x, y) if x_first else (y, x)
        self.cores = 4 if far else 0
        self.copies = [copy(i, far(4 + i), other) for i in range(self.cores)]
        self.copies += [copy(self.cores + i, near.at[self.away[i]], one) for i in range(2)]
        self.copies.append(copy(self.cores + 2, near.at[self.stay[1]], two))

    def start(self):
        for i in (3, self.away[0], self.stay[1], 0):
            self.copies[i].start()

    def add(self, place, i):
        step = 64

        @pl.loop(0, self.near.shape[1] // step)
        def _(r):
            at = pl.ds(pl.multiple_of(r * step, step), step)
            self.near[place, at, :] = (
                self.near[place, at, :].astype(F32) + self.came[i, at, :].astype(F32)
            ).astype(BF)

    def core_sums(self):
        for i in (1, 0):
            p = self.away[i]
            self.copies[p].wait_recv()
            self.add(p, p)
            self.copies[4 + i].start()
        for p in (self.stay[1], self.stay[0]):
            self.copies[p].wait_recv()
            self.add(p, p)

    def start_first(self):
        for i in (1, 0):
            self.copies[self.cores + i].start()

    def first_sums(self, step):
        i = 1 - step
        self.copies[self.cores + i].wait_recv()
        self.add(self.stay[i], self.cores + i)
        if i == 1:
            self.copies[self.cores + 2].start()

    def finish(self, out_ref):
        self.copies[self.cores + 2].wait_recv()
        self.add(self.stay[0], self.cores + 2)
        out_ref[...] = self.near[0]
        for i, c in enumerate(self.copies):
            if i not in self.waited:
                c.wait_send()


def far_slot(i, x_first):
    return ((3, 1, 2, 0) if x_first else (3, 2, 1, 0)).index(i) % 2


def close_rows_kernel(
    xa_ref,
    xb_ref,
    wa_ref,
    wb_ref,
    one_ref,
    tok_ref,
    hid_ref,
    gain_ref,
    gain_two_ref,
    out_ref,
    sum_a_ref,
    sum_b_ref,
    gains_ref,
    held,
    came,
    near_a,
    near_b,
    far_a,
    far_b,
    came_a,
    came_b,
    gain_sum,
    small,
    small_came,
    small_line,
    send,
    recv,
    psend,
    precv,
    ssend,
    srecv,
):
    chip, core, z = (lax.axis_index(a) for a in AXES)
    rows = out_ref.shape[0] // 2
    length = one_ref.shape[0] // 2
    width = out_ref.shape[1] // 8
    greet(every=True, whole=True)

    def make(a, to):
        at = [
            pl.ds(pl.multiple_of(m * length + a * rows, rows), rows) for m in range(2)
        ]
        xa = jnp.concatenate([xa_ref[i, :] for i in at], axis=0)
        xb = jnp.concatenate([xb_ref[i, :] for i in at], axis=0)

        @pl.loop(0, 8)
        def _(p):
            part = pl.ds(pl.multiple_of(p * width, width), width)
            to[:, chunk_of(p, width)] = (
                dot_nt(xa, wa_ref[part, :]) + dot_nt(xb, wb_ref[part, :])
            ).astype(to.dtype)

    line = LineReduce(make, out_ref, held, came, send, recv)
    sets = []
    for i, (x_ref, near, far, got, x_first) in enumerate(
        (
            (xa_ref, near_a, far_a, came_a, True),
            (xb_ref, near_b, far_b, came_b, False),
        )
    ):
        group = PlaneReduce(
            lambda p, far=far, x=x_first: far.at[far_slot(p - 4, x)],
            near,
            got,
            x_first,
            psend.at[i],
            precv.at[i],
        )
        group.waited = tuple((3, group.away[0]))
        sets.append((group, x_ref, near, far, got))

    tile = 512

    def product(x_ref, place, to, more=None):
        @pl.loop(0, x_ref.shape[1] // tile)
        def _(n):
            cols = pl.ds(pl.multiple_of(n * tile, tile), tile)
            r = dot_tn(one_ref[:, place * width : (place + 1) * width], x_ref[:, cols])
            if more is not None:
                r = r + more[:, cols].astype(F32)
            to[:, cols] = r.astype(BF)

    line.step(3)
    for n in range(4):
        for group, x_ref, near, far, got in sets:
            order = (3, group.away[0], group.stay[1], 0)
            if n >= 2:
                group.copies[order[n - 2]].wait_send()
            product(x_ref, 4 + order[n], far.at[n % 2])
            group.copies[order[n]].start()

    def add_near(n):
        for group, x_ref, near, far, got in sets:
            i = (3, group.away[0], group.stay[1], 0)[n]
            group.copies[i].wait_recv()
            product(x_ref, i, near.at[i], got.at[i])
            if n < 2:
                group.copies[4 + (1 - n)].start()

    add_near(0)
    add_near(1)
    line.step(2)
    add_near(2)
    add_near(3)
    line.step(1)
    for group, *_ in sets:
        group.first_sums(0)
    line.close()
    step = 32
    gain_sum[...] = jnp.zeros_like(gain_sum)

    @pl.loop(0, 2 * rows // step)
    def _(r):
        at = pl.ds(pl.multiple_of(r * step, step), step)
        hat, scale = normed(tok_ref[at, :].astype(F32))
        grad = out_ref[at, :]
        gain_sum[...] += jnp.sum(grad * hat, axis=0, keepdims=True)
        out_ref[at, :] = norm_back(grad * gain_ref[0:1, :], hat, scale)
        for k in range(4):
            out_ref[at, chip_chunk(k, 2 * width)] += hid_ref[
                at, k * 2 * width : (k + 1) * 2 * width
            ]

    small[...] = jnp.zeros_like(small)
    for p in range(8):
        small[p, 0:1, :] = gain_sum[:, chunk_of(p, width)]
        small[p, 1:2, :] = gain_two_ref[:, chip_order(p, width)]

    def pass_small(i, src, dst, to):
        return pltpu.make_async_remote_copy(
            src_ref=src,
            dst_ref=dst,
            send_sem=ssend.at[i],
            recv_sem=srecv.at[i],
            device_id=to,
            device_id_type=MESH,
        )

    sent = [
        pass_small(
            p - 1,
            small.at[p],
            small_came.at[p],
            {"chip": chip ^ (p % 4), "core": core ^ (p // 4)},
        )
        for p in range(1, 8)
    ]
    for c in sent:
        c.start()
    for group, *_ in sets:
        group.first_sums(1)
    total = small[0]
    for p in range(1, 8):
        sent[p - 1].wait_recv()
        total = total + small_came[p]
    small_line[0] = total
    last = [
        pass_small(6 + k, small_line.at[0], small_line.at[k], {"uly": z ^ k}) for k in range(1, 4)
    ]
    for c in last:
        c.start()
    for (group, *_), out in zip(sets, (sum_a_ref, sum_b_ref)):
        group.finish(out)
    for k in range(1, 4):
        last[k - 1].wait_recv()
        total = total + small_line[k]
    gains_ref[...] = total
    for c in sent + last:
        c.wait_send()


class StateExchange:
    def __init__(self, weights, own, sib, chips, mine, came, final, send, recv):
        self.core = lax.axis_index("core")
        self.weights, self.own, self.sib, self.chips = weights, own, sib, chips
        self.mine, self.came, self.final = mine, came, final

        def copy(i, src, dst):
            return pltpu.make_async_remote_copy(
                src_ref=src,
                dst_ref=dst,
                send_sem=send.at[2, i],
                recv_sem=recv.at[2, i],
                device_id={"core": 1 - self.core},
                device_id_type=MESH,
            )

        self.first = copy(0, own, sib)
        self.second = copy(1, mine, came)
        self.items = [
            PlaneGather(
                chips.at[0, h], lambda p, h=h: chips.at[p, h], h == 0, send.at[h], recv.at[h], False
            )
            for h in range(2)
        ]

    def start(self):
        self.first.start()

    def join(self):
        self.first.wait_recv()
        m = self.core
        for h in range(2):
            mine, other = self.weights.joined(m, h)
            self.chips[0, h] = (
                mine * self.own[m, h].astype(F32) + other * self.sib[m, h].astype(F32)
            ).astype(BF)
            self.items[h].start()

    def near(self):
        for item in self.items:
            item.near()

    def far(self):
        for item in self.items:
            item.far()

    def settle(self):
        for item in self.items:
            item.corner()
        m = self.core
        for h in range(2):
            total = self.weights.chip(m, h, 1) * self.chips[1, h].astype(F32)
            for k in (2, 3):
                total = total + self.weights.chip(m, h, k) * self.chips[k, h].astype(F32)
            self.mine[h] = total.astype(BF)
        self.second.start()
        self.last(m, self.mine)
        self.second.wait_recv()
        self.last(1 - m, self.came)

    def last(self, m, chip_state):
        for h in range(2):
            whole, other = self.weights.final(m, h)
            self.final[m, h] = (
                whole * chip_state[h].astype(F32) + other * self.sib[m, h].astype(F32)
            ).astype(BF)

    def finish(self):
        self.first.wait_send()
        self.second.wait_send()
        for item in self.items:
            item.finish()


def state_scratch(shape):
    half = shape[1:]
    return [
        pltpu.VMEM(shape, BF),
        pltpu.VMEM(shape, BF),
        pltpu.VMEM((4, *half), BF),
        pltpu.VMEM(half, BF),
        pltpu.VMEM(half, BF),
        sems(3, 3),
        sems(3, 3),
    ]


class Places:
    def __init__(self, lengths_ref, m, length):
        self.length = length
        self.base = (lax.axis_index("chip") * 2 + lax.axis_index("core")) * length
        self.bounds = []
        total = 0
        for n in range(lengths_ref.shape[1]):
            self.bounds.append(total)
            total = total + lengths_ref[m, n]

    def segment(self, at):
        found = jnp.zeros_like(at)
        for b in self.bounds:
            found = found + jnp.where(self.base + at >= b, 1, 0)
        return found

    def table(self, rate, start, count, across):
        shape = (count, self.length)
        rows = start + lax.broadcasted_iota(jnp.int32, shape, 0)
        cols = lax.broadcasted_iota(jnp.int32, shape, 1)
        off = cols - rows if across else rows - cols
        seg_rows = self.segment(start + lax.broadcasted_iota(jnp.int32, (count, 1), 0))
        seg_cols = self.segment(lax.broadcasted_iota(jnp.int32, (1, self.length), 1))
        far = jnp.maximum(off, 0).astype(F32)
        return jnp.where((off >= 0) & (seg_rows == seg_cols), jnp.exp(-rate * far), 0.0)

    def entry(self, rate, start, count):
        at = start + lax.broadcasted_iota(jnp.int32, (count, 1), 0)
        same = self.segment(at) == self.segment(jnp.full((1, 1), -1, jnp.int32))
        return jnp.where(same, jnp.exp(-rate * (at + 1).astype(F32)), 0.0)

    def leave(self, rate, start, count):
        at = start + lax.broadcasted_iota(jnp.int32, (count, 1), 0)
        end = jnp.full((1, 1), self.length - 1, jnp.int32)
        same = self.segment(at) == self.segment(end)
        return jnp.where(same, jnp.exp(-rate * (self.length - 1 - at).astype(F32)), 0.0)


def rate_of(rates_ref, h):
    return rates_ref[lax.axis_index("uly") * 2 + h]


class StateWeights:
    def __init__(self, rates_ref, lengths_ref, length, back):
        self.rates, self.lengths, self.length, self.back = rates_ref, lengths_ref, length, back
        self.chip_at, self.core = lax.axis_index("chip"), lax.axis_index("core")

    def end(self, m, block):
        at = jnp.full((1, 1), (block + 1) * self.length - 1, jnp.int32)
        found = jnp.zeros_like(at)
        total = 0
        for n in range(self.lengths.shape[1]):
            found = found + jnp.where(at >= total, 1, 0)
            total = total + self.lengths[m, n]
        return found

    def decay(self, h, count):
        far = jnp.full((1, 1), count * self.length, jnp.int32).astype(F32)
        return jnp.exp(-rate_of(self.rates, h) * far)

    def through(self, m, h, block):
        same = self.end(m, block) == self.end(m, block - 1)
        return jnp.where(same, self.decay(h, 1), 0.0)

    def pick(self, first, second):
        return jnp.where(jnp.full((1, 1), self.core, jnp.int32) == 0, first, second)

    def joined(self, m, h):
        one = jnp.ones((1, 1), F32)
        if self.back:
            even = self.through(m, h, 2 * self.chip_at)
            return self.pick(one, even), self.pick(even, one)
        odd = self.through(m, h, 2 * self.chip_at + 1)
        return self.pick(odd, one), self.pick(one, odd)

    def final(self, m, h):
        one, zero = jnp.ones((1, 1), F32), jnp.zeros((1, 1), F32)
        if self.back:
            return self.pick(self.through(m, h, 2 * self.chip_at + 1), one), self.pick(one, zero)
        return self.pick(one, self.through(m, h, 2 * self.chip_at)), self.pick(zero, one)

    def chip(self, m, h, k):
        here, there = self.chip_at, self.chip_at ^ k
        low, high = (here, there) if self.back else (there, here)
        before = jnp.full((1, 1), low, jnp.int32) < jnp.full((1, 1), high, jnp.int32)
        same = self.end(m, 2 * low + 1) == self.end(m, 2 * high - 1)
        return jnp.where(before & same, self.decay(h, 2 * jnp.maximum(high - 1 - low, 0)), 0.0)


ROWS = 128


def retain_part(
    rates_ref,
    lengths_ref,
    a_ref,
    high_ref,
    gate_ref,
    mixed_ref,
    kept_ref,
    state_ref,
    douts_ref,
    send_rows,
    own,
    sib,
    chips,
    mine,
    came,
    send,
    recv,
):
    _, length, vd = high_ref.shape
    qk = (a_ref.shape[2] - vd) // 2
    hd = qk // 2
    weights = StateWeights(rates_ref, lengths_ref, length, False)
    states = StateExchange(weights, own, sib, chips, mine, came, state_ref, send, recv)
    to_pair, to_other, through = send_rows

    def values(m, h):
        return high_ref[m] if h else a_ref[m, :, 2 * qk :]

    def keys(m, h):
        return a_ref[m, :, qk + h * hd : qk + (h + 1) * hd]

    for h in range(2):

        @pl.loop(0, 2)
        def _(m):
            leave = Places(lengths_ref, m, length).leave(rate_of(rates_ref, h), 0, length)
            k = (keys(m, h).astype(F32) * leave).astype(BF)
            own[m, h] = dot_tn(k, values(m, h), BF)

    states.start()
    parts = length // ROWS

    def local(h):
        @pl.loop(0, 2 * parts)
        def _(i):
            m, r = i // parts, i % parts
            at = pl.ds(pl.multiple_of(r * ROWS, ROWS), ROWS)
            table = Places(lengths_ref, m, length).table(rate_of(rates_ref, h), r * ROWS, ROWS, False)
            q = a_ref[m, at, h * hd : (h + 1) * hd]
            scores = (dot_nt(q, keys(m, h)) * table).astype(BF)
            kept_ref[m, at, h * vd : (h + 1) * vd] = jnp.dot(
                scores, values(m, h), preferred_element_type=F32
            )

    states.join()
    to_other.start()
    local(0)
    states.near()
    local(1)
    states.far()
    to_pair.wait_recv()
    through.start()
    states.settle()
    for h in range(2):

        @pl.loop(0, 2 * parts)
        def _(i):
            m, r = i // parts, i % parts
            at = pl.ds(pl.multiple_of(r * ROWS, ROWS), ROWS)
            cols = slice(h * vd, (h + 1) * vd)
            entry = Places(lengths_ref, m, length).entry(rate_of(rates_ref, h), r * ROWS, ROWS)
            q = a_ref[m, at, h * hd : (h + 1) * hd]
            kept = kept_ref[m, at, cols] + entry * jnp.dot(
                q, state_ref[m, h], preferred_element_type=F32
            )
            kept_ref[m, at, cols] = kept
            g = gate_ref[m, at, cols]
            mixed_ref[m, at, cols] = (g * sigmoid(g) * normed(kept)[0]).astype(BF)

    states.finish()
    to_other.wait_recv()
    through.wait_recv()
    for c in send_rows:
        c.wait_send()


def sigmoid(v):
    return 0.5 * jnp.tanh(0.5 * v) + 0.5


def retain_back_kernel(
    rates_ref,
    lengths_ref,
    a_ref,
    high_ref,
    gate_ref,
    kept_ref,
    grad_ref,
    state_ref,
    part_hbm,
    keep_ref,
    give_hbm,
    up_sum_ref,
    down_sum_ref,
    xa_ref,
    xb_ref,
    sum_ref,
    out_ref,
    up_ref,
    down_ref,
    pulled,
    grad_k,
    grad_v,
    final,
    own,
    sib,
    chips,
    mine,
    came,
    send,
    recv,
    near,
    got,
    psend,
    precv,
    lsem,
    came_rows,
    rsend,
    rrecv,
    came_up,
    came_down,
    swap_up,
    swap_down,
    came_swap_up,
    came_swap_down,
    fsend,
    frecv,
):
    _, length, vd = high_ref.shape
    qk = (a_ref.shape[2] - vd) // 2
    hd = qk // 2
    greet(plane=True, cores=True, pair=True, across=True)
    core, z = lax.axis_index("core"), lax.axis_index("uly")

    def feed_copy(i, src, dst, to):
        return pltpu.make_async_remote_copy(
            src_ref=src,
            dst_ref=dst,
            send_sem=fsend.at[i],
            recv_sem=frecv.at[i],
            device_id=to,
            device_id_type=MESH,
        )

    units = came_up.shape[1]
    across = [
        feed_copy(0, up_sum_ref.at[:, pl.ds(units, units)], came_up, {"uly": z ^ 2}),
        feed_copy(1, down_sum_ref.at[pl.ds(units, units)], came_down, {"uly": z ^ 2}),
    ]
    swaps = [
        feed_copy(2, swap_up, came_swap_up, {"core": 1 - core}),
        feed_copy(3, swap_down, came_swap_down, {"core": 1 - core}),
    ]
    for c in across:
        c.start()
    give = pltpu.make_async_remote_copy(
        src_ref=give_hbm,
        dst_ref=came_rows,
        send_sem=rsend,
        recv_sem=rrecv,
        device_id={"uly": lax.axis_index("uly") ^ 1},
        device_id_type=MESH,
    )
    give.start()
    groups = [
        PlaneReduce(
            lambda p, i=i: part_hbm.at[i, p],
            near.at[i],
            got.at[i],
            i == 0,
            psend.at[i],
            precv.at[i],
        )
        for i in range(2)
    ]
    local = [
        pltpu.make_async_copy(part_hbm.at[i, pl.ds(0, 4)], near.at[i], lsem.at[i]) for i in range(2)
    ]
    for c in local:
        c.start()
    for group in groups:
        group.start()
    weights = StateWeights(rates_ref, lengths_ref, length, True)
    states = StateExchange(weights, own, sib, chips, mine, came, final, send, recv)
    parts = length // ROWS

    def values(m, h, at=slice(None)):
        return high_ref[m, at, :] if h else a_ref[m, at, 2 * qk :]

    def keys(m, h, at=slice(None)):
        return a_ref[m, at, qk + h * hd : qk + (h + 1) * hd]

    def queries(m, h, at=slice(None)):
        return a_ref[m, at, h * hd : (h + 1) * hd]

    for h in range(2):
        cols = slice(h * vd, (h + 1) * vd)

        @pl.loop(0, 2 * parts)
        def _(i):
            m, r = i // parts, i % parts
            at = pl.ds(pl.multiple_of(r * ROWS, ROWS), ROWS)
            g, gm = gate_ref[m, at, cols], grad_ref[m, at, cols]
            sigma = sigmoid(g)
            hat, scale = normed(kept_ref[m, at, cols])
            xb_ref[m, at, vd + h * vd : vd + (h + 1) * vd] = (
                gm * hat * (sigma + g * sigma * (1.0 - sigma))
            ).astype(BF)
            pulled[m, at, cols] = norm_back(gm * g * sigma, hat, scale).astype(BF)

        @pl.loop(0, 2)
        def _(m):
            entry = Places(lengths_ref, m, length).entry(rate_of(rates_ref, h), 0, length)
            q = (queries(m, h).astype(F32) * entry).astype(BF)
            own[m, h] = dot_tn(q, pulled[m, :, cols], BF)

    states.start()

    def local_q(h):
        cols = slice(h * vd, (h + 1) * vd)

        @pl.loop(0, 2 * parts)
        def _(i):
            m, r = i // parts, i % parts
            at = pl.ds(pl.multiple_of(r * ROWS, ROWS), ROWS)
            places = Places(lengths_ref, m, length)
            table = places.table(rate_of(rates_ref, h), r * ROWS, ROWS, False)
            gr = pulled[m, at, cols]
            p = (dot_nt(gr, values(m, h)) * table).astype(BF)
            entry = places.entry(rate_of(rates_ref, h), r * ROWS, ROWS)
            xa_ref[m, at, h * hd : (h + 1) * hd] = (
                jnp.dot(p, keys(m, h), preferred_element_type=F32)
                + entry * dot_nt(gr, state_ref[m, h])
            ).astype(BF)

    def local_kv(h):
        cols = slice(h * vd, (h + 1) * vd)

        @pl.loop(0, 2 * parts)
        def _(i):
            m, r = i // parts, i % parts
            at = pl.ds(pl.multiple_of(r * ROWS, ROWS), ROWS)
            table = Places(lengths_ref, m, length).table(rate_of(rates_ref, h), r * ROWS, ROWS, True)
            p = (dot_nt(values(m, h, at), pulled[m, :, cols]) * table).astype(BF)
            scores = (dot_nt(keys(m, h, at), queries(m, h)) * table).astype(BF)
            grad_k[m, at, h * hd : (h + 1) * hd] = jnp.dot(
                p, queries(m, h), preferred_element_type=F32
            )
            grad_v[m, at, cols] = jnp.dot(
                scores, pulled[m, :, cols], preferred_element_type=F32
            )

    states.join()
    local_q(0)
    states.near()
    states.far()
    for c in local:
        c.wait()
    for group in groups:
        group.core_sums()
    local_q(1)
    states.settle()
    local_kv(0)
    for group in groups:
        group.first_sums(0)
    for group in groups:
        group.first_sums(1)
    local_kv(1)
    for h in range(2):

        @pl.loop(0, 2 * parts)
        def _(i):
            m, r = i // parts, i % parts
            at = pl.ds(pl.multiple_of(r * ROWS, ROWS), ROWS)
            leave = Places(lengths_ref, m, length).leave(rate_of(rates_ref, h), r * ROWS, ROWS)
            xa_ref[m, at, qk + h * hd : qk + (h + 1) * hd] = (
                grad_k[m, at, h * hd : (h + 1) * hd]
                + leave * dot_nt(values(m, h, at), final[m, h])
            ).astype(BF)
            gv = (
                grad_v[m, at, h * vd : (h + 1) * vd]
                + leave * jnp.dot(keys(m, h, at), final[m, h], preferred_element_type=F32)
            ).astype(BF)
            if h:
                xb_ref[m, at, :vd] = gv
            else:
                xa_ref[m, at, 2 * qk :] = gv

    states.finish()
    give.wait()
    quarter = keep_ref.shape[1] // 4
    for k in range(4):
        cols = slice(k * quarter, (k + 1) * quarter)
        out_ref[:, chip_chunk(k, quarter)] = (
            keep_ref[:, cols] + came_rows[:, cols].astype(F32)
        ).astype(BF)
    for i, group in enumerate(groups):
        group.finish(sum_ref.at[i])
    rows, cols = up_ref.shape[0], down_ref.shape[1]

    def mine(size, own):
        return pl.ds(pl.multiple_of((core if own else 1 - core) * size, size), size)

    for c in across:
        c.wait()
    kept_units = slice(0, units)

    def up_total(own):
        at = mine(rows, own)
        return up_sum_ref[at, kept_units].astype(F32) + came_up[at, :].astype(F32)

    def down_total(own):
        at = mine(cols, own)
        return down_sum_ref[kept_units, at].astype(F32) + came_down[:, at].astype(F32)

    swap_up[...] = up_total(False).astype(BF)
    swap_down[...] = down_total(False).astype(BF)
    for c in swaps:
        c.start()
    up_ref[:, mine(units, True)] = up_total(True)
    down_ref[mine(units, True), :] = down_total(True)
    for c in swaps:
        c.wait()
    up_ref[:, mine(units, False)] = came_swap_up[...].astype(F32)
    down_ref[mine(units, False), :] = came_swap_down[...].astype(F32)


def sems(*shape):
    return pltpu.SemaphoreType.DMA(shape)


def like(shape, kind):
    return jax.ShapeDtypeStruct(shape, kind)


def call(kernel, number, ins, outs, scratch, flops, *args):
    moved = sum(a.size * a.dtype.itemsize for a in args)
    return pl.pallas_call(
        kernel,
        out_shape=[like(s, t) for s, t, _ in outs],
        in_specs=ins,
        out_specs=[spec for _, _, spec in outs],
        scratch_shapes=scratch,
        compiler_params=pltpu.CompilerParams(
            collective_id=number, has_side_effects=True, vmem_limit_bytes=VMEM_LIMIT
        ),
        cost_estimate=pl.CostEstimate(flops=flops, bytes_accessed=moved, transcendentals=0),
    )(*args)


def smem():
    return pl.BlockSpec(memory_space=pltpu.SMEM)


def settle_kernel(
    block_in, input_in, first_in, second_in, out_in, up_in, down_in, *outs
):
    block, inputs, query, key, value, gate, output, up, down = outs
    qk, half = query.shape[1], out_in.shape[2]
    high = value.shape[1] // 2
    block[...] = block_in[...]
    inputs[...] = input_in[...]
    query[...] = first_in[:, :qk].astype(F32)
    key[...] = first_in[:, qk : 2 * qk].astype(F32)
    value[:, :high] = first_in[:, 2 * qk :].astype(F32)
    value[:, high:] = second_in[:, :high].astype(F32)
    gate[...] = second_in[:, high:].astype(F32)
    for i in range(2):
        output[i * half : (i + 1) * half, :] = out_in[i].astype(F32).T
    up[...] = up_in[...]
    down[...] = down_in[...]


def settle(block_out, input_grad, first_sum, second_sum, out_sum, up_grad, down_grad, qk):
    piece = first_sum.shape[0]
    high = first_sum.shape[1] - 2 * qk
    args = (block_out, input_grad, first_sum, second_sum, out_sum, up_grad, down_grad)
    shapes = [
        (block_out.shape, BF),
        (input_grad.shape, F32),
        ((piece, qk), F32),
        ((piece, qk), F32),
        ((piece, 2 * high), F32),
        ((piece, second_sum.shape[1] - high), F32),
        ((2 * out_sum.shape[2], piece), F32),
        (up_grad.shape, F32),
        (down_grad.shape, F32),
    ]
    return pl.pallas_call(
        settle_kernel,
        out_shape=[like(s, t) for s, t in shapes],
        in_specs=[vmem()] * len(args),
        out_specs=[vmem()] * len(shapes),
        compiler_params=pltpu.CompilerParams(vmem_limit_bytes=VMEM_LIMIT),
    )(*args)


def retain_back(
    rates, lengths, a, high, gate, kept, grad_mixed, state, part, keep, give, up_sum, down_sum
):
    units = up_sum.shape[1] // 2
    rows, cols = up_sum.shape[0] // 2, down_sum.shape[1] // 2
    micro, length, vd = high.shape
    hd = (a.shape[2] - vd) // 4
    return call(
        retain_back_kernel,
        6,
        [smem()] * 2 + [vmem()] * 6 + [anywhere(), vmem(), anywhere(), vmem(), vmem()],
        [
            ((micro, length, a.shape[2]), BF, vmem()),
            ((micro, length, 3 * vd), BF, vmem()),
            ((2, *part.shape[2:]), BF, vmem()),
            (give.shape, BF, vmem()),
            ((rows, 2 * units), F32, vmem()),
            ((2 * units, cols), F32, vmem()),
        ],
        [
            pltpu.VMEM((micro, length, 2 * vd), BF),
            pltpu.VMEM((micro, length, 2 * hd), F32),
            pltpu.VMEM((micro, length, 2 * vd), F32),
            pltpu.VMEM(state.shape, BF),
        ]
        + state_scratch(state.shape)
        + [
            pltpu.VMEM((2, 4, *part.shape[2:]), BF),
            pltpu.VMEM((2, 7, *part.shape[2:]), BF),
            sems(2, 7),
            sems(2, 7),
            sems(2),
            pltpu.VMEM(give.shape, BF),
            pltpu.SemaphoreType.DMA,
            pltpu.SemaphoreType.DMA,
            pltpu.VMEM((2 * rows, units), BF),
            pltpu.VMEM((units, 2 * cols), BF),
            pltpu.VMEM((rows, units), BF),
            pltpu.VMEM((units, cols), BF),
            pltpu.VMEM((rows, units), BF),
            pltpu.VMEM((units, cols), BF),
            sems(4),
            sems(4),
        ],
        12 * micro * length * length * (hd + vd),
        rates,
        lengths,
        a,
        high,
        gate,
        kept,
        grad_mixed,
        state,
        part,
        keep,
        give,
        up_sum,
        down_sum,
    )


def front(rates, lengths, tokens, out_grad, gains, weights, out_weight, up_weight, down_weight):
    micro, rows, width = tokens.shape
    count = lax.axis_size("uly")
    query, key, value, gate = weights
    high = value.shape[1] // 2
    if not is_cube():
        first = jnp.concatenate([query, key, value[:, :high]], axis=1)
        second = jnp.concatenate([value[:, high:], gate], axis=1)
        full = lax.all_gather(jnp.stack(gains), BLK, axis=1, tiled=True)
        w_first = lax.all_gather(first, BLK, axis=0, tiled=True)
        w_second = lax.all_gather(second, BLK, axis=0, tiled=True)
        w_out = lax.all_gather(out_weight, BLK, axis=1, tiled=True)
        one = (normed(spread(tokens).astype(F32))[0] * full[0].astype(F32)).astype(BF)
        a, v_high = dot_nn(one, w_first, BF), dot_nn(one, w_second[:, :high], BF)
        gate_rows = dot_nn(one, w_second[:, high:])
        heads_here = rates.shape[0] // count
        own_rates = lax.dynamic_slice_in_dim(
            rates, lax.axis_index("uly") * heads_here, heads_here
        )
        mixed, kept = plain_forward(own_rates, lengths, a, v_high, gate_rows)
        return (
            one,
            a,
            v_high,
            gate_rows,
            w_first,
            w_second,
            w_out,
            full.astype(F32),
            up_weight,
            down_weight,
            mixed,
            kept,
            None,
            None,
        )
    wide = count * rows
    own = micro * rows
    piece = width // 8
    na, nb, no = 2 * query.shape[1] + high, high + gate.shape[1], out_weight.shape[0]
    units = up_weight.shape[1]
    state = (micro, 2, query.shape[1] // 2, high)
    return call(
        front_kernel,
        0,
        [smem()] * 2 + [vmem()] * 3 + [anywhere()] * 7,
        [
            ((micro, wide, width), BF, vmem()),
            ((micro, wide, na), BF, vmem()),
            ((micro, wide, high), BF, vmem()),
            ((micro, wide, nb - high), F32, vmem()),
            ((width, na), BF, anywhere()),
            ((width, nb), BF, anywhere()),
            ((no, width), BF, anywhere()),
            ((8, width), F32, vmem()),
            ((2 * piece, units), BF, anywhere()),
            ((units, 2 * piece), BF, anywhere()),
            ((micro, wide, 2 * high), BF, vmem()),
            ((micro, wide, 2 * high), F32, vmem()),
            (state, BF, vmem()),
            ((4 * own, width), BF, vmem()),
        ],
        [
            pltpu.VMEM((count, own, width), BF),
            pltpu.VMEM((width, na), BF),
            pltpu.VMEM((width, nb), BF),
            pltpu.VMEM((8, 8, piece), F32),
            sems(5, 7),
            sems(5, 7),
            sems(2, count - 1),
            sems(2, count - 1),
            sems(4),
            sems(4),
            sems(3),
            sems(3),
            sems(10),
        ]
        + state_scratch(state),
        2 * micro * wide * width * (na + nb),
        rates,
        lengths,
        tokens.reshape(own, width),
        out_grad.reshape(own, width),
        jnp.stack(gains).astype(F32),
        query,
        key,
        value,
        gate,
        out_weight,
        up_weight,
        down_weight,
    )


def line_scratch(count, rows, width):
    return [
        pltpu.VMEM((count - 1, rows, width), BF),
        pltpu.VMEM((2, count - 1, rows, width), BF),
    ]


def add_rows(mixed, w_out, tokens, up, down):
    micro, wide, hidden = mixed.shape
    count = lax.axis_size("uly")
    rows = wide // count
    width = w_out.shape[1]
    units = up.shape[1]
    out = call(
        add_rows_kernel,
        1,
        [vmem()] * 3 + [anywhere()] * 2,
        [
            ((micro * rows, width), F32, vmem()),
            ((width, units), BF, anywhere()),
            ((units, width), BF, anywhere()),
        ],
        line_scratch(count, micro * rows, width)
        + [sems(2, count - 1)] * 2
        + [sems(2, 3), sems(2, 3), sems(2)],
        2 * micro * wide * hidden * width,
        mixed,
        w_out,
        tokens,
        up,
        down,
    )
    return out


def fan_out(rows_bf, w_out, mixed, up_grad, down_grad):
    own, width = rows_bf.shape
    micro, rows = 2, own // 2
    count = lax.axis_size("uly")
    hidden = w_out.shape[0]
    up_shape, down_shape = up_grad.shape[1:], down_grad.shape[1:]
    return call(
        fan_out_kernel,
        2,
        [vmem()] * 3 + [anywhere()] * 2,
        [
            ((micro, count * rows, hidden), F32, vmem()),
            ((2, 8, width // 8, hidden // 2), BF, vmem()),
            (up_shape, BF, vmem()),
            (down_shape, BF, vmem()),
        ],
        [
            pltpu.VMEM((count, own, width), BF),
            pltpu.VMEM((own, width), BF),
            pltpu.VMEM((8, width // 8, hidden), F32),
            pltpu.VMEM((4, *up_shape), BF),
            pltpu.VMEM((4, *down_shape), BF),
            pltpu.VMEM((3, *up_shape), BF),
            pltpu.VMEM((3, *down_shape), BF),
            sems(2, count - 1),
            sems(2, count - 1),
            sems(2, 3),
            sems(2, 3),
            sems(2),
        ],
        4 * micro * count * rows * hidden * width,
        rows_bf,
        w_out,
        mixed,
        up_grad,
        down_grad,
    )


def feed_all(hidden, douts, gain, ups, downs):
    own, width = hidden.shape
    units = ups.shape[1]
    return call(
        feed_kernel,
        4,
        [vmem()] * 5,
        [
            ((own, width), F32, vmem()),
            ((own, width), BF, vmem()),
            ((own, width), F32, vmem()),
            ((own, width), BF, vmem()),
            ((1, width), F32, vmem()),
            ((4, width // 4, units), BF, vmem()),
            ((4, units, width // 4), BF, vmem()),
        ],
        [
            pltpu.VMEM((4 * own, width), BF),
            pltpu.VMEM((4 * own, units), BF),
            pltpu.VMEM((4 * own, units), BF),
            pltpu.VMEM((2, own, width), F32),
            pltpu.VMEM((3, 2, own, width), BF),
            pltpu.VMEM((5, own, width), BF),
            sems(8),
            sems(8),
        ],
        2 * 6 * 4 * own * units * width,
        hidden,
        douts,
        gain,
        ups,
        downs,
    )


def middle(tokens, out_grad, douts, gains, mixed, w_out, up_weight, down_weight):
    micro, rows, width = tokens.shape
    own = micro * rows
    if not is_cube():
        gain_two = gains[1]
        hidden = tokens.astype(F32) + collect(
            jnp.stack([dot_nn(mixed[m], w_out) for m in range(micro)])
        )
        pair = feed_weights(up_weight, down_weight)
        hat, scale = normed(hidden)
        two = (hat * gain_two).astype(BF)
        flat_two, flat_out = two.reshape(own, width), out_grad.reshape(own, width)
        two_both = jnp.concatenate([flat_two, swap(flat_two, 1)], axis=0)
        out_both = jnp.concatenate([flat_out, swap(flat_out, 1)], axis=0)
        down_rows, grad_two, up_part, down_part = feed(two_both, out_both, pair)
        grad_two = grad_two[:own] + swap(grad_two[own:].astype(BF), 1).astype(F32)
        down_rows = down_rows[:own] + swap(down_rows[own:].astype(BF), 1).astype(F32)
        up_grad, down_grad = feed_reduce(up_part, down_part)
        block_out = (hidden + down_rows.reshape(micro, rows, width)).astype(BF)
        grad_two = grad_two.reshape(micro, rows, width)
        gain_part = jnp.sum(grad_two * hat, axis=(0, 1))
        grad_hidden = out_grad.astype(F32) + norm_back(grad_two * gain_two, hat, scale)
        wide_att = spread(grad_hidden.astype(BF))
        grad_mixed = jnp.stack([dot_nt(wide_att[m], w_out) for m in range(micro)])
        part = dot_tn(
            mixed.reshape(-1, mixed.shape[2]), wide_att.reshape(-1, wide_att.shape[2]), BF
        )
        return block_out, up_grad, down_grad, gain_part, grad_hidden, grad_mixed, part
    hidden, ups, downs = add_rows(mixed, w_out, tokens.reshape(own, width), up_weight, down_weight)
    keep, give, grad_hidden, rows_bf, gain_part, up_part, down_part = feed_all(
        hidden, douts, gains, ups, downs
    )
    grad_mixed, part, up_sum, down_sum = fan_out(rows_bf, w_out, mixed, up_part, down_part)
    return (
        (keep, give),
        up_sum,
        down_sum,
        gain_part,
        grad_hidden,
        grad_mixed,
        part,
    )


def close_rows(xa, xb, w_first, w_second, one, tokens, grad_hidden, gains, gain_two):
    micro, wide, na = xa.shape
    nb = xb.shape[2]
    width = w_first.shape[0]
    flat_a, flat_b = xa.reshape(micro * wide, na), xb.reshape(micro * wide, nb)
    flat_one = one.reshape(micro * wide, width)
    if not is_cube():
        partial = jnp.stack(
            [dot_nt(xa[m], w_first) + dot_nt(xb[m], w_second) for m in range(micro)]
        )
        grad_one = collect(partial)
        hat, scale = normed(tokens.astype(F32))
        both_gains = jnp.stack([jnp.sum(grad_one * hat, axis=(0, 1)), gain_two])
        total = lax.psum_scatter(both_gains, BLK, scatter_dimension=1, tiled=True)
        return (
            grad_hidden + norm_back(grad_one * gains[0], hat, scale),
            lax.psum_scatter(dot_tn(flat_one, flat_a, BF), BLK, scatter_dimension=0, tiled=True),
            lax.psum_scatter(dot_tn(flat_one, flat_b, BF), BLK, scatter_dimension=0, tiled=True),
            lax.psum(total, "uly"),
        )
    count = lax.axis_size("uly")
    rows = wide // count
    piece = width // 8
    out = call(
        close_rows_kernel,
        3,
        [vmem()] * 9,
        [
            ((micro * rows, width), F32, vmem()),
            ((piece, na), BF, vmem()),
            ((piece, nb), BF, vmem()),
            ((8, piece), F32, vmem()),
        ],
        line_scratch(count, micro * rows, width)
        + [
            pltpu.VMEM((4, piece, na), BF),
            pltpu.VMEM((4, piece, nb), BF),
            pltpu.VMEM((2, piece, na), BF),
            pltpu.VMEM((2, piece, nb), BF),
            pltpu.VMEM((7, piece, na), BF),
            pltpu.VMEM((7, piece, nb), BF),
            pltpu.VMEM((1, width), F32),
            pltpu.VMEM((8, 8, piece), F32),
            pltpu.VMEM((8, 8, piece), F32),
            pltpu.VMEM((4, 8, piece), F32),
            sems(2, count - 1),
            sems(2, count - 1),
            sems(2, 7),
            sems(2, 7),
            sems(10),
            sems(10),
        ],
        4 * micro * wide * width * (na + nb),
        flat_a,
        flat_b,
        w_first,
        w_second,
        flat_one,
        tokens.reshape(micro * rows, width),
        grad_hidden,
        gains,
        gain_two,
    )
    return out


def feed(norm_two, out_rows, pair):
    chips, count, _, rows, hidden = pair.shape
    up = pair[:, :, 0].transpose(0, 2, 1, 3).reshape(chips * rows, count * hidden)
    down_t = pair[:, :, 1].transpose(0, 2, 1, 3).reshape(chips * rows, count * hidden)
    upward = dot_nn(norm_two, up)
    act, slope = gelu_pair(upward)
    act = act.astype(BF)
    grad_act = dot_nn(out_rows, down_t)
    grad_up = (grad_act * slope).astype(BF)

    def by_owner(grad):
        return grad.reshape(chips, rows, count, hidden).transpose(0, 2, 1, 3)

    return (
        dot_nt(act, down_t),
        dot_nt(grad_up, up),
        by_owner(dot_tn(norm_two, grad_up, BF)),
        by_owner(dot_tn(out_rows, act, BF)),
    )


def plain_forward(rates, lengths, a, v_high, gate):
    micro, length = a.shape[:2]
    heads_here = rates.shape[0]
    cut_v = v_high.shape[2]
    qk = (a.shape[2] - cut_v) // 2
    hd, vd = qk // heads_here, 2 * cut_v // heads_here
    sets, parts, states = [], [], []
    for m in range(micro):
        values = jnp.concatenate([a[m, :, 2 * qk :], v_high[m]], axis=1)
        heads = [
            (
                a[m, :, h * hd : (h + 1) * hd],
                a[m, :, qk + h * hd : qk + (h + 1) * hd],
                values[:, h * vd : (h + 1) * vd],
            )
            for h in range(heads_here)
        ]
        part = decay_parts(rates, lengths[m], length)
        states.append(retention_state(heads, part[2]))
        sets.append(heads)
        parts.append(part)

    all_states = exchange(states)
    state_in, retained, mixed = [], [], []
    for m in range(micro):
        state = state_sum(parts[m][3], all_states[m])
        kept = retention(sets[m], parts[m], state)
        state_in.append(state)
        retained.append(kept)
        mixed.append(mix(gate[m], kept))
    mixed = jnp.stack(mixed)
    return mixed, (sets, parts, state_in, retained)


def plain_backward(gate, kept, grad_mixed):
    sets, parts, state_in, retained = kept
    micro, cut_v = len(sets), gate.shape[2] // 2
    grad_gates, grad_rets, grad_states = [], [], []
    for m in range(micro):
        gg, gr = mix_back(gate[m], retained[m], grad_mixed[m])
        grad_gates.append(gg)
        grad_rets.append(gr)
        grad_states.append(
            jnp.stack(
                [
                    dot_tn((q.astype(F32) * parts[m][1][h]).astype(BF), gr[h], BF)
                    for h, (q, k, v) in enumerate(sets[m])
                ]
            )
        )
    all_back = exchange(grad_states)
    xa, xb = [], []
    for m in range(micro):
        back = state_sum(parts[m][4], all_back[m])
        grads = retention_back(sets[m], parts[m], state_in[m], grad_rets[m], back)
        gq = jnp.concatenate([g[0] for g in grads], axis=1)
        gk = jnp.concatenate([g[1] for g in grads], axis=1)
        gv = jnp.concatenate([g[2] for g in grads], axis=1)
        xa.append(jnp.concatenate([gq, gk, gv[:, :cut_v]], axis=1))
        xb.append(jnp.concatenate([gv[:, cut_v:], grad_gates[m]], axis=1))
    xa, xb = jnp.stack(xa), jnp.stack(xb)
    return xa, xb


def body(
    tokens,
    retain_gain,
    query_weight,
    key_weight,
    value_weight,
    gate_matrix,
    output_weight,
    feed_gain,
    up_weight,
    down_weight,
    decay_rate,
    lengths,
    out_grad,
):
    micro, rows, width = tokens.shape
    qk = query_weight.shape[1]
    cut_v = value_weight.shape[1] // 2

    (
        one,
        a,
        v_high,
        gate,
        w_first,
        w_second,
        w_out,
        gains,
        up,
        down,
        mixed,
        kept,
        state,
        douts,
    ) = front(
        decay_rate,
        lengths,
        tokens,
        out_grad,
        (retain_gain, feed_gain),
        (query_weight, key_weight, value_weight, gate_matrix),
        output_weight,
        up_weight,
        down_weight,
    )
    block_out, up_grad, down_grad, gain_two, grad_hidden, grad_mixed, part = middle(
        tokens, out_grad, douts, gains, mixed, w_out, up, down
    )

    if is_cube():
        xa, xb, out_sum, block_out, up_grad, down_grad = retain_back(
            decay_rate,
            lengths,
            a,
            v_high,
            gate,
            kept,
            grad_mixed,
            state,
            part,
            *block_out,
            up_grad,
            down_grad,
        )
    else:
        xa, xb = plain_backward(gate, kept, grad_mixed)
        out_sum = lax.psum_scatter(part, BLK, scatter_dimension=1, tiled=True)

    input_grad, first_sum, second_sum, gain_sums = close_rows(
        xa, xb, w_first, w_second, one, tokens, grad_hidden, gains, gain_two
    )
    if is_cube():
        block_out, input_grad, query, key, value, gates, output, up_grad, down_grad = settle(
            block_out, input_grad, first_sum, second_sum, out_sum, up_grad, down_grad, qk
        )
        block_out = block_out.reshape(tokens.shape)
        input_grad = input_grad.reshape(tokens.shape)
    else:
        first_sum, second_sum = first_sum.astype(F32), second_sum.astype(F32)
        query, key = first_sum[:, :qk], first_sum[:, qk : 2 * qk]
        value = jnp.concatenate([first_sum[:, 2 * qk :], second_sum[:, :cut_v]], axis=1)
        gates, output = second_sum[:, cut_v:], out_sum.astype(F32)
    return (
        block_out,
        input_grad,
        gain_sums[0],
        query,
        key,
        value,
        gates,
        output,
        gain_sums[1],
        up_grad,
        down_grad,
    )


def solution(mesh):
    blocks, count = mesh.devices.shape
    split = Mesh(mesh.devices.reshape(blocks // 2, 2, count), AXES)
    rows = P(None, AXES, None)
    gain, wide, tall = P(BLK), P(BLK, "uly"), P("uly", BLK)
    return jax.shard_map(
        body,
        mesh=split,
        in_specs=(rows, gain, wide, wide, wide, wide, tall, gain, wide, tall, P(), P(), rows),
        out_specs=(rows, rows, gain, wide, wide, wide, wide, tall, gain, wide, tall),
        check_vma=False,
    )
```

```python
import functools

import jax
import jax.numpy as jnp
from jax import lax
from jax.experimental import pallas as pl
from jax.experimental.pallas import tpu as pltpu
from jax.sharding import Mesh
from jax.sharding import PartitionSpec as P

EPSILON = 1e-05
BF = jnp.bfloat16
F32 = jnp.float32
AXES = ("chip", "core", "uly")
BLK = ("chip", "core")
MESH = pl.DeviceIdType.MESH
VMEM_LIMIT = 62 * 1024 * 1024


def dot_nn(left, right, kind=F32):
    return jnp.dot(left, right, preferred_element_type=F32).astype(kind)


def dot_tn(left, right, kind=F32):
    return lax.dot_general(
        left, right, (((0,), (0,)), ((), ())), preferred_element_type=F32
    ).astype(kind)


def dot_nt(left, right, kind=F32):
    return lax.dot_general(
        left, right, (((1,), (1,)), ((), ())), preferred_element_type=F32
    ).astype(kind)


def block_index():
    return lax.axis_index("chip") * 2 + lax.axis_index("core")


def block_count():
    return lax.axis_size("chip") * 2


def swap(array, mask):
    if mask == 1:
        return lax.ppermute(array, "core", [(0, 1), (1, 0)])
    count = lax.axis_size("chip")
    return lax.ppermute(array, "chip", [(b, b ^ (mask // 2)) for b in range(count)])


def shift(array, step):
    count = lax.axis_size("uly")
    return lax.ppermute(array, "uly", [(z, (z + step) % count) for z in range(count)])


def is_cube():
    return lax.axis_size("chip") == 4 and lax.axis_size("uly") == 4


def masks():
    return [2 * k + j for j in range(2) for k in range(4)]


def plane_gather(first, second):
    first_x = swap(first, 2)
    second_y = swap(second, 4)
    first_y, first_xy = swap(first, 4), swap(first_x, 4)
    second_x, second_xy = swap(second, 2), swap(second_y, 2)
    return [first, first_x, first_y, first_xy], [second, second_x, second_y, second_xy]


def exchange(pieces):
    if not is_cube():
        return [lax.all_gather(p, BLK) for p in pieces]
    half = len(pieces) // 2
    a, b = plane_gather(jnp.stack(pieces[:half]), jnp.stack(pieces[half:]))
    got = []
    for four in (a, b):
        full = jnp.stack(four + [swap(p, 1) for p in four])
        got += [full[:, i] for i in range(full.shape[1])]
    return got


def spread(rows):
    return lax.all_gather(rows, "uly", axis=1, tiled=True)


def collect(partial):
    return lax.psum_scatter(partial.astype(BF), "uly", scatter_dimension=1, tiled=True).astype(F32)


def core_cut(array, dim):
    core = lax.axis_index("core")
    half = array.shape[dim] // 2
    own = lax.dynamic_slice_in_dim(array, core * half, half, dim)
    other = lax.dynamic_slice_in_dim(array, (1 - core) * half, half, dim)
    return own, other


def core_join(own, other, dim):
    first = lax.axis_index("core") == 0
    return jnp.concatenate([jnp.where(first, own, other), jnp.where(first, other, own)], axis=dim)


def feed_weights(up_shard, down_shard):
    own, other = core_cut(up_shard, 1)
    up = core_join(own, swap(other, 1), 0)
    own, other = core_cut(down_shard, 0)
    down = core_join(own, swap(other, 1), 1)
    pair = lax.all_gather(jnp.stack([up, down.T]), ("chip", "uly"), axis=0, tiled=False)
    chips, count = lax.axis_size("chip"), lax.axis_size("uly")
    rows, hidden = up.shape
    pair = pair.reshape(chips, count, 2, rows, hidden)
    return pair


def feed_reduce(up_grad, down_grad):
    pair = jnp.stack([up_grad, down_grad], axis=2)
    chips, count = pair.shape[:2]
    pair = pair.reshape(chips * count * 2, *pair.shape[3:])
    total = lax.psum_scatter(pair, ("chip", "uly"), scatter_dimension=0, tiled=True)
    half = total.shape[1] // 2
    own, other = core_cut(total, 1)
    both_halves = core_join(own, swap(other, 1), 2).astype(F32)
    return both_halves[0], both_halves[1].T


def normed(values):
    center = values - jnp.mean(values, axis=-1, keepdims=True)
    scale = lax.rsqrt(jnp.mean(center * center, axis=-1, keepdims=True) + EPSILON)
    return center * scale, scale


def norm_back(grad, hat, scale):
    return scale * (
        grad
        - jnp.mean(grad, axis=-1, keepdims=True)
        - hat * jnp.mean(grad * hat, axis=-1, keepdims=True)
    )


GELU_A = 0.7978845608028654
GELU_B = 0.044715


def gelu_pair(u):
    square = u * u
    tanh = jnp.tanh(GELU_A * u * (1.0 + GELU_B * square))
    slope = 0.5 * (1.0 + tanh) + 0.5 * u * (1.0 - tanh * tanh) * GELU_A * (
        1.0 + 3.0 * GELU_B * square
    )
    return 0.5 * u * (1.0 + tanh), slope


def segment_ids(positions, lengths_row):
    count = lengths_row.shape[0]
    before = jnp.arange(count)[None, :] < jnp.arange(count)[:, None]
    bounds = jnp.sum(jnp.where(before, lengths_row[None, :], 0), axis=1)
    return jnp.sum((bounds[None, :] <= positions[:, None]).astype(jnp.int32), axis=1)


def decay_parts(rates, lengths_row, length):
    me = block_index()
    count = block_count()
    places = jnp.arange(length, dtype=jnp.int32)
    seg = segment_ids(me * length + places, lengths_row)
    ends = segment_ids((jnp.arange(count, dtype=jnp.int32) + 1) * length - 1, lengths_row)
    seg_prev = segment_ids(jnp.reshape(me * length - 1, (1,)), lengths_row)[0]
    offset = places[:, None] - places[None, :]
    causal = (offset >= 0) & (seg[:, None] == seg[None, :])
    far = jnp.maximum(offset, 0).astype(F32)
    inner = jnp.where(causal[None], jnp.exp(-rates[:, None, None] * far[None]), 0.0)
    at = places.astype(F32)
    entry = jnp.where(seg == seg_prev, jnp.exp(-rates[:, None] * (at + 1.0)), 0.0)
    leave = jnp.where(seg == seg[length - 1], jnp.exp(-rates[:, None] * (length - 1.0 - at)), 0.0)
    if is_cube():
        source = me ^ jnp.asarray(masks(), jnp.int32)
    else:
        source = jnp.arange(count, dtype=jnp.int32)
    end_of = ends[source]
    end_before = jnp.where(source > 0, ends[jnp.maximum(source - 1, 0)], 0)
    past = jnp.maximum(me - 1 - source, 0).astype(F32)
    ahead = jnp.maximum(source - 1 - me, 0).astype(F32)
    from_past = jnp.where(
        (source < me) & (end_of == seg_prev), jnp.exp(-rates[:, None] * (length * past)), 0.0
    )
    from_ahead = jnp.where(
        (source > me) & (end_before == ends[me]), jnp.exp(-rates[:, None] * (length * ahead)), 0.0
    )
    return inner, entry[:, :, None], leave[:, :, None], from_past, from_ahead


def state_sum(weights, states):
    return jnp.einsum("hb,bhde->hde", weights, states.astype(F32))


def retention_state(heads, leave):
    return jnp.stack(
        [
            dot_tn((k.astype(F32) * leave[h]).astype(BF), v, BF)
            for h, (q, k, v) in enumerate(heads)
        ]
    )


def retention(heads, parts, state):
    inner, entry = parts[0], parts[1]
    out = []
    for h, (q, k, v) in enumerate(heads):
        scores = (dot_nt(q, k) * inner[h]).astype(BF)
        out.append(dot_nn(scores, v) + entry[h] * dot_nn(q, state[h].astype(BF)))
    return out


def mix(gate, retained):
    out = []
    for h, r in enumerate(retained):
        g = gate[:, h * r.shape[1] : (h + 1) * r.shape[1]]
        out.append((g * jax.nn.sigmoid(g) * normed(r)[0]).astype(BF))
    return jnp.concatenate(out, axis=1)


def mix_back(gate, retained, grad_mixed):
    grad_gate, grad_retained = [], []
    for h, r in enumerate(retained):
        cols = slice(h * r.shape[1], (h + 1) * r.shape[1])
        g, gm = gate[:, cols], grad_mixed[:, cols]
        sigma = jax.nn.sigmoid(g)
        hat, scale = normed(r)
        grad_gate.append((gm * hat * (sigma + g * sigma * (1.0 - sigma))).astype(BF))
        grad_retained.append(norm_back(gm * g * sigma, hat, scale).astype(BF))
    return jnp.concatenate(grad_gate, axis=1), grad_retained


def retention_back(heads, parts, state, grad_retained, grad_state):
    inner, entry, leave = parts[0], parts[1], parts[2]
    grads = []
    for h, (q, k, v) in enumerate(heads):
        gr = grad_retained[h]
        scores = (dot_nt(q, k) * inner[h]).astype(BF)
        pulls = (dot_nt(gr, v) * inner[h]).astype(BF)
        gs, st = grad_state[h].astype(BF), state[h].astype(BF)
        gq = dot_nn(pulls, k) + entry[h] * dot_nt(gr, st)
        gk = dot_tn(pulls, q) + leave[h] * dot_nt(v, gs)
        gv = dot_tn(scores, gr) + leave[h] * dot_nn(k, gs)
        grads.append((gq.astype(BF), gk.astype(BF), gv.astype(BF)))
    return grads


def vmem():
    return pl.BlockSpec(memory_space=pltpu.VMEM)


def anywhere():
    return pl.BlockSpec(memory_space=pl.ANY)


def greet(plane=False, line=False, cores=False, pair=False, across=False, whole=False, every=False):
    barrier = pltpu.get_barrier_semaphore()
    chip, core, z = (lax.axis_index(a) for a in AXES)
    others = []
    if plane:
        others += [{"chip": chip ^ 1}, {"chip": chip ^ 2}]
    if cores:
        others.append({"core": 1 - core})
    if pair:
        others.append({"uly": z ^ 1})
    if across:
        others.append({"uly": z ^ 2})
    if whole:
        others += [{"uly": z ^ k} for k in range(1, 4)]
    if every:
        others += [{"chip": chip ^ (p % 4), "core": core ^ (p // 4)} for p in range(1, 8)]
    for to in others:
        pl.semaphore_signal(barrier, inc=1, device_id=to, device_id_type=MESH)
    count = len(others)
    if line:
        last = lax.axis_size("uly") - 1

        @pl.when(z > 0)
        def _():
            pl.semaphore_signal(barrier, inc=1, device_id={"uly": z - 1}, device_id_type=MESH)

        @pl.when(z < last)
        def _():
            pl.semaphore_signal(barrier, inc=1, device_id={"uly": z + 1}, device_id_type=MESH)

        count = count + jnp.where(z > 0, 1, 0) + jnp.where(z < last, 1, 0)
    pl.semaphore_wait(barrier, count)


class PlaneGather:
    def __init__(self, own, at, x_first, send, recv, cores=True):
        chip, core = lax.axis_index("chip"), lax.axis_index("core")
        x, y, other = {"chip": chip ^ 1}, {"chip": chip ^ 2}, {"core": 1 - core}

        def copy(i, src, place, to):
            return pltpu.make_async_remote_copy(
                src_ref=src,
                dst_ref=at(place),
                send_sem=send.at[i],
                recv_sem=recv.at[i],
                device_id=to,
                device_id_type=MESH,
            )

        self.x_first = x_first
        self.copies = [
            copy(0, own, 1, x),
            copy(1, own, 2, y),
            copy(2, at(1), 3, y) if x_first else copy(2, at(2), 3, x),
        ]
        self.cores = cores
        if cores:
            self.copies += [
                copy(3, own, 4, other),
                copy(4, at(1), 5, other),
                copy(5, at(2), 6, other),
                copy(6, at(3), 7, other),
            ]

    def start(self):
        for i in (0, 1) if self.x_first else (1, 0):
            self.copies[i].start()
        if self.cores:
            self.copies[3].start()

    def near(self):
        first = 0 if self.x_first else 1
        self.copies[first].wait_recv()
        self.copies[2].start()
        if self.cores:
            self.copies[4 + first].start()

    def far(self):
        second = 1 if self.x_first else 0
        self.copies[second].wait_recv()
        if self.cores:
            self.copies[4 + second].start()

    def corner(self):
        self.copies[2].wait_recv()
        if self.cores:
            self.copies[6].start()

    def finish(self):
        for c in self.copies[3:]:
            c.wait_recv()
        for c in self.copies:
            c.wait_send()


class LineGather:
    def __init__(self, slots, send, recv):
        self.z = lax.axis_index("uly")
        self.last = lax.axis_size("uly") - 1
        self.slots, self.send, self.recv = slots, send, recv

    def copy(self, right, d):
        z, last = self.z, self.last
        at = jnp.maximum(z - d, 0) if right else jnp.minimum(z + d, last)
        to = jnp.minimum(z + 1, last) if right else jnp.maximum(z - 1, 0)
        way = 0 if right else 1
        return pltpu.make_async_remote_copy(
            src_ref=self.slots.at[at],
            dst_ref=self.slots.at[at],
            send_sem=self.send.at[way, d],
            recv_sem=self.recv.at[way, d],
            device_id={"uly": to},
            device_id_type=MESH,
        )

    def pass_on(self, d):
        z, last = self.z, self.last

        @pl.when((z - d >= 0) & (z < last))
        def _():
            self.copy(True, d).start()

        @pl.when((z + d <= last) & (z > 0))
        def _():
            self.copy(False, d).start()

    def take(self, d, then):
        z, last = self.z, self.last

        @pl.when(z - d >= 0)
        def _():
            self.copy(True, d - 1).wait_recv()

        @pl.when(z + d <= last)
        def _():
            self.copy(False, d - 1).wait_recv()

        if d < last:
            self.pass_on(d)
        self.each(d, then)

    def each(self, d, then):
        z, last = self.z, self.last

        @pl.when(z - d >= 0)
        def _():
            then(jnp.maximum(z - d, 0))

        @pl.when(z + d <= last)
        def _():
            then(jnp.minimum(z + d, last))

    def finish(self):
        z, last = self.z, self.last
        for d in range(last):

            @pl.when((z - d >= 0) & (z < last))
            def _():
                self.copy(True, d).wait_send()

            @pl.when((z + d <= last) & (z > 0))
            def _():
                self.copy(False, d).wait_send()


class LineReduce:
    def __init__(self, make, out, held, came, send, recv):
        self.z = lax.axis_index("uly")
        self.last = lax.axis_size("uly") - 1
        self.make, self.out, self.held, self.came = make, out, held, came
        self.send, self.recv = send, recv

    def copy(self, right, d):
        z, last = self.z, self.last
        way = 0 if right else 1
        to = jnp.minimum(z + 1, last) if right else jnp.maximum(z - 1, 0)
        return pltpu.make_async_remote_copy(
            src_ref=self.held.at[self.place(right, d)],
            dst_ref=self.came.at[way, d - 1],
            send_sem=self.send.at[way, d - 1],
            recv_sem=self.recv.at[way, d - 1],
            device_id={"uly": to},
            device_id_type=MESH,
        )

    def place(self, right, d):
        return d - 1 if right else self.last - d

    def step(self, d):
        z, last = self.z, self.last
        for right in (True, False):
            way = 0 if right else 1
            held = self.held.at[self.place(right, d)]
            valid = (z + d <= last) if right else (z - d >= 0)
            more = (z > 0) if right else (z < last)
            to = jnp.minimum(z + d, last) if right else jnp.maximum(z - d, 0)

            @pl.when(valid)
            def _():
                self.make(to, held)

                if d < last:

                    @pl.when(more)
                    def _():
                        self.copy(right, d + 1).wait_recv()
                        held[...] = (held[...].astype(F32) + self.came[way, d].astype(F32)).astype(
                            BF
                        )

                self.copy(right, d).start()

    def close(self):
        z, last = self.z, self.last
        self.make(z, self.out)

        @pl.when(z > 0)
        def _():
            self.copy(True, 1).wait_recv()
            self.out[...] += self.came[0, 0].astype(F32)

        @pl.when(z < last)
        def _():
            self.copy(False, 1).wait_recv()
            self.out[...] += self.came[1, 0].astype(F32)

        for d in range(1, last + 1):

            @pl.when(z + d <= last)
            def _():
                self.copy(True, d).wait_send()

            @pl.when(z - d >= 0)
            def _():
                self.copy(False, d).wait_send()


def chunk_of(place, width):
    chip, core = lax.axis_index("chip"), lax.axis_index("core")
    block = (chip ^ (place % 4)) * 2 + (core ^ (place // 4))
    return pl.ds(pl.multiple_of(block * width, width), width)


def chip_chunk(k, width):
    return pl.ds(pl.multiple_of((lax.axis_index("chip") ^ k) * width, width), width)


def chip_order(place, width):
    core = lax.axis_index("core")
    return pl.ds(pl.multiple_of((place % 4) * (2 * width) + (core ^ (place // 4)) * width, width), width)


def front_kernel(
    io,
    rates_ref,
    lengths_ref,
    tok_ref,
    dout_ref,
    gain_ref,
    q_hbm,
    k_hbm,
    v_hbm,
    g_hbm,
    out_hbm,
    up_hbm,
    down_hbm,
    one_ref,
    first_ref,
    high_ref,
    gate_ref,
    w_first_hbm,
    w_second_hbm,
    w_out_hbm,
    gains_ref,
    up_own_hbm,
    down_own_hbm,
    mixed_ref,
    kept_ref,
    state_ref,
    douts_ref,
    slots,
    wa,
    wb,
    gains,
    psend,
    precv,
    zsend,
    zrecv,
    fsend,
    frecv,
    dsend,
    drecv,
    lsem,
    *state_refs,
):
    core, z = lax.axis_index("core"), lax.axis_index("uly")
    rows = tok_ref.shape[0] // 2
    width = tok_ref.shape[1]
    piece = width // 8
    qk, high = q_hbm.shape[1], high_ref.shape[2]
    gains[0] = jnp.zeros_like(gains[0])
    gains[0, 0:2, :] = gain_ref[...]
    line = LineGather(slots, zsend, zrecv)
    slots[z] = tok_ref[...]
    greet(every=True, line=True, across=True)
    chip = lax.axis_index("chip")
    small = [
        pltpu.make_async_remote_copy(
            src_ref=gains.at[0],
            dst_ref=gains.at[p],
            send_sem=psend.at[0, p - 1],
            recv_sem=precv.at[0, p - 1],
            device_id={"chip": chip ^ (p % 4), "core": core ^ (p // 4)},
            device_id_type=MESH,
        )
        for p in range(1, 8)
    ]
    for c in small:
        c.start()
    line.pass_on(0)
    own = pl.ds(0, piece)
    local = [
        pltpu.make_async_copy(src, dst, lsem.at[i])
        for i, (src, dst) in enumerate(
            (
                (q_hbm, wa.at[own, pl.ds(0, qk)]),
                (k_hbm, wa.at[own, pl.ds(qk, qk)]),
                (v_hbm.at[:, pl.ds(0, high)], wa.at[own, pl.ds(2 * qk, high)]),
                (v_hbm.at[:, pl.ds(high, high)], wb.at[own, pl.ds(0, high)]),
                (g_hbm, wb.at[own, pl.ds(high, g_hbm.shape[1])]),
                (out_hbm, w_out_hbm.at[:, own]),
            )
        )
    ]
    for c in local:
        c.start()
    items = [None]
    for i, w in enumerate((wa, wb)):
        items.append(
            PlaneGather(
                w.at[own],
                lambda p, w=w: w.at[pl.ds(p * piece, piece)],
                i == 0,
                psend.at[1 + i],
                precv.at[1 + i],
            )
        )
    half = out_hbm.shape[0] // 2
    for i in range(2):
        part = pl.ds(i * half, half)
        items.append(
            PlaneGather(
                out_hbm.at[part],
                lambda p, part=part: w_out_hbm.at[part, pl.ds(p * piece, piece)],
                i == 0,
                psend.at[3 + i],
                precv.at[3 + i],
            )
        )
    units, cols = up_hbm.shape[1] // 2, down_hbm.shape[1]
    first_half = pl.ds(0, units)
    mine, theirs = (pl.ds(pl.multiple_of(c * units, units), units) for c in (core, 1 - core))
    here = pl.ds(pl.multiple_of(core * cols, cols), cols)

    def remote(i, src, dst, to):
        return pltpu.make_async_remote_copy(
            src_ref=src,
            dst_ref=dst,
            send_sem=fsend.at[i],
            recv_sem=frecv.at[i],
            device_id=to,
            device_id_type=MESH,
        )

    cut = [
        pltpu.make_async_copy(up_hbm.at[:, mine], up_own_hbm.at[here, first_half], lsem.at[6]),
        pltpu.make_async_copy(down_hbm.at[mine], down_own_hbm.at[first_half, here], lsem.at[7]),
    ]
    give = [
        remote(0, up_hbm.at[:, theirs], up_own_hbm.at[here, first_half], {"core": 1 - core}),
        remote(1, down_hbm.at[theirs], down_own_hbm.at[first_half, here], {"core": 1 - core}),
    ]
    first_wide, second_wide = up_own_hbm.at[:, first_half], up_own_hbm.at[:, pl.ds(units, units)]
    first_tall, second_tall = down_own_hbm.at[first_half], down_own_hbm.at[pl.ds(units, units)]
    away = [
        remote(2, first_wide, second_wide, {"uly": z ^ 2}),
        remote(3, first_tall, second_tall, {"uly": z ^ 2}),
    ]
    own_rows = 2 * rows

    def rows_to(i, src, dst, to):
        return pltpu.make_async_remote_copy(
            src_ref=douts_ref.at[pl.ds(src * own_rows, own_rows)],
            dst_ref=douts_ref.at[pl.ds(dst * own_rows, own_rows)],
            send_sem=dsend.at[i],
            recv_sem=drecv.at[i],
            device_id=to,
            device_id_type=MESH,
        )

    send_rows = [
        rows_to(0, 0, 2, {"uly": z ^ 1}),
        rows_to(1, 0, 1, {"core": 1 - core}),
        rows_to(2, 2, 3, {"core": 1 - core}),
    ]
    for c in cut:
        c.start()
    for c in local[:5]:
        c.wait()
    for item in items[1:3]:
        item.start()
    for c in give:
        c.start()
    for c in small:
        c.wait()
    gains_ref[...] = jnp.zeros_like(gains_ref)
    for p in range(8):
        gains_ref[0:1, chunk_of(p, piece)] = gains[p, 0:1, :]
        gains_ref[1:2, chip_order(p, piece)] = gains[p, 1:2, :]

    def normalize(slot):
        step = 32
        for m in range(2):

            @pl.loop(0, rows // step)
            def _(i):
                at = pl.multiple_of(i * step, step)
                v = slots[slot, pl.ds(m * rows + at, step), :].astype(F32)
                mean = jnp.mean(v, axis=-1, keepdims=True)
                center = v - mean
                scale = lax.rsqrt(jnp.mean(center * center, axis=-1, keepdims=True) + EPSILON)
                to = pl.ds(pl.multiple_of(slot * rows + at, step), step)
                for p in range(8):
                    src = slots[slot, pl.ds(m * rows + at, step), chunk_of(p, piece)].astype(F32)
                    one_ref[m, to, pl.ds(p * piece, piece)] = (
                        (src - mean) * scale * gains[p, 0:1, :]
                    ).astype(BF)

    for k in range(4):
        douts_ref[0:own_rows, k * 2 * piece : (k + 1) * 2 * piece] = dout_ref[
            :, chip_chunk(k, 2 * piece)
        ]
    at_end = (z == 0) | (z == line.last)
    inside = (z > 0) & (z < line.last)
    normalize(z)
    line.take(1, normalize)

    @pl.when(at_end)
    def _():
        send_rows[0].start()

    for item in items[1:3]:
        item.near()
    for item in items[1:3]:
        item.far()
    for item in items[3:]:
        item.start()
    line.take(2, normalize)
    for c in cut:
        c.wait()
    for c in give:
        c.wait()

    @pl.when(at_end)
    def _():
        for c in away:
            c.start()

    for item in items[1:3]:
        item.corner()
    for item in items[1:3]:
        item.finish()
    outs = [
        pltpu.make_async_copy(wa, w_first_hbm, lsem.at[8]),
        pltpu.make_async_copy(wb, w_second_hbm, lsem.at[9]),
    ]
    for c in outs:
        c.start()
    tile = 512

    def multiply(slot):
        at = pl.ds(pl.multiple_of(slot * rows, rows), rows)
        x = jnp.concatenate([one_ref[0, at, :], one_ref[1, at, :]], axis=0)

        def tiles(w, start, to_ref):
            @pl.loop(0, to_ref.shape[2] // tile)
            def _(n):
                cols = pl.ds(pl.multiple_of(n * tile, tile), tile)
                from_ = pl.ds(pl.multiple_of(start + n * tile, tile), tile)
                r = jnp.dot(x, w[:, from_], preferred_element_type=F32).astype(to_ref.dtype)
                for m in range(2):
                    to_ref[m, at, cols] = r[m * rows : (m + 1) * rows]

        tiles(wa, 0, first_ref)
        tiles(wb, 0, high_ref)
        tiles(wb, high, gate_ref)

    multiply(z)
    line.each(1, multiply)
    for item in items[3:]:
        item.near()
    for item in items[3:]:
        item.far()
    line.each(2, multiply)

    def both_steps(slot):
        normalize(slot)
        multiply(slot)

    line.take(3, both_steps)

    @pl.when(inside)
    def _():
        for c in away:
            c.wait_recv()
        for c in away:
            c.start()
        send_rows[0].start()

    io.done("one", "first", "high", "gate")
    for item in items[3:]:
        item.corner()
    for item in items[3:]:
        item.finish()
    line.finish()
    retain_part(
        io,
        rates_ref,
        lengths_ref,
        first_ref,
        high_ref,
        gate_ref,
        mixed_ref,
        kept_ref,
        state_ref,
        douts_ref,
        send_rows,
        *state_refs,
    )
    local[5].wait()
    for c in outs:
        c.wait()

    @pl.when(at_end)
    def _():
        for c in away:
            c.wait_recv()

    for c in away:
        c.wait_send()


def add_rows_kernel(
    io,
    x_ref,
    w_ref,
    tok_ref,
    up_hbm,
    down_hbm,
    out_ref,
    ups_hbm,
    downs_hbm,
    held,
    came,
    send,
    recv,
    psend,
    precv,
    lsem,
):
    rows = out_ref.shape[0] // 2
    width = out_ref.shape[1] // 8
    greet(plane=True, line=True)
    part = up_hbm.shape[0]

    def up_at(p):
        return ups_hbm.at[pl.ds(p * part, part)]

    def down_at(p):
        return downs_hbm.at[:, pl.ds(p * part, part)]

    items = [
        PlaneGather(up_hbm, up_at, True, psend.at[0], precv.at[0], False),
        PlaneGather(down_hbm, down_at, False, psend.at[1], precv.at[1], False),
    ]
    local = [
        pltpu.make_async_copy(up_hbm, up_at(0), lsem.at[0]),
        pltpu.make_async_copy(down_hbm, down_at(0), lsem.at[1]),
    ]

    def make(a, to):
        at = pl.ds(pl.multiple_of(a * rows, rows), rows)
        x = jnp.concatenate([x_ref[0, at, :], x_ref[1, at, :]], axis=0)

        @pl.loop(0, 8)
        def _(p):
            cols = w_ref[:, pl.ds(pl.multiple_of(p * width, width), width)]
            to[:, chip_order(p, width)] = jnp.dot(x, cols, preferred_element_type=F32).astype(
                to.dtype
            )

    line = LineReduce(make, out_ref, held, came, send, recv)
    for item in items:
        item.start()
    io.ready("x", "w")
    line.step(3)
    io.start(1)
    for c in local:
        c.start()
    line.step(2)
    for item in items:
        item.near()
    for item in items:
        item.far()
    line.step(1)
    line.close()
    io.ready("tokens")
    for k in range(4):
        cols = pl.ds(k * 2 * width, 2 * width)
        out_ref[:, cols] += tok_ref[:, chip_chunk(k, 2 * width)].astype(F32)
    for item in items:
        item.corner()
    for item in items:
        item.finish()
    for c in local:
        c.wait()


def fan_out_kernel(
    io,
    rows_ref,
    w_ref,
    mixed_ref,
    up_hbm,
    down_hbm,
    grad_ref,
    part_ref,
    up_ref,
    down_ref,
    slots,
    ordered,
    total,
    near_up,
    near_down,
    came_up,
    came_down,
    send,
    recv,
    psend,
    precv,
    lsem,
):
    z = lax.axis_index("uly")
    rows = rows_ref.shape[0] // 2
    width = rows_ref.shape[1] // 8
    greet(plane=True, line=True)
    line = LineGather(slots, send, recv)
    slots[z] = rows_ref[...]
    line.pass_on(0)
    local = [
        pltpu.make_async_copy(up_hbm, near_up, lsem.at[0]),
        pltpu.make_async_copy(down_hbm, near_down, lsem.at[1]),
    ]
    for c in local:
        c.start()
    groups = [
        PlaneReduce(None, near_up, came_up, True, psend.at[0], precv.at[0]),
        PlaneReduce(None, near_down, came_down, False, psend.at[1], precv.at[1]),
    ]
    for c in local:
        c.wait()
    for g in groups:
        g.start_first()

    def multiply(slot):
        at = pl.ds(pl.multiple_of(slot * rows, rows), rows)
        for p in range(8):
            ordered[:, p * width : (p + 1) * width] = slots[slot, :, chip_order(p, width)]
        tile = 256

        @pl.loop(0, w_ref.shape[0] // tile)
        def _(n):
            part = pl.ds(pl.multiple_of(n * tile, tile), tile)
            product = dot_nt(ordered[...], w_ref[part, :])
            for m in range(2):
                grad_ref[m, at, part] = product[m * rows : (m + 1) * rows]

        mixed = jnp.concatenate([mixed_ref[0, at, :], mixed_ref[1, at, :]], axis=0)

        @pl.loop(0, 8)
        def _(p):
            cols = pl.ds(pl.multiple_of(p * width, width), width)
            total[p] += dot_tn(ordered[:, cols], mixed)

    total[...] = jnp.zeros_like(total)
    io.ready("w", "mixed")
    multiply(z)
    line.take(1, multiply)
    for g in groups:
        g.first_sums(0)
    line.take(2, multiply)
    for g in groups:
        g.first_sums(1)
    line.take(3, multiply)
    io.done("grad")
    half = part_ref.shape[3]
    for i in range(2):
        part_ref[i] = total[:, :, i * half : (i + 1) * half].astype(BF)
    io.done("part")
    groups[0].finish(up_ref)
    groups[1].finish(down_ref)
    line.finish()


def feed_kernel(
    io,
    hid_ref,
    douts_ref,
    gain_ref,
    ups_ref,
    downs_ref,
    keep_ref,
    give_ref,
    grad_ref,
    rows_ref,
    gain_grad_ref,
    up_grad_ref,
    down_grad_ref,
    two,
    act,
    gu,
    sums,
    held,
    came,
    send,
    recv,
):
    core, z = lax.axis_index("core"), lax.axis_index("uly")
    rows, width = hid_ref.shape
    hidden = ups_ref.shape[1]
    other, pair = {"core": 1 - core}, {"uly": z ^ 1}
    greet(cores=True, pair=True)

    half = rows // 2

    def group(g, part=None):
        return pl.ds(g * rows, rows) if part is None else pl.ds(g * rows + part * half, half)

    def copy(i, src, dst, to):
        return pltpu.make_async_remote_copy(
            src_ref=src,
            dst_ref=dst,
            send_sem=send.at[i],
            recv_sem=recv.at[i],
            device_id=to,
            device_id_type=MESH,
        )

    parts = [pl.ds(part * half, half) for part in range(2)]
    to_pair = [copy(p, two.at[group(0, p)], two.at[group(2, p)], pair) for p in range(2)]
    through = [copy(2 + p, two.at[group(2, p)], two.at[group(3, p)], other) for p in range(2)]
    to_other = copy(4, two.at[group(0)], two.at[group(1)], other)
    step = 32
    io.ready("hid")
    io.start(1)
    for part in range(2):

        @pl.loop(0, half // step)
        def _(i):
            at = pl.ds(pl.multiple_of(part * half + i * step, step), step)
            hat, _scale = normed(hid_ref[at, :])
            two[at, :] = (hat * gain_ref[1:2, :]).astype(BF)

        to_pair[part].start()
    to_other.start()

    def work(g, part=None):
        at = group(g, part)
        to = slice(None) if part is None else parts[part]
        tile = 256

        @pl.loop(0, hidden // tile)
        def _(n):
            cols = pl.ds(pl.multiple_of(n * tile, tile), tile)
            upward = jnp.dot(two[at, :], ups_ref[:, cols], preferred_element_type=F32)
            value, slope = gelu_pair(upward)
            act[at, cols] = value.astype(BF)
            pulled = dot_nt(douts_ref[at, :], downs_ref[cols, :])
            gu[at, cols] = (pulled * slope).astype(BF)

        tile = 512

        @pl.loop(0, width // tile)
        def _(n):
            cols = pl.ds(pl.multiple_of(n * tile, tile), tile)
            back = dot_nt(gu[at, :], ups_ref[cols, :])
            down = jnp.dot(act[at, :], downs_ref[:, cols], preferred_element_type=F32)
            if g == 0:
                sums[0, :, cols] = back
                sums[1, :, cols] = down
            else:
                held[g - 1, 0, to, cols] = back.astype(BF)
                held[g - 1, 1, to, cols] = down.astype(BF)

    own_back = [copy(5 + i, held.at[0, i], came.at[3 * i], other) for i in range(2)]
    pair_back = [
        [
            copy(7 + 2 * p + i, held.at[2, i, parts[p]], came.at[1 + 3 * i, parts[p]], other)
            for i in range(2)
        ]
        for p in range(2)
    ]
    last = [copy(11 + p, held.at[1, 0, parts[p]], came.at[2, parts[p]], pair) for p in range(2)]

    io.ready("ups", "downs", "douts")
    work(0)
    to_other.wait_recv()
    work(1)
    for c in own_back:
        c.start()
    for p in range(2):
        to_pair[p].wait_recv()
        through[p].start()
        work(2, p)
        through[p].wait_recv()
        work(3, p)
        for c in pair_back[p]:
            c.start()
        for i in range(2):
            pair_back[p][i].wait_recv()

            @pl.loop(0, half // step)
            def _(r):
                at = pl.ds(pl.multiple_of(p * half + r * step, step), step)
                held[1, i, at, :] = (
                    held[1, i, at, :].astype(F32) + came[1 + 3 * i, at, :].astype(F32)
                ).astype(BF)

            if i == 0:
                last[p].start()
    give_ref[...] = held[1, 1]
    io.done("give")
    tile = 512

    @pl.loop(0, width // tile)
    def _(n):
        cols = pl.ds(pl.multiple_of(n * tile, tile), tile)
        up_grad_ref[n] = dot_tn(two[:, cols], gu[...], BF)
        down_grad_ref[n] = dot_tn(act[...], douts_ref[:, cols], BF)

    io.done("up", "down")
    for c in own_back + last:
        c.wait_recv()
    gain_grad_ref[...] = jnp.zeros_like(gain_grad_ref)

    @pl.loop(0, rows // step)
    def _(r):
        at = pl.ds(pl.multiple_of(r * step, step), step)
        back = sums[0, at, :] + came[0, at, :].astype(F32) + came[2, at, :].astype(F32)
        hat, scale = normed(hid_ref[at, :])
        gain_grad_ref[...] += jnp.sum(back * hat, axis=0, keepdims=True)
        grad = douts_ref[at, :].astype(F32) + norm_back(back * gain_ref[1:2, :], hat, scale)
        grad_ref[at, :] = grad
        rows_ref[at, :] = grad.astype(BF)
        keep_ref[at, :] = hid_ref[at, :] + sums[1, at, :] + came[3, at, :].astype(F32)

    for c in to_pair + through + own_back + pair_back[0] + pair_back[1] + last + [to_other]:
        c.wait_send()


class PlaneReduce:
    def __init__(self, far, near, came, x_first, send, recv):
        chip, core = lax.axis_index("chip"), lax.axis_index("core")
        x, y, other = {"chip": chip ^ 1}, {"chip": chip ^ 2}, {"core": 1 - core}
        self.near, self.came, self.x_first = near, came, x_first
        self.waited = ()

        def copy(i, src, to):
            return pltpu.make_async_remote_copy(
                src_ref=src,
                dst_ref=came.at[i],
                send_sem=send.at[i],
                recv_sem=recv.at[i],
                device_id=to,
                device_id_type=MESH,
            )

        self.away = (1, 3) if x_first else (2, 3)
        self.stay = (0, 2) if x_first else (0, 1)
        one, two = (x, y) if x_first else (y, x)
        self.cores = 4 if far else 0
        self.copies = [copy(i, far(4 + i), other) for i in range(self.cores)]
        self.copies += [copy(self.cores + i, near.at[self.away[i]], one) for i in range(2)]
        self.copies.append(copy(self.cores + 2, near.at[self.stay[1]], two))

    def start(self):
        for i in (3, self.away[0], self.stay[1], 0):
            self.copies[i].start()

    def add(self, place, i):
        step = 64

        @pl.loop(0, self.near.shape[1] // step)
        def _(r):
            at = pl.ds(pl.multiple_of(r * step, step), step)
            self.near[place, at, :] = (
                self.near[place, at, :].astype(F32) + self.came[i, at, :].astype(F32)
            ).astype(BF)

    def core_sums(self):
        for i in (1, 0):
            p = self.away[i]
            self.copies[p].wait_recv()
            self.add(p, p)
            self.copies[4 + i].start()
        for p in (self.stay[1], self.stay[0]):
            self.copies[p].wait_recv()
            self.add(p, p)

    def start_first(self):
        for i in (1, 0):
            self.copies[self.cores + i].start()

    def first_sums(self, step):
        i = 1 - step
        self.copies[self.cores + i].wait_recv()
        self.add(self.stay[i], self.cores + i)
        if i == 1:
            self.copies[self.cores + 2].start()

    def finish(self, out_ref):
        self.copies[self.cores + 2].wait_recv()
        self.add(self.stay[0], self.cores + 2)
        out_ref[...] = self.near[0]
        for i, c in enumerate(self.copies):
            if i not in self.waited:
                c.wait_send()


def far_slot(i, x_first):
    return ((3, 1, 2, 0) if x_first else (3, 2, 1, 0)).index(i) % 2


def close_rows_kernel(
    io,
    xa_ref,
    xb_ref,
    wa_ref,
    wb_ref,
    one_ref,
    tok_ref,
    hid_ref,
    gain_ref,
    gain_two_ref,
    out_ref,
    sum_a_ref,
    sum_b_ref,
    gains_ref,
    held,
    came,
    near_a,
    near_b,
    far_a,
    far_b,
    came_a,
    came_b,
    gain_sum,
    small,
    small_came,
    small_line,
    send,
    recv,
    psend,
    precv,
    ssend,
    srecv,
):
    chip, core, z = (lax.axis_index(a) for a in AXES)
    rows = out_ref.shape[0] // 2
    length = one_ref.shape[0] // 2
    width = out_ref.shape[1] // 8
    greet(every=True, whole=True)

    def make(a, to):
        at = [
            pl.ds(pl.multiple_of(m * length + a * rows, rows), rows) for m in range(2)
        ]
        xa = jnp.concatenate([xa_ref[i, :] for i in at], axis=0)
        xb = jnp.concatenate([xb_ref[i, :] for i in at], axis=0)

        @pl.loop(0, 8)
        def _(p):
            part = pl.ds(pl.multiple_of(p * width, width), width)
            to[:, chunk_of(p, width)] = (
                dot_nt(xa, wa_ref[part, :]) + dot_nt(xb, wb_ref[part, :])
            ).astype(to.dtype)

    line = LineReduce(make, out_ref, held, came, send, recv)
    sets = []
    for i, (x_ref, near, far, got, x_first) in enumerate(
        (
            (xa_ref, near_a, far_a, came_a, True),
            (xb_ref, near_b, far_b, came_b, False),
        )
    ):
        group = PlaneReduce(
            lambda p, far=far, x=x_first: far.at[far_slot(p - 4, x)],
            near,
            got,
            x_first,
            psend.at[i],
            precv.at[i],
        )
        group.waited = tuple((3, group.away[0]))
        sets.append((group, x_ref, near, far, got))

    tile = 512

    def product(x_ref, place, to, more=None):
        @pl.loop(0, x_ref.shape[1] // tile)
        def _(n):
            cols = pl.ds(pl.multiple_of(n * tile, tile), tile)
            r = dot_tn(one_ref[:, place * width : (place + 1) * width], x_ref[:, cols])
            if more is not None:
                r = r + more[:, cols].astype(F32)
            to[:, cols] = r.astype(BF)

    io.ready("xa", "xb", "wa", "wb")
    io.start(1)
    line.step(3)
    io.ready("one")
    for n in range(4):
        for group, x_ref, near, far, got in sets:
            order = (3, group.away[0], group.stay[1], 0)
            if n >= 2:
                group.copies[order[n - 2]].wait_send()
            product(x_ref, 4 + order[n], far.at[n % 2])
            group.copies[order[n]].start()

    def add_near(n):
        for group, x_ref, near, far, got in sets:
            i = (3, group.away[0], group.stay[1], 0)[n]
            group.copies[i].wait_recv()
            product(x_ref, i, near.at[i], got.at[i])
            if n < 2:
                group.copies[4 + (1 - n)].start()

    add_near(0)
    add_near(1)
    line.step(2)
    add_near(2)
    add_near(3)
    line.step(1)
    for group, *_ in sets:
        group.first_sums(0)
    line.close()
    step = 32
    gain_sum[...] = jnp.zeros_like(gain_sum)
    io.ready("tokens", "hid")

    @pl.loop(0, 2 * rows // step)
    def _(r):
        at = pl.ds(pl.multiple_of(r * step, step), step)
        hat, scale = normed(tok_ref[at, :].astype(F32))
        grad = out_ref[at, :]
        gain_sum[...] += jnp.sum(grad * hat, axis=0, keepdims=True)
        out_ref[at, :] = norm_back(grad * gain_ref[0:1, :], hat, scale)
        for k in range(4):
            out_ref[at, chip_chunk(k, 2 * width)] += hid_ref[
                at, k * 2 * width : (k + 1) * 2 * width
            ]

    small[...] = jnp.zeros_like(small)
    for p in range(8):
        small[p, 0:1, :] = gain_sum[:, chunk_of(p, width)]
        small[p, 1:2, :] = gain_two_ref[:, chip_order(p, width)]

    def pass_small(i, src, dst, to):
        return pltpu.make_async_remote_copy(
            src_ref=src,
            dst_ref=dst,
            send_sem=ssend.at[i],
            recv_sem=srecv.at[i],
            device_id=to,
            device_id_type=MESH,
        )

    sent = [
        pass_small(
            p - 1,
            small.at[p],
            small_came.at[p],
            {"chip": chip ^ (p % 4), "core": core ^ (p // 4)},
        )
        for p in range(1, 8)
    ]
    for c in sent:
        c.start()
    for group, *_ in sets:
        group.first_sums(1)
    total = small[0]
    for p in range(1, 8):
        sent[p - 1].wait_recv()
        total = total + small_came[p]
    small_line[0] = total
    last = [
        pass_small(6 + k, small_line.at[0], small_line.at[k], {"uly": z ^ k}) for k in range(1, 4)
    ]
    for c in last:
        c.start()
    for (group, *_), out in zip(sets, (sum_a_ref, sum_b_ref)):
        group.finish(out)
    for k in range(1, 4):
        last[k - 1].wait_recv()
        total = total + small_line[k]
    gains_ref[...] = total
    for c in sent + last:
        c.wait_send()


class StateExchange:
    def __init__(self, weights, own, sib, chips, mine, came, final, send, recv):
        self.core = lax.axis_index("core")
        self.weights, self.own, self.sib, self.chips = weights, own, sib, chips
        self.mine, self.came, self.final = mine, came, final

        def copy(i, src, dst):
            return pltpu.make_async_remote_copy(
                src_ref=src,
                dst_ref=dst,
                send_sem=send.at[2, i],
                recv_sem=recv.at[2, i],
                device_id={"core": 1 - self.core},
                device_id_type=MESH,
            )

        self.first = copy(0, own, sib)
        self.second = copy(1, mine, came)
        self.items = [
            PlaneGather(
                chips.at[0, h], lambda p, h=h: chips.at[p, h], h == 0, send.at[h], recv.at[h], False
            )
            for h in range(2)
        ]

    def start(self):
        self.first.start()

    def join(self):
        self.first.wait_recv()
        m = self.core
        for h in range(2):
            mine, other = self.weights.joined(m, h)
            self.chips[0, h] = (
                mine * self.own[m, h].astype(F32) + other * self.sib[m, h].astype(F32)
            ).astype(BF)
            self.items[h].start()

    def near(self):
        for item in self.items:
            item.near()

    def far(self):
        for item in self.items:
            item.far()

    def settle(self):
        for item in self.items:
            item.corner()
        m = self.core
        for h in range(2):
            total = self.weights.chip(m, h, 1) * self.chips[1, h].astype(F32)
            for k in (2, 3):
                total = total + self.weights.chip(m, h, k) * self.chips[k, h].astype(F32)
            self.mine[h] = total.astype(BF)
        self.second.start()
        self.last(m, self.mine)
        self.second.wait_recv()
        self.last(1 - m, self.came)

    def last(self, m, chip_state):
        for h in range(2):
            whole, other = self.weights.final(m, h)
            self.final[m, h] = (
                whole * chip_state[h].astype(F32) + other * self.sib[m, h].astype(F32)
            ).astype(BF)

    def finish(self):
        self.first.wait_send()
        self.second.wait_send()
        for item in self.items:
            item.finish()


def state_scratch(shape):
    half = shape[1:]
    return [
        pltpu.VMEM(shape, BF),
        pltpu.VMEM(shape, BF),
        pltpu.VMEM((4, *half), BF),
        pltpu.VMEM(half, BF),
        pltpu.VMEM(half, BF),
        sems(3, 3),
        sems(3, 3),
    ]


class Places:
    def __init__(self, lengths_ref, m, length):
        self.length = length
        self.base = (lax.axis_index("chip") * 2 + lax.axis_index("core")) * length
        self.bounds = []
        total = 0
        for n in range(lengths_ref.shape[1]):
            self.bounds.append(total)
            total = total + lengths_ref[m, n]

    def segment(self, at):
        found = jnp.zeros_like(at)
        for b in self.bounds:
            found = found + jnp.where(self.base + at >= b, 1, 0)
        return found

    def table(self, rate, start, count, across):
        shape = (count, self.length)
        rows = start + lax.broadcasted_iota(jnp.int32, shape, 0)
        cols = lax.broadcasted_iota(jnp.int32, shape, 1)
        off = cols - rows if across else rows - cols
        seg_rows = self.segment(start + lax.broadcasted_iota(jnp.int32, (count, 1), 0))
        seg_cols = self.segment(lax.broadcasted_iota(jnp.int32, (1, self.length), 1))
        far = jnp.maximum(off, 0).astype(F32)
        return jnp.where((off >= 0) & (seg_rows == seg_cols), jnp.exp(-rate * far), 0.0)

    def entry(self, rate, start, count):
        at = start + lax.broadcasted_iota(jnp.int32, (count, 1), 0)
        same = self.segment(at) == self.segment(jnp.full((1, 1), -1, jnp.int32))
        return jnp.where(same, jnp.exp(-rate * (at + 1).astype(F32)), 0.0)

    def leave(self, rate, start, count):
        at = start + lax.broadcasted_iota(jnp.int32, (count, 1), 0)
        end = jnp.full((1, 1), self.length - 1, jnp.int32)
        same = self.segment(at) == self.segment(end)
        return jnp.where(same, jnp.exp(-rate * (self.length - 1 - at).astype(F32)), 0.0)


def rate_of(rates_ref, h):
    return rates_ref[lax.axis_index("uly") * 2 + h]


class StateWeights:
    def __init__(self, rates_ref, lengths_ref, length, back):
        self.rates, self.lengths, self.length, self.back = rates_ref, lengths_ref, length, back
        self.chip_at, self.core = lax.axis_index("chip"), lax.axis_index("core")

    def end(self, m, block):
        at = jnp.full((1, 1), (block + 1) * self.length - 1, jnp.int32)
        found = jnp.zeros_like(at)
        total = 0
        for n in range(self.lengths.shape[1]):
            found = found + jnp.where(at >= total, 1, 0)
            total = total + self.lengths[m, n]
        return found

    def decay(self, h, count):
        far = jnp.full((1, 1), count * self.length, jnp.int32).astype(F32)
        return jnp.exp(-rate_of(self.rates, h) * far)

    def through(self, m, h, block):
        same = self.end(m, block) == self.end(m, block - 1)
        return jnp.where(same, self.decay(h, 1), 0.0)

    def pick(self, first, second):
        return jnp.where(jnp.full((1, 1), self.core, jnp.int32) == 0, first, second)

    def joined(self, m, h):
        one = jnp.ones((1, 1), F32)
        if self.back:
            even = self.through(m, h, 2 * self.chip_at)
            return self.pick(one, even), self.pick(even, one)
        odd = self.through(m, h, 2 * self.chip_at + 1)
        return self.pick(odd, one), self.pick(one, odd)

    def final(self, m, h):
        one, zero = jnp.ones((1, 1), F32), jnp.zeros((1, 1), F32)
        if self.back:
            return self.pick(self.through(m, h, 2 * self.chip_at + 1), one), self.pick(one, zero)
        return self.pick(one, self.through(m, h, 2 * self.chip_at)), self.pick(zero, one)

    def chip(self, m, h, k):
        here, there = self.chip_at, self.chip_at ^ k
        low, high = (here, there) if self.back else (there, here)
        before = jnp.full((1, 1), low, jnp.int32) < jnp.full((1, 1), high, jnp.int32)
        same = self.end(m, 2 * low + 1) == self.end(m, 2 * high - 1)
        return jnp.where(before & same, self.decay(h, 2 * jnp.maximum(high - 1 - low, 0)), 0.0)


ROWS = 128


def retain_part(
    io,
    rates_ref,
    lengths_ref,
    a_ref,
    high_ref,
    gate_ref,
    mixed_ref,
    kept_ref,
    state_ref,
    douts_ref,
    send_rows,
    own,
    sib,
    chips,
    mine,
    came,
    send,
    recv,
):
    _, length, vd = high_ref.shape
    qk = (a_ref.shape[2] - vd) // 2
    hd = qk // 2
    weights = StateWeights(rates_ref, lengths_ref, length, False)
    states = StateExchange(weights, own, sib, chips, mine, came, state_ref, send, recv)
    to_pair, to_other, through = send_rows

    def values(m, h):
        return high_ref[m] if h else a_ref[m, :, 2 * qk :]

    def keys(m, h):
        return a_ref[m, :, qk + h * hd : qk + (h + 1) * hd]

    for h in range(2):

        @pl.loop(0, 2)
        def _(m):
            leave = Places(lengths_ref, m, length).leave(rate_of(rates_ref, h), 0, length)
            k = (keys(m, h).astype(F32) * leave).astype(BF)
            own[m, h] = dot_tn(k, values(m, h), BF)

    states.start()
    parts = length // ROWS

    def local(h):
        @pl.loop(0, 2 * parts)
        def _(i):
            m, r = i // parts, i % parts
            at = pl.ds(pl.multiple_of(r * ROWS, ROWS), ROWS)
            table = Places(lengths_ref, m, length).table(rate_of(rates_ref, h), r * ROWS, ROWS, False)
            q = a_ref[m, at, h * hd : (h + 1) * hd]
            scores = (dot_nt(q, keys(m, h)) * table).astype(BF)
            kept_ref[m, at, h * vd : (h + 1) * vd] = jnp.dot(
                scores, values(m, h), preferred_element_type=F32
            )

    states.join()
    to_other.start()
    local(0)
    states.near()
    local(1)
    states.far()
    to_pair.wait_recv()
    through.start()
    states.settle()
    for h in range(2):

        @pl.loop(0, 2 * parts)
        def _(i):
            m, r = i // parts, i % parts
            at = pl.ds(pl.multiple_of(r * ROWS, ROWS), ROWS)
            cols = slice(h * vd, (h + 1) * vd)
            entry = Places(lengths_ref, m, length).entry(rate_of(rates_ref, h), r * ROWS, ROWS)
            q = a_ref[m, at, h * hd : (h + 1) * hd]
            kept = kept_ref[m, at, cols] + entry * jnp.dot(
                q, state_ref[m, h], preferred_element_type=F32
            )
            kept_ref[m, at, cols] = kept
            g = gate_ref[m, at, cols]
            mixed_ref[m, at, cols] = (g * sigmoid(g) * normed(kept)[0]).astype(BF)

        if h == 0:
            to_other.wait_recv()
            through.wait_recv()
            io.done("douts")

    states.finish()
    for c in send_rows:
        c.wait_send()


def sigmoid(v):
    return 0.5 * jnp.tanh(0.5 * v) + 0.5


def retain_back_kernel(
    io,
    rates_ref,
    lengths_ref,
    a_ref,
    high_ref,
    gate_ref,
    kept_ref,
    grad_ref,
    state_ref,
    part_hbm,
    keep_ref,
    give_hbm,
    up_sum_ref,
    down_sum_ref,
    xa_ref,
    xb_ref,
    sum_ref,
    out_ref,
    up_ref,
    down_ref,
    pulled,
    grad_k,
    grad_v,
    final,
    own,
    sib,
    chips,
    mine,
    came,
    send,
    recv,
    near,
    got,
    psend,
    precv,
    lsem,
    came_rows,
    rsend,
    rrecv,
    came_up,
    came_down,
    swap_up,
    swap_down,
    came_swap_up,
    came_swap_down,
    fsend,
    frecv,
):
    _, length, vd = high_ref.shape
    qk = (a_ref.shape[2] - vd) // 2
    hd = qk // 2
    greet(plane=True, cores=True, pair=True, across=True)
    core, z = lax.axis_index("core"), lax.axis_index("uly")

    def feed_copy(i, src, dst, to):
        return pltpu.make_async_remote_copy(
            src_ref=src,
            dst_ref=dst,
            send_sem=fsend.at[i],
            recv_sem=frecv.at[i],
            device_id=to,
            device_id_type=MESH,
        )

    units = came_up.shape[1]
    across = [
        feed_copy(0, up_sum_ref.at[:, pl.ds(units, units)], came_up, {"uly": z ^ 2}),
        feed_copy(1, down_sum_ref.at[pl.ds(units, units)], came_down, {"uly": z ^ 2}),
    ]
    swaps = [
        feed_copy(2, swap_up, came_swap_up, {"core": 1 - core}),
        feed_copy(3, swap_down, came_swap_down, {"core": 1 - core}),
    ]
    io.ready("up", "down")
    for c in across:
        c.start()
    give = pltpu.make_async_remote_copy(
        src_ref=give_hbm,
        dst_ref=came_rows,
        send_sem=rsend,
        recv_sem=rrecv,
        device_id={"uly": lax.axis_index("uly") ^ 1},
        device_id_type=MESH,
    )
    give.start()
    groups = [
        PlaneReduce(
            lambda p, i=i: part_hbm.at[i, p],
            near.at[i],
            got.at[i],
            i == 0,
            psend.at[i],
            precv.at[i],
        )
        for i in range(2)
    ]
    local = [
        pltpu.make_async_copy(part_hbm.at[i, pl.ds(0, 4)], near.at[i], lsem.at[i]) for i in range(2)
    ]
    for c in local:
        c.start()
    for group in groups:
        group.start()
    io.ready("gate", "kept", "grad")
    io.start(1)
    weights = StateWeights(rates_ref, lengths_ref, length, True)
    states = StateExchange(weights, own, sib, chips, mine, came, final, send, recv)
    parts = length // ROWS

    def values(m, h, at=slice(None)):
        return high_ref[m, at, :] if h else a_ref[m, at, 2 * qk :]

    def keys(m, h, at=slice(None)):
        return a_ref[m, at, qk + h * hd : qk + (h + 1) * hd]

    def queries(m, h, at=slice(None)):
        return a_ref[m, at, h * hd : (h + 1) * hd]

    for h in range(2):
        cols = slice(h * vd, (h + 1) * vd)

        @pl.loop(0, 2 * parts)
        def _(i):
            m, r = i // parts, i % parts
            at = pl.ds(pl.multiple_of(r * ROWS, ROWS), ROWS)
            g, gm = gate_ref[m, at, cols], grad_ref[m, at, cols]
            sigma = sigmoid(g)
            hat, scale = normed(kept_ref[m, at, cols])
            xb_ref[m, at, vd + h * vd : vd + (h + 1) * vd] = (
                gm * hat * (sigma + g * sigma * (1.0 - sigma))
            ).astype(BF)
            pulled[m, at, cols] = norm_back(gm * g * sigma, hat, scale).astype(BF)

        if h == 0:
            io.ready("a", "high", "state")

        @pl.loop(0, 2)
        def _(m):
            entry = Places(lengths_ref, m, length).entry(rate_of(rates_ref, h), 0, length)
            q = (queries(m, h).astype(F32) * entry).astype(BF)
            own[m, h] = dot_tn(q, pulled[m, :, cols], BF)

    states.start()

    def local_q(h):
        cols = slice(h * vd, (h + 1) * vd)

        @pl.loop(0, 2 * parts)
        def _(i):
            m, r = i // parts, i % parts
            at = pl.ds(pl.multiple_of(r * ROWS, ROWS), ROWS)
            places = Places(lengths_ref, m, length)
            table = places.table(rate_of(rates_ref, h), r * ROWS, ROWS, False)
            gr = pulled[m, at, cols]
            p = (dot_nt(gr, values(m, h)) * table).astype(BF)
            entry = places.entry(rate_of(rates_ref, h), r * ROWS, ROWS)
            xa_ref[m, at, h * hd : (h + 1) * hd] = (
                jnp.dot(p, keys(m, h), preferred_element_type=F32)
                + entry * dot_nt(gr, state_ref[m, h])
            ).astype(BF)

    def local_kv(h):
        cols = slice(h * vd, (h + 1) * vd)

        @pl.loop(0, 2 * parts)
        def _(i):
            m, r = i // parts, i % parts
            at = pl.ds(pl.multiple_of(r * ROWS, ROWS), ROWS)
            table = Places(lengths_ref, m, length).table(rate_of(rates_ref, h), r * ROWS, ROWS, True)
            p = (dot_nt(values(m, h, at), pulled[m, :, cols]) * table).astype(BF)
            scores = (dot_nt(keys(m, h, at), queries(m, h)) * table).astype(BF)
            grad_k[m, at, h * hd : (h + 1) * hd] = jnp.dot(
                p, queries(m, h), preferred_element_type=F32
            )
            grad_v[m, at, cols] = jnp.dot(
                scores, pulled[m, :, cols], preferred_element_type=F32
            )

    states.join()
    local_q(0)
    states.near()
    states.far()
    for c in local:
        c.wait()
    for group in groups:
        group.core_sums()
    local_q(1)
    states.settle()
    local_kv(0)
    for group in groups:
        group.first_sums(0)
    for group in groups:
        group.first_sums(1)
    local_kv(1)
    for h in range(2):

        @pl.loop(0, 2 * parts)
        def _(i):
            m, r = i // parts, i % parts
            at = pl.ds(pl.multiple_of(r * ROWS, ROWS), ROWS)
            leave = Places(lengths_ref, m, length).leave(rate_of(rates_ref, h), r * ROWS, ROWS)
            xa_ref[m, at, qk + h * hd : qk + (h + 1) * hd] = (
                grad_k[m, at, h * hd : (h + 1) * hd]
                + leave * dot_nt(values(m, h, at), final[m, h])
            ).astype(BF)
            gv = (
                grad_v[m, at, h * vd : (h + 1) * vd]
                + leave * jnp.dot(keys(m, h, at), final[m, h], preferred_element_type=F32)
            ).astype(BF)
            if h:
                xb_ref[m, at, :vd] = gv
            else:
                xa_ref[m, at, 2 * qk :] = gv

    states.finish()
    give.wait()
    io.ready("keep")
    quarter = keep_ref.shape[1] // 4
    for k in range(4):
        cols = slice(k * quarter, (k + 1) * quarter)
        out_ref[:, chip_chunk(k, quarter)] = (
            keep_ref[:, cols] + came_rows[:, cols].astype(F32)
        ).astype(BF)
    for i, group in enumerate(groups):
        group.finish(sum_ref.at[i])
    rows, cols = up_ref.shape[0], down_ref.shape[1]

    def mine(size, own):
        return pl.ds(pl.multiple_of((core if own else 1 - core) * size, size), size)

    for c in across:
        c.wait()
    kept_units = slice(0, units)

    def up_total(own):
        at = mine(rows, own)
        return up_sum_ref[at, kept_units].astype(F32) + came_up[at, :].astype(F32)

    def down_total(own):
        at = mine(cols, own)
        return down_sum_ref[kept_units, at].astype(F32) + came_down[:, at].astype(F32)

    swap_up[...] = up_total(False).astype(BF)
    swap_down[...] = down_total(False).astype(BF)
    for c in swaps:
        c.start()
    up_ref[:, mine(units, True)] = up_total(True)
    down_ref[mine(units, True), :] = down_total(True)
    for c in swaps:
        c.wait()
    up_ref[:, mine(units, False)] = came_swap_up[...].astype(F32)
    down_ref[mine(units, False), :] = came_swap_down[...].astype(F32)


def sems(*shape):
    return pltpu.SemaphoreType.DMA(shape)


def like(shape, kind):
    return jax.ShapeDtypeStruct(shape, kind)


class Late:
    def __init__(self, name, order=0):
        self.name, self.order = name, order


class Early:
    def __init__(self, name):
        self.name = name


class Moves:
    def __init__(self, loads, stores):
        self.loads, self.stores = loads, stores
        self.waited, self.begun = set(), set()

    def start(self, order):
        for copy, at in self.loads.values():
            if at == order:
                copy.start()

    def ready(self, *names):
        for name in names:
            self.loads[name][0].wait()
            self.waited.add(name)

    def done(self, *names):
        for name in names:
            self.stores[name].start()
            self.begun.add(name)

    def finish(self):
        self.done(*[n for n in self.stores if n not in self.begun])
        self.ready(*[n for n in self.loads if n not in self.waited])
        for copy in self.stores.values():
            copy.wait()


def call(kernel, number, ins, outs, scratch, flops, *args):
    moved = sum(a.size * a.dtype.itemsize for a in args)
    late = [i for i, spec in enumerate(ins) if isinstance(spec, Late)]
    early = [i for i, out in enumerate(outs) if isinstance(out[2], Early)]

    def whole(*refs):
        refs = list(refs)
        in_refs, refs = refs[: len(ins)], refs[len(ins) :]
        out_refs, refs = refs[: len(outs)], refs[len(outs) :]
        own, refs = refs[: len(scratch)], refs[len(scratch) :]
        load_sem, store_sem = refs[-2:]
        loads, stores = {}, {}
        for n, i in enumerate(late):
            copy = pltpu.make_async_copy(in_refs[i], refs[n], load_sem.at[n])
            loads[ins[i].name] = (copy, ins[i].order)
            in_refs[i] = refs[n]
        for n, i in enumerate(early):
            ref = refs[len(late) + n]
            stores[outs[i][2].name] = pltpu.make_async_copy(ref, out_refs[i], store_sem.at[n])
            out_refs[i] = ref
        io = Moves(loads, stores)
        io.start(0)
        kernel(io, *in_refs, *out_refs, *own)
        io.finish()

    extra = [pltpu.VMEM(args[i].shape, args[i].dtype) for i in late]
    extra += [pltpu.VMEM(outs[i][0], outs[i][1]) for i in early]
    return pl.pallas_call(
        whole,
        out_shape=[like(shape, kind) for shape, kind, _ in outs],
        in_specs=[anywhere() if i in late else spec for i, spec in enumerate(ins)],
        out_specs=[anywhere() if i in early else out[2] for i, out in enumerate(outs)],
        scratch_shapes=list(scratch)
        + extra
        + [sems(max(len(late), 1)), sems(max(len(early), 1))],
        compiler_params=pltpu.CompilerParams(
            collective_id=number, has_side_effects=True, vmem_limit_bytes=VMEM_LIMIT
        ),
        cost_estimate=pl.CostEstimate(flops=flops, bytes_accessed=moved, transcendentals=0),
    )(*args)


def smem():
    return pl.BlockSpec(memory_space=pltpu.SMEM)


def settle_kernel(
    block_in, input_in, first_in, second_in, out_in, up_in, down_in, *outs
):
    block, inputs, query, key, value, gate, output, up, down = outs
    qk, half = query.shape[1], out_in.shape[2]
    high = value.shape[1] // 2
    block[...] = block_in[...]
    inputs[...] = input_in[...]
    query[...] = first_in[:, :qk].astype(F32)
    key[...] = first_in[:, qk : 2 * qk].astype(F32)
    value[:, :high] = first_in[:, 2 * qk :].astype(F32)
    value[:, high:] = second_in[:, :high].astype(F32)
    gate[...] = second_in[:, high:].astype(F32)
    for i in range(2):
        output[i * half : (i + 1) * half, :] = out_in[i].astype(F32).T
    up[...] = up_in[...]
    down[...] = down_in[...]


def settle(block_out, input_grad, first_sum, second_sum, out_sum, up_grad, down_grad, qk):
    piece = first_sum.shape[0]
    high = first_sum.shape[1] - 2 * qk
    args = (block_out, input_grad, first_sum, second_sum, out_sum, up_grad, down_grad)
    shapes = [
        (block_out.shape, BF),
        (input_grad.shape, F32),
        ((piece, qk), F32),
        ((piece, qk), F32),
        ((piece, 2 * high), F32),
        ((piece, second_sum.shape[1] - high), F32),
        ((2 * out_sum.shape[2], piece), F32),
        (up_grad.shape, F32),
        (down_grad.shape, F32),
    ]
    return pl.pallas_call(
        settle_kernel,
        out_shape=[like(s, t) for s, t in shapes],
        in_specs=[vmem()] * len(args),
        out_specs=[vmem()] * len(shapes),
        compiler_params=pltpu.CompilerParams(vmem_limit_bytes=VMEM_LIMIT),
    )(*args)


def retain_back(
    rates, lengths, a, high, gate, kept, grad_mixed, state, part, keep, give, up_sum, down_sum
):
    units = up_sum.shape[1] // 2
    rows, cols = up_sum.shape[0] // 2, down_sum.shape[1] // 2
    micro, length, vd = high.shape
    hd = (a.shape[2] - vd) // 4
    return call(
        retain_back_kernel,
        6,
        [smem()] * 2
        + [Late("a", 1), Late("high", 1), Late("gate"), Late("kept"), Late("grad"), Late("state", 1)]
        + [anywhere(), Late("keep", 1), anywhere(), Late("up"), Late("down")],
        [
            ((micro, length, a.shape[2]), BF, vmem()),
            ((micro, length, 3 * vd), BF, vmem()),
            ((2, *part.shape[2:]), BF, vmem()),
            (give.shape, BF, vmem()),
            ((rows, 2 * units), F32, vmem()),
            ((2 * units, cols), F32, vmem()),
        ],
        [
            pltpu.VMEM((micro, length, 2 * vd), BF),
            pltpu.VMEM((micro, length, 2 * hd), F32),
            pltpu.VMEM((micro, length, 2 * vd), F32),
            pltpu.VMEM(state.shape, BF),
        ]
        + state_scratch(state.shape)
        + [
            pltpu.VMEM((2, 4, *part.shape[2:]), BF),
            pltpu.VMEM((2, 7, *part.shape[2:]), BF),
            sems(2, 7),
            sems(2, 7),
            sems(2),
            pltpu.VMEM(give.shape, BF),
            pltpu.SemaphoreType.DMA,
            pltpu.SemaphoreType.DMA,
            pltpu.VMEM((2 * rows, units), BF),
            pltpu.VMEM((units, 2 * cols), BF),
            pltpu.VMEM((rows, units), BF),
            pltpu.VMEM((units, cols), BF),
            pltpu.VMEM((rows, units), BF),
            pltpu.VMEM((units, cols), BF),
            sems(4),
            sems(4),
        ],
        12 * micro * length * length * (hd + vd),
        rates,
        lengths,
        a,
        high,
        gate,
        kept,
        grad_mixed,
        state,
        part,
        keep,
        give,
        up_sum,
        down_sum,
    )


def front(rates, lengths, tokens, out_grad, gains, weights, out_weight, up_weight, down_weight):
    micro, rows, width = tokens.shape
    count = lax.axis_size("uly")
    query, key, value, gate = weights
    high = value.shape[1] // 2
    if not is_cube():
        first = jnp.concatenate([query, key, value[:, :high]], axis=1)
        second = jnp.concatenate([value[:, high:], gate], axis=1)
        full = lax.all_gather(jnp.stack(gains), BLK, axis=1, tiled=True)
        w_first = lax.all_gather(first, BLK, axis=0, tiled=True)
        w_second = lax.all_gather(second, BLK, axis=0, tiled=True)
        w_out = lax.all_gather(out_weight, BLK, axis=1, tiled=True)
        one = (normed(spread(tokens).astype(F32))[0] * full[0].astype(F32)).astype(BF)
        a, v_high = dot_nn(one, w_first, BF), dot_nn(one, w_second[:, :high], BF)
        gate_rows = dot_nn(one, w_second[:, high:])
        heads_here = rates.shape[0] // count
        own_rates = lax.dynamic_slice_in_dim(
            rates, lax.axis_index("uly") * heads_here, heads_here
        )
        mixed, kept = plain_forward(own_rates, lengths, a, v_high, gate_rows)
        return (
            one,
            a,
            v_high,
            gate_rows,
            w_first,
            w_second,
            w_out,
            full.astype(F32),
            up_weight,
            down_weight,
            mixed,
            kept,
            None,
            None,
        )
    wide = count * rows
    own = micro * rows
    piece = width // 8
    na, nb, no = 2 * query.shape[1] + high, high + gate.shape[1], out_weight.shape[0]
    units = up_weight.shape[1]
    state = (micro, 2, query.shape[1] // 2, high)
    return call(
        front_kernel,
        0,
        [smem()] * 2 + [vmem()] * 3 + [anywhere()] * 7,
        [
            ((micro, wide, width), BF, Early("one")),
            ((micro, wide, na), BF, Early("first")),
            ((micro, wide, high), BF, Early("high")),
            ((micro, wide, nb - high), F32, Early("gate")),
            ((width, na), BF, anywhere()),
            ((width, nb), BF, anywhere()),
            ((no, width), BF, anywhere()),
            ((8, width), F32, vmem()),
            ((2 * piece, units), BF, anywhere()),
            ((units, 2 * piece), BF, anywhere()),
            ((micro, wide, 2 * high), BF, vmem()),
            ((micro, wide, 2 * high), F32, vmem()),
            (state, BF, vmem()),
            ((4 * own, width), BF, Early("douts")),
        ],
        [
            pltpu.VMEM((count, own, width), BF),
            pltpu.VMEM((width, na), BF),
            pltpu.VMEM((width, nb), BF),
            pltpu.VMEM((8, 8, piece), F32),
            sems(5, 7),
            sems(5, 7),
            sems(2, count - 1),
            sems(2, count - 1),
            sems(4),
            sems(4),
            sems(3),
            sems(3),
            sems(10),
        ]
        + state_scratch(state),
        2 * micro * wide * width * (na + nb),
        rates,
        lengths,
        tokens.reshape(own, width),
        out_grad.reshape(own, width),
        jnp.stack(gains).astype(F32),
        query,
        key,
        value,
        gate,
        out_weight,
        up_weight,
        down_weight,
    )


def line_scratch(count, rows, width):
    return [
        pltpu.VMEM((count - 1, rows, width), BF),
        pltpu.VMEM((2, count - 1, rows, width), BF),
    ]


def add_rows(mixed, w_out, tokens, up, down):
    micro, wide, hidden = mixed.shape
    count = lax.axis_size("uly")
    rows = wide // count
    width = w_out.shape[1]
    units = up.shape[1]
    out = call(
        add_rows_kernel,
        1,
        [Late("x"), Late("w"), Late("tokens", 1)] + [anywhere()] * 2,
        [
            ((micro * rows, width), F32, vmem()),
            ((width, units), BF, anywhere()),
            ((units, width), BF, anywhere()),
        ],
        line_scratch(count, micro * rows, width)
        + [sems(2, count - 1)] * 2
        + [sems(2, 3), sems(2, 3), sems(2)],
        2 * micro * wide * hidden * width,
        mixed,
        w_out,
        tokens,
        up,
        down,
    )
    return out


def fan_out(rows_bf, w_out, mixed, up_grad, down_grad):
    own, width = rows_bf.shape
    micro, rows = 2, own // 2
    count = lax.axis_size("uly")
    hidden = w_out.shape[0]
    up_shape, down_shape = up_grad.shape[1:], down_grad.shape[1:]
    return call(
        fan_out_kernel,
        2,
        [vmem(), Late("w"), Late("mixed")] + [anywhere()] * 2,
        [
            ((micro, count * rows, hidden), F32, Early("grad")),
            ((2, 8, width // 8, hidden // 2), BF, Early("part")),
            (up_shape, BF, vmem()),
            (down_shape, BF, vmem()),
        ],
        [
            pltpu.VMEM((count, own, width), BF),
            pltpu.VMEM((own, width), BF),
            pltpu.VMEM((8, width // 8, hidden), F32),
            pltpu.VMEM((4, *up_shape), BF),
            pltpu.VMEM((4, *down_shape), BF),
            pltpu.VMEM((3, *up_shape), BF),
            pltpu.VMEM((3, *down_shape), BF),
            sems(2, count - 1),
            sems(2, count - 1),
            sems(2, 3),
            sems(2, 3),
            sems(2),
        ],
        4 * micro * count * rows * hidden * width,
        rows_bf,
        w_out,
        mixed,
        up_grad,
        down_grad,
    )


def feed_all(hidden, douts, gain, ups, downs):
    own, width = hidden.shape
    units = ups.shape[1]
    return call(
        feed_kernel,
        4,
        [Late("hid"), Late("douts", 1), vmem(), Late("ups", 1), Late("downs", 1)],
        [
            ((own, width), F32, vmem()),
            ((own, width), BF, Early("give")),
            ((own, width), F32, vmem()),
            ((own, width), BF, vmem()),
            ((1, width), F32, vmem()),
            ((4, width // 4, units), BF, Early("up")),
            ((4, units, width // 4), BF, Early("down")),
        ],
        [
            pltpu.VMEM((4 * own, width), BF),
            pltpu.VMEM((4 * own, units), BF),
            pltpu.VMEM((4 * own, units), BF),
            pltpu.VMEM((2, own, width), F32),
            pltpu.VMEM((3, 2, own, width), BF),
            pltpu.VMEM((5, own, width), BF),
            sems(13),
            sems(13),
        ],
        2 * 6 * 4 * own * units * width,
        hidden,
        douts,
        gain,
        ups,
        downs,
    )


def middle(tokens, out_grad, douts, gains, mixed, w_out, up_weight, down_weight):
    micro, rows, width = tokens.shape
    own = micro * rows
    if not is_cube():
        gain_two = gains[1]
        hidden = tokens.astype(F32) + collect(
            jnp.stack([dot_nn(mixed[m], w_out) for m in range(micro)])
        )
        pair = feed_weights(up_weight, down_weight)
        hat, scale = normed(hidden)
        two = (hat * gain_two).astype(BF)
        flat_two, flat_out = two.reshape(own, width), out_grad.reshape(own, width)
        two_both = jnp.concatenate([flat_two, swap(flat_two, 1)], axis=0)
        out_both = jnp.concatenate([flat_out, swap(flat_out, 1)], axis=0)
        down_rows, grad_two, up_part, down_part = feed(two_both, out_both, pair)
        grad_two = grad_two[:own] + swap(grad_two[own:].astype(BF), 1).astype(F32)
        down_rows = down_rows[:own] + swap(down_rows[own:].astype(BF), 1).astype(F32)
        up_grad, down_grad = feed_reduce(up_part, down_part)
        block_out = (hidden + down_rows.reshape(micro, rows, width)).astype(BF)
        grad_two = grad_two.reshape(micro, rows, width)
        gain_part = jnp.sum(grad_two * hat, axis=(0, 1))
        grad_hidden = out_grad.astype(F32) + norm_back(grad_two * gain_two, hat, scale)
        wide_att = spread(grad_hidden.astype(BF))
        grad_mixed = jnp.stack([dot_nt(wide_att[m], w_out) for m in range(micro)])
        part = dot_tn(
            mixed.reshape(-1, mixed.shape[2]), wide_att.reshape(-1, wide_att.shape[2]), BF
        )
        return block_out, up_grad, down_grad, gain_part, grad_hidden, grad_mixed, part
    hidden, ups, downs = add_rows(mixed, w_out, tokens.reshape(own, width), up_weight, down_weight)
    keep, give, grad_hidden, rows_bf, gain_part, up_part, down_part = feed_all(
        hidden, douts, gains, ups, downs
    )
    grad_mixed, part, up_sum, down_sum = fan_out(rows_bf, w_out, mixed, up_part, down_part)
    return (
        (keep, give),
        up_sum,
        down_sum,
        gain_part,
        grad_hidden,
        grad_mixed,
        part,
    )


def close_rows(xa, xb, w_first, w_second, one, tokens, grad_hidden, gains, gain_two):
    micro, wide, na = xa.shape
    nb = xb.shape[2]
    width = w_first.shape[0]
    flat_a, flat_b = xa.reshape(micro * wide, na), xb.reshape(micro * wide, nb)
    flat_one = one.reshape(micro * wide, width)
    if not is_cube():
        partial = jnp.stack(
            [dot_nt(xa[m], w_first) + dot_nt(xb[m], w_second) for m in range(micro)]
        )
        grad_one = collect(partial)
        hat, scale = normed(tokens.astype(F32))
        both_gains = jnp.stack([jnp.sum(grad_one * hat, axis=(0, 1)), gain_two])
        total = lax.psum_scatter(both_gains, BLK, scatter_dimension=1, tiled=True)
        return (
            grad_hidden + norm_back(grad_one * gains[0], hat, scale),
            lax.psum_scatter(dot_tn(flat_one, flat_a, BF), BLK, scatter_dimension=0, tiled=True),
            lax.psum_scatter(dot_tn(flat_one, flat_b, BF), BLK, scatter_dimension=0, tiled=True),
            lax.psum(total, "uly"),
        )
    count = lax.axis_size("uly")
    rows = wide // count
    piece = width // 8
    out = call(
        close_rows_kernel,
        3,
        [Late("xa"), Late("xb"), Late("wa"), Late("wb"), Late("one", 1), Late("tokens", 1)]
        + [Late("hid", 1), vmem(), vmem()],
        [
            ((micro * rows, width), F32, vmem()),
            ((piece, na), BF, vmem()),
            ((piece, nb), BF, vmem()),
            ((8, piece), F32, vmem()),
        ],
        line_scratch(count, micro * rows, width)
        + [
            pltpu.VMEM((4, piece, na), BF),
            pltpu.VMEM((4, piece, nb), BF),
            pltpu.VMEM((2, piece, na), BF),
            pltpu.VMEM((2, piece, nb), BF),
            pltpu.VMEM((7, piece, na), BF),
            pltpu.VMEM((7, piece, nb), BF),
            pltpu.VMEM((1, width), F32),
            pltpu.VMEM((8, 8, piece), F32),
            pltpu.VMEM((8, 8, piece), F32),
            pltpu.VMEM((4, 8, piece), F32),
            sems(2, count - 1),
            sems(2, count - 1),
            sems(2, 7),
            sems(2, 7),
            sems(10),
            sems(10),
        ],
        4 * micro * wide * width * (na + nb),
        flat_a,
        flat_b,
        w_first,
        w_second,
        flat_one,
        tokens.reshape(micro * rows, width),
        grad_hidden,
        gains,
        gain_two,
    )
    return out


def feed(norm_two, out_rows, pair):
    chips, count, _, rows, hidden = pair.shape
    up = pair[:, :, 0].transpose(0, 2, 1, 3).reshape(chips * rows, count * hidden)
    down_t = pair[:, :, 1].transpose(0, 2, 1, 3).reshape(chips * rows, count * hidden)
    upward = dot_nn(norm_two, up)
    act, slope = gelu_pair(upward)
    act = act.astype(BF)
    grad_act = dot_nn(out_rows, down_t)
    grad_up = (grad_act * slope).astype(BF)

    def by_owner(grad):
        return grad.reshape(chips, rows, count, hidden).transpose(0, 2, 1, 3)

    return (
        dot_nt(act, down_t),
        dot_nt(grad_up, up),
        by_owner(dot_tn(norm_two, grad_up, BF)),
        by_owner(dot_tn(out_rows, act, BF)),
    )


def plain_forward(rates, lengths, a, v_high, gate):
    micro, length = a.shape[:2]
    heads_here = rates.shape[0]
    cut_v = v_high.shape[2]
    qk = (a.shape[2] - cut_v) // 2
    hd, vd = qk // heads_here, 2 * cut_v // heads_here
    sets, parts, states = [], [], []
    for m in range(micro):
        values = jnp.concatenate([a[m, :, 2 * qk :], v_high[m]], axis=1)
        heads = [
            (
                a[m, :, h * hd : (h + 1) * hd],
                a[m, :, qk + h * hd : qk + (h + 1) * hd],
                values[:, h * vd : (h + 1) * vd],
            )
            for h in range(heads_here)
        ]
        part = decay_parts(rates, lengths[m], length)
        states.append(retention_state(heads, part[2]))
        sets.append(heads)
        parts.append(part)

    all_states = exchange(states)
    state_in, retained, mixed = [], [], []
    for m in range(micro):
        state = state_sum(parts[m][3], all_states[m])
        kept = retention(sets[m], parts[m], state)
        state_in.append(state)
        retained.append(kept)
        mixed.append(mix(gate[m], kept))
    mixed = jnp.stack(mixed)
    return mixed, (sets, parts, state_in, retained)


def plain_backward(gate, kept, grad_mixed):
    sets, parts, state_in, retained = kept
    micro, cut_v = len(sets), gate.shape[2] // 2
    grad_gates, grad_rets, grad_states = [], [], []
    for m in range(micro):
        gg, gr = mix_back(gate[m], retained[m], grad_mixed[m])
        grad_gates.append(gg)
        grad_rets.append(gr)
        grad_states.append(
            jnp.stack(
                [
                    dot_tn((q.astype(F32) * parts[m][1][h]).astype(BF), gr[h], BF)
                    for h, (q, k, v) in enumerate(sets[m])
                ]
            )
        )
    all_back = exchange(grad_states)
    xa, xb = [], []
    for m in range(micro):
        back = state_sum(parts[m][4], all_back[m])
        grads = retention_back(sets[m], parts[m], state_in[m], grad_rets[m], back)
        gq = jnp.concatenate([g[0] for g in grads], axis=1)
        gk = jnp.concatenate([g[1] for g in grads], axis=1)
        gv = jnp.concatenate([g[2] for g in grads], axis=1)
        xa.append(jnp.concatenate([gq, gk, gv[:, :cut_v]], axis=1))
        xb.append(jnp.concatenate([gv[:, cut_v:], grad_gates[m]], axis=1))
    xa, xb = jnp.stack(xa), jnp.stack(xb)
    return xa, xb


def body(
    tokens,
    retain_gain,
    query_weight,
    key_weight,
    value_weight,
    gate_matrix,
    output_weight,
    feed_gain,
    up_weight,
    down_weight,
    decay_rate,
    lengths,
    out_grad,
):
    micro, rows, width = tokens.shape
    qk = query_weight.shape[1]
    cut_v = value_weight.shape[1] // 2

    (
        one,
        a,
        v_high,
        gate,
        w_first,
        w_second,
        w_out,
        gains,
        up,
        down,
        mixed,
        kept,
        state,
        douts,
    ) = front(
        decay_rate,
        lengths,
        tokens,
        out_grad,
        (retain_gain, feed_gain),
        (query_weight, key_weight, value_weight, gate_matrix),
        output_weight,
        up_weight,
        down_weight,
    )
    block_out, up_grad, down_grad, gain_two, grad_hidden, grad_mixed, part = middle(
        tokens, out_grad, douts, gains, mixed, w_out, up, down
    )

    if is_cube():
        xa, xb, out_sum, block_out, up_grad, down_grad = retain_back(
            decay_rate,
            lengths,
            a,
            v_high,
            gate,
            kept,
            grad_mixed,
            state,
            part,
            *block_out,
            up_grad,
            down_grad,
        )
    else:
        xa, xb = plain_backward(gate, kept, grad_mixed)
        out_sum = lax.psum_scatter(part, BLK, scatter_dimension=1, tiled=True)

    input_grad, first_sum, second_sum, gain_sums = close_rows(
        xa, xb, w_first, w_second, one, tokens, grad_hidden, gains, gain_two
    )
    if is_cube():
        block_out, input_grad, query, key, value, gates, output, up_grad, down_grad = settle(
            block_out, input_grad, first_sum, second_sum, out_sum, up_grad, down_grad, qk
        )
        block_out = block_out.reshape(tokens.shape)
        input_grad = input_grad.reshape(tokens.shape)
    else:
        first_sum, second_sum = first_sum.astype(F32), second_sum.astype(F32)
        query, key = first_sum[:, :qk], first_sum[:, qk : 2 * qk]
        value = jnp.concatenate([first_sum[:, 2 * qk :], second_sum[:, :cut_v]], axis=1)
        gates, output = second_sum[:, cut_v:], out_sum.astype(F32)
    return (
        block_out,
        input_grad,
        gain_sums[0],
        query,
        key,
        value,
        gates,
        output,
        gain_sums[1],
        up_grad,
        down_grad,
    )


def solution(mesh):
    blocks, count = mesh.devices.shape
    split = Mesh(mesh.devices.reshape(blocks // 2, 2, count), AXES)
    rows = P(None, AXES, None)
    gain, wide, tall = P(BLK), P(BLK, "uly"), P("uly", BLK)
    return jax.shard_map(
        body,
        mesh=split,
        in_specs=(rows, gain, wide, wide, wide, wide, tall, gain, wide, tall, P(), P(), rows),
        out_specs=(rows, rows, gain, wide, wide, wide, wide, tall, gain, wide, tall),
        check_vma=False,
    )
```

```python
import functools

import jax
import jax.numpy as jnp
from jax import lax
from jax.experimental import pallas as pl
from jax.experimental.pallas import tpu as pltpu
from jax.sharding import Mesh
from jax.sharding import PartitionSpec as P

EPSILON = 1e-05
BF = jnp.bfloat16
F32 = jnp.float32
AXES = ("chip", "core", "uly")
BLK = ("chip", "core")
MESH = pl.DeviceIdType.MESH
VMEM_LIMIT = 62 * 1024 * 1024


def dot_nn(left, right, kind=F32):
    return jnp.dot(left, right, preferred_element_type=F32).astype(kind)


def dot_tn(left, right, kind=F32):
    return lax.dot_general(
        left, right, (((0,), (0,)), ((), ())), preferred_element_type=F32
    ).astype(kind)


def dot_nt(left, right, kind=F32):
    return lax.dot_general(
        left, right, (((1,), (1,)), ((), ())), preferred_element_type=F32
    ).astype(kind)


def block_index():
    return lax.axis_index("chip") * 2 + lax.axis_index("core")


def block_count():
    return lax.axis_size("chip") * 2


def swap(array, mask):
    if mask == 1:
        return lax.ppermute(array, "core", [(0, 1), (1, 0)])
    count = lax.axis_size("chip")
    return lax.ppermute(array, "chip", [(b, b ^ (mask // 2)) for b in range(count)])


def shift(array, step):
    count = lax.axis_size("uly")
    return lax.ppermute(array, "uly", [(z, (z + step) % count) for z in range(count)])


def is_cube():
    return lax.axis_size("chip") == 4 and lax.axis_size("uly") == 4


def masks():
    return [2 * k + j for j in range(2) for k in range(4)]


def plane_gather(first, second):
    first_x = swap(first, 2)
    second_y = swap(second, 4)
    first_y, first_xy = swap(first, 4), swap(first_x, 4)
    second_x, second_xy = swap(second, 2), swap(second_y, 2)
    return [first, first_x, first_y, first_xy], [second, second_x, second_y, second_xy]


def exchange(pieces):
    if not is_cube():
        return [lax.all_gather(p, BLK) for p in pieces]
    half = len(pieces) // 2
    a, b = plane_gather(jnp.stack(pieces[:half]), jnp.stack(pieces[half:]))
    got = []
    for four in (a, b):
        full = jnp.stack(four + [swap(p, 1) for p in four])
        got += [full[:, i] for i in range(full.shape[1])]
    return got


def spread(rows):
    return lax.all_gather(rows, "uly", axis=1, tiled=True)


def collect(partial):
    return lax.psum_scatter(partial.astype(BF), "uly", scatter_dimension=1, tiled=True).astype(F32)


def core_cut(array, dim):
    core = lax.axis_index("core")
    half = array.shape[dim] // 2
    own = lax.dynamic_slice_in_dim(array, core * half, half, dim)
    other = lax.dynamic_slice_in_dim(array, (1 - core) * half, half, dim)
    return own, other


def core_join(own, other, dim):
    first = lax.axis_index("core") == 0
    return jnp.concatenate([jnp.where(first, own, other), jnp.where(first, other, own)], axis=dim)


def feed_weights(up_shard, down_shard):
    own, other = core_cut(up_shard, 1)
    up = core_join(own, swap(other, 1), 0)
    own, other = core_cut(down_shard, 0)
    down = core_join(own, swap(other, 1), 1)
    pair = lax.all_gather(jnp.stack([up, down.T]), ("chip", "uly"), axis=0, tiled=False)
    chips, count = lax.axis_size("chip"), lax.axis_size("uly")
    rows, hidden = up.shape
    pair = pair.reshape(chips, count, 2, rows, hidden)
    return pair


def feed_reduce(up_grad, down_grad):
    pair = jnp.stack([up_grad, down_grad], axis=2)
    chips, count = pair.shape[:2]
    pair = pair.reshape(chips * count * 2, *pair.shape[3:])
    total = lax.psum_scatter(pair, ("chip", "uly"), scatter_dimension=0, tiled=True)
    half = total.shape[1] // 2
    own, other = core_cut(total, 1)
    both_halves = core_join(own, swap(other, 1), 2).astype(F32)
    return both_halves[0], both_halves[1].T


def normed(values):
    center = values - jnp.mean(values, axis=-1, keepdims=True)
    scale = lax.rsqrt(jnp.mean(center * center, axis=-1, keepdims=True) + EPSILON)
    return center * scale, scale


def norm_back(grad, hat, scale):
    return scale * (
        grad
        - jnp.mean(grad, axis=-1, keepdims=True)
        - hat * jnp.mean(grad * hat, axis=-1, keepdims=True)
    )


GELU_A = 0.7978845608028654
GELU_B = 0.044715


def gelu_pair(u):
    square = u * u
    tanh = jnp.tanh(GELU_A * u * (1.0 + GELU_B * square))
    slope = 0.5 * (1.0 + tanh) + 0.5 * u * (1.0 - tanh * tanh) * GELU_A * (
        1.0 + 3.0 * GELU_B * square
    )
    return 0.5 * u * (1.0 + tanh), slope


def segment_ids(positions, lengths_row):
    count = lengths_row.shape[0]
    before = jnp.arange(count)[None, :] < jnp.arange(count)[:, None]
    bounds = jnp.sum(jnp.where(before, lengths_row[None, :], 0), axis=1)
    return jnp.sum((bounds[None, :] <= positions[:, None]).astype(jnp.int32), axis=1)


def decay_parts(rates, lengths_row, length):
    me = block_index()
    count = block_count()
    places = jnp.arange(length, dtype=jnp.int32)
    seg = segment_ids(me * length + places, lengths_row)
    ends = segment_ids((jnp.arange(count, dtype=jnp.int32) + 1) * length - 1, lengths_row)
    seg_prev = segment_ids(jnp.reshape(me * length - 1, (1,)), lengths_row)[0]
    offset = places[:, None] - places[None, :]
    causal = (offset >= 0) & (seg[:, None] == seg[None, :])
    far = jnp.maximum(offset, 0).astype(F32)
    inner = jnp.where(causal[None], jnp.exp(-rates[:, None, None] * far[None]), 0.0)
    at = places.astype(F32)
    entry = jnp.where(seg == seg_prev, jnp.exp(-rates[:, None] * (at + 1.0)), 0.0)
    leave = jnp.where(seg == seg[length - 1], jnp.exp(-rates[:, None] * (length - 1.0 - at)), 0.0)
    if is_cube():
        source = me ^ jnp.asarray(masks(), jnp.int32)
    else:
        source = jnp.arange(count, dtype=jnp.int32)
    end_of = ends[source]
    end_before = jnp.where(source > 0, ends[jnp.maximum(source - 1, 0)], 0)
    past = jnp.maximum(me - 1 - source, 0).astype(F32)
    ahead = jnp.maximum(source - 1 - me, 0).astype(F32)
    from_past = jnp.where(
        (source < me) & (end_of == seg_prev), jnp.exp(-rates[:, None] * (length * past)), 0.0
    )
    from_ahead = jnp.where(
        (source > me) & (end_before == ends[me]), jnp.exp(-rates[:, None] * (length * ahead)), 0.0
    )
    return inner, entry[:, :, None], leave[:, :, None], from_past, from_ahead


def state_sum(weights, states):
    return jnp.einsum("hb,bhde->hde", weights, states.astype(F32))


def retention_state(heads, leave):
    return jnp.stack(
        [
            dot_tn((k.astype(F32) * leave[h]).astype(BF), v, BF)
            for h, (q, k, v) in enumerate(heads)
        ]
    )


def retention(heads, parts, state):
    inner, entry = parts[0], parts[1]
    out = []
    for h, (q, k, v) in enumerate(heads):
        scores = (dot_nt(q, k) * inner[h]).astype(BF)
        out.append(dot_nn(scores, v) + entry[h] * dot_nn(q, state[h].astype(BF)))
    return out


def mix(gate, retained):
    out = []
    for h, r in enumerate(retained):
        g = gate[:, h * r.shape[1] : (h + 1) * r.shape[1]]
        out.append((g * jax.nn.sigmoid(g) * normed(r)[0]).astype(BF))
    return jnp.concatenate(out, axis=1)


def mix_back(gate, retained, grad_mixed):
    grad_gate, grad_retained = [], []
    for h, r in enumerate(retained):
        cols = slice(h * r.shape[1], (h + 1) * r.shape[1])
        g, gm = gate[:, cols], grad_mixed[:, cols]
        sigma = jax.nn.sigmoid(g)
        hat, scale = normed(r)
        grad_gate.append((gm * hat * (sigma + g * sigma * (1.0 - sigma))).astype(BF))
        grad_retained.append(norm_back(gm * g * sigma, hat, scale).astype(BF))
    return jnp.concatenate(grad_gate, axis=1), grad_retained


def retention_back(heads, parts, state, grad_retained, grad_state):
    inner, entry, leave = parts[0], parts[1], parts[2]
    grads = []
    for h, (q, k, v) in enumerate(heads):
        gr = grad_retained[h]
        scores = (dot_nt(q, k) * inner[h]).astype(BF)
        pulls = (dot_nt(gr, v) * inner[h]).astype(BF)
        gs, st = grad_state[h].astype(BF), state[h].astype(BF)
        gq = dot_nn(pulls, k) + entry[h] * dot_nt(gr, st)
        gk = dot_tn(pulls, q) + leave[h] * dot_nt(v, gs)
        gv = dot_tn(scores, gr) + leave[h] * dot_nn(k, gs)
        grads.append((gq.astype(BF), gk.astype(BF), gv.astype(BF)))
    return grads


def vmem():
    return pl.BlockSpec(memory_space=pltpu.VMEM)


def anywhere():
    return pl.BlockSpec(memory_space=pl.ANY)


def greet(plane=False, line=False, cores=False, pair=False, across=False, whole=False, every=False):
    barrier = pltpu.get_barrier_semaphore()
    chip, core, z = (lax.axis_index(a) for a in AXES)
    others = []
    if plane:
        others += [{"chip": chip ^ 1}, {"chip": chip ^ 2}]
    if cores:
        others.append({"core": 1 - core})
    if pair:
        others.append({"uly": z ^ 1})
    if across:
        others.append({"uly": z ^ 2})
    if whole:
        others += [{"uly": z ^ k} for k in range(1, 4)]
    if every:
        others += [{"chip": chip ^ (p % 4), "core": core ^ (p // 4)} for p in range(1, 8)]
    for to in others:
        pl.semaphore_signal(barrier, inc=1, device_id=to, device_id_type=MESH)
    count = len(others)
    if line:
        last = lax.axis_size("uly") - 1

        @pl.when(z > 0)
        def _():
            pl.semaphore_signal(barrier, inc=1, device_id={"uly": z - 1}, device_id_type=MESH)

        @pl.when(z < last)
        def _():
            pl.semaphore_signal(barrier, inc=1, device_id={"uly": z + 1}, device_id_type=MESH)

        count = count + jnp.where(z > 0, 1, 0) + jnp.where(z < last, 1, 0)
    pl.semaphore_wait(barrier, count)


class PlaneGather:
    def __init__(self, own, at, x_first, send, recv, cores=True):
        chip, core = lax.axis_index("chip"), lax.axis_index("core")
        x, y, other = {"chip": chip ^ 1}, {"chip": chip ^ 2}, {"core": 1 - core}

        def copy(i, src, place, to):
            return pltpu.make_async_remote_copy(
                src_ref=src,
                dst_ref=at(place),
                send_sem=send.at[i],
                recv_sem=recv.at[i],
                device_id=to,
                device_id_type=MESH,
            )

        self.x_first = x_first
        self.copies = [
            copy(0, own, 1, x),
            copy(1, own, 2, y),
            copy(2, at(1), 3, y) if x_first else copy(2, at(2), 3, x),
        ]
        self.cores = cores
        if cores:
            self.copies += [
                copy(3, own, 4, other),
                copy(4, at(1), 5, other),
                copy(5, at(2), 6, other),
                copy(6, at(3), 7, other),
            ]

    def start(self):
        for i in (0, 1) if self.x_first else (1, 0):
            self.copies[i].start()
        if self.cores:
            self.copies[3].start()

    def near(self):
        first = 0 if self.x_first else 1
        self.copies[first].wait_recv()
        self.copies[2].start()
        if self.cores:
            self.copies[4 + first].start()

    def far(self):
        second = 1 if self.x_first else 0
        self.copies[second].wait_recv()
        if self.cores:
            self.copies[4 + second].start()

    def corner(self):
        self.copies[2].wait_recv()
        if self.cores:
            self.copies[6].start()

    def finish(self):
        for c in self.copies[3:]:
            c.wait_recv()
        for c in self.copies:
            c.wait_send()


class LineGather:
    def __init__(self, slots, send, recv):
        self.z = lax.axis_index("uly")
        self.last = lax.axis_size("uly") - 1
        self.slots, self.send, self.recv = slots, send, recv

    def copy(self, right, d):
        z, last = self.z, self.last
        at = jnp.maximum(z - d, 0) if right else jnp.minimum(z + d, last)
        to = jnp.minimum(z + 1, last) if right else jnp.maximum(z - 1, 0)
        way = 0 if right else 1
        return pltpu.make_async_remote_copy(
            src_ref=self.slots.at[at],
            dst_ref=self.slots.at[at],
            send_sem=self.send.at[way, d],
            recv_sem=self.recv.at[way, d],
            device_id={"uly": to},
            device_id_type=MESH,
        )

    def pass_on(self, d):
        z, last = self.z, self.last

        @pl.when((z - d >= 0) & (z < last))
        def _():
            self.copy(True, d).start()

        @pl.when((z + d <= last) & (z > 0))
        def _():
            self.copy(False, d).start()

    def take(self, d, then):
        z, last = self.z, self.last

        @pl.when(z - d >= 0)
        def _():
            self.copy(True, d - 1).wait_recv()

        @pl.when(z + d <= last)
        def _():
            self.copy(False, d - 1).wait_recv()

        if d < last:
            self.pass_on(d)
        self.each(d, then)

    def each(self, d, then):
        z, last = self.z, self.last

        @pl.when(z - d >= 0)
        def _():
            then(jnp.maximum(z - d, 0))

        @pl.when(z + d <= last)
        def _():
            then(jnp.minimum(z + d, last))

    def finish(self):
        z, last = self.z, self.last
        for d in range(last):

            @pl.when((z - d >= 0) & (z < last))
            def _():
                self.copy(True, d).wait_send()

            @pl.when((z + d <= last) & (z > 0))
            def _():
                self.copy(False, d).wait_send()


class LineReduce:
    def __init__(self, make, out, held, came, send, recv):
        self.z = lax.axis_index("uly")
        self.last = lax.axis_size("uly") - 1
        self.make, self.out, self.held, self.came = make, out, held, came
        self.send, self.recv = send, recv

    def copy(self, right, d):
        z, last = self.z, self.last
        way = 0 if right else 1
        to = jnp.minimum(z + 1, last) if right else jnp.maximum(z - 1, 0)
        return pltpu.make_async_remote_copy(
            src_ref=self.held.at[self.place(right, d)],
            dst_ref=self.came.at[way, d - 1],
            send_sem=self.send.at[way, d - 1],
            recv_sem=self.recv.at[way, d - 1],
            device_id={"uly": to},
            device_id_type=MESH,
        )

    def place(self, right, d):
        return d - 1 if right else self.last - d

    def step(self, d):
        z, last = self.z, self.last
        for right in (True, False):
            way = 0 if right else 1
            held = self.held.at[self.place(right, d)]
            valid = (z + d <= last) if right else (z - d >= 0)
            more = (z > 0) if right else (z < last)
            to = jnp.minimum(z + d, last) if right else jnp.maximum(z - d, 0)

            @pl.when(valid)
            def _():
                self.make(to, held)

                if d < last:

                    @pl.when(more)
                    def _():
                        self.copy(right, d + 1).wait_recv()
                        held[...] = (held[...].astype(F32) + self.came[way, d].astype(F32)).astype(
                            BF
                        )

                self.copy(right, d).start()

    def own(self):
        self.make(self.z, self.out)

    def close(self):
        z, last = self.z, self.last

        @pl.when(z > 0)
        def _():
            self.copy(True, 1).wait_recv()
            self.out[...] += self.came[0, 0].astype(F32)

        @pl.when(z < last)
        def _():
            self.copy(False, 1).wait_recv()
            self.out[...] += self.came[1, 0].astype(F32)

        for d in range(1, last + 1):

            @pl.when(z + d <= last)
            def _():
                self.copy(True, d).wait_send()

            @pl.when(z - d >= 0)
            def _():
                self.copy(False, d).wait_send()


def chunk_of(place, width):
    chip, core = lax.axis_index("chip"), lax.axis_index("core")
    block = (chip ^ (place % 4)) * 2 + (core ^ (place // 4))
    return pl.ds(pl.multiple_of(block * width, width), width)


def chip_chunk(k, width):
    return pl.ds(pl.multiple_of((lax.axis_index("chip") ^ k) * width, width), width)


def chip_order(place, width):
    core = lax.axis_index("core")
    return pl.ds(pl.multiple_of((place % 4) * (2 * width) + (core ^ (place // 4)) * width, width), width)


def front_kernel(
    io,
    rates_ref,
    lengths_ref,
    tok_ref,
    dout_ref,
    gain_ref,
    q_hbm,
    k_hbm,
    v_hbm,
    g_hbm,
    out_hbm,
    up_hbm,
    down_hbm,
    one_ref,
    first_ref,
    high_ref,
    gate_ref,
    w_first_hbm,
    w_second_hbm,
    w_out_hbm,
    gains_ref,
    up_own_hbm,
    down_own_hbm,
    mixed_ref,
    kept_ref,
    state_ref,
    douts_ref,
    slots,
    wa,
    wb,
    gains,
    psend,
    precv,
    zsend,
    zrecv,
    fsend,
    frecv,
    dsend,
    drecv,
    lsem,
    stage_out,
    stage_up,
    stage_down,
    *state_refs,
):
    core, z = lax.axis_index("core"), lax.axis_index("uly")
    rows = tok_ref.shape[0] // 2
    width = tok_ref.shape[1]
    piece = width // 8
    qk, high = q_hbm.shape[1], high_ref.shape[2]
    gains[0] = jnp.zeros_like(gains[0])
    gains[0, 0:2, :] = gain_ref[...]
    line = LineGather(slots, zsend, zrecv)
    slots[z] = tok_ref[...]
    greet(every=True, line=True, across=True)
    chip = lax.axis_index("chip")
    small = [
        pltpu.make_async_remote_copy(
            src_ref=gains.at[0],
            dst_ref=gains.at[p],
            send_sem=psend.at[0, p - 1],
            recv_sem=precv.at[0, p - 1],
            device_id={"chip": chip ^ (p % 4), "core": core ^ (p // 4)},
            device_id_type=MESH,
        )
        for p in range(1, 8)
    ]
    for c in small:
        c.start()
    line.pass_on(0)
    own = pl.ds(0, piece)
    local = [
        pltpu.make_async_copy(src, dst, lsem.at[i])
        for i, (src, dst) in enumerate(
            (
                (q_hbm, wa.at[own, pl.ds(0, qk)]),
                (k_hbm, wa.at[own, pl.ds(qk, qk)]),
                (v_hbm.at[:, pl.ds(0, high)], wa.at[own, pl.ds(2 * qk, high)]),
                (v_hbm.at[:, pl.ds(high, high)], wb.at[own, pl.ds(0, high)]),
                (g_hbm, wb.at[own, pl.ds(high, g_hbm.shape[1])]),
                (out_hbm, stage_out),
            )
        )
    ]
    for c in local:
        c.start()
    items = [None]
    for i, w in enumerate((wa, wb)):
        items.append(
            PlaneGather(
                w.at[own],
                lambda p, w=w: w.at[pl.ds(p * piece, piece)],
                i == 0,
                psend.at[1 + i],
                precv.at[1 + i],
            )
        )
    half = out_hbm.shape[0] // 2
    for i in range(2):
        part = pl.ds(i * half, half)
        items.append(
            PlaneGather(
                out_hbm.at[part],
                lambda p, part=part: w_out_hbm.at[part, pl.ds(p * piece, piece)],
                i == 0,
                psend.at[3 + i],
                precv.at[3 + i],
            )
        )
    units, cols = up_hbm.shape[1] // 2, down_hbm.shape[1]
    first_half = pl.ds(0, units)
    mine, theirs = (pl.ds(pl.multiple_of(c * units, units), units) for c in (core, 1 - core))
    here = pl.ds(pl.multiple_of(core * cols, cols), cols)

    def remote(i, src, dst, to):
        return pltpu.make_async_remote_copy(
            src_ref=src,
            dst_ref=dst,
            send_sem=fsend.at[i],
            recv_sem=frecv.at[i],
            device_id=to,
            device_id_type=MESH,
        )

    stage = [
        local[5],
        pltpu.make_async_copy(up_hbm.at[:, mine], stage_up, lsem.at[6]),
        pltpu.make_async_copy(down_hbm.at[mine], stage_down, lsem.at[7]),
    ]
    cut = [
        pltpu.make_async_copy(stage_out, w_out_hbm.at[:, own], lsem.at[10]),
        pltpu.make_async_copy(stage_up, up_own_hbm.at[here, first_half], lsem.at[11]),
        pltpu.make_async_copy(stage_down, down_own_hbm.at[first_half, here], lsem.at[12]),
    ]
    give = [
        remote(0, up_hbm.at[:, theirs], up_own_hbm.at[here, first_half], {"core": 1 - core}),
        remote(1, down_hbm.at[theirs], down_own_hbm.at[first_half, here], {"core": 1 - core}),
    ]
    first_wide, second_wide = up_own_hbm.at[:, first_half], up_own_hbm.at[:, pl.ds(units, units)]
    first_tall, second_tall = down_own_hbm.at[first_half], down_own_hbm.at[pl.ds(units, units)]
    away = [
        remote(2, first_wide, second_wide, {"uly": z ^ 2}),
        remote(3, first_tall, second_tall, {"uly": z ^ 2}),
    ]
    own_rows = 2 * rows

    def rows_to(i, src, dst, to):
        return pltpu.make_async_remote_copy(
            src_ref=douts_ref.at[pl.ds(src * own_rows, own_rows)],
            dst_ref=douts_ref.at[pl.ds(dst * own_rows, own_rows)],
            send_sem=dsend.at[i],
            recv_sem=drecv.at[i],
            device_id=to,
            device_id_type=MESH,
        )

    send_rows = [
        rows_to(0, 0, 2, {"uly": z ^ 1}),
        rows_to(1, 0, 1, {"core": 1 - core}),
        rows_to(2, 2, 3, {"core": 1 - core}),
    ]
    for c in stage[1:]:
        c.start()
    for c in local[:5]:
        c.wait()
    for item in items[1:3]:
        item.start()
    for c in give:
        c.start()
    for c in small:
        c.wait()
    gains_ref[...] = jnp.zeros_like(gains_ref)
    for p in range(8):
        gains_ref[0:1, chunk_of(p, piece)] = gains[p, 0:1, :]
        gains_ref[1:2, chip_order(p, piece)] = gains[p, 1:2, :]

    def normalize(slot):
        step = 32
        for m in range(2):

            @pl.loop(0, rows // step)
            def _(i):
                at = pl.multiple_of(i * step, step)
                v = slots[slot, pl.ds(m * rows + at, step), :].astype(F32)
                mean = jnp.mean(v, axis=-1, keepdims=True)
                center = v - mean
                scale = lax.rsqrt(jnp.mean(center * center, axis=-1, keepdims=True) + EPSILON)
                to = pl.ds(pl.multiple_of(slot * rows + at, step), step)
                for p in range(8):
                    src = slots[slot, pl.ds(m * rows + at, step), chunk_of(p, piece)].astype(F32)
                    one_ref[m, to, pl.ds(p * piece, piece)] = (
                        (src - mean) * scale * gains[p, 0:1, :]
                    ).astype(BF)

    for c in stage:
        c.wait()
    for c in cut:
        c.start()
    for k in range(4):
        douts_ref[0:own_rows, k * 2 * piece : (k + 1) * 2 * piece] = dout_ref[
            :, chip_chunk(k, 2 * piece)
        ]
    at_end = (z == 0) | (z == line.last)
    inside = (z > 0) & (z < line.last)
    normalize(z)
    line.take(1, normalize)

    @pl.when(at_end)
    def _():
        send_rows[0].start()

    for item in items[1:3]:
        item.near()
    for item in items[1:3]:
        item.far()
    for item in items[3:]:
        item.start()
    line.take(2, normalize)
    for c in cut:
        c.wait()
    for c in give:
        c.wait()

    @pl.when(at_end)
    def _():
        for c in away:
            c.start()

    for item in items[1:3]:
        item.corner()
    for item in items[1:3]:
        item.finish()
    outs = [
        pltpu.make_async_copy(wa, w_first_hbm, lsem.at[8]),
        pltpu.make_async_copy(wb, w_second_hbm, lsem.at[9]),
    ]
    for c in outs:
        c.start()
    tile = 512

    def multiply(slot):
        at = pl.ds(pl.multiple_of(slot * rows, rows), rows)
        x = jnp.concatenate([one_ref[0, at, :], one_ref[1, at, :]], axis=0)

        def tiles(w, start, to_ref):
            @pl.loop(0, to_ref.shape[2] // tile)
            def _(n):
                cols = pl.ds(pl.multiple_of(n * tile, tile), tile)
                from_ = pl.ds(pl.multiple_of(start + n * tile, tile), tile)
                r = jnp.dot(x, w[:, from_], preferred_element_type=F32).astype(to_ref.dtype)
                for m in range(2):
                    to_ref[m, at, cols] = r[m * rows : (m + 1) * rows]

        tiles(wa, 0, first_ref)
        tiles(wb, 0, high_ref)
        tiles(wb, high, gate_ref)

    multiply(z)
    line.each(1, multiply)
    for item in items[3:]:
        item.near()
    for item in items[3:]:
        item.far()
    line.each(2, multiply)

    def both_steps(slot):
        normalize(slot)
        multiply(slot)

    line.take(3, both_steps)

    @pl.when(inside)
    def _():
        for c in away:
            c.wait_recv()
        send_rows[0].start()
        for c in away:
            c.start()

    io.done("one", "first", "high", "gate")
    for item in items[3:]:
        item.corner()
    for item in items[3:]:
        item.finish()
    line.finish()
    retain_part(
        io,
        rates_ref,
        lengths_ref,
        first_ref,
        high_ref,
        gate_ref,
        mixed_ref,
        kept_ref,
        state_ref,
        douts_ref,
        send_rows,
        *state_refs,
    )
    for c in outs:
        c.wait()

    @pl.when(at_end)
    def _():
        for c in away:
            c.wait_recv()

    for c in away:
        c.wait_send()


def add_rows_kernel(
    io,
    x_ref,
    w_ref,
    tok_ref,
    up_hbm,
    down_hbm,
    out_ref,
    ups_hbm,
    downs_hbm,
    held,
    came,
    send,
    recv,
    psend,
    precv,
    lsem,
    stage_up,
    stage_down,
):
    rows = out_ref.shape[0] // 2
    width = out_ref.shape[1] // 8
    greet(plane=True, line=True)
    part = up_hbm.shape[0]

    def up_at(p):
        return ups_hbm.at[pl.ds(p * part, part)]

    def down_at(p):
        return downs_hbm.at[:, pl.ds(p * part, part)]

    items = [
        PlaneGather(up_hbm, up_at, True, psend.at[0], precv.at[0], False),
        PlaneGather(down_hbm, down_at, False, psend.at[1], precv.at[1], False),
    ]
    stage = [
        pltpu.make_async_copy(up_hbm, stage_up, lsem.at[2]),
        pltpu.make_async_copy(down_hbm, stage_down, lsem.at[3]),
    ]
    local = [
        pltpu.make_async_copy(stage_up, up_at(0), lsem.at[0]),
        pltpu.make_async_copy(stage_down, down_at(0), lsem.at[1]),
    ]

    def make(a, to):
        at = pl.ds(pl.multiple_of(a * rows, rows), rows)
        x = jnp.concatenate([x_ref[0, at, :], x_ref[1, at, :]], axis=0)

        @pl.loop(0, 8)
        def _(p):
            cols = w_ref[:, pl.ds(pl.multiple_of(p * width, width), width)]
            to[:, chip_order(p, width)] = jnp.dot(x, cols, preferred_element_type=F32).astype(
                to.dtype
            )

    line = LineReduce(make, out_ref, held, came, send, recv)
    for item in items:
        item.start()
    io.ready("x", "w")
    line.step(3)
    io.start(1)
    for c in stage:
        c.start()
    line.step(2)
    for c in stage:
        c.wait()
    for c in local:
        c.start()
    for item in items:
        item.near()
    for item in items:
        item.far()
    line.step(1)
    line.own()
    line.close()
    io.ready("tokens")
    for k in range(4):
        cols = pl.ds(k * 2 * width, 2 * width)
        out_ref[:, cols] += tok_ref[:, chip_chunk(k, 2 * width)].astype(F32)
    for item in items:
        item.corner()
    for item in items:
        item.finish()
    for c in local:
        c.wait()


def fan_out_kernel(
    io,
    rows_ref,
    w_ref,
    mixed_ref,
    up_hbm,
    down_hbm,
    grad_ref,
    part_ref,
    up_ref,
    down_ref,
    slots,
    ordered,
    total,
    near_up,
    near_down,
    came_up,
    came_down,
    send,
    recv,
    psend,
    precv,
    lsem,
):
    z = lax.axis_index("uly")
    rows = rows_ref.shape[0] // 2
    width = rows_ref.shape[1] // 8
    greet(plane=True, line=True)
    line = LineGather(slots, send, recv)
    slots[z] = rows_ref[...]
    line.pass_on(0)
    local = [
        pltpu.make_async_copy(up_hbm, near_up, lsem.at[0]),
        pltpu.make_async_copy(down_hbm, near_down, lsem.at[1]),
    ]
    for c in local:
        c.start()
    groups = [
        PlaneReduce(None, near_up, came_up, True, psend.at[0], precv.at[0]),
        PlaneReduce(None, near_down, came_down, False, psend.at[1], precv.at[1]),
    ]
    for c in local:
        c.wait()
    for g in groups:
        g.start_first()

    def multiply(slot):
        at = pl.ds(pl.multiple_of(slot * rows, rows), rows)
        for p in range(8):
            ordered[:, p * width : (p + 1) * width] = slots[slot, :, chip_order(p, width)]
        tile = 256

        @pl.loop(0, w_ref.shape[0] // tile)
        def _(n):
            part = pl.ds(pl.multiple_of(n * tile, tile), tile)
            product = dot_nt(ordered[...], w_ref[part, :])
            for m in range(2):
                grad_ref[m, at, part] = product[m * rows : (m + 1) * rows]

        mixed = jnp.concatenate([mixed_ref[0, at, :], mixed_ref[1, at, :]], axis=0)

        @pl.loop(0, 8)
        def _(p):
            cols = pl.ds(pl.multiple_of(p * width, width), width)
            total[p] += dot_tn(ordered[:, cols], mixed)

    total[...] = jnp.zeros_like(total)
    io.ready("w", "mixed")
    multiply(z)
    line.take(1, multiply)
    for g in groups:
        g.first_sums(0)
    line.take(2, multiply)
    for g in groups:
        g.first_sums(1)
    line.take(3, multiply)
    io.done("grad")
    half = part_ref.shape[3]
    for i in range(2):
        part_ref[i] = total[:, :, i * half : (i + 1) * half].astype(BF)
    io.done("part")
    groups[0].finish(up_ref)
    groups[1].finish(down_ref)
    line.finish()


def feed_kernel(
    io,
    hid_ref,
    douts_ref,
    gain_ref,
    ups_ref,
    downs_ref,
    keep_ref,
    give_ref,
    grad_ref,
    rows_ref,
    gain_grad_ref,
    up_grad_ref,
    down_grad_ref,
    two,
    act,
    gu,
    sums,
    held,
    came,
    send,
    recv,
):
    core, z = lax.axis_index("core"), lax.axis_index("uly")
    rows, width = hid_ref.shape
    hidden = ups_ref.shape[1]
    other, pair = {"core": 1 - core}, {"uly": z ^ 1}
    greet(cores=True, pair=True)

    half = rows // 2

    def group(g, part=None):
        return pl.ds(g * rows, rows) if part is None else pl.ds(g * rows + part * half, half)

    def copy(i, src, dst, to):
        return pltpu.make_async_remote_copy(
            src_ref=src,
            dst_ref=dst,
            send_sem=send.at[i],
            recv_sem=recv.at[i],
            device_id=to,
            device_id_type=MESH,
        )

    parts = [pl.ds(part * half, half) for part in range(2)]
    to_pair = [copy(p, two.at[group(0, p)], two.at[group(2, p)], pair) for p in range(2)]
    through = [copy(2 + p, two.at[group(2, p)], two.at[group(3, p)], other) for p in range(2)]
    to_other = copy(4, two.at[group(0)], two.at[group(1)], other)
    step = 32
    io.ready("hid")
    io.start(1)
    for part in range(2):

        @pl.loop(0, half // step)
        def _(i):
            at = pl.ds(pl.multiple_of(part * half + i * step, step), step)
            hat, _scale = normed(hid_ref[at, :])
            two[at, :] = (hat * gain_ref[1:2, :]).astype(BF)

        to_pair[part].start()
    to_other.start()

    def work(g, part=None):
        at = group(g, part)
        to = slice(None) if part is None else parts[part]
        tile = 256

        @pl.loop(0, hidden // tile)
        def _(n):
            cols = pl.ds(pl.multiple_of(n * tile, tile), tile)
            upward = jnp.dot(two[at, :], ups_ref[:, cols], preferred_element_type=F32)
            value, slope = gelu_pair(upward)
            act[at, cols] = value.astype(BF)
            pulled = dot_nt(douts_ref[at, :], downs_ref[cols, :])
            gu[at, cols] = (pulled * slope).astype(BF)

        tile = 512

        @pl.loop(0, width // tile)
        def _(n):
            cols = pl.ds(pl.multiple_of(n * tile, tile), tile)
            back = dot_nt(gu[at, :], ups_ref[cols, :])
            down = jnp.dot(act[at, :], downs_ref[:, cols], preferred_element_type=F32)
            if g == 0:
                sums[0, :, cols] = back
                sums[1, :, cols] = down
            else:
                held[g - 1, 0, to, cols] = back.astype(BF)
                held[g - 1, 1, to, cols] = down.astype(BF)

    own_back = [copy(5 + i, held.at[0, i], came.at[3 * i], other) for i in range(2)]
    pair_back = [
        [
            copy(7 + 2 * p + i, held.at[2, i, parts[p]], came.at[1 + 3 * i, parts[p]], other)
            for i in range(2)
        ]
        for p in range(2)
    ]
    last = [copy(11 + p, held.at[1, 0, parts[p]], came.at[2, parts[p]], pair) for p in range(2)]

    io.ready("ups", "downs", "douts")
    work(0)
    to_other.wait_recv()
    work(1)
    for c in own_back:
        c.start()
    for p in range(2):
        to_pair[p].wait_recv()
        through[p].start()
        work(2, p)
        through[p].wait_recv()
        work(3, p)
        for c in pair_back[p]:
            c.start()
        for i in range(2):
            pair_back[p][i].wait_recv()

            @pl.loop(0, half // step)
            def _(r):
                at = pl.ds(pl.multiple_of(p * half + r * step, step), step)
                held[1, i, at, :] = (
                    held[1, i, at, :].astype(F32) + came[1 + 3 * i, at, :].astype(F32)
                ).astype(BF)

            if i == 0:
                last[p].start()
    give_ref[...] = held[1, 1]
    io.done("give")
    tile = 512

    @pl.loop(0, width // tile)
    def _(n):
        cols = pl.ds(pl.multiple_of(n * tile, tile), tile)
        up_grad_ref[n] = dot_tn(two[:, cols], gu[...], BF)
        down_grad_ref[n] = dot_tn(act[...], douts_ref[:, cols], BF)

    io.done("up", "down")
    for c in own_back + last:
        c.wait_recv()
    gain_grad_ref[...] = jnp.zeros_like(gain_grad_ref)

    @pl.loop(0, rows // step)
    def _(r):
        at = pl.ds(pl.multiple_of(r * step, step), step)
        back = sums[0, at, :] + came[0, at, :].astype(F32) + came[2, at, :].astype(F32)
        hat, scale = normed(hid_ref[at, :])
        gain_grad_ref[...] += jnp.sum(back * hat, axis=0, keepdims=True)
        grad = douts_ref[at, :].astype(F32) + norm_back(back * gain_ref[1:2, :], hat, scale)
        grad_ref[at, :] = grad
        rows_ref[at, :] = grad.astype(BF)
        keep_ref[at, :] = hid_ref[at, :] + sums[1, at, :] + came[3, at, :].astype(F32)

    for c in to_pair + through + own_back + pair_back[0] + pair_back[1] + last + [to_other]:
        c.wait_send()


class PlaneReduce:
    def __init__(self, far, near, came, x_first, send, recv):
        chip, core = lax.axis_index("chip"), lax.axis_index("core")
        x, y, other = {"chip": chip ^ 1}, {"chip": chip ^ 2}, {"core": 1 - core}
        self.near, self.came, self.x_first = near, came, x_first
        self.waited = ()

        def copy(i, src, to):
            return pltpu.make_async_remote_copy(
                src_ref=src,
                dst_ref=came.at[i],
                send_sem=send.at[i],
                recv_sem=recv.at[i],
                device_id=to,
                device_id_type=MESH,
            )

        self.away = (1, 3) if x_first else (2, 3)
        self.stay = (0, 2) if x_first else (0, 1)
        one, two = (x, y) if x_first else (y, x)
        self.cores = 4 if far else 0
        self.copies = [copy(i, far(4 + i), other) for i in range(self.cores)]
        self.copies += [copy(self.cores + i, near.at[self.away[i]], one) for i in range(2)]
        self.copies.append(copy(self.cores + 2, near.at[self.stay[1]], two))

    def start(self):
        for i in (3, self.away[0], self.stay[1], 0):
            self.copies[i].start()

    def add(self, place, i):
        step = 64

        @pl.loop(0, self.near.shape[1] // step)
        def _(r):
            at = pl.ds(pl.multiple_of(r * step, step), step)
            self.near[place, at, :] = (
                self.near[place, at, :].astype(F32) + self.came[i, at, :].astype(F32)
            ).astype(BF)

    def core_sums(self):
        for i in (1, 0):
            p = self.away[i]
            self.copies[p].wait_recv()
            self.add(p, p)
            self.copies[4 + i].start()
        for p in (self.stay[1], self.stay[0]):
            self.copies[p].wait_recv()
            self.add(p, p)

    def start_first(self):
        for i in (1, 0):
            self.copies[self.cores + i].start()

    def first_sums(self, step):
        i = 1 - step
        self.copies[self.cores + i].wait_recv()
        self.add(self.stay[i], self.cores + i)
        if i == 1:
            self.copies[self.cores + 2].start()

    def finish(self, out_ref):
        self.copies[self.cores + 2].wait_recv()
        self.add(self.stay[0], self.cores + 2)
        out_ref[...] = self.near[0]
        for i, c in enumerate(self.copies):
            if i not in self.waited:
                c.wait_send()


def far_slot(i, x_first):
    return ((3, 1, 2, 0) if x_first else (3, 2, 1, 0)).index(i) % 2


def close_rows_kernel(
    io,
    xa_ref,
    xb_ref,
    wa_ref,
    wb_ref,
    one_ref,
    tok_ref,
    hid_ref,
    gain_ref,
    gain_two_ref,
    out_ref,
    sum_a_ref,
    sum_b_ref,
    gains_ref,
    held,
    came,
    near_a,
    near_b,
    far_a,
    far_b,
    came_a,
    came_b,
    small,
    small_came,
    small_line,
    send,
    recv,
    psend,
    precv,
    ssend,
    srecv,
):
    chip, core, z = (lax.axis_index(a) for a in AXES)
    rows = out_ref.shape[0] // 2
    length = one_ref.shape[0] // 2
    width = out_ref.shape[1] // 8
    greet(every=True, whole=True)

    def make(a, to):
        at = [
            pl.ds(pl.multiple_of(m * length + a * rows, rows), rows) for m in range(2)
        ]
        xa = jnp.concatenate([xa_ref[i, :] for i in at], axis=0)
        xb = jnp.concatenate([xb_ref[i, :] for i in at], axis=0)

        @pl.loop(0, 8)
        def _(p):
            part = pl.ds(pl.multiple_of(p * width, width), width)
            r = dot_nt(xa, wa_ref[part, :]) + dot_nt(xb, wb_ref[part, :])
            to[:, chunk_of(p, width)] = r.astype(to.dtype)
            ones = jnp.concatenate([one_ref[i, part] for i in at], axis=0)
            small[p, 0:1, :] += jnp.sum(r * ones.astype(F32), axis=0, keepdims=True)

    small[...] = jnp.zeros_like(small)
    line = LineReduce(make, out_ref, held, came, send, recv)
    sets = []
    for i, (x_ref, near, far, got, x_first) in enumerate(
        (
            (xa_ref, near_a, far_a, came_a, True),
            (xb_ref, near_b, far_b, came_b, False),
        )
    ):
        group = PlaneReduce(
            lambda p, far=far, x=x_first: far.at[far_slot(p - 4, x)],
            near,
            got,
            x_first,
            psend.at[i],
            precv.at[i],
        )
        group.waited = tuple((3, group.away[0]))
        sets.append((group, x_ref, near, far, got))

    tile = 512

    def product(x_ref, place, to, more=None):
        @pl.loop(0, x_ref.shape[1] // tile)
        def _(n):
            cols = pl.ds(pl.multiple_of(n * tile, tile), tile)
            r = dot_tn(one_ref[:, place * width : (place + 1) * width], x_ref[:, cols])
            if more is not None:
                r = r + more[:, cols].astype(F32)
            to[:, cols] = r.astype(BF)

    io.ready("xa", "xb", "wa", "wb", "one")
    io.start(1)
    line.step(3)
    for n in range(4):
        for group, x_ref, near, far, got in sets:
            order = (3, group.away[0], group.stay[1], 0)
            if n >= 2:
                group.copies[order[n - 2]].wait_send()
            product(x_ref, 4 + order[n], far.at[n % 2])
            group.copies[order[n]].start()

    def add_near(n):
        for group, x_ref, near, far, got in sets:
            i = (3, group.away[0], group.stay[1], 0)[n]
            group.copies[i].wait_recv()
            product(x_ref, i, near.at[i], got.at[i])
            if n < 2:
                group.copies[4 + (1 - n)].start()

    add_near(0)
    add_near(1)
    line.step(2)
    add_near(2)
    add_near(3)
    line.step(1)
    line.own()
    for p in range(8):
        small[p, 0:1, :] = small[p, 0:1, :] / gain_ref[0:1, chunk_of(p, width)]
        small[p, 1:2, :] = gain_two_ref[:, chip_order(p, width)]

    def pass_small(i, src, dst, to):
        return pltpu.make_async_remote_copy(
            src_ref=src,
            dst_ref=dst,
            send_sem=ssend.at[i],
            recv_sem=srecv.at[i],
            device_id=to,
            device_id_type=MESH,
        )

    sent = [
        pass_small(
            p - 1,
            small.at[p],
            small_came.at[p],
            {"chip": chip ^ (p % 4), "core": core ^ (p // 4)},
        )
        for p in range(1, 8)
    ]
    for c in sent:
        c.start()
    for group, *_ in sets:
        group.first_sums(0)
    for group, *_ in sets:
        group.first_sums(1)
    total = small[0]
    for p in range(1, 8):
        sent[p - 1].wait_recv()
        total = total + small_came[p]
    small_line[0] = total
    last = [
        pass_small(6 + k, small_line.at[0], small_line.at[k], {"uly": z ^ k}) for k in range(1, 4)
    ]
    for c in last:
        c.start()
    io.ready("tokens", "hid")
    line.close()
    step = 32

    @pl.loop(0, 2 * rows // step)
    def _(r):
        at = pl.ds(pl.multiple_of(r * step, step), step)
        hat, scale = normed(tok_ref[at, :].astype(F32))
        out_ref[at, :] = norm_back(out_ref[at, :] * gain_ref[0:1, :], hat, scale)
        for k in range(4):
            out_ref[at, chip_chunk(k, 2 * width)] += hid_ref[
                at, k * 2 * width : (k + 1) * 2 * width
            ]

    for (group, *_), out in zip(sets, (sum_a_ref, sum_b_ref)):
        group.finish(out)
    for k in range(1, 4):
        last[k - 1].wait_recv()
        total = total + small_line[k]
    gains_ref[...] = total
    for c in sent + last:
        c.wait_send()


class StateExchange:
    def __init__(self, weights, own, sib, chips, mine, came, final, send, recv):
        self.core = lax.axis_index("core")
        self.weights, self.own, self.sib, self.chips = weights, own, sib, chips
        self.mine, self.came, self.final = mine, came, final

        def copy(i, src, dst):
            return pltpu.make_async_remote_copy(
                src_ref=src,
                dst_ref=dst,
                send_sem=send.at[2, i],
                recv_sem=recv.at[2, i],
                device_id={"core": 1 - self.core},
                device_id_type=MESH,
            )

        self.first = copy(0, own, sib)
        self.second = copy(1, mine, came)
        self.items = [
            PlaneGather(
                chips.at[0, h], lambda p, h=h: chips.at[p, h], h == 0, send.at[h], recv.at[h], False
            )
            for h in range(2)
        ]

    def start(self):
        self.first.start()

    def join(self):
        self.first.wait_recv()
        m = self.core
        for h in range(2):
            mine, other = self.weights.joined(m, h)
            self.chips[0, h] = (
                mine * self.own[m, h].astype(F32) + other * self.sib[m, h].astype(F32)
            ).astype(BF)
            self.items[h].start()

    def near(self):
        for item in self.items:
            item.near()

    def far(self):
        for item in self.items:
            item.far()

    def settle(self):
        for item in self.items:
            item.corner()
        m = self.core
        for h in range(2):
            total = self.weights.chip(m, h, 1) * self.chips[1, h].astype(F32)
            for k in (2, 3):
                total = total + self.weights.chip(m, h, k) * self.chips[k, h].astype(F32)
            self.mine[h] = total.astype(BF)
        self.second.start()
        self.last(m, self.mine)
        self.second.wait_recv()
        self.last(1 - m, self.came)

    def last(self, m, chip_state):
        for h in range(2):
            whole, other = self.weights.final(m, h)
            self.final[m, h] = (
                whole * chip_state[h].astype(F32) + other * self.sib[m, h].astype(F32)
            ).astype(BF)

    def finish(self):
        self.first.wait_send()
        self.second.wait_send()
        for item in self.items:
            item.finish()


def state_scratch(shape):
    half = shape[1:]
    return [
        pltpu.VMEM(shape, BF),
        pltpu.VMEM(shape, BF),
        pltpu.VMEM((4, *half), BF),
        pltpu.VMEM(half, BF),
        pltpu.VMEM(half, BF),
        sems(3, 3),
        sems(3, 3),
    ]


class Places:
    def __init__(self, lengths_ref, m, length):
        self.length = length
        self.base = (lax.axis_index("chip") * 2 + lax.axis_index("core")) * length
        self.bounds = []
        total = 0
        for n in range(lengths_ref.shape[1]):
            self.bounds.append(total)
            total = total + lengths_ref[m, n]

    def segment(self, at):
        found = jnp.zeros_like(at)
        for b in self.bounds:
            found = found + jnp.where(self.base + at >= b, 1, 0)
        return found

    def table(self, rate, start, count, across):
        shape = (count, self.length)
        rows = start + lax.broadcasted_iota(jnp.int32, shape, 0)
        cols = lax.broadcasted_iota(jnp.int32, shape, 1)
        off = cols - rows if across else rows - cols
        seg_rows = self.segment(start + lax.broadcasted_iota(jnp.int32, (count, 1), 0))
        seg_cols = self.segment(lax.broadcasted_iota(jnp.int32, (1, self.length), 1))
        far = jnp.maximum(off, 0).astype(F32)
        return jnp.where((off >= 0) & (seg_rows == seg_cols), jnp.exp(-rate * far), 0.0)

    def entry(self, rate, start, count):
        at = start + lax.broadcasted_iota(jnp.int32, (count, 1), 0)
        same = self.segment(at) == self.segment(jnp.full((1, 1), -1, jnp.int32))
        return jnp.where(same, jnp.exp(-rate * (at + 1).astype(F32)), 0.0)

    def leave(self, rate, start, count):
        at = start + lax.broadcasted_iota(jnp.int32, (count, 1), 0)
        end = jnp.full((1, 1), self.length - 1, jnp.int32)
        same = self.segment(at) == self.segment(end)
        return jnp.where(same, jnp.exp(-rate * (self.length - 1 - at).astype(F32)), 0.0)


def rate_of(rates_ref, h):
    return rates_ref[lax.axis_index("uly") * 2 + h]


class StateWeights:
    def __init__(self, rates_ref, lengths_ref, length, back):
        self.rates, self.lengths, self.length, self.back = rates_ref, lengths_ref, length, back
        self.chip_at, self.core = lax.axis_index("chip"), lax.axis_index("core")

    def end(self, m, block):
        at = jnp.full((1, 1), (block + 1) * self.length - 1, jnp.int32)
        found = jnp.zeros_like(at)
        total = 0
        for n in range(self.lengths.shape[1]):
            found = found + jnp.where(at >= total, 1, 0)
            total = total + self.lengths[m, n]
        return found

    def decay(self, h, count):
        far = jnp.full((1, 1), count * self.length, jnp.int32).astype(F32)
        return jnp.exp(-rate_of(self.rates, h) * far)

    def through(self, m, h, block):
        same = self.end(m, block) == self.end(m, block - 1)
        return jnp.where(same, self.decay(h, 1), 0.0)

    def pick(self, first, second):
        return jnp.where(jnp.full((1, 1), self.core, jnp.int32) == 0, first, second)

    def joined(self, m, h):
        one = jnp.ones((1, 1), F32)
        if self.back:
            even = self.through(m, h, 2 * self.chip_at)
            return self.pick(one, even), self.pick(even, one)
        odd = self.through(m, h, 2 * self.chip_at + 1)
        return self.pick(odd, one), self.pick(one, odd)

    def final(self, m, h):
        one, zero = jnp.ones((1, 1), F32), jnp.zeros((1, 1), F32)
        if self.back:
            return self.pick(self.through(m, h, 2 * self.chip_at + 1), one), self.pick(one, zero)
        return self.pick(one, self.through(m, h, 2 * self.chip_at)), self.pick(zero, one)

    def chip(self, m, h, k):
        here, there = self.chip_at, self.chip_at ^ k
        low, high = (here, there) if self.back else (there, here)
        before = jnp.full((1, 1), low, jnp.int32) < jnp.full((1, 1), high, jnp.int32)
        same = self.end(m, 2 * low + 1) == self.end(m, 2 * high - 1)
        return jnp.where(before & same, self.decay(h, 2 * jnp.maximum(high - 1 - low, 0)), 0.0)


ROWS = 128


def retain_part(
    io,
    rates_ref,
    lengths_ref,
    a_ref,
    high_ref,
    gate_ref,
    mixed_ref,
    kept_ref,
    state_ref,
    douts_ref,
    send_rows,
    own,
    sib,
    chips,
    mine,
    came,
    send,
    recv,
):
    _, length, vd = high_ref.shape
    qk = (a_ref.shape[2] - vd) // 2
    hd = qk // 2
    weights = StateWeights(rates_ref, lengths_ref, length, False)
    states = StateExchange(weights, own, sib, chips, mine, came, state_ref, send, recv)
    to_pair, to_other, through = send_rows

    def values(m, h):
        return high_ref[m] if h else a_ref[m, :, 2 * qk :]

    def keys(m, h):
        return a_ref[m, :, qk + h * hd : qk + (h + 1) * hd]

    for h in range(2):

        @pl.loop(0, 2)
        def _(m):
            leave = Places(lengths_ref, m, length).leave(rate_of(rates_ref, h), 0, length)
            k = (keys(m, h).astype(F32) * leave).astype(BF)
            own[m, h] = dot_tn(k, values(m, h), BF)

    states.start()
    parts = length // ROWS

    def local(h):
        @pl.loop(0, 2 * parts)
        def _(i):
            m, r = i // parts, i % parts
            at = pl.ds(pl.multiple_of(r * ROWS, ROWS), ROWS)
            table = Places(lengths_ref, m, length).table(rate_of(rates_ref, h), r * ROWS, ROWS, False)
            q = a_ref[m, at, h * hd : (h + 1) * hd]
            scores = (dot_nt(q, keys(m, h)) * table).astype(BF)
            kept_ref[m, at, h * vd : (h + 1) * vd] = jnp.dot(
                scores, values(m, h), preferred_element_type=F32
            )

    states.join()
    to_other.start()
    local(0)
    states.near()
    local(1)
    states.far()
    states.settle()
    for h in range(2):

        @pl.loop(0, 2 * parts)
        def _(i):
            m, r = i // parts, i % parts
            at = pl.ds(pl.multiple_of(r * ROWS, ROWS), ROWS)
            cols = slice(h * vd, (h + 1) * vd)
            entry = Places(lengths_ref, m, length).entry(rate_of(rates_ref, h), r * ROWS, ROWS)
            q = a_ref[m, at, h * hd : (h + 1) * hd]
            kept = kept_ref[m, at, cols] + entry * jnp.dot(
                q, state_ref[m, h], preferred_element_type=F32
            )
            kept_ref[m, at, cols] = kept
            g = gate_ref[m, at, cols]
            mixed_ref[m, at, cols] = (g * sigmoid(g) * normed(kept)[0]).astype(BF)

    states.finish()
    to_pair.wait_recv()
    through.start()
    to_other.wait_recv()
    through.wait_recv()
    io.done("douts")
    for c in send_rows:
        c.wait_send()


def sigmoid(v):
    return 0.5 * jnp.tanh(0.5 * v) + 0.5


def retain_back_kernel(
    io,
    rates_ref,
    lengths_ref,
    a_ref,
    high_ref,
    gate_ref,
    kept_ref,
    grad_ref,
    state_ref,
    part_hbm,
    keep_ref,
    give_hbm,
    up_sum_ref,
    down_sum_ref,
    xa_ref,
    xb_ref,
    sum_ref,
    out_ref,
    up_ref,
    down_ref,
    pulled,
    grad_k,
    grad_v,
    final,
    own,
    sib,
    chips,
    mine,
    came,
    send,
    recv,
    near,
    got,
    psend,
    precv,
    lsem,
    came_rows,
    rsend,
    rrecv,
    came_up,
    came_down,
    swap_up,
    swap_down,
    came_swap_up,
    came_swap_down,
    fsend,
    frecv,
):
    _, length, vd = high_ref.shape
    qk = (a_ref.shape[2] - vd) // 2
    hd = qk // 2
    greet(plane=True, cores=True, pair=True, across=True)
    core, z = lax.axis_index("core"), lax.axis_index("uly")

    def feed_copy(i, src, dst, to):
        return pltpu.make_async_remote_copy(
            src_ref=src,
            dst_ref=dst,
            send_sem=fsend.at[i],
            recv_sem=frecv.at[i],
            device_id=to,
            device_id_type=MESH,
        )

    units = came_up.shape[1]
    across = [
        feed_copy(0, up_sum_ref.at[:, pl.ds(units, units)], came_up, {"uly": z ^ 2}),
        feed_copy(1, down_sum_ref.at[pl.ds(units, units)], came_down, {"uly": z ^ 2}),
    ]
    swaps = [
        feed_copy(2, swap_up, came_swap_up, {"core": 1 - core}),
        feed_copy(3, swap_down, came_swap_down, {"core": 1 - core}),
    ]
    io.ready("up", "down")
    for c in across:
        c.start()
    give = pltpu.make_async_remote_copy(
        src_ref=give_hbm,
        dst_ref=came_rows,
        send_sem=rsend,
        recv_sem=rrecv,
        device_id={"uly": lax.axis_index("uly") ^ 1},
        device_id_type=MESH,
    )
    give.start()
    groups = [
        PlaneReduce(
            lambda p, i=i: part_hbm.at[i, p],
            near.at[i],
            got.at[i],
            i == 0,
            psend.at[i],
            precv.at[i],
        )
        for i in range(2)
    ]
    local = [
        pltpu.make_async_copy(part_hbm.at[i, pl.ds(0, 4)], near.at[i], lsem.at[i]) for i in range(2)
    ]
    for c in local:
        c.start()
    for group in groups:
        group.start()
    io.ready("gate", "kept", "grad")
    io.start(1)
    weights = StateWeights(rates_ref, lengths_ref, length, True)
    states = StateExchange(weights, own, sib, chips, mine, came, final, send, recv)
    parts = length // ROWS

    def values(m, h, at=slice(None)):
        return high_ref[m, at, :] if h else a_ref[m, at, 2 * qk :]

    def keys(m, h, at=slice(None)):
        return a_ref[m, at, qk + h * hd : qk + (h + 1) * hd]

    def queries(m, h, at=slice(None)):
        return a_ref[m, at, h * hd : (h + 1) * hd]

    for h in range(2):
        cols = slice(h * vd, (h + 1) * vd)

        @pl.loop(0, 2 * parts)
        def _(i):
            m, r = i // parts, i % parts
            at = pl.ds(pl.multiple_of(r * ROWS, ROWS), ROWS)
            g, gm = gate_ref[m, at, cols], grad_ref[m, at, cols]
            sigma = sigmoid(g)
            hat, scale = normed(kept_ref[m, at, cols])
            xb_ref[m, at, vd + h * vd : vd + (h + 1) * vd] = (
                gm * hat * (sigma + g * sigma * (1.0 - sigma))
            ).astype(BF)
            pulled[m, at, cols] = norm_back(gm * g * sigma, hat, scale).astype(BF)

        if h == 0:
            io.ready("a", "high", "state")

        @pl.loop(0, 2)
        def _(m):
            entry = Places(lengths_ref, m, length).entry(rate_of(rates_ref, h), 0, length)
            q = (queries(m, h).astype(F32) * entry).astype(BF)
            own[m, h] = dot_tn(q, pulled[m, :, cols], BF)

    states.start()

    def local_q(h):
        cols = slice(h * vd, (h + 1) * vd)

        @pl.loop(0, 2 * parts)
        def _(i):
            m, r = i // parts, i % parts
            at = pl.ds(pl.multiple_of(r * ROWS, ROWS), ROWS)
            places = Places(lengths_ref, m, length)
            table = places.table(rate_of(rates_ref, h), r * ROWS, ROWS, False)
            gr = pulled[m, at, cols]
            p = (dot_nt(gr, values(m, h)) * table).astype(BF)
            entry = places.entry(rate_of(rates_ref, h), r * ROWS, ROWS)
            xa_ref[m, at, h * hd : (h + 1) * hd] = (
                jnp.dot(p, keys(m, h), preferred_element_type=F32)
                + entry * dot_nt(gr, state_ref[m, h])
            ).astype(BF)

    def local_kv(h):
        cols = slice(h * vd, (h + 1) * vd)

        @pl.loop(0, 2 * parts)
        def _(i):
            m, r = i // parts, i % parts
            at = pl.ds(pl.multiple_of(r * ROWS, ROWS), ROWS)
            table = Places(lengths_ref, m, length).table(rate_of(rates_ref, h), r * ROWS, ROWS, True)
            p = (dot_nt(values(m, h, at), pulled[m, :, cols]) * table).astype(BF)
            scores = (dot_nt(keys(m, h, at), queries(m, h)) * table).astype(BF)
            grad_k[m, at, h * hd : (h + 1) * hd] = jnp.dot(
                p, queries(m, h), preferred_element_type=F32
            )
            grad_v[m, at, cols] = jnp.dot(
                scores, pulled[m, :, cols], preferred_element_type=F32
            )

    states.join()
    local_q(0)
    states.near()
    states.far()
    for c in local:
        c.wait()
    for group in groups:
        group.core_sums()
    local_q(1)
    states.settle()
    local_kv(0)
    for group in groups:
        group.first_sums(0)
    for group in groups:
        group.first_sums(1)
    local_kv(1)
    for h in range(2):

        @pl.loop(0, 2 * parts)
        def _(i):
            m, r = i // parts, i % parts
            at = pl.ds(pl.multiple_of(r * ROWS, ROWS), ROWS)
            leave = Places(lengths_ref, m, length).leave(rate_of(rates_ref, h), r * ROWS, ROWS)
            xa_ref[m, at, qk + h * hd : qk + (h + 1) * hd] = (
                grad_k[m, at, h * hd : (h + 1) * hd]
                + leave * dot_nt(values(m, h, at), final[m, h])
            ).astype(BF)
            gv = (
                grad_v[m, at, h * vd : (h + 1) * vd]
                + leave * jnp.dot(keys(m, h, at), final[m, h], preferred_element_type=F32)
            ).astype(BF)
            if h:
                xb_ref[m, at, :vd] = gv
            else:
                xa_ref[m, at, 2 * qk :] = gv

    states.finish()
    give.wait()
    io.ready("keep")
    quarter = keep_ref.shape[1] // 4
    for k in range(4):
        cols = slice(k * quarter, (k + 1) * quarter)
        out_ref[:, chip_chunk(k, quarter)] = (
            keep_ref[:, cols] + came_rows[:, cols].astype(F32)
        ).astype(BF)
    for i, group in enumerate(groups):
        group.finish(sum_ref.at[i])
    rows, cols = up_ref.shape[0], down_ref.shape[1]

    def mine(size, own):
        return pl.ds(pl.multiple_of((core if own else 1 - core) * size, size), size)

    for c in across:
        c.wait()
    kept_units = slice(0, units)

    def up_total(own):
        at = mine(rows, own)
        return up_sum_ref[at, kept_units].astype(F32) + came_up[at, :].astype(F32)

    def down_total(own):
        at = mine(cols, own)
        return down_sum_ref[kept_units, at].astype(F32) + came_down[:, at].astype(F32)

    swap_up[...] = up_total(False).astype(BF)
    swap_down[...] = down_total(False).astype(BF)
    for c in swaps:
        c.start()
    up_ref[:, mine(units, True)] = up_total(True)
    down_ref[mine(units, True), :] = down_total(True)
    for c in swaps:
        c.wait()
    up_ref[:, mine(units, False)] = came_swap_up[...].astype(F32)
    down_ref[mine(units, False), :] = came_swap_down[...].astype(F32)


def sems(*shape):
    return pltpu.SemaphoreType.DMA(shape)


def like(shape, kind):
    return jax.ShapeDtypeStruct(shape, kind)


class Late:
    def __init__(self, name, order=0):
        self.name, self.order = name, order


class Early:
    def __init__(self, name):
        self.name = name


class Moves:
    def __init__(self, loads, stores):
        self.loads, self.stores = loads, stores
        self.waited, self.begun = set(), set()

    def start(self, order):
        for copy, at in self.loads.values():
            if at == order:
                copy.start()

    def ready(self, *names):
        for name in names:
            self.loads[name][0].wait()
            self.waited.add(name)

    def done(self, *names):
        for name in names:
            self.stores[name].start()
            self.begun.add(name)

    def finish(self):
        self.done(*[n for n in self.stores if n not in self.begun])
        self.ready(*[n for n in self.loads if n not in self.waited])
        for copy in self.stores.values():
            copy.wait()


def call(kernel, number, ins, outs, scratch, flops, *args):
    moved = sum(a.size * a.dtype.itemsize for a in args)
    late = [i for i, spec in enumerate(ins) if isinstance(spec, Late)]
    early = [i for i, out in enumerate(outs) if isinstance(out[2], Early)]

    def whole(*refs):
        refs = list(refs)
        in_refs, refs = refs[: len(ins)], refs[len(ins) :]
        out_refs, refs = refs[: len(outs)], refs[len(outs) :]
        own, refs = refs[: len(scratch)], refs[len(scratch) :]
        load_sem, store_sem = refs[-2:]
        loads, stores = {}, {}
        for n, i in enumerate(late):
            copy = pltpu.make_async_copy(in_refs[i], refs[n], load_sem.at[n])
            loads[ins[i].name] = (copy, ins[i].order)
            in_refs[i] = refs[n]
        for n, i in enumerate(early):
            ref = refs[len(late) + n]
            stores[outs[i][2].name] = pltpu.make_async_copy(ref, out_refs[i], store_sem.at[n])
            out_refs[i] = ref
        io = Moves(loads, stores)
        io.start(0)
        kernel(io, *in_refs, *out_refs, *own)
        io.finish()

    extra = [pltpu.VMEM(args[i].shape, args[i].dtype) for i in late]
    extra += [pltpu.VMEM(outs[i][0], outs[i][1]) for i in early]
    return pl.pallas_call(
        whole,
        out_shape=[like(shape, kind) for shape, kind, _ in outs],
        in_specs=[anywhere() if i in late else spec for i, spec in enumerate(ins)],
        out_specs=[anywhere() if i in early else out[2] for i, out in enumerate(outs)],
        scratch_shapes=list(scratch)
        + extra
        + [sems(max(len(late), 1)), sems(max(len(early), 1))],
        compiler_params=pltpu.CompilerParams(
            collective_id=number, has_side_effects=True, vmem_limit_bytes=VMEM_LIMIT
        ),
        cost_estimate=pl.CostEstimate(flops=flops, bytes_accessed=moved, transcendentals=0),
    )(*args)


def smem():
    return pl.BlockSpec(memory_space=pltpu.SMEM)


def settle_kernel(
    block_in, input_in, first_in, second_in, out_in, up_in, down_in, *outs
):
    block, inputs, query, key, value, gate, output, up, down = outs
    qk, half = query.shape[1], out_in.shape[2]
    high = value.shape[1] // 2
    block[...] = block_in[...]
    inputs[...] = input_in[...]
    query[...] = first_in[:, :qk].astype(F32)
    key[...] = first_in[:, qk : 2 * qk].astype(F32)
    value[:, :high] = first_in[:, 2 * qk :].astype(F32)
    value[:, high:] = second_in[:, :high].astype(F32)
    gate[...] = second_in[:, high:].astype(F32)
    for i in range(2):
        output[i * half : (i + 1) * half, :] = out_in[i].astype(F32).T
    up[...] = up_in[...]
    down[...] = down_in[...]


def settle(block_out, input_grad, first_sum, second_sum, out_sum, up_grad, down_grad, qk):
    piece = first_sum.shape[0]
    high = first_sum.shape[1] - 2 * qk
    args = (block_out, input_grad, first_sum, second_sum, out_sum, up_grad, down_grad)
    shapes = [
        (block_out.shape, BF),
        (input_grad.shape, F32),
        ((piece, qk), F32),
        ((piece, qk), F32),
        ((piece, 2 * high), F32),
        ((piece, second_sum.shape[1] - high), F32),
        ((2 * out_sum.shape[2], piece), F32),
        (up_grad.shape, F32),
        (down_grad.shape, F32),
    ]
    return pl.pallas_call(
        settle_kernel,
        out_shape=[like(s, t) for s, t in shapes],
        in_specs=[vmem()] * len(args),
        out_specs=[vmem()] * len(shapes),
        compiler_params=pltpu.CompilerParams(vmem_limit_bytes=VMEM_LIMIT),
    )(*args)


def retain_back(
    rates, lengths, a, high, gate, kept, grad_mixed, state, part, keep, give, up_sum, down_sum
):
    units = up_sum.shape[1] // 2
    rows, cols = up_sum.shape[0] // 2, down_sum.shape[1] // 2
    micro, length, vd = high.shape
    hd = (a.shape[2] - vd) // 4
    return call(
        retain_back_kernel,
        6,
        [smem()] * 2
        + [Late("a", 1), Late("high", 1), Late("gate"), Late("kept"), Late("grad"), Late("state", 1)]
        + [anywhere(), Late("keep", 1), anywhere(), Late("up"), Late("down")],
        [
            ((micro, length, a.shape[2]), BF, vmem()),
            ((micro, length, 3 * vd), BF, vmem()),
            ((2, *part.shape[2:]), BF, vmem()),
            (give.shape, BF, vmem()),
            ((rows, 2 * units), F32, vmem()),
            ((2 * units, cols), F32, vmem()),
        ],
        [
            pltpu.VMEM((micro, length, 2 * vd), BF),
            pltpu.VMEM((micro, length, 2 * hd), F32),
            pltpu.VMEM((micro, length, 2 * vd), F32),
            pltpu.VMEM(state.shape, BF),
        ]
        + state_scratch(state.shape)
        + [
            pltpu.VMEM((2, 4, *part.shape[2:]), BF),
            pltpu.VMEM((2, 7, *part.shape[2:]), BF),
            sems(2, 7),
            sems(2, 7),
            sems(2),
            pltpu.VMEM(give.shape, BF),
            pltpu.SemaphoreType.DMA,
            pltpu.SemaphoreType.DMA,
            pltpu.VMEM((2 * rows, units), BF),
            pltpu.VMEM((units, 2 * cols), BF),
            pltpu.VMEM((rows, units), BF),
            pltpu.VMEM((units, cols), BF),
            pltpu.VMEM((rows, units), BF),
            pltpu.VMEM((units, cols), BF),
            sems(4),
            sems(4),
        ],
        12 * micro * length * length * (hd + vd),
        rates,
        lengths,
        a,
        high,
        gate,
        kept,
        grad_mixed,
        state,
        part,
        keep,
        give,
        up_sum,
        down_sum,
    )


def front(rates, lengths, tokens, out_grad, gains, weights, out_weight, up_weight, down_weight):
    micro, rows, width = tokens.shape
    count = lax.axis_size("uly")
    query, key, value, gate = weights
    high = value.shape[1] // 2
    if not is_cube():
        first = jnp.concatenate([query, key, value[:, :high]], axis=1)
        second = jnp.concatenate([value[:, high:], gate], axis=1)
        full = lax.all_gather(jnp.stack(gains), BLK, axis=1, tiled=True)
        w_first = lax.all_gather(first, BLK, axis=0, tiled=True)
        w_second = lax.all_gather(second, BLK, axis=0, tiled=True)
        w_out = lax.all_gather(out_weight, BLK, axis=1, tiled=True)
        one = (normed(spread(tokens).astype(F32))[0] * full[0].astype(F32)).astype(BF)
        a, v_high = dot_nn(one, w_first, BF), dot_nn(one, w_second[:, :high], BF)
        gate_rows = dot_nn(one, w_second[:, high:])
        heads_here = rates.shape[0] // count
        own_rates = lax.dynamic_slice_in_dim(
            rates, lax.axis_index("uly") * heads_here, heads_here
        )
        mixed, kept = plain_forward(own_rates, lengths, a, v_high, gate_rows)
        return (
            one,
            a,
            v_high,
            gate_rows,
            w_first,
            w_second,
            w_out,
            full.astype(F32),
            up_weight,
            down_weight,
            mixed,
            kept,
            None,
            None,
        )
    wide = count * rows
    own = micro * rows
    piece = width // 8
    na, nb, no = 2 * query.shape[1] + high, high + gate.shape[1], out_weight.shape[0]
    units = up_weight.shape[1]
    state = (micro, 2, query.shape[1] // 2, high)
    return call(
        front_kernel,
        0,
        [smem()] * 2 + [vmem()] * 3 + [anywhere()] * 7,
        [
            ((micro, wide, width), BF, Early("one")),
            ((micro, wide, na), BF, Early("first")),
            ((micro, wide, high), BF, Early("high")),
            ((micro, wide, nb - high), F32, Early("gate")),
            ((width, na), BF, anywhere()),
            ((width, nb), BF, anywhere()),
            ((no, width), BF, anywhere()),
            ((8, width), F32, vmem()),
            ((2 * piece, units), BF, anywhere()),
            ((units, 2 * piece), BF, anywhere()),
            ((micro, wide, 2 * high), BF, vmem()),
            ((micro, wide, 2 * high), F32, vmem()),
            (state, BF, vmem()),
            ((4 * own, width), BF, Early("douts")),
        ],
        [
            pltpu.VMEM((count, own, width), BF),
            pltpu.VMEM((width, na), BF),
            pltpu.VMEM((width, nb), BF),
            pltpu.VMEM((8, 8, piece), F32),
            sems(5, 7),
            sems(5, 7),
            sems(2, count - 1),
            sems(2, count - 1),
            sems(4),
            sems(4),
            sems(3),
            sems(3),
            sems(13),
            pltpu.VMEM(out_weight.shape, BF),
            pltpu.VMEM((up_weight.shape[0], units // 2), BF),
            pltpu.VMEM((units // 2, down_weight.shape[1]), BF),
        ]
        + state_scratch(state),
        2 * micro * wide * width * (na + nb),
        rates,
        lengths,
        tokens.reshape(own, width),
        out_grad.reshape(own, width),
        jnp.stack(gains).astype(F32),
        query,
        key,
        value,
        gate,
        out_weight,
        up_weight,
        down_weight,
    )


def line_scratch(count, rows, width):
    return [
        pltpu.VMEM((count - 1, rows, width), BF),
        pltpu.VMEM((2, count - 1, rows, width), BF),
    ]


def add_rows(mixed, w_out, tokens, up, down):
    micro, wide, hidden = mixed.shape
    count = lax.axis_size("uly")
    rows = wide // count
    width = w_out.shape[1]
    units = up.shape[1]
    out = call(
        add_rows_kernel,
        1,
        [Late("x"), Late("w"), Late("tokens", 1)] + [anywhere()] * 2,
        [
            ((micro * rows, width), F32, vmem()),
            ((width, units), BF, anywhere()),
            ((units, width), BF, anywhere()),
        ],
        line_scratch(count, micro * rows, width)
        + [sems(2, count - 1)] * 2
        + [sems(2, 3), sems(2, 3), sems(4), pltpu.VMEM(up.shape, BF), pltpu.VMEM(down.shape, BF)],
        2 * micro * wide * hidden * width,
        mixed,
        w_out,
        tokens,
        up,
        down,
    )
    return out


def fan_out(rows_bf, w_out, mixed, up_grad, down_grad):
    own, width = rows_bf.shape
    micro, rows = 2, own // 2
    count = lax.axis_size("uly")
    hidden = w_out.shape[0]
    up_shape, down_shape = up_grad.shape[1:], down_grad.shape[1:]
    return call(
        fan_out_kernel,
        2,
        [vmem(), Late("w"), Late("mixed")] + [anywhere()] * 2,
        [
            ((micro, count * rows, hidden), F32, Early("grad")),
            ((2, 8, width // 8, hidden // 2), BF, Early("part")),
            (up_shape, BF, vmem()),
            (down_shape, BF, vmem()),
        ],
        [
            pltpu.VMEM((count, own, width), BF),
            pltpu.VMEM((own, width), BF),
            pltpu.VMEM((8, width // 8, hidden), F32),
            pltpu.VMEM((4, *up_shape), BF),
            pltpu.VMEM((4, *down_shape), BF),
            pltpu.VMEM((3, *up_shape), BF),
            pltpu.VMEM((3, *down_shape), BF),
            sems(2, count - 1),
            sems(2, count - 1),
            sems(2, 3),
            sems(2, 3),
            sems(2),
        ],
        4 * micro * count * rows * hidden * width,
        rows_bf,
        w_out,
        mixed,
        up_grad,
        down_grad,
    )


def feed_all(hidden, douts, gain, ups, downs):
    own, width = hidden.shape
    units = ups.shape[1]
    return call(
        feed_kernel,
        4,
        [Late("hid"), Late("douts", 1), vmem(), Late("ups", 1), Late("downs", 1)],
        [
            ((own, width), F32, vmem()),
            ((own, width), BF, Early("give")),
            ((own, width), F32, vmem()),
            ((own, width), BF, vmem()),
            ((1, width), F32, vmem()),
            ((4, width // 4, units), BF, Early("up")),
            ((4, units, width // 4), BF, Early("down")),
        ],
        [
            pltpu.VMEM((4 * own, width), BF),
            pltpu.VMEM((4 * own, units), BF),
            pltpu.VMEM((4 * own, units), BF),
            pltpu.VMEM((2, own, width), F32),
            pltpu.VMEM((3, 2, own, width), BF),
            pltpu.VMEM((5, own, width), BF),
            sems(13),
            sems(13),
        ],
        2 * 6 * 4 * own * units * width,
        hidden,
        douts,
        gain,
        ups,
        downs,
    )


def middle(tokens, out_grad, douts, gains, mixed, w_out, up_weight, down_weight):
    micro, rows, width = tokens.shape
    own = micro * rows
    if not is_cube():
        gain_two = gains[1]
        hidden = tokens.astype(F32) + collect(
            jnp.stack([dot_nn(mixed[m], w_out) for m in range(micro)])
        )
        pair = feed_weights(up_weight, down_weight)
        hat, scale = normed(hidden)
        two = (hat * gain_two).astype(BF)
        flat_two, flat_out = two.reshape(own, width), out_grad.reshape(own, width)
        two_both = jnp.concatenate([flat_two, swap(flat_two, 1)], axis=0)
        out_both = jnp.concatenate([flat_out, swap(flat_out, 1)], axis=0)
        down_rows, grad_two, up_part, down_part = feed(two_both, out_both, pair)
        grad_two = grad_two[:own] + swap(grad_two[own:].astype(BF), 1).astype(F32)
        down_rows = down_rows[:own] + swap(down_rows[own:].astype(BF), 1).astype(F32)
        up_grad, down_grad = feed_reduce(up_part, down_part)
        block_out = (hidden + down_rows.reshape(micro, rows, width)).astype(BF)
        grad_two = grad_two.reshape(micro, rows, width)
        gain_part = jnp.sum(grad_two * hat, axis=(0, 1))
        grad_hidden = out_grad.astype(F32) + norm_back(grad_two * gain_two, hat, scale)
        wide_att = spread(grad_hidden.astype(BF))
        grad_mixed = jnp.stack([dot_nt(wide_att[m], w_out) for m in range(micro)])
        part = dot_tn(
            mixed.reshape(-1, mixed.shape[2]), wide_att.reshape(-1, wide_att.shape[2]), BF
        )
        return block_out, up_grad, down_grad, gain_part, grad_hidden, grad_mixed, part
    hidden, ups, downs = add_rows(mixed, w_out, tokens.reshape(own, width), up_weight, down_weight)
    keep, give, grad_hidden, rows_bf, gain_part, up_part, down_part = feed_all(
        hidden, douts, gains, ups, downs
    )
    grad_mixed, part, up_sum, down_sum = fan_out(rows_bf, w_out, mixed, up_part, down_part)
    return (
        (keep, give),
        up_sum,
        down_sum,
        gain_part,
        grad_hidden,
        grad_mixed,
        part,
    )


def close_rows(xa, xb, w_first, w_second, one, tokens, grad_hidden, gains, gain_two):
    micro, wide, na = xa.shape
    nb = xb.shape[2]
    width = w_first.shape[0]
    flat_a, flat_b = xa.reshape(micro * wide, na), xb.reshape(micro * wide, nb)
    flat_one = one.reshape(micro * wide, width)
    if not is_cube():
        partial = jnp.stack(
            [dot_nt(xa[m], w_first) + dot_nt(xb[m], w_second) for m in range(micro)]
        )
        grad_one = collect(partial)
        hat, scale = normed(tokens.astype(F32))
        both_gains = jnp.stack([jnp.sum(grad_one * hat, axis=(0, 1)), gain_two])
        total = lax.psum_scatter(both_gains, BLK, scatter_dimension=1, tiled=True)
        return (
            grad_hidden + norm_back(grad_one * gains[0], hat, scale),
            lax.psum_scatter(dot_tn(flat_one, flat_a, BF), BLK, scatter_dimension=0, tiled=True),
            lax.psum_scatter(dot_tn(flat_one, flat_b, BF), BLK, scatter_dimension=0, tiled=True),
            lax.psum(total, "uly"),
        )
    count = lax.axis_size("uly")
    rows = wide // count
    piece = width // 8
    out = call(
        close_rows_kernel,
        3,
        [Late("xa"), Late("xb"), Late("wa"), Late("wb"), Late("one"), Late("tokens", 1)]
        + [Late("hid", 1), vmem(), vmem()],
        [
            ((micro * rows, width), F32, vmem()),
            ((piece, na), BF, vmem()),
            ((piece, nb), BF, vmem()),
            ((8, piece), F32, vmem()),
        ],
        line_scratch(count, micro * rows, width)
        + [
            pltpu.VMEM((4, piece, na), BF),
            pltpu.VMEM((4, piece, nb), BF),
            pltpu.VMEM((2, piece, na), BF),
            pltpu.VMEM((2, piece, nb), BF),
            pltpu.VMEM((7, piece, na), BF),
            pltpu.VMEM((7, piece, nb), BF),
            pltpu.VMEM((8, 8, piece), F32),
            pltpu.VMEM((8, 8, piece), F32),
            pltpu.VMEM((4, 8, piece), F32),
            sems(2, count - 1),
            sems(2, count - 1),
            sems(2, 7),
            sems(2, 7),
            sems(10),
            sems(10),
        ],
        4 * micro * wide * width * (na + nb),
        flat_a,
        flat_b,
        w_first,
        w_second,
        flat_one,
        tokens.reshape(micro * rows, width),
        grad_hidden,
        gains,
        gain_two,
    )
    return out


def feed(norm_two, out_rows, pair):
    chips, count, _, rows, hidden = pair.shape
    up = pair[:, :, 0].transpose(0, 2, 1, 3).reshape(chips * rows, count * hidden)
    down_t = pair[:, :, 1].transpose(0, 2, 1, 3).reshape(chips * rows, count * hidden)
    upward = dot_nn(norm_two, up)
    act, slope = gelu_pair(upward)
    act = act.astype(BF)
    grad_act = dot_nn(out_rows, down_t)
    grad_up = (grad_act * slope).astype(BF)

    def by_owner(grad):
        return grad.reshape(chips, rows, count, hidden).transpose(0, 2, 1, 3)

    return (
        dot_nt(act, down_t),
        dot_nt(grad_up, up),
        by_owner(dot_tn(norm_two, grad_up, BF)),
        by_owner(dot_tn(out_rows, act, BF)),
    )


def plain_forward(rates, lengths, a, v_high, gate):
    micro, length = a.shape[:2]
    heads_here = rates.shape[0]
    cut_v = v_high.shape[2]
    qk = (a.shape[2] - cut_v) // 2
    hd, vd = qk // heads_here, 2 * cut_v // heads_here
    sets, parts, states = [], [], []
    for m in range(micro):
        values = jnp.concatenate([a[m, :, 2 * qk :], v_high[m]], axis=1)
        heads = [
            (
                a[m, :, h * hd : (h + 1) * hd],
                a[m, :, qk + h * hd : qk + (h + 1) * hd],
                values[:, h * vd : (h + 1) * vd],
            )
            for h in range(heads_here)
        ]
        part = decay_parts(rates, lengths[m], length)
        states.append(retention_state(heads, part[2]))
        sets.append(heads)
        parts.append(part)

    all_states = exchange(states)
    state_in, retained, mixed = [], [], []
    for m in range(micro):
        state = state_sum(parts[m][3], all_states[m])
        kept = retention(sets[m], parts[m], state)
        state_in.append(state)
        retained.append(kept)
        mixed.append(mix(gate[m], kept))
    mixed = jnp.stack(mixed)
    return mixed, (sets, parts, state_in, retained)


def plain_backward(gate, kept, grad_mixed):
    sets, parts, state_in, retained = kept
    micro, cut_v = len(sets), gate.shape[2] // 2
    grad_gates, grad_rets, grad_states = [], [], []
    for m in range(micro):
        gg, gr = mix_back(gate[m], retained[m], grad_mixed[m])
        grad_gates.append(gg)
        grad_rets.append(gr)
        grad_states.append(
            jnp.stack(
                [
                    dot_tn((q.astype(F32) * parts[m][1][h]).astype(BF), gr[h], BF)
                    for h, (q, k, v) in enumerate(sets[m])
                ]
            )
        )
    all_back = exchange(grad_states)
    xa, xb = [], []
    for m in range(micro):
        back = state_sum(parts[m][4], all_back[m])
        grads = retention_back(sets[m], parts[m], state_in[m], grad_rets[m], back)
        gq = jnp.concatenate([g[0] for g in grads], axis=1)
        gk = jnp.concatenate([g[1] for g in grads], axis=1)
        gv = jnp.concatenate([g[2] for g in grads], axis=1)
        xa.append(jnp.concatenate([gq, gk, gv[:, :cut_v]], axis=1))
        xb.append(jnp.concatenate([gv[:, cut_v:], grad_gates[m]], axis=1))
    xa, xb = jnp.stack(xa), jnp.stack(xb)
    return xa, xb


def body(
    tokens,
    retain_gain,
    query_weight,
    key_weight,
    value_weight,
    gate_matrix,
    output_weight,
    feed_gain,
    up_weight,
    down_weight,
    decay_rate,
    lengths,
    out_grad,
):
    micro, rows, width = tokens.shape
    qk = query_weight.shape[1]
    cut_v = value_weight.shape[1] // 2

    (
        one,
        a,
        v_high,
        gate,
        w_first,
        w_second,
        w_out,
        gains,
        up,
        down,
        mixed,
        kept,
        state,
        douts,
    ) = front(
        decay_rate,
        lengths,
        tokens,
        out_grad,
        (retain_gain, feed_gain),
        (query_weight, key_weight, value_weight, gate_matrix),
        output_weight,
        up_weight,
        down_weight,
    )
    block_out, up_grad, down_grad, gain_two, grad_hidden, grad_mixed, part = middle(
        tokens, out_grad, douts, gains, mixed, w_out, up, down
    )

    if is_cube():
        xa, xb, out_sum, block_out, up_grad, down_grad = retain_back(
            decay_rate,
            lengths,
            a,
            v_high,
            gate,
            kept,
            grad_mixed,
            state,
            part,
            *block_out,
            up_grad,
            down_grad,
        )
    else:
        xa, xb = plain_backward(gate, kept, grad_mixed)
        out_sum = lax.psum_scatter(part, BLK, scatter_dimension=1, tiled=True)

    input_grad, first_sum, second_sum, gain_sums = close_rows(
        xa, xb, w_first, w_second, one, tokens, grad_hidden, gains, gain_two
    )
    if is_cube():
        block_out, input_grad, query, key, value, gates, output, up_grad, down_grad = settle(
            block_out, input_grad, first_sum, second_sum, out_sum, up_grad, down_grad, qk
        )
        block_out = block_out.reshape(tokens.shape)
        input_grad = input_grad.reshape(tokens.shape)
    else:
        first_sum, second_sum = first_sum.astype(F32), second_sum.astype(F32)
        query, key = first_sum[:, :qk], first_sum[:, qk : 2 * qk]
        value = jnp.concatenate([first_sum[:, 2 * qk :], second_sum[:, :cut_v]], axis=1)
        gates, output = second_sum[:, cut_v:], out_sum.astype(F32)
    return (
        block_out,
        input_grad,
        gain_sums[0],
        query,
        key,
        value,
        gates,
        output,
        gain_sums[1],
        up_grad,
        down_grad,
    )


def solution(mesh):
    blocks, count = mesh.devices.shape
    split = Mesh(mesh.devices.reshape(blocks // 2, 2, count), AXES)
    rows = P(None, AXES, None)
    gain, wide, tall = P(BLK), P(BLK, "uly"), P("uly", BLK)
    return jax.shard_map(
        body,
        mesh=split,
        in_specs=(rows, gain, wide, wide, wide, wide, tall, gain, wide, tall, P(), P(), rows),
        out_specs=(rows, rows, gain, wide, wide, wide, wide, tall, gain, wide, tall),
        check_vma=False,
    )
```

```python
import functools

import jax
import jax.numpy as jnp
from jax import lax
from jax.experimental import pallas as pl
from jax.experimental.pallas import tpu as pltpu
from jax.sharding import Mesh
from jax.sharding import PartitionSpec as P

EPSILON = 1e-05
BF = jnp.bfloat16
F32 = jnp.float32
AXES = ("chip", "core", "uly")
BLK = ("chip", "core")
MESH = pl.DeviceIdType.MESH
VMEM_LIMIT = 62 * 1024 * 1024


def dot_nn(left, right, kind=F32):
    return jnp.dot(left, right, preferred_element_type=F32).astype(kind)


def dot_tn(left, right, kind=F32):
    return lax.dot_general(
        left, right, (((0,), (0,)), ((), ())), preferred_element_type=F32
    ).astype(kind)


def dot_nt(left, right, kind=F32):
    return lax.dot_general(
        left, right, (((1,), (1,)), ((), ())), preferred_element_type=F32
    ).astype(kind)


def block_index():
    return lax.axis_index("chip") * 2 + lax.axis_index("core")


def block_count():
    return lax.axis_size("chip") * 2


def swap(array, mask):
    if mask == 1:
        return lax.ppermute(array, "core", [(0, 1), (1, 0)])
    count = lax.axis_size("chip")
    return lax.ppermute(array, "chip", [(b, b ^ (mask // 2)) for b in range(count)])


def shift(array, step):
    count = lax.axis_size("uly")
    return lax.ppermute(array, "uly", [(z, (z + step) % count) for z in range(count)])


def is_cube():
    return lax.axis_size("chip") == 4 and lax.axis_size("uly") == 4


def masks():
    return [2 * k + j for j in range(2) for k in range(4)]


def plane_gather(first, second):
    first_x = swap(first, 2)
    second_y = swap(second, 4)
    first_y, first_xy = swap(first, 4), swap(first_x, 4)
    second_x, second_xy = swap(second, 2), swap(second_y, 2)
    return [first, first_x, first_y, first_xy], [second, second_x, second_y, second_xy]


def exchange(pieces):
    if not is_cube():
        return [lax.all_gather(p, BLK) for p in pieces]
    half = len(pieces) // 2
    a, b = plane_gather(jnp.stack(pieces[:half]), jnp.stack(pieces[half:]))
    got = []
    for four in (a, b):
        full = jnp.stack(four + [swap(p, 1) for p in four])
        got += [full[:, i] for i in range(full.shape[1])]
    return got


def spread(rows):
    return lax.all_gather(rows, "uly", axis=1, tiled=True)


def collect(partial):
    return lax.psum_scatter(partial.astype(BF), "uly", scatter_dimension=1, tiled=True).astype(F32)


def core_cut(array, dim):
    core = lax.axis_index("core")
    half = array.shape[dim] // 2
    own = lax.dynamic_slice_in_dim(array, core * half, half, dim)
    other = lax.dynamic_slice_in_dim(array, (1 - core) * half, half, dim)
    return own, other


def core_join(own, other, dim):
    first = lax.axis_index("core") == 0
    return jnp.concatenate([jnp.where(first, own, other), jnp.where(first, other, own)], axis=dim)


def feed_weights(up_shard, down_shard):
    own, other = core_cut(up_shard, 1)
    up = core_join(own, swap(other, 1), 0)
    own, other = core_cut(down_shard, 0)
    down = core_join(own, swap(other, 1), 1)
    pair = lax.all_gather(jnp.stack([up, down.T]), ("chip", "uly"), axis=0, tiled=False)
    chips, count = lax.axis_size("chip"), lax.axis_size("uly")
    rows, hidden = up.shape
    pair = pair.reshape(chips, count, 2, rows, hidden)
    return pair


def feed_reduce(up_grad, down_grad):
    pair = jnp.stack([up_grad, down_grad], axis=2)
    chips, count = pair.shape[:2]
    pair = pair.reshape(chips * count * 2, *pair.shape[3:])
    total = lax.psum_scatter(pair, ("chip", "uly"), scatter_dimension=0, tiled=True)
    half = total.shape[1] // 2
    own, other = core_cut(total, 1)
    both_halves = core_join(own, swap(other, 1), 2).astype(F32)
    return both_halves[0], both_halves[1].T


def normed(values):
    center = values - jnp.mean(values, axis=-1, keepdims=True)
    scale = lax.rsqrt(jnp.mean(center * center, axis=-1, keepdims=True) + EPSILON)
    return center * scale, scale


def norm_back(grad, hat, scale):
    return scale * (
        grad
        - jnp.mean(grad, axis=-1, keepdims=True)
        - hat * jnp.mean(grad * hat, axis=-1, keepdims=True)
    )


GELU_A = 0.7978845608028654
GELU_B = 0.044715


def gelu_pair(u):
    square = u * u
    tanh = jnp.tanh(GELU_A * u * (1.0 + GELU_B * square))
    slope = 0.5 * (1.0 + tanh) + 0.5 * u * (1.0 - tanh * tanh) * GELU_A * (
        1.0 + 3.0 * GELU_B * square
    )
    return 0.5 * u * (1.0 + tanh), slope


def segment_ids(positions, lengths_row):
    count = lengths_row.shape[0]
    before = jnp.arange(count)[None, :] < jnp.arange(count)[:, None]
    bounds = jnp.sum(jnp.where(before, lengths_row[None, :], 0), axis=1)
    return jnp.sum((bounds[None, :] <= positions[:, None]).astype(jnp.int32), axis=1)


def decay_parts(rates, lengths_row, length):
    me = block_index()
    count = block_count()
    places = jnp.arange(length, dtype=jnp.int32)
    seg = segment_ids(me * length + places, lengths_row)
    ends = segment_ids((jnp.arange(count, dtype=jnp.int32) + 1) * length - 1, lengths_row)
    seg_prev = segment_ids(jnp.reshape(me * length - 1, (1,)), lengths_row)[0]
    offset = places[:, None] - places[None, :]
    causal = (offset >= 0) & (seg[:, None] == seg[None, :])
    far = jnp.maximum(offset, 0).astype(F32)
    inner = jnp.where(causal[None], jnp.exp(-rates[:, None, None] * far[None]), 0.0)
    at = places.astype(F32)
    entry = jnp.where(seg == seg_prev, jnp.exp(-rates[:, None] * (at + 1.0)), 0.0)
    leave = jnp.where(seg == seg[length - 1], jnp.exp(-rates[:, None] * (length - 1.0 - at)), 0.0)
    if is_cube():
        source = me ^ jnp.asarray(masks(), jnp.int32)
    else:
        source = jnp.arange(count, dtype=jnp.int32)
    end_of = ends[source]
    end_before = jnp.where(source > 0, ends[jnp.maximum(source - 1, 0)], 0)
    past = jnp.maximum(me - 1 - source, 0).astype(F32)
    ahead = jnp.maximum(source - 1 - me, 0).astype(F32)
    from_past = jnp.where(
        (source < me) & (end_of == seg_prev), jnp.exp(-rates[:, None] * (length * past)), 0.0
    )
    from_ahead = jnp.where(
        (source > me) & (end_before == ends[me]), jnp.exp(-rates[:, None] * (length * ahead)), 0.0
    )
    return inner, entry[:, :, None], leave[:, :, None], from_past, from_ahead


def state_sum(weights, states):
    return jnp.einsum("hb,bhde->hde", weights, states.astype(F32))


def retention_state(heads, leave):
    return jnp.stack(
        [
            dot_tn((k.astype(F32) * leave[h]).astype(BF), v, BF)
            for h, (q, k, v) in enumerate(heads)
        ]
    )


def retention(heads, parts, state):
    inner, entry = parts[0], parts[1]
    out = []
    for h, (q, k, v) in enumerate(heads):
        scores = (dot_nt(q, k) * inner[h]).astype(BF)
        out.append(dot_nn(scores, v) + entry[h] * dot_nn(q, state[h].astype(BF)))
    return out


def mix(gate, retained):
    out = []
    for h, r in enumerate(retained):
        g = gate[:, h * r.shape[1] : (h + 1) * r.shape[1]]
        out.append((g * jax.nn.sigmoid(g) * normed(r)[0]).astype(BF))
    return jnp.concatenate(out, axis=1)


def mix_back(gate, retained, grad_mixed):
    grad_gate, grad_retained = [], []
    for h, r in enumerate(retained):
        cols = slice(h * r.shape[1], (h + 1) * r.shape[1])
        g, gm = gate[:, cols], grad_mixed[:, cols]
        sigma = jax.nn.sigmoid(g)
        hat, scale = normed(r)
        grad_gate.append((gm * hat * (sigma + g * sigma * (1.0 - sigma))).astype(BF))
        grad_retained.append(norm_back(gm * g * sigma, hat, scale).astype(BF))
    return jnp.concatenate(grad_gate, axis=1), grad_retained


def retention_back(heads, parts, state, grad_retained, grad_state):
    inner, entry, leave = parts[0], parts[1], parts[2]
    grads = []
    for h, (q, k, v) in enumerate(heads):
        gr = grad_retained[h]
        scores = (dot_nt(q, k) * inner[h]).astype(BF)
        pulls = (dot_nt(gr, v) * inner[h]).astype(BF)
        gs, st = grad_state[h].astype(BF), state[h].astype(BF)
        gq = dot_nn(pulls, k) + entry[h] * dot_nt(gr, st)
        gk = dot_tn(pulls, q) + leave[h] * dot_nt(v, gs)
        gv = dot_tn(scores, gr) + leave[h] * dot_nn(k, gs)
        grads.append((gq.astype(BF), gk.astype(BF), gv.astype(BF)))
    return grads


def vmem():
    return pl.BlockSpec(memory_space=pltpu.VMEM)


def anywhere():
    return pl.BlockSpec(memory_space=pl.ANY)


def greet(plane=False, line=False, cores=False, pair=False, across=False, whole=False, every=False):
    barrier = pltpu.get_barrier_semaphore()
    chip, core, z = (lax.axis_index(a) for a in AXES)
    others = []
    if plane:
        others += [{"chip": chip ^ 1}, {"chip": chip ^ 2}]
    if cores:
        others.append({"core": 1 - core})
    if pair:
        others.append({"uly": z ^ 1})
    if across:
        others.append({"uly": z ^ 2})
    if whole:
        others += [{"uly": z ^ k} for k in range(1, 4)]
    if every:
        others += [{"chip": chip ^ (p % 4), "core": core ^ (p // 4)} for p in range(1, 8)]
    for to in others:
        pl.semaphore_signal(barrier, inc=1, device_id=to, device_id_type=MESH)
    count = len(others)
    if line:
        last = lax.axis_size("uly") - 1

        @pl.when(z > 0)
        def _():
            pl.semaphore_signal(barrier, inc=1, device_id={"uly": z - 1}, device_id_type=MESH)

        @pl.when(z < last)
        def _():
            pl.semaphore_signal(barrier, inc=1, device_id={"uly": z + 1}, device_id_type=MESH)

        count = count + jnp.where(z > 0, 1, 0) + jnp.where(z < last, 1, 0)
    pl.semaphore_wait(barrier, count)


class PlaneGather:
    def __init__(self, own, at, x_first, send, recv, cores=True):
        chip, core = lax.axis_index("chip"), lax.axis_index("core")
        x, y, other = {"chip": chip ^ 1}, {"chip": chip ^ 2}, {"core": 1 - core}

        def copy(i, src, place, to):
            return pltpu.make_async_remote_copy(
                src_ref=src,
                dst_ref=at(place),
                send_sem=send.at[i],
                recv_sem=recv.at[i],
                device_id=to,
                device_id_type=MESH,
            )

        self.x_first = x_first
        self.copies = [
            copy(0, own, 1, x),
            copy(1, own, 2, y),
            copy(2, at(1), 3, y) if x_first else copy(2, at(2), 3, x),
        ]
        self.cores = cores
        if cores:
            self.copies += [
                copy(3, own, 4, other),
                copy(4, at(1), 5, other),
                copy(5, at(2), 6, other),
                copy(6, at(3), 7, other),
            ]

    def start(self):
        for i in (0, 1) if self.x_first else (1, 0):
            self.copies[i].start()
        if self.cores:
            self.copies[3].start()

    def near(self):
        first = 0 if self.x_first else 1
        self.copies[first].wait_recv()
        self.copies[2].start()
        if self.cores:
            self.copies[4 + first].start()

    def far(self):
        second = 1 if self.x_first else 0
        self.copies[second].wait_recv()
        if self.cores:
            self.copies[4 + second].start()

    def corner(self):
        self.copies[2].wait_recv()
        if self.cores:
            self.copies[6].start()

    def finish(self):
        for c in self.copies[3:]:
            c.wait_recv()
        for c in self.copies:
            c.wait_send()


class LineGather:
    def __init__(self, slots, send, recv):
        self.z = lax.axis_index("uly")
        self.last = lax.axis_size("uly") - 1
        self.slots, self.send, self.recv = slots, send, recv

    def copy(self, right, d):
        z, last = self.z, self.last
        at = jnp.maximum(z - d, 0) if right else jnp.minimum(z + d, last)
        to = jnp.minimum(z + 1, last) if right else jnp.maximum(z - 1, 0)
        way = 0 if right else 1
        return pltpu.make_async_remote_copy(
            src_ref=self.slots.at[at],
            dst_ref=self.slots.at[at],
            send_sem=self.send.at[way, d],
            recv_sem=self.recv.at[way, d],
            device_id={"uly": to},
            device_id_type=MESH,
        )

    def pass_on(self, d):
        z, last = self.z, self.last

        @pl.when((z - d >= 0) & (z < last))
        def _():
            self.copy(True, d).start()

        @pl.when((z + d <= last) & (z > 0))
        def _():
            self.copy(False, d).start()

    def take(self, d, then):
        z, last = self.z, self.last

        @pl.when(z - d >= 0)
        def _():
            self.copy(True, d - 1).wait_recv()

        @pl.when(z + d <= last)
        def _():
            self.copy(False, d - 1).wait_recv()

        if d < last:
            self.pass_on(d)
        self.each(d, then)

    def each(self, d, then):
        z, last = self.z, self.last

        @pl.when(z - d >= 0)
        def _():
            then(jnp.maximum(z - d, 0))

        @pl.when(z + d <= last)
        def _():
            then(jnp.minimum(z + d, last))

    def finish(self):
        z, last = self.z, self.last
        for d in range(last):

            @pl.when((z - d >= 0) & (z < last))
            def _():
                self.copy(True, d).wait_send()

            @pl.when((z + d <= last) & (z > 0))
            def _():
                self.copy(False, d).wait_send()


class LineReduce:
    def __init__(self, make, out, held, came, send, recv):
        self.z = lax.axis_index("uly")
        self.last = lax.axis_size("uly") - 1
        self.make, self.out, self.held, self.came = make, out, held, came
        self.send, self.recv = send, recv

    def copy(self, right, d):
        z, last = self.z, self.last
        way = 0 if right else 1
        to = jnp.minimum(z + 1, last) if right else jnp.maximum(z - 1, 0)
        return pltpu.make_async_remote_copy(
            src_ref=self.held.at[self.place(right, d)],
            dst_ref=self.came.at[way, d - 1],
            send_sem=self.send.at[way, d - 1],
            recv_sem=self.recv.at[way, d - 1],
            device_id={"uly": to},
            device_id_type=MESH,
        )

    def place(self, right, d):
        return d - 1 if right else self.last - d

    def step(self, d):
        z, last = self.z, self.last
        for right in (True, False):
            way = 0 if right else 1
            held = self.held.at[self.place(right, d)]
            valid = (z + d <= last) if right else (z - d >= 0)
            more = (z > 0) if right else (z < last)
            to = jnp.minimum(z + d, last) if right else jnp.maximum(z - d, 0)

            @pl.when(valid)
            def _():
                self.make(to, held)

                if d < last:

                    @pl.when(more)
                    def _():
                        self.copy(right, d + 1).wait_recv()
                        held[...] = (held[...].astype(F32) + self.came[way, d].astype(F32)).astype(
                            BF
                        )

                self.copy(right, d).start()

    def own(self):
        self.make(self.z, self.out)

    def close(self):
        z, last = self.z, self.last

        @pl.when(z > 0)
        def _():
            self.copy(True, 1).wait_recv()
            self.out[...] += self.came[0, 0].astype(F32)

        @pl.when(z < last)
        def _():
            self.copy(False, 1).wait_recv()
            self.out[...] += self.came[1, 0].astype(F32)

        for d in range(1, last + 1):

            @pl.when(z + d <= last)
            def _():
                self.copy(True, d).wait_send()

            @pl.when(z - d >= 0)
            def _():
                self.copy(False, d).wait_send()


def chunk_of(place, width):
    chip, core = lax.axis_index("chip"), lax.axis_index("core")
    block = (chip ^ (place % 4)) * 2 + (core ^ (place // 4))
    return pl.ds(pl.multiple_of(block * width, width), width)


def chip_chunk(k, width):
    return pl.ds(pl.multiple_of((lax.axis_index("chip") ^ k) * width, width), width)


def chip_order(place, width):
    core = lax.axis_index("core")
    return pl.ds(pl.multiple_of((place % 4) * (2 * width) + (core ^ (place // 4)) * width, width), width)


def front_kernel(
    io,
    rates_ref,
    lengths_ref,
    tok_ref,
    dout_ref,
    gain_ref,
    q_hbm,
    k_hbm,
    v_hbm,
    g_hbm,
    out_hbm,
    up_hbm,
    down_hbm,
    one_ref,
    first_ref,
    high_ref,
    gate_ref,
    w_first_hbm,
    w_second_hbm,
    w_out_hbm,
    gains_ref,
    up_own_hbm,
    down_own_hbm,
    mixed_ref,
    kept_ref,
    state_ref,
    douts_ref,
    slots,
    wa,
    wb,
    gains,
    psend,
    precv,
    zsend,
    zrecv,
    fsend,
    frecv,
    dsend,
    drecv,
    lsem,
    stage_out,
    stage_up,
    stage_down,
    *state_refs,
):
    core, z = lax.axis_index("core"), lax.axis_index("uly")
    rows = tok_ref.shape[0] // 2
    width = tok_ref.shape[1]
    piece = width // 8
    qk, high = q_hbm.shape[1], high_ref.shape[2]
    gains[0] = jnp.zeros_like(gains[0])
    gains[0, 0:2, :] = gain_ref[...]
    line = LineGather(slots, zsend, zrecv)
    slots[z] = tok_ref[...]
    greet(every=True, line=True, across=True)
    chip = lax.axis_index("chip")
    small = [
        pltpu.make_async_remote_copy(
            src_ref=gains.at[0],
            dst_ref=gains.at[p],
            send_sem=psend.at[0, p - 1],
            recv_sem=precv.at[0, p - 1],
            device_id={"chip": chip ^ (p % 4), "core": core ^ (p // 4)},
            device_id_type=MESH,
        )
        for p in range(1, 8)
    ]
    for c in small:
        c.start()
    line.pass_on(0)
    own = pl.ds(0, piece)
    local = [
        pltpu.make_async_copy(src, dst, lsem.at[i])
        for i, (src, dst) in enumerate(
            (
                (q_hbm, wa.at[own, pl.ds(0, qk)]),
                (k_hbm, wa.at[own, pl.ds(qk, qk)]),
                (v_hbm.at[:, pl.ds(0, high)], wa.at[own, pl.ds(2 * qk, high)]),
                (v_hbm.at[:, pl.ds(high, high)], wb.at[own, pl.ds(0, high)]),
                (g_hbm, wb.at[own, pl.ds(high, g_hbm.shape[1])]),
                (out_hbm, stage_out),
            )
        )
    ]
    for c in local:
        c.start()
    items = [None]
    for i, w in enumerate((wa, wb)):
        items.append(
            PlaneGather(
                w.at[own],
                lambda p, w=w: w.at[pl.ds(p * piece, piece)],
                i == 0,
                psend.at[1 + i],
                precv.at[1 + i],
            )
        )
    half = out_hbm.shape[0] // 2
    for i in range(2):
        part = pl.ds(i * half, half)
        items.append(
            PlaneGather(
                out_hbm.at[part],
                lambda p, part=part: w_out_hbm.at[part, pl.ds(p * piece, piece)],
                i == 0,
                psend.at[3 + i],
                precv.at[3 + i],
            )
        )
    units, cols = up_hbm.shape[1] // 2, down_hbm.shape[1]
    first_half = pl.ds(0, units)
    mine, theirs = (pl.ds(pl.multiple_of(c * units, units), units) for c in (core, 1 - core))
    here = pl.ds(pl.multiple_of(core * cols, cols), cols)

    def remote(i, src, dst, to):
        return pltpu.make_async_remote_copy(
            src_ref=src,
            dst_ref=dst,
            send_sem=fsend.at[i],
            recv_sem=frecv.at[i],
            device_id=to,
            device_id_type=MESH,
        )

    stage = [
        local[5],
        pltpu.make_async_copy(up_hbm.at[:, mine], stage_up, lsem.at[6]),
        pltpu.make_async_copy(down_hbm.at[mine], stage_down, lsem.at[7]),
    ]
    cut = [
        pltpu.make_async_copy(stage_out, w_out_hbm.at[:, own], lsem.at[10]),
        pltpu.make_async_copy(stage_up, up_own_hbm.at[here, first_half], lsem.at[11]),
        pltpu.make_async_copy(stage_down, down_own_hbm.at[first_half, here], lsem.at[12]),
    ]
    give = [
        remote(0, up_hbm.at[:, theirs], up_own_hbm.at[here, first_half], {"core": 1 - core}),
        remote(1, down_hbm.at[theirs], down_own_hbm.at[first_half, here], {"core": 1 - core}),
    ]
    first_wide, second_wide = up_own_hbm.at[:, first_half], up_own_hbm.at[:, pl.ds(units, units)]
    first_tall, second_tall = down_own_hbm.at[first_half], down_own_hbm.at[pl.ds(units, units)]
    away = [
        remote(2, first_wide, second_wide, {"uly": z ^ 2}),
        remote(3, first_tall, second_tall, {"uly": z ^ 2}),
    ]
    own_rows = 2 * rows

    def rows_to(i, src, dst, to):
        return pltpu.make_async_remote_copy(
            src_ref=douts_ref.at[pl.ds(src * own_rows, own_rows)],
            dst_ref=douts_ref.at[pl.ds(dst * own_rows, own_rows)],
            send_sem=dsend.at[i],
            recv_sem=drecv.at[i],
            device_id=to,
            device_id_type=MESH,
        )

    send_rows = [
        rows_to(0, 0, 2, {"uly": z ^ 1}),
        rows_to(1, 0, 1, {"core": 1 - core}),
        rows_to(2, 2, 3, {"core": 1 - core}),
    ]
    for c in stage[1:]:
        c.start()
    for c in local[:5]:
        c.wait()
    for item in items[1:3]:
        item.start()
    for c in give:
        c.start()
    for c in small:
        c.wait()
    gains_ref[...] = jnp.zeros_like(gains_ref)
    for p in range(8):
        gains_ref[0:1, chunk_of(p, piece)] = gains[p, 0:1, :]
        gains_ref[1:2, chip_order(p, piece)] = gains[p, 1:2, :]

    def normalize(slot):
        step = 32
        for m in range(2):

            @pl.loop(0, rows // step)
            def _(i):
                at = pl.multiple_of(i * step, step)
                v = slots[slot, pl.ds(m * rows + at, step), :].astype(F32)
                mean = jnp.mean(v, axis=-1, keepdims=True)
                center = v - mean
                scale = lax.rsqrt(jnp.mean(center * center, axis=-1, keepdims=True) + EPSILON)
                to = pl.ds(pl.multiple_of(slot * rows + at, step), step)
                for p in range(8):
                    src = slots[slot, pl.ds(m * rows + at, step), chunk_of(p, piece)].astype(F32)
                    one_ref[m, to, pl.ds(p * piece, piece)] = (
                        (src - mean) * scale * gains[p, 0:1, :]
                    ).astype(BF)

    for c in stage:
        c.wait()
    for c in cut:
        c.start()
    for k in range(4):
        douts_ref[0:own_rows, k * 2 * piece : (k + 1) * 2 * piece] = dout_ref[
            :, chip_chunk(k, 2 * piece)
        ]
    at_end = (z == 0) | (z == line.last)
    inside = (z > 0) & (z < line.last)
    normalize(z)
    line.take(1, normalize)

    @pl.when(at_end)
    def _():
        send_rows[0].start()

    for item in items[1:3]:
        item.near()
    for item in items[1:3]:
        item.far()
    for item in items[3:]:
        item.start()
    line.take(2, normalize)
    for c in cut:
        c.wait()
    for c in give:
        c.wait()

    @pl.when(at_end)
    def _():
        for c in away:
            c.start()

    @pl.when(inside)
    def _():
        send_rows[0].start()

    for item in items[1:3]:
        item.corner()
    for item in items[1:3]:
        item.finish()
    outs = [
        pltpu.make_async_copy(wa, w_first_hbm, lsem.at[8]),
        pltpu.make_async_copy(wb, w_second_hbm, lsem.at[9]),
    ]
    for c in outs:
        c.start()
    tile = 512

    def multiply(slot):
        at = pl.ds(pl.multiple_of(slot * rows, rows), rows)
        x = jnp.concatenate([one_ref[0, at, :], one_ref[1, at, :]], axis=0)

        def tiles(w, start, to_ref):
            @pl.loop(0, to_ref.shape[2] // tile)
            def _(n):
                cols = pl.ds(pl.multiple_of(n * tile, tile), tile)
                from_ = pl.ds(pl.multiple_of(start + n * tile, tile), tile)
                r = jnp.dot(x, w[:, from_], preferred_element_type=F32).astype(to_ref.dtype)
                for m in range(2):
                    to_ref[m, at, cols] = r[m * rows : (m + 1) * rows]

        tiles(wa, 0, first_ref)
        tiles(wb, 0, high_ref)
        tiles(wb, high, gate_ref)

    multiply(z)
    line.each(1, multiply)
    for item in items[3:]:
        item.near()
    for item in items[3:]:
        item.far()
    line.each(2, multiply)

    def both_steps(slot):
        normalize(slot)
        multiply(slot)

    line.take(3, both_steps)

    @pl.when(inside)
    def _():
        for c in away:
            c.wait_recv()
        for c in away:
            c.start()

    io.done("one", "first", "high", "gate")
    for item in items[3:]:
        item.corner()
    for item in items[3:]:
        item.finish()
    line.finish()
    retain_part(
        io,
        rates_ref,
        lengths_ref,
        first_ref,
        high_ref,
        gate_ref,
        mixed_ref,
        kept_ref,
        state_ref,
        douts_ref,
        send_rows,
        *state_refs,
    )
    for c in outs:
        c.wait()

    @pl.when(at_end)
    def _():
        for c in away:
            c.wait_recv()

    for c in away:
        c.wait_send()


def add_rows_kernel(
    io,
    x_ref,
    w_ref,
    tok_ref,
    up_hbm,
    down_hbm,
    out_ref,
    ups_hbm,
    downs_hbm,
    held,
    came,
    send,
    recv,
    psend,
    precv,
    lsem,
    stage_up,
    stage_down,
):
    rows = out_ref.shape[0] // 2
    width = out_ref.shape[1] // 8
    greet(plane=True, line=True)
    part = up_hbm.shape[0]

    def up_at(p):
        return ups_hbm.at[pl.ds(p * part, part)]

    def down_at(p):
        return downs_hbm.at[:, pl.ds(p * part, part)]

    items = [
        PlaneGather(up_hbm, up_at, True, psend.at[0], precv.at[0], False),
        PlaneGather(down_hbm, down_at, False, psend.at[1], precv.at[1], False),
    ]
    stage = [
        pltpu.make_async_copy(up_hbm, stage_up, lsem.at[2]),
        pltpu.make_async_copy(down_hbm, stage_down, lsem.at[3]),
    ]
    local = [
        pltpu.make_async_copy(stage_up, up_at(0), lsem.at[0]),
        pltpu.make_async_copy(stage_down, down_at(0), lsem.at[1]),
    ]

    def make(a, to):
        at = pl.ds(pl.multiple_of(a * rows, rows), rows)
        x = jnp.concatenate([x_ref[0, at, :], x_ref[1, at, :]], axis=0)

        @pl.loop(0, 8)
        def _(p):
            cols = w_ref[:, pl.ds(pl.multiple_of(p * width, width), width)]
            to[:, chip_order(p, width)] = jnp.dot(x, cols, preferred_element_type=F32).astype(
                to.dtype
            )

    line = LineReduce(make, out_ref, held, came, send, recv)
    for item in items:
        item.start()
    io.ready("x", "w")
    line.step(3)
    io.start(1)
    for c in stage:
        c.start()
    line.step(2)
    for c in stage:
        c.wait()
    for c in local:
        c.start()
    for item in items:
        item.near()
    for item in items:
        item.far()
    line.step(1)
    line.own()
    line.close()
    io.ready("tokens")
    for k in range(4):
        cols = pl.ds(k * 2 * width, 2 * width)
        out_ref[:, cols] += tok_ref[:, chip_chunk(k, 2 * width)].astype(F32)
    for item in items:
        item.corner()
    for item in items:
        item.finish()
    for c in local:
        c.wait()


def fan_out_kernel(
    io,
    rows_ref,
    w_ref,
    mixed_ref,
    up_hbm,
    down_hbm,
    grad_ref,
    part_ref,
    up_ref,
    down_ref,
    slots,
    ordered,
    total,
    near_up,
    near_down,
    came_up,
    came_down,
    send,
    recv,
    psend,
    precv,
    lsem,
):
    z = lax.axis_index("uly")
    rows = rows_ref.shape[0] // 2
    width = rows_ref.shape[1] // 8
    greet(plane=True, line=True)
    line = LineGather(slots, send, recv)
    slots[z] = rows_ref[...]
    line.pass_on(0)
    local = [
        pltpu.make_async_copy(up_hbm, near_up, lsem.at[0]),
        pltpu.make_async_copy(down_hbm, near_down, lsem.at[1]),
    ]
    for c in local:
        c.start()
    groups = [
        PlaneReduce(None, near_up, came_up, True, psend.at[0], precv.at[0]),
        PlaneReduce(None, near_down, came_down, False, psend.at[1], precv.at[1]),
    ]
    for c in local:
        c.wait()
    for g in groups:
        g.start_first()

    def multiply(slot):
        at = pl.ds(pl.multiple_of(slot * rows, rows), rows)
        for p in range(8):
            ordered[:, p * width : (p + 1) * width] = slots[slot, :, chip_order(p, width)]
        tile = 256

        @pl.loop(0, w_ref.shape[0] // tile)
        def _(n):
            part = pl.ds(pl.multiple_of(n * tile, tile), tile)
            product = dot_nt(ordered[...], w_ref[part, :])
            for m in range(2):
                grad_ref[m, at, part] = product[m * rows : (m + 1) * rows]

        mixed = jnp.concatenate([mixed_ref[0, at, :], mixed_ref[1, at, :]], axis=0)

        @pl.loop(0, 8)
        def _(p):
            cols = pl.ds(pl.multiple_of(p * width, width), width)
            total[p] += dot_tn(ordered[:, cols], mixed)

    total[...] = jnp.zeros_like(total)
    io.ready("w", "mixed")
    multiply(z)
    line.take(1, multiply)
    for g in groups:
        g.first_sums(0)
    line.take(2, multiply)
    for g in groups:
        g.first_sums(1)
    line.take(3, multiply)
    io.done("grad")
    half = part_ref.shape[3]
    for i in range(2):
        part_ref[i] = total[:, :, i * half : (i + 1) * half].astype(BF)
    io.done("part")
    groups[0].finish(up_ref)
    groups[1].finish(down_ref)
    line.finish()


def feed_kernel(
    io,
    hid_ref,
    douts_ref,
    gain_ref,
    ups_ref,
    downs_ref,
    keep_ref,
    give_ref,
    grad_ref,
    rows_ref,
    gain_grad_ref,
    up_grad_ref,
    down_grad_ref,
    two,
    act,
    gu,
    sums,
    held,
    came,
    send,
    recv,
):
    core, z = lax.axis_index("core"), lax.axis_index("uly")
    rows, width = hid_ref.shape
    hidden = ups_ref.shape[1]
    other, pair = {"core": 1 - core}, {"uly": z ^ 1}
    greet(cores=True, pair=True)

    half = rows // 2

    def group(g, part=None):
        return pl.ds(g * rows, rows) if part is None else pl.ds(g * rows + part * half, half)

    def copy(i, src, dst, to):
        return pltpu.make_async_remote_copy(
            src_ref=src,
            dst_ref=dst,
            send_sem=send.at[i],
            recv_sem=recv.at[i],
            device_id=to,
            device_id_type=MESH,
        )

    parts = [pl.ds(part * half, half) for part in range(2)]
    to_pair = [copy(p, two.at[group(0, p)], two.at[group(2, p)], pair) for p in range(2)]
    through = [copy(2 + p, two.at[group(2, p)], two.at[group(3, p)], other) for p in range(2)]
    to_other = copy(4, two.at[group(0)], two.at[group(1)], other)
    step = 32
    io.ready("hid")
    io.start(1)
    for part in range(2):

        @pl.loop(0, half // step)
        def _(i):
            at = pl.ds(pl.multiple_of(part * half + i * step, step), step)
            hat, _scale = normed(hid_ref[at, :])
            two[at, :] = (hat * gain_ref[1:2, :]).astype(BF)

        to_pair[part].start()
    to_other.start()

    def work(g, part=None):
        at = group(g, part)
        to = slice(None) if part is None else parts[part]
        tile = 256

        @pl.loop(0, hidden // tile)
        def _(n):
            cols = pl.ds(pl.multiple_of(n * tile, tile), tile)
            upward = jnp.dot(two[at, :], ups_ref[:, cols], preferred_element_type=F32)
            value, slope = gelu_pair(upward)
            act[at, cols] = value.astype(BF)
            pulled = dot_nt(douts_ref[at, :], downs_ref[cols, :])
            gu[at, cols] = (pulled * slope).astype(BF)

        tile = 512

        @pl.loop(0, width // tile)
        def _(n):
            cols = pl.ds(pl.multiple_of(n * tile, tile), tile)
            back = dot_nt(gu[at, :], ups_ref[cols, :])
            down = jnp.dot(act[at, :], downs_ref[:, cols], preferred_element_type=F32)
            if g == 0:
                sums[0, :, cols] = back
                sums[1, :, cols] = down
            else:
                held[g - 1, 0, to, cols] = back.astype(BF)
                held[g - 1, 1, to, cols] = down.astype(BF)

    own_back = [copy(5 + i, held.at[0, i], came.at[3 * i], other) for i in range(2)]
    pair_back = [
        [
            copy(7 + 2 * p + i, held.at[2, i, parts[p]], came.at[1 + 3 * i, parts[p]], other)
            for i in range(2)
        ]
        for p in range(2)
    ]
    last = [copy(11 + p, held.at[1, 0, parts[p]], came.at[2, parts[p]], pair) for p in range(2)]

    io.ready("ups", "downs", "douts")
    work(0)
    to_other.wait_recv()
    work(1)
    for c in own_back:
        c.start()
    for p in range(2):
        to_pair[p].wait_recv()
        through[p].start()
        work(2, p)
        through[p].wait_recv()
        work(3, p)
        for c in pair_back[p]:
            c.start()
        for i in range(2):
            pair_back[p][i].wait_recv()

            @pl.loop(0, half // step)
            def _(r):
                at = pl.ds(pl.multiple_of(p * half + r * step, step), step)
                held[1, i, at, :] = (
                    held[1, i, at, :].astype(F32) + came[1 + 3 * i, at, :].astype(F32)
                ).astype(BF)

            if i == 0:
                last[p].start()
    give_ref[...] = held[1, 1]
    io.done("give")
    tile = 512

    @pl.loop(0, width // tile)
    def _(n):
        cols = pl.ds(pl.multiple_of(n * tile, tile), tile)
        up_grad_ref[n] = dot_tn(two[:, cols], gu[...], BF)
        down_grad_ref[n] = dot_tn(act[...], douts_ref[:, cols], BF)

    io.done("up", "down")
    for c in own_back + last:
        c.wait_recv()
    gain_grad_ref[...] = jnp.zeros_like(gain_grad_ref)

    @pl.loop(0, rows // step)
    def _(r):
        at = pl.ds(pl.multiple_of(r * step, step), step)
        back = sums[0, at, :] + came[0, at, :].astype(F32) + came[2, at, :].astype(F32)
        hat, scale = normed(hid_ref[at, :])
        gain_grad_ref[...] += jnp.sum(back * hat, axis=0, keepdims=True)
        grad = douts_ref[at, :].astype(F32) + norm_back(back * gain_ref[1:2, :], hat, scale)
        grad_ref[at, :] = grad
        rows_ref[at, :] = grad.astype(BF)
        keep_ref[at, :] = hid_ref[at, :] + sums[1, at, :] + came[3, at, :].astype(F32)

    for c in to_pair + through + own_back + pair_back[0] + pair_back[1] + last + [to_other]:
        c.wait_send()


class PlaneReduce:
    def __init__(self, far, near, came, x_first, send, recv):
        chip, core = lax.axis_index("chip"), lax.axis_index("core")
        x, y, other = {"chip": chip ^ 1}, {"chip": chip ^ 2}, {"core": 1 - core}
        self.near, self.came, self.x_first = near, came, x_first
        self.waited = ()

        def copy(i, src, to):
            return pltpu.make_async_remote_copy(
                src_ref=src,
                dst_ref=came.at[i],
                send_sem=send.at[i],
                recv_sem=recv.at[i],
                device_id=to,
                device_id_type=MESH,
            )

        self.away = (1, 3) if x_first else (2, 3)
        self.stay = (0, 2) if x_first else (0, 1)
        one, two = (x, y) if x_first else (y, x)
        self.cores = 4 if far else 0
        self.copies = [copy(i, far(4 + i), other) for i in range(self.cores)]
        self.copies += [copy(self.cores + i, near.at[self.away[i]], one) for i in range(2)]
        self.copies.append(copy(self.cores + 2, near.at[self.stay[1]], two))

    def start(self):
        for i in (3, self.away[0], self.stay[1], 0):
            self.copies[i].start()

    def add(self, place, i):
        step = 64

        @pl.loop(0, self.near.shape[1] // step)
        def _(r):
            at = pl.ds(pl.multiple_of(r * step, step), step)
            self.near[place, at, :] = (
                self.near[place, at, :].astype(F32) + self.came[i, at, :].astype(F32)
            ).astype(BF)

    def core_sums(self):
        for i in (1, 0):
            p = self.away[i]
            self.copies[p].wait_recv()
            self.add(p, p)
            self.copies[4 + i].start()
        for p in (self.stay[1], self.stay[0]):
            self.copies[p].wait_recv()
            self.add(p, p)

    def start_first(self):
        for i in (1, 0):
            self.copies[self.cores + i].start()

    def first_sums(self, step):
        i = 1 - step
        self.copies[self.cores + i].wait_recv()
        self.add(self.stay[i], self.cores + i)
        if i == 1:
            self.copies[self.cores + 2].start()

    def finish(self, out_ref):
        self.copies[self.cores + 2].wait_recv()
        self.add(self.stay[0], self.cores + 2)
        out_ref[...] = self.near[0]
        for i, c in enumerate(self.copies):
            if i not in self.waited:
                c.wait_send()


def far_slot(i, x_first):
    return ((3, 1, 2, 0) if x_first else (3, 2, 1, 0)).index(i) % 2


def close_rows_kernel(
    io,
    xa_ref,
    xb_ref,
    wa_ref,
    wb_ref,
    one_ref,
    tok_ref,
    hid_ref,
    gain_ref,
    gain_two_ref,
    out_ref,
    sum_a_ref,
    sum_b_ref,
    gains_ref,
    held,
    came,
    near_a,
    near_b,
    far_a,
    far_b,
    came_a,
    came_b,
    small,
    small_came,
    small_line,
    send,
    recv,
    psend,
    precv,
    ssend,
    srecv,
):
    chip, core, z = (lax.axis_index(a) for a in AXES)
    rows = out_ref.shape[0] // 2
    length = one_ref.shape[0] // 2
    width = out_ref.shape[1] // 8
    greet(every=True, whole=True)

    def make(a, to):
        at = [
            pl.ds(pl.multiple_of(m * length + a * rows, rows), rows) for m in range(2)
        ]
        xa = jnp.concatenate([xa_ref[i, :] for i in at], axis=0)
        xb = jnp.concatenate([xb_ref[i, :] for i in at], axis=0)

        @pl.loop(0, 8)
        def _(p):
            part = pl.ds(pl.multiple_of(p * width, width), width)
            r = dot_nt(xa, wa_ref[part, :]) + dot_nt(xb, wb_ref[part, :])
            to[:, chunk_of(p, width)] = r.astype(to.dtype)
            ones = jnp.concatenate([one_ref[i, part] for i in at], axis=0)
            small[p, 0:1, :] += jnp.sum(r * ones.astype(F32), axis=0, keepdims=True)

    small[...] = jnp.zeros_like(small)
    line = LineReduce(make, out_ref, held, came, send, recv)
    sets = []
    for i, (x_ref, near, far, got, x_first) in enumerate(
        (
            (xa_ref, near_a, far_a, came_a, True),
            (xb_ref, near_b, far_b, came_b, False),
        )
    ):
        group = PlaneReduce(
            lambda p, far=far, x=x_first: far.at[far_slot(p - 4, x)],
            near,
            got,
            x_first,
            psend.at[i],
            precv.at[i],
        )
        group.waited = tuple((3, group.away[0]))
        sets.append((group, x_ref, near, far, got))

    tile = 512

    def product(x_ref, place, to, more=None):
        @pl.loop(0, x_ref.shape[1] // tile)
        def _(n):
            cols = pl.ds(pl.multiple_of(n * tile, tile), tile)
            r = dot_tn(one_ref[:, place * width : (place + 1) * width], x_ref[:, cols])
            if more is not None:
                r = r + more[:, cols].astype(F32)
            to[:, cols] = r.astype(BF)

    io.ready("xa", "xb", "wa", "wb", "one")
    io.start(1)
    line.step(3)
    for n in range(4):
        for group, x_ref, near, far, got in sets:
            order = (3, group.away[0], group.stay[1], 0)
            if n >= 2:
                group.copies[order[n - 2]].wait_send()
            product(x_ref, 4 + order[n], far.at[n % 2])
            group.copies[order[n]].start()

    def add_near(n):
        for group, x_ref, near, far, got in sets:
            i = (3, group.away[0], group.stay[1], 0)[n]
            group.copies[i].wait_recv()
            product(x_ref, i, near.at[i], got.at[i])
            if n < 2:
                group.copies[4 + (1 - n)].start()

    add_near(0)
    add_near(1)
    line.step(2)
    add_near(2)
    add_near(3)
    line.step(1)
    line.own()
    for p in range(8):
        small[p, 0:1, :] = small[p, 0:1, :] / gain_ref[0:1, chunk_of(p, width)]
        small[p, 1:2, :] = gain_two_ref[:, chip_order(p, width)]

    def pass_small(i, src, dst, to):
        return pltpu.make_async_remote_copy(
            src_ref=src,
            dst_ref=dst,
            send_sem=ssend.at[i],
            recv_sem=srecv.at[i],
            device_id=to,
            device_id_type=MESH,
        )

    sent = [
        pass_small(
            p - 1,
            small.at[p],
            small_came.at[p],
            {"chip": chip ^ (p % 4), "core": core ^ (p // 4)},
        )
        for p in range(1, 8)
    ]
    for c in sent:
        c.start()
    for group, *_ in sets:
        group.first_sums(0)
    for group, *_ in sets:
        group.first_sums(1)
    total = small[0]
    for p in range(1, 8):
        sent[p - 1].wait_recv()
        total = total + small_came[p]
    small_line[0] = total
    last = [
        pass_small(6 + k, small_line.at[0], small_line.at[k], {"uly": z ^ k}) for k in range(1, 4)
    ]
    for c in last:
        c.start()
    io.ready("tokens", "hid")
    line.close()
    step = 32

    @pl.loop(0, 2 * rows // step)
    def _(r):
        at = pl.ds(pl.multiple_of(r * step, step), step)
        hat, scale = normed(tok_ref[at, :].astype(F32))
        out_ref[at, :] = norm_back(out_ref[at, :] * gain_ref[0:1, :], hat, scale)
        for k in range(4):
            out_ref[at, chip_chunk(k, 2 * width)] += hid_ref[
                at, k * 2 * width : (k + 1) * 2 * width
            ]

    for (group, *_), out in zip(sets, (sum_a_ref, sum_b_ref)):
        group.finish(out)
    for k in range(1, 4):
        last[k - 1].wait_recv()
        total = total + small_line[k]
    gains_ref[...] = total
    for c in sent + last:
        c.wait_send()


class StateExchange:
    def __init__(self, weights, own, sib, chips, mine, came, final, send, recv):
        self.core = lax.axis_index("core")
        self.weights, self.own, self.sib, self.chips = weights, own, sib, chips
        self.mine, self.came, self.final = mine, came, final

        def copy(i, src, dst):
            return pltpu.make_async_remote_copy(
                src_ref=src,
                dst_ref=dst,
                send_sem=send.at[2, i],
                recv_sem=recv.at[2, i],
                device_id={"core": 1 - self.core},
                device_id_type=MESH,
            )

        self.first = copy(0, own, sib)
        self.second = copy(1, mine, came)
        self.items = [
            PlaneGather(
                chips.at[0, h], lambda p, h=h: chips.at[p, h], h == 0, send.at[h], recv.at[h], False
            )
            for h in range(2)
        ]

    def start(self):
        self.first.start()

    def join(self):
        self.first.wait_recv()
        m = self.core
        for h in range(2):
            mine, other = self.weights.joined(m, h)
            self.chips[0, h] = (
                mine * self.own[m, h].astype(F32) + other * self.sib[m, h].astype(F32)
            ).astype(BF)
            self.items[h].start()

    def near(self):
        for item in self.items:
            item.near()

    def far(self):
        for item in self.items:
            item.far()

    def settle(self):
        for item in self.items:
            item.corner()
        m = self.core
        for h in range(2):
            total = self.weights.chip(m, h, 1) * self.chips[1, h].astype(F32)
            for k in (2, 3):
                total = total + self.weights.chip(m, h, k) * self.chips[k, h].astype(F32)
            self.mine[h] = total.astype(BF)
        self.second.start()
        self.last(m, self.mine)
        self.second.wait_recv()
        self.last(1 - m, self.came)

    def last(self, m, chip_state):
        for h in range(2):
            whole, other = self.weights.final(m, h)
            self.final[m, h] = (
                whole * chip_state[h].astype(F32) + other * self.sib[m, h].astype(F32)
            ).astype(BF)

    def finish(self):
        self.first.wait_send()
        self.second.wait_send()
        for item in self.items:
            item.finish()


def state_scratch(shape):
    half = shape[1:]
    return [
        pltpu.VMEM(shape, BF),
        pltpu.VMEM(shape, BF),
        pltpu.VMEM((4, *half), BF),
        pltpu.VMEM(half, BF),
        pltpu.VMEM(half, BF),
        sems(3, 3),
        sems(3, 3),
    ]


class Places:
    def __init__(self, lengths_ref, m, length):
        self.length = length
        self.base = (lax.axis_index("chip") * 2 + lax.axis_index("core")) * length
        self.bounds = []
        total = 0
        for n in range(lengths_ref.shape[1]):
            self.bounds.append(total)
            total = total + lengths_ref[m, n]

    def segment(self, at):
        found = jnp.zeros_like(at)
        for b in self.bounds:
            found = found + jnp.where(self.base + at >= b, 1, 0)
        return found

    def table(self, rate, start, count, across):
        shape = (count, self.length)
        rows = start + lax.broadcasted_iota(jnp.int32, shape, 0)
        cols = lax.broadcasted_iota(jnp.int32, shape, 1)
        off = cols - rows if across else rows - cols
        seg_rows = self.segment(start + lax.broadcasted_iota(jnp.int32, (count, 1), 0))
        seg_cols = self.segment(lax.broadcasted_iota(jnp.int32, (1, self.length), 1))
        far = jnp.maximum(off, 0).astype(F32)
        return jnp.where((off >= 0) & (seg_rows == seg_cols), jnp.exp(-rate * far), 0.0)

    def entry(self, rate, start, count):
        at = start + lax.broadcasted_iota(jnp.int32, (count, 1), 0)
        same = self.segment(at) == self.segment(jnp.full((1, 1), -1, jnp.int32))
        return jnp.where(same, jnp.exp(-rate * (at + 1).astype(F32)), 0.0)

    def leave(self, rate, start, count):
        at = start + lax.broadcasted_iota(jnp.int32, (count, 1), 0)
        end = jnp.full((1, 1), self.length - 1, jnp.int32)
        same = self.segment(at) == self.segment(end)
        return jnp.where(same, jnp.exp(-rate * (self.length - 1 - at).astype(F32)), 0.0)


def rate_of(rates_ref, h):
    return rates_ref[lax.axis_index("uly") * 2 + h]


class StateWeights:
    def __init__(self, rates_ref, lengths_ref, length, back):
        self.rates, self.lengths, self.length, self.back = rates_ref, lengths_ref, length, back
        self.chip_at, self.core = lax.axis_index("chip"), lax.axis_index("core")

    def end(self, m, block):
        at = jnp.full((1, 1), (block + 1) * self.length - 1, jnp.int32)
        found = jnp.zeros_like(at)
        total = 0
        for n in range(self.lengths.shape[1]):
            found = found + jnp.where(at >= total, 1, 0)
            total = total + self.lengths[m, n]
        return found

    def decay(self, h, count):
        far = jnp.full((1, 1), count * self.length, jnp.int32).astype(F32)
        return jnp.exp(-rate_of(self.rates, h) * far)

    def through(self, m, h, block):
        same = self.end(m, block) == self.end(m, block - 1)
        return jnp.where(same, self.decay(h, 1), 0.0)

    def pick(self, first, second):
        return jnp.where(jnp.full((1, 1), self.core, jnp.int32) == 0, first, second)

    def joined(self, m, h):
        one = jnp.ones((1, 1), F32)
        if self.back:
            even = self.through(m, h, 2 * self.chip_at)
            return self.pick(one, even), self.pick(even, one)
        odd = self.through(m, h, 2 * self.chip_at + 1)
        return self.pick(odd, one), self.pick(one, odd)

    def final(self, m, h):
        one, zero = jnp.ones((1, 1), F32), jnp.zeros((1, 1), F32)
        if self.back:
            return self.pick(self.through(m, h, 2 * self.chip_at + 1), one), self.pick(one, zero)
        return self.pick(one, self.through(m, h, 2 * self.chip_at)), self.pick(zero, one)

    def chip(self, m, h, k):
        here, there = self.chip_at, self.chip_at ^ k
        low, high = (here, there) if self.back else (there, here)
        before = jnp.full((1, 1), low, jnp.int32) < jnp.full((1, 1), high, jnp.int32)
        same = self.end(m, 2 * low + 1) == self.end(m, 2 * high - 1)
        return jnp.where(before & same, self.decay(h, 2 * jnp.maximum(high - 1 - low, 0)), 0.0)


ROWS = 128


def retain_part(
    io,
    rates_ref,
    lengths_ref,
    a_ref,
    high_ref,
    gate_ref,
    mixed_ref,
    kept_ref,
    state_ref,
    douts_ref,
    send_rows,
    own,
    sib,
    chips,
    mine,
    came,
    send,
    recv,
):
    _, length, vd = high_ref.shape
    qk = (a_ref.shape[2] - vd) // 2
    hd = qk // 2
    weights = StateWeights(rates_ref, lengths_ref, length, False)
    states = StateExchange(weights, own, sib, chips, mine, came, state_ref, send, recv)
    to_pair, to_other, through = send_rows

    def values(m, h):
        return high_ref[m] if h else a_ref[m, :, 2 * qk :]

    def keys(m, h):
        return a_ref[m, :, qk + h * hd : qk + (h + 1) * hd]

    for h in range(2):

        @pl.loop(0, 2)
        def _(m):
            leave = Places(lengths_ref, m, length).leave(rate_of(rates_ref, h), 0, length)
            k = (keys(m, h).astype(F32) * leave).astype(BF)
            own[m, h] = dot_tn(k, values(m, h), BF)

    states.start()
    parts = length // ROWS

    def local(h):
        @pl.loop(0, 2 * parts)
        def _(i):
            m, r = i // parts, i % parts
            at = pl.ds(pl.multiple_of(r * ROWS, ROWS), ROWS)
            table = Places(lengths_ref, m, length).table(rate_of(rates_ref, h), r * ROWS, ROWS, False)
            q = a_ref[m, at, h * hd : (h + 1) * hd]
            scores = (dot_nt(q, keys(m, h)) * table).astype(BF)
            kept_ref[m, at, h * vd : (h + 1) * vd] = jnp.dot(
                scores, values(m, h), preferred_element_type=F32
            )

    states.join()
    to_other.start()
    local(0)
    states.near()
    local(1)
    states.far()
    states.settle()
    for h in range(2):

        @pl.loop(0, 2 * parts)
        def _(i):
            m, r = i // parts, i % parts
            at = pl.ds(pl.multiple_of(r * ROWS, ROWS), ROWS)
            cols = slice(h * vd, (h + 1) * vd)
            entry = Places(lengths_ref, m, length).entry(rate_of(rates_ref, h), r * ROWS, ROWS)
            q = a_ref[m, at, h * hd : (h + 1) * hd]
            kept = kept_ref[m, at, cols] + entry * jnp.dot(
                q, state_ref[m, h], preferred_element_type=F32
            )
            kept_ref[m, at, cols] = kept
            g = gate_ref[m, at, cols]
            mixed_ref[m, at, cols] = (g * sigmoid(g) * normed(kept)[0]).astype(BF)

    states.finish()
    to_pair.wait_recv()
    through.start()
    to_other.wait_recv()
    through.wait_recv()
    io.done("douts")
    for c in send_rows:
        c.wait_send()


def sigmoid(v):
    return 0.5 * jnp.tanh(0.5 * v) + 0.5


def retain_back_kernel(
    io,
    rates_ref,
    lengths_ref,
    a_ref,
    high_ref,
    gate_ref,
    kept_ref,
    grad_ref,
    state_ref,
    part_hbm,
    keep_ref,
    give_hbm,
    up_sum_ref,
    down_sum_ref,
    xa_ref,
    xb_ref,
    sum_ref,
    out_ref,
    up_ref,
    down_ref,
    pulled,
    grad_k,
    grad_v,
    final,
    own,
    sib,
    chips,
    mine,
    came,
    send,
    recv,
    near,
    got,
    psend,
    precv,
    lsem,
    came_rows,
    rsend,
    rrecv,
    came_up,
    came_down,
    swap_up,
    swap_down,
    came_swap_up,
    came_swap_down,
    fsend,
    frecv,
):
    _, length, vd = high_ref.shape
    qk = (a_ref.shape[2] - vd) // 2
    hd = qk // 2
    greet(plane=True, cores=True, pair=True, across=True)
    core, z = lax.axis_index("core"), lax.axis_index("uly")

    def feed_copy(i, src, dst, to):
        return pltpu.make_async_remote_copy(
            src_ref=src,
            dst_ref=dst,
            send_sem=fsend.at[i],
            recv_sem=frecv.at[i],
            device_id=to,
            device_id_type=MESH,
        )

    units = came_up.shape[1]
    across = [
        feed_copy(0, up_sum_ref.at[:, pl.ds(units, units)], came_up, {"uly": z ^ 2}),
        feed_copy(1, down_sum_ref.at[pl.ds(units, units)], came_down, {"uly": z ^ 2}),
    ]
    swaps = [
        feed_copy(2, swap_up, came_swap_up, {"core": 1 - core}),
        feed_copy(3, swap_down, came_swap_down, {"core": 1 - core}),
    ]
    io.ready("up", "down")
    for c in across:
        c.start()
    give = pltpu.make_async_remote_copy(
        src_ref=give_hbm,
        dst_ref=came_rows,
        send_sem=rsend,
        recv_sem=rrecv,
        device_id={"uly": lax.axis_index("uly") ^ 1},
        device_id_type=MESH,
    )
    give.start()
    groups = [
        PlaneReduce(
            lambda p, i=i: part_hbm.at[i, p],
            near.at[i],
            got.at[i],
            i == 0,
            psend.at[i],
            precv.at[i],
        )
        for i in range(2)
    ]
    local = [
        pltpu.make_async_copy(part_hbm.at[i, pl.ds(0, 4)], near.at[i], lsem.at[i]) for i in range(2)
    ]
    for c in local:
        c.start()
    for group in groups:
        group.start()
    io.ready("gate", "kept", "grad")
    io.start(1)
    weights = StateWeights(rates_ref, lengths_ref, length, True)
    states = StateExchange(weights, own, sib, chips, mine, came, final, send, recv)
    parts = length // ROWS

    def values(m, h, at=slice(None)):
        return high_ref[m, at, :] if h else a_ref[m, at, 2 * qk :]

    def keys(m, h, at=slice(None)):
        return a_ref[m, at, qk + h * hd : qk + (h + 1) * hd]

    def queries(m, h, at=slice(None)):
        return a_ref[m, at, h * hd : (h + 1) * hd]

    for h in range(2):
        cols = slice(h * vd, (h + 1) * vd)

        @pl.loop(0, 2 * parts)
        def _(i):
            m, r = i // parts, i % parts
            at = pl.ds(pl.multiple_of(r * ROWS, ROWS), ROWS)
            g, gm = gate_ref[m, at, cols], grad_ref[m, at, cols]
            sigma = sigmoid(g)
            hat, scale = normed(kept_ref[m, at, cols])
            xb_ref[m, at, vd + h * vd : vd + (h + 1) * vd] = (
                gm * hat * (sigma + g * sigma * (1.0 - sigma))
            ).astype(BF)
            pulled[m, at, cols] = norm_back(gm * g * sigma, hat, scale).astype(BF)

        if h == 0:
            io.ready("a", "high", "state")

        @pl.loop(0, 2)
        def _(m):
            entry = Places(lengths_ref, m, length).entry(rate_of(rates_ref, h), 0, length)
            q = (queries(m, h).astype(F32) * entry).astype(BF)
            own[m, h] = dot_tn(q, pulled[m, :, cols], BF)

    states.start()

    def local_q(h):
        cols = slice(h * vd, (h + 1) * vd)

        @pl.loop(0, 2 * parts)
        def _(i):
            m, r = i // parts, i % parts
            at = pl.ds(pl.multiple_of(r * ROWS, ROWS), ROWS)
            places = Places(lengths_ref, m, length)
            table = places.table(rate_of(rates_ref, h), r * ROWS, ROWS, False)
            gr = pulled[m, at, cols]
            p = (dot_nt(gr, values(m, h)) * table).astype(BF)
            entry = places.entry(rate_of(rates_ref, h), r * ROWS, ROWS)
            xa_ref[m, at, h * hd : (h + 1) * hd] = (
                jnp.dot(p, keys(m, h), preferred_element_type=F32)
                + entry * dot_nt(gr, state_ref[m, h])
            ).astype(BF)

    def local_kv(h):
        cols = slice(h * vd, (h + 1) * vd)

        @pl.loop(0, 2 * parts)
        def _(i):
            m, r = i // parts, i % parts
            at = pl.ds(pl.multiple_of(r * ROWS, ROWS), ROWS)
            table = Places(lengths_ref, m, length).table(rate_of(rates_ref, h), r * ROWS, ROWS, True)
            p = (dot_nt(values(m, h, at), pulled[m, :, cols]) * table).astype(BF)
            scores = (dot_nt(keys(m, h, at), queries(m, h)) * table).astype(BF)
            grad_k[m, at, h * hd : (h + 1) * hd] = jnp.dot(
                p, queries(m, h), preferred_element_type=F32
            )
            grad_v[m, at, cols] = jnp.dot(
                scores, pulled[m, :, cols], preferred_element_type=F32
            )

    states.join()
    local_q(0)
    states.near()
    states.far()
    for c in local:
        c.wait()
    for group in groups:
        group.core_sums()
    local_q(1)
    states.settle()
    local_kv(0)
    for group in groups:
        group.first_sums(0)
    for group in groups:
        group.first_sums(1)
    local_kv(1)
    for h in range(2):

        @pl.loop(0, 2 * parts)
        def _(i):
            m, r = i // parts, i % parts
            at = pl.ds(pl.multiple_of(r * ROWS, ROWS), ROWS)
            leave = Places(lengths_ref, m, length).leave(rate_of(rates_ref, h), r * ROWS, ROWS)
            xa_ref[m, at, qk + h * hd : qk + (h + 1) * hd] = (
                grad_k[m, at, h * hd : (h + 1) * hd]
                + leave * dot_nt(values(m, h, at), final[m, h])
            ).astype(BF)
            gv = (
                grad_v[m, at, h * vd : (h + 1) * vd]
                + leave * jnp.dot(keys(m, h, at), final[m, h], preferred_element_type=F32)
            ).astype(BF)
            if h:
                xb_ref[m, at, :vd] = gv
            else:
                xa_ref[m, at, 2 * qk :] = gv

    states.finish()
    give.wait()
    io.ready("keep")
    quarter = keep_ref.shape[1] // 4
    for k in range(4):
        cols = slice(k * quarter, (k + 1) * quarter)
        out_ref[:, chip_chunk(k, quarter)] = (
            keep_ref[:, cols] + came_rows[:, cols].astype(F32)
        ).astype(BF)
    for i, group in enumerate(groups):
        group.finish(sum_ref.at[i])
    rows, cols = up_ref.shape[0], down_ref.shape[1]

    def mine(size, own):
        return pl.ds(pl.multiple_of((core if own else 1 - core) * size, size), size)

    for c in across:
        c.wait()
    kept_units = slice(0, units)

    def up_total(own):
        at = mine(rows, own)
        return up_sum_ref[at, kept_units].astype(F32) + came_up[at, :].astype(F32)

    def down_total(own):
        at = mine(cols, own)
        return down_sum_ref[kept_units, at].astype(F32) + came_down[:, at].astype(F32)

    swap_up[...] = up_total(False).astype(BF)
    swap_down[...] = down_total(False).astype(BF)
    for c in swaps:
        c.start()
    up_ref[:, mine(units, True)] = up_total(True)
    down_ref[mine(units, True), :] = down_total(True)
    for c in swaps:
        c.wait()
    up_ref[:, mine(units, False)] = came_swap_up[...].astype(F32)
    down_ref[mine(units, False), :] = came_swap_down[...].astype(F32)


def sems(*shape):
    return pltpu.SemaphoreType.DMA(shape)


def like(shape, kind):
    return jax.ShapeDtypeStruct(shape, kind)


class Late:
    def __init__(self, name, order=0):
        self.name, self.order = name, order


class Early:
    def __init__(self, name):
        self.name = name


class Moves:
    def __init__(self, loads, stores):
        self.loads, self.stores = loads, stores
        self.waited, self.begun = set(), set()

    def start(self, order):
        for copy, at in self.loads.values():
            if at == order:
                copy.start()

    def ready(self, *names):
        for name in names:
            self.loads[name][0].wait()
            self.waited.add(name)

    def done(self, *names):
        for name in names:
            self.stores[name].start()
            self.begun.add(name)

    def finish(self):
        self.done(*[n for n in self.stores if n not in self.begun])
        self.ready(*[n for n in self.loads if n not in self.waited])
        for copy in self.stores.values():
            copy.wait()


def call(kernel, number, ins, outs, scratch, flops, *args):
    moved = sum(a.size * a.dtype.itemsize for a in args)
    late = [i for i, spec in enumerate(ins) if isinstance(spec, Late)]
    early = [i for i, out in enumerate(outs) if isinstance(out[2], Early)]

    def whole(*refs):
        refs = list(refs)
        in_refs, refs = refs[: len(ins)], refs[len(ins) :]
        out_refs, refs = refs[: len(outs)], refs[len(outs) :]
        own, refs = refs[: len(scratch)], refs[len(scratch) :]
        load_sem, store_sem = refs[-2:]
        loads, stores = {}, {}
        for n, i in enumerate(late):
            copy = pltpu.make_async_copy(in_refs[i], refs[n], load_sem.at[n])
            loads[ins[i].name] = (copy, ins[i].order)
            in_refs[i] = refs[n]
        for n, i in enumerate(early):
            ref = refs[len(late) + n]
            stores[outs[i][2].name] = pltpu.make_async_copy(ref, out_refs[i], store_sem.at[n])
            out_refs[i] = ref
        io = Moves(loads, stores)
        io.start(0)
        kernel(io, *in_refs, *out_refs, *own)
        io.finish()

    extra = [pltpu.VMEM(args[i].shape, args[i].dtype) for i in late]
    extra += [pltpu.VMEM(outs[i][0], outs[i][1]) for i in early]
    return pl.pallas_call(
        whole,
        out_shape=[like(shape, kind) for shape, kind, _ in outs],
        in_specs=[anywhere() if i in late else spec for i, spec in enumerate(ins)],
        out_specs=[anywhere() if i in early else out[2] for i, out in enumerate(outs)],
        scratch_shapes=list(scratch)
        + extra
        + [sems(max(len(late), 1)), sems(max(len(early), 1))],
        compiler_params=pltpu.CompilerParams(
            collective_id=number, has_side_effects=True, vmem_limit_bytes=VMEM_LIMIT
        ),
        cost_estimate=pl.CostEstimate(flops=flops, bytes_accessed=moved, transcendentals=0),
    )(*args)


def smem():
    return pl.BlockSpec(memory_space=pltpu.SMEM)


def settle_kernel(
    block_in, input_in, first_in, second_in, out_in, up_in, down_in, *outs
):
    block, inputs, query, key, value, gate, output, up, down = outs
    qk, half = query.shape[1], out_in.shape[2]
    high = value.shape[1] // 2
    block[...] = block_in[...]
    inputs[...] = input_in[...]
    query[...] = first_in[:, :qk].astype(F32)
    key[...] = first_in[:, qk : 2 * qk].astype(F32)
    value[:, :high] = first_in[:, 2 * qk :].astype(F32)
    value[:, high:] = second_in[:, :high].astype(F32)
    gate[...] = second_in[:, high:].astype(F32)
    for i in range(2):
        output[i * half : (i + 1) * half, :] = out_in[i].astype(F32).T
    up[...] = up_in[...]
    down[...] = down_in[...]


def settle(block_out, input_grad, first_sum, second_sum, out_sum, up_grad, down_grad, qk):
    piece = first_sum.shape[0]
    high = first_sum.shape[1] - 2 * qk
    args = (block_out, input_grad, first_sum, second_sum, out_sum, up_grad, down_grad)
    shapes = [
        (block_out.shape, BF),
        (input_grad.shape, F32),
        ((piece, qk), F32),
        ((piece, qk), F32),
        ((piece, 2 * high), F32),
        ((piece, second_sum.shape[1] - high), F32),
        ((2 * out_sum.shape[2], piece), F32),
        (up_grad.shape, F32),
        (down_grad.shape, F32),
    ]
    return pl.pallas_call(
        settle_kernel,
        out_shape=[like(s, t) for s, t in shapes],
        in_specs=[vmem()] * len(args),
        out_specs=[vmem()] * len(shapes),
        compiler_params=pltpu.CompilerParams(vmem_limit_bytes=VMEM_LIMIT),
    )(*args)


def retain_back(
    rates, lengths, a, high, gate, kept, grad_mixed, state, part, keep, give, up_sum, down_sum
):
    units = up_sum.shape[1] // 2
    rows, cols = up_sum.shape[0] // 2, down_sum.shape[1] // 2
    micro, length, vd = high.shape
    hd = (a.shape[2] - vd) // 4
    return call(
        retain_back_kernel,
        6,
        [smem()] * 2
        + [Late("a", 1), Late("high", 1), Late("gate"), Late("kept"), Late("grad"), Late("state", 1)]
        + [anywhere(), Late("keep", 1), anywhere(), Late("up"), Late("down")],
        [
            ((micro, length, a.shape[2]), BF, vmem()),
            ((micro, length, 3 * vd), BF, vmem()),
            ((2, *part.shape[2:]), BF, vmem()),
            (give.shape, BF, vmem()),
            ((rows, 2 * units), F32, vmem()),
            ((2 * units, cols), F32, vmem()),
        ],
        [
            pltpu.VMEM((micro, length, 2 * vd), BF),
            pltpu.VMEM((micro, length, 2 * hd), F32),
            pltpu.VMEM((micro, length, 2 * vd), F32),
            pltpu.VMEM(state.shape, BF),
        ]
        + state_scratch(state.shape)
        + [
            pltpu.VMEM((2, 4, *part.shape[2:]), BF),
            pltpu.VMEM((2, 7, *part.shape[2:]), BF),
            sems(2, 7),
            sems(2, 7),
            sems(2),
            pltpu.VMEM(give.shape, BF),
            pltpu.SemaphoreType.DMA,
            pltpu.SemaphoreType.DMA,
            pltpu.VMEM((2 * rows, units), BF),
            pltpu.VMEM((units, 2 * cols), BF),
            pltpu.VMEM((rows, units), BF),
            pltpu.VMEM((units, cols), BF),
            pltpu.VMEM((rows, units), BF),
            pltpu.VMEM((units, cols), BF),
            sems(4),
            sems(4),
        ],
        12 * micro * length * length * (hd + vd),
        rates,
        lengths,
        a,
        high,
        gate,
        kept,
        grad_mixed,
        state,
        part,
        keep,
        give,
        up_sum,
        down_sum,
    )


def front(rates, lengths, tokens, out_grad, gains, weights, out_weight, up_weight, down_weight):
    micro, rows, width = tokens.shape
    count = lax.axis_size("uly")
    query, key, value, gate = weights
    high = value.shape[1] // 2
    if not is_cube():
        first = jnp.concatenate([query, key, value[:, :high]], axis=1)
        second = jnp.concatenate([value[:, high:], gate], axis=1)
        full = lax.all_gather(jnp.stack(gains), BLK, axis=1, tiled=True)
        w_first = lax.all_gather(first, BLK, axis=0, tiled=True)
        w_second = lax.all_gather(second, BLK, axis=0, tiled=True)
        w_out = lax.all_gather(out_weight, BLK, axis=1, tiled=True)
        one = (normed(spread(tokens).astype(F32))[0] * full[0].astype(F32)).astype(BF)
        a, v_high = dot_nn(one, w_first, BF), dot_nn(one, w_second[:, :high], BF)
        gate_rows = dot_nn(one, w_second[:, high:])
        heads_here = rates.shape[0] // count
        own_rates = lax.dynamic_slice_in_dim(
            rates, lax.axis_index("uly") * heads_here, heads_here
        )
        mixed, kept = plain_forward(own_rates, lengths, a, v_high, gate_rows)
        return (
            one,
            a,
            v_high,
            gate_rows,
            w_first,
            w_second,
            w_out,
            full.astype(F32),
            up_weight,
            down_weight,
            mixed,
            kept,
            None,
            None,
        )
    wide = count * rows
    own = micro * rows
    piece = width // 8
    na, nb, no = 2 * query.shape[1] + high, high + gate.shape[1], out_weight.shape[0]
    units = up_weight.shape[1]
    state = (micro, 2, query.shape[1] // 2, high)
    return call(
        front_kernel,
        0,
        [smem()] * 2 + [vmem()] * 3 + [anywhere()] * 7,
        [
            ((micro, wide, width), BF, Early("one")),
            ((micro, wide, na), BF, Early("first")),
            ((micro, wide, high), BF, Early("high")),
            ((micro, wide, nb - high), F32, Early("gate")),
            ((width, na), BF, anywhere()),
            ((width, nb), BF, anywhere()),
            ((no, width), BF, anywhere()),
            ((8, width), F32, vmem()),
            ((2 * piece, units), BF, anywhere()),
            ((units, 2 * piece), BF, anywhere()),
            ((micro, wide, 2 * high), BF, vmem()),
            ((micro, wide, 2 * high), F32, vmem()),
            (state, BF, vmem()),
            ((4 * own, width), BF, Early("douts")),
        ],
        [
            pltpu.VMEM((count, own, width), BF),
            pltpu.VMEM((width, na), BF),
            pltpu.VMEM((width, nb), BF),
            pltpu.VMEM((8, 8, piece), F32),
            sems(5, 7),
            sems(5, 7),
            sems(2, count - 1),
            sems(2, count - 1),
            sems(4),
            sems(4),
            sems(3),
            sems(3),
            sems(13),
            pltpu.VMEM(out_weight.shape, BF),
            pltpu.VMEM((up_weight.shape[0], units // 2), BF),
            pltpu.VMEM((units // 2, down_weight.shape[1]), BF),
        ]
        + state_scratch(state),
        2 * micro * wide * width * (na + nb),
        rates,
        lengths,
        tokens.reshape(own, width),
        out_grad.reshape(own, width),
        jnp.stack(gains).astype(F32),
        query,
        key,
        value,
        gate,
        out_weight,
        up_weight,
        down_weight,
    )


def line_scratch(count, rows, width):
    return [
        pltpu.VMEM((count - 1, rows, width), BF),
        pltpu.VMEM((2, count - 1, rows, width), BF),
    ]


def add_rows(mixed, w_out, tokens, up, down):
    micro, wide, hidden = mixed.shape
    count = lax.axis_size("uly")
    rows = wide // count
    width = w_out.shape[1]
    units = up.shape[1]
    out = call(
        add_rows_kernel,
        1,
        [Late("x"), Late("w"), Late("tokens", 1)] + [anywhere()] * 2,
        [
            ((micro * rows, width), F32, vmem()),
            ((width, units), BF, anywhere()),
            ((units, width), BF, anywhere()),
        ],
        line_scratch(count, micro * rows, width)
        + [sems(2, count - 1)] * 2
        + [sems(2, 3), sems(2, 3), sems(4), pltpu.VMEM(up.shape, BF), pltpu.VMEM(down.shape, BF)],
        2 * micro * wide * hidden * width,
        mixed,
        w_out,
        tokens,
        up,
        down,
    )
    return out


def fan_out(rows_bf, w_out, mixed, up_grad, down_grad):
    own, width = rows_bf.shape
    micro, rows = 2, own // 2
    count = lax.axis_size("uly")
    hidden = w_out.shape[0]
    up_shape, down_shape = up_grad.shape[1:], down_grad.shape[1:]
    return call(
        fan_out_kernel,
        2,
        [vmem(), Late("w"), Late("mixed")] + [anywhere()] * 2,
        [
            ((micro, count * rows, hidden), F32, Early("grad")),
            ((2, 8, width // 8, hidden // 2), BF, Early("part")),
            (up_shape, BF, vmem()),
            (down_shape, BF, vmem()),
        ],
        [
            pltpu.VMEM((count, own, width), BF),
            pltpu.VMEM((own, width), BF),
            pltpu.VMEM((8, width // 8, hidden), F32),
            pltpu.VMEM((4, *up_shape), BF),
            pltpu.VMEM((4, *down_shape), BF),
            pltpu.VMEM((3, *up_shape), BF),
            pltpu.VMEM((3, *down_shape), BF),
            sems(2, count - 1),
            sems(2, count - 1),
            sems(2, 3),
            sems(2, 3),
            sems(2),
        ],
        4 * micro * count * rows * hidden * width,
        rows_bf,
        w_out,
        mixed,
        up_grad,
        down_grad,
    )


def feed_all(hidden, douts, gain, ups, downs):
    own, width = hidden.shape
    units = ups.shape[1]
    return call(
        feed_kernel,
        4,
        [Late("hid"), Late("douts", 1), vmem(), Late("ups", 1), Late("downs", 1)],
        [
            ((own, width), F32, vmem()),
            ((own, width), BF, Early("give")),
            ((own, width), F32, vmem()),
            ((own, width), BF, vmem()),
            ((1, width), F32, vmem()),
            ((4, width // 4, units), BF, Early("up")),
            ((4, units, width // 4), BF, Early("down")),
        ],
        [
            pltpu.VMEM((4 * own, width), BF),
            pltpu.VMEM((4 * own, units), BF),
            pltpu.VMEM((4 * own, units), BF),
            pltpu.VMEM((2, own, width), F32),
            pltpu.VMEM((3, 2, own, width), BF),
            pltpu.VMEM((5, own, width), BF),
            sems(13),
            sems(13),
        ],
        2 * 6 * 4 * own * units * width,
        hidden,
        douts,
        gain,
        ups,
        downs,
    )


def middle(tokens, out_grad, douts, gains, mixed, w_out, up_weight, down_weight):
    micro, rows, width = tokens.shape
    own = micro * rows
    if not is_cube():
        gain_two = gains[1]
        hidden = tokens.astype(F32) + collect(
            jnp.stack([dot_nn(mixed[m], w_out) for m in range(micro)])
        )
        pair = feed_weights(up_weight, down_weight)
        hat, scale = normed(hidden)
        two = (hat * gain_two).astype(BF)
        flat_two, flat_out = two.reshape(own, width), out_grad.reshape(own, width)
        two_both = jnp.concatenate([flat_two, swap(flat_two, 1)], axis=0)
        out_both = jnp.concatenate([flat_out, swap(flat_out, 1)], axis=0)
        down_rows, grad_two, up_part, down_part = feed(two_both, out_both, pair)
        grad_two = grad_two[:own] + swap(grad_two[own:].astype(BF), 1).astype(F32)
        down_rows = down_rows[:own] + swap(down_rows[own:].astype(BF), 1).astype(F32)
        up_grad, down_grad = feed_reduce(up_part, down_part)
        block_out = (hidden + down_rows.reshape(micro, rows, width)).astype(BF)
        grad_two = grad_two.reshape(micro, rows, width)
        gain_part = jnp.sum(grad_two * hat, axis=(0, 1))
        grad_hidden = out_grad.astype(F32) + norm_back(grad_two * gain_two, hat, scale)
        wide_att = spread(grad_hidden.astype(BF))
        grad_mixed = jnp.stack([dot_nt(wide_att[m], w_out) for m in range(micro)])
        part = dot_tn(
            mixed.reshape(-1, mixed.shape[2]), wide_att.reshape(-1, wide_att.shape[2]), BF
        )
        return block_out, up_grad, down_grad, gain_part, grad_hidden, grad_mixed, part
    hidden, ups, downs = add_rows(mixed, w_out, tokens.reshape(own, width), up_weight, down_weight)
    keep, give, grad_hidden, rows_bf, gain_part, up_part, down_part = feed_all(
        hidden, douts, gains, ups, downs
    )
    grad_mixed, part, up_sum, down_sum = fan_out(rows_bf, w_out, mixed, up_part, down_part)
    return (
        (keep, give),
        up_sum,
        down_sum,
        gain_part,
        grad_hidden,
        grad_mixed,
        part,
    )


def close_rows(xa, xb, w_first, w_second, one, tokens, grad_hidden, gains, gain_two):
    micro, wide, na = xa.shape
    nb = xb.shape[2]
    width = w_first.shape[0]
    flat_a, flat_b = xa.reshape(micro * wide, na), xb.reshape(micro * wide, nb)
    flat_one = one.reshape(micro * wide, width)
    if not is_cube():
        partial = jnp.stack(
            [dot_nt(xa[m], w_first) + dot_nt(xb[m], w_second) for m in range(micro)]
        )
        grad_one = collect(partial)
        hat, scale = normed(tokens.astype(F32))
        both_gains = jnp.stack([jnp.sum(grad_one * hat, axis=(0, 1)), gain_two])
        total = lax.psum_scatter(both_gains, BLK, scatter_dimension=1, tiled=True)
        return (
            grad_hidden + norm_back(grad_one * gains[0], hat, scale),
            lax.psum_scatter(dot_tn(flat_one, flat_a, BF), BLK, scatter_dimension=0, tiled=True),
            lax.psum_scatter(dot_tn(flat_one, flat_b, BF), BLK, scatter_dimension=0, tiled=True),
            lax.psum(total, "uly"),
        )
    count = lax.axis_size("uly")
    rows = wide // count
    piece = width // 8
    out = call(
        close_rows_kernel,
        3,
        [Late("xa"), Late("xb"), Late("wa"), Late("wb"), Late("one"), Late("tokens", 1)]
        + [Late("hid", 1), vmem(), vmem()],
        [
            ((micro * rows, width), F32, vmem()),
            ((piece, na), BF, vmem()),
            ((piece, nb), BF, vmem()),
            ((8, piece), F32, vmem()),
        ],
        line_scratch(count, micro * rows, width)
        + [
            pltpu.VMEM((4, piece, na), BF),
            pltpu.VMEM((4, piece, nb), BF),
            pltpu.VMEM((2, piece, na), BF),
            pltpu.VMEM((2, piece, nb), BF),
            pltpu.VMEM((7, piece, na), BF),
            pltpu.VMEM((7, piece, nb), BF),
            pltpu.VMEM((8, 8, piece), F32),
            pltpu.VMEM((8, 8, piece), F32),
            pltpu.VMEM((4, 8, piece), F32),
            sems(2, count - 1),
            sems(2, count - 1),
            sems(2, 7),
            sems(2, 7),
            sems(10),
            sems(10),
        ],
        4 * micro * wide * width * (na + nb),
        flat_a,
        flat_b,
        w_first,
        w_second,
        flat_one,
        tokens.reshape(micro * rows, width),
        grad_hidden,
        gains,
        gain_two,
    )
    return out


def feed(norm_two, out_rows, pair):
    chips, count, _, rows, hidden = pair.shape
    up = pair[:, :, 0].transpose(0, 2, 1, 3).reshape(chips * rows, count * hidden)
    down_t = pair[:, :, 1].transpose(0, 2, 1, 3).reshape(chips * rows, count * hidden)
    upward = dot_nn(norm_two, up)
    act, slope = gelu_pair(upward)
    act = act.astype(BF)
    grad_act = dot_nn(out_rows, down_t)
    grad_up = (grad_act * slope).astype(BF)

    def by_owner(grad):
        return grad.reshape(chips, rows, count, hidden).transpose(0, 2, 1, 3)

    return (
        dot_nt(act, down_t),
        dot_nt(grad_up, up),
        by_owner(dot_tn(norm_two, grad_up, BF)),
        by_owner(dot_tn(out_rows, act, BF)),
    )


def plain_forward(rates, lengths, a, v_high, gate):
    micro, length = a.shape[:2]
    heads_here = rates.shape[0]
    cut_v = v_high.shape[2]
    qk = (a.shape[2] - cut_v) // 2
    hd, vd = qk // heads_here, 2 * cut_v // heads_here
    sets, parts, states = [], [], []
    for m in range(micro):
        values = jnp.concatenate([a[m, :, 2 * qk :], v_high[m]], axis=1)
        heads = [
            (
                a[m, :, h * hd : (h + 1) * hd],
                a[m, :, qk + h * hd : qk + (h + 1) * hd],
                values[:, h * vd : (h + 1) * vd],
            )
            for h in range(heads_here)
        ]
        part = decay_parts(rates, lengths[m], length)
        states.append(retention_state(heads, part[2]))
        sets.append(heads)
        parts.append(part)

    all_states = exchange(states)
    state_in, retained, mixed = [], [], []
    for m in range(micro):
        state = state_sum(parts[m][3], all_states[m])
        kept = retention(sets[m], parts[m], state)
        state_in.append(state)
        retained.append(kept)
        mixed.append(mix(gate[m], kept))
    mixed = jnp.stack(mixed)
    return mixed, (sets, parts, state_in, retained)


def plain_backward(gate, kept, grad_mixed):
    sets, parts, state_in, retained = kept
    micro, cut_v = len(sets), gate.shape[2] // 2
    grad_gates, grad_rets, grad_states = [], [], []
    for m in range(micro):
        gg, gr = mix_back(gate[m], retained[m], grad_mixed[m])
        grad_gates.append(gg)
        grad_rets.append(gr)
        grad_states.append(
            jnp.stack(
                [
                    dot_tn((q.astype(F32) * parts[m][1][h]).astype(BF), gr[h], BF)
                    for h, (q, k, v) in enumerate(sets[m])
                ]
            )
        )
    all_back = exchange(grad_states)
    xa, xb = [], []
    for m in range(micro):
        back = state_sum(parts[m][4], all_back[m])
        grads = retention_back(sets[m], parts[m], state_in[m], grad_rets[m], back)
        gq = jnp.concatenate([g[0] for g in grads], axis=1)
        gk = jnp.concatenate([g[1] for g in grads], axis=1)
        gv = jnp.concatenate([g[2] for g in grads], axis=1)
        xa.append(jnp.concatenate([gq, gk, gv[:, :cut_v]], axis=1))
        xb.append(jnp.concatenate([gv[:, cut_v:], grad_gates[m]], axis=1))
    xa, xb = jnp.stack(xa), jnp.stack(xb)
    return xa, xb


def body(
    tokens,
    retain_gain,
    query_weight,
    key_weight,
    value_weight,
    gate_matrix,
    output_weight,
    feed_gain,
    up_weight,
    down_weight,
    decay_rate,
    lengths,
    out_grad,
):
    micro, rows, width = tokens.shape
    qk = query_weight.shape[1]
    cut_v = value_weight.shape[1] // 2

    (
        one,
        a,
        v_high,
        gate,
        w_first,
        w_second,
        w_out,
        gains,
        up,
        down,
        mixed,
        kept,
        state,
        douts,
    ) = front(
        decay_rate,
        lengths,
        tokens,
        out_grad,
        (retain_gain, feed_gain),
        (query_weight, key_weight, value_weight, gate_matrix),
        output_weight,
        up_weight,
        down_weight,
    )
    block_out, up_grad, down_grad, gain_two, grad_hidden, grad_mixed, part = middle(
        tokens, out_grad, douts, gains, mixed, w_out, up, down
    )

    if is_cube():
        xa, xb, out_sum, block_out, up_grad, down_grad = retain_back(
            decay_rate,
            lengths,
            a,
            v_high,
            gate,
            kept,
            grad_mixed,
            state,
            part,
            *block_out,
            up_grad,
            down_grad,
        )
    else:
        xa, xb = plain_backward(gate, kept, grad_mixed)
        out_sum = lax.psum_scatter(part, BLK, scatter_dimension=1, tiled=True)

    input_grad, first_sum, second_sum, gain_sums = close_rows(
        xa, xb, w_first, w_second, one, tokens, grad_hidden, gains, gain_two
    )
    if is_cube():
        block_out, input_grad, query, key, value, gates, output, up_grad, down_grad = settle(
            block_out, input_grad, first_sum, second_sum, out_sum, up_grad, down_grad, qk
        )
        block_out = block_out.reshape(tokens.shape)
        input_grad = input_grad.reshape(tokens.shape)
    else:
        first_sum, second_sum = first_sum.astype(F32), second_sum.astype(F32)
        query, key = first_sum[:, :qk], first_sum[:, qk : 2 * qk]
        value = jnp.concatenate([first_sum[:, 2 * qk :], second_sum[:, :cut_v]], axis=1)
        gates, output = second_sum[:, cut_v:], out_sum.astype(F32)
    return (
        block_out,
        input_grad,
        gain_sums[0],
        query,
        key,
        value,
        gates,
        output,
        gain_sums[1],
        up_grad,
        down_grad,
    )


def solution(mesh):
    blocks, count = mesh.devices.shape
    split = Mesh(mesh.devices.reshape(blocks // 2, 2, count), AXES)
    rows = P(None, AXES, None)
    gain, wide, tall = P(BLK), P(BLK, "uly"), P("uly", BLK)
    return jax.shard_map(
        body,
        mesh=split,
        in_specs=(rows, gain, wide, wide, wide, wide, tall, gain, wide, tall, P(), P(), rows),
        out_specs=(rows, rows, gain, wide, wide, wide, wide, tall, gain, wide, tall),
        check_vma=False,
    )
```

```python
import functools

import jax
import jax.numpy as jnp
from jax import lax
from jax.experimental import pallas as pl
from jax.experimental.pallas import tpu as pltpu
from jax.sharding import Mesh
from jax.sharding import PartitionSpec as P

EPSILON = 1e-05
BF = jnp.bfloat16
F32 = jnp.float32
AXES = ("chip", "core", "uly")
BLK = ("chip", "core")
MESH = pl.DeviceIdType.MESH
VMEM_LIMIT = 62 * 1024 * 1024


def dot_nn(left, right, kind=F32):
    return jnp.dot(left, right, preferred_element_type=F32).astype(kind)


def dot_tn(left, right, kind=F32):
    return lax.dot_general(
        left, right, (((0,), (0,)), ((), ())), preferred_element_type=F32
    ).astype(kind)


def dot_nt(left, right, kind=F32):
    return lax.dot_general(
        left, right, (((1,), (1,)), ((), ())), preferred_element_type=F32
    ).astype(kind)


def block_index():
    return lax.axis_index("chip") * 2 + lax.axis_index("core")


def block_count():
    return lax.axis_size("chip") * 2


def swap(array, mask):
    if mask == 1:
        return lax.ppermute(array, "core", [(0, 1), (1, 0)])
    count = lax.axis_size("chip")
    return lax.ppermute(array, "chip", [(b, b ^ (mask // 2)) for b in range(count)])


def shift(array, step):
    count = lax.axis_size("uly")
    return lax.ppermute(array, "uly", [(z, (z + step) % count) for z in range(count)])


def is_cube():
    return lax.axis_size("chip") == 4 and lax.axis_size("uly") == 4


def masks():
    return [2 * k + j for j in range(2) for k in range(4)]


def plane_gather(first, second):
    first_x = swap(first, 2)
    second_y = swap(second, 4)
    first_y, first_xy = swap(first, 4), swap(first_x, 4)
    second_x, second_xy = swap(second, 2), swap(second_y, 2)
    return [first, first_x, first_y, first_xy], [second, second_x, second_y, second_xy]


def exchange(pieces):
    if not is_cube():
        return [lax.all_gather(p, BLK) for p in pieces]
    half = len(pieces) // 2
    a, b = plane_gather(jnp.stack(pieces[:half]), jnp.stack(pieces[half:]))
    got = []
    for four in (a, b):
        full = jnp.stack(four + [swap(p, 1) for p in four])
        got += [full[:, i] for i in range(full.shape[1])]
    return got


def spread(rows):
    return lax.all_gather(rows, "uly", axis=1, tiled=True)


def collect(partial):
    return lax.psum_scatter(partial.astype(BF), "uly", scatter_dimension=1, tiled=True).astype(F32)


def core_cut(array, dim):
    core = lax.axis_index("core")
    half = array.shape[dim] // 2
    own = lax.dynamic_slice_in_dim(array, core * half, half, dim)
    other = lax.dynamic_slice_in_dim(array, (1 - core) * half, half, dim)
    return own, other


def core_join(own, other, dim):
    first = lax.axis_index("core") == 0
    return jnp.concatenate([jnp.where(first, own, other), jnp.where(first, other, own)], axis=dim)


def feed_weights(up_shard, down_shard):
    own, other = core_cut(up_shard, 1)
    up = core_join(own, swap(other, 1), 0)
    own, other = core_cut(down_shard, 0)
    down = core_join(own, swap(other, 1), 1)
    pair = lax.all_gather(jnp.stack([up, down.T]), ("chip", "uly"), axis=0, tiled=False)
    chips, count = lax.axis_size("chip"), lax.axis_size("uly")
    rows, hidden = up.shape
    pair = pair.reshape(chips, count, 2, rows, hidden)
    return pair


def feed_reduce(up_grad, down_grad):
    pair = jnp.stack([up_grad, down_grad], axis=2)
    chips, count = pair.shape[:2]
    pair = pair.reshape(chips * count * 2, *pair.shape[3:])
    total = lax.psum_scatter(pair, ("chip", "uly"), scatter_dimension=0, tiled=True)
    half = total.shape[1] // 2
    own, other = core_cut(total, 1)
    both_halves = core_join(own, swap(other, 1), 2).astype(F32)
    return both_halves[0], both_halves[1].T


def normed(values):
    center = values - jnp.mean(values, axis=-1, keepdims=True)
    scale = lax.rsqrt(jnp.mean(center * center, axis=-1, keepdims=True) + EPSILON)
    return center * scale, scale


def norm_back(grad, hat, scale):
    return scale * (
        grad
        - jnp.mean(grad, axis=-1, keepdims=True)
        - hat * jnp.mean(grad * hat, axis=-1, keepdims=True)
    )


GELU_A = 0.7978845608028654
GELU_B = 0.044715


def gelu_pair(u):
    square = u * u
    tanh = jnp.tanh(GELU_A * u * (1.0 + GELU_B * square))
    slope = 0.5 * (1.0 + tanh) + 0.5 * u * (1.0 - tanh * tanh) * GELU_A * (
        1.0 + 3.0 * GELU_B * square
    )
    return 0.5 * u * (1.0 + tanh), slope


def segment_ids(positions, lengths_row):
    count = lengths_row.shape[0]
    before = jnp.arange(count)[None, :] < jnp.arange(count)[:, None]
    bounds = jnp.sum(jnp.where(before, lengths_row[None, :], 0), axis=1)
    return jnp.sum((bounds[None, :] <= positions[:, None]).astype(jnp.int32), axis=1)


def decay_parts(rates, lengths_row, length):
    me = block_index()
    count = block_count()
    places = jnp.arange(length, dtype=jnp.int32)
    seg = segment_ids(me * length + places, lengths_row)
    ends = segment_ids((jnp.arange(count, dtype=jnp.int32) + 1) * length - 1, lengths_row)
    seg_prev = segment_ids(jnp.reshape(me * length - 1, (1,)), lengths_row)[0]
    offset = places[:, None] - places[None, :]
    causal = (offset >= 0) & (seg[:, None] == seg[None, :])
    far = jnp.maximum(offset, 0).astype(F32)
    inner = jnp.where(causal[None], jnp.exp(-rates[:, None, None] * far[None]), 0.0)
    at = places.astype(F32)
    entry = jnp.where(seg == seg_prev, jnp.exp(-rates[:, None] * (at + 1.0)), 0.0)
    leave = jnp.where(seg == seg[length - 1], jnp.exp(-rates[:, None] * (length - 1.0 - at)), 0.0)
    if is_cube():
        source = me ^ jnp.asarray(masks(), jnp.int32)
    else:
        source = jnp.arange(count, dtype=jnp.int32)
    end_of = ends[source]
    end_before = jnp.where(source > 0, ends[jnp.maximum(source - 1, 0)], 0)
    past = jnp.maximum(me - 1 - source, 0).astype(F32)
    ahead = jnp.maximum(source - 1 - me, 0).astype(F32)
    from_past = jnp.where(
        (source < me) & (end_of == seg_prev), jnp.exp(-rates[:, None] * (length * past)), 0.0
    )
    from_ahead = jnp.where(
        (source > me) & (end_before == ends[me]), jnp.exp(-rates[:, None] * (length * ahead)), 0.0
    )
    return inner, entry[:, :, None], leave[:, :, None], from_past, from_ahead


def state_sum(weights, states):
    return jnp.einsum("hb,bhde->hde", weights, states.astype(F32))


def retention_state(heads, leave):
    return jnp.stack(
        [
            dot_tn((k.astype(F32) * leave[h]).astype(BF), v, BF)
            for h, (q, k, v) in enumerate(heads)
        ]
    )


def retention(heads, parts, state):
    inner, entry = parts[0], parts[1]
    out = []
    for h, (q, k, v) in enumerate(heads):
        scores = (dot_nt(q, k) * inner[h]).astype(BF)
        out.append(dot_nn(scores, v) + entry[h] * dot_nn(q, state[h].astype(BF)))
    return out


def mix(gate, retained):
    out = []
    for h, r in enumerate(retained):
        g = gate[:, h * r.shape[1] : (h + 1) * r.shape[1]]
        out.append((g * jax.nn.sigmoid(g) * normed(r)[0]).astype(BF))
    return jnp.concatenate(out, axis=1)


def mix_back(gate, retained, grad_mixed):
    grad_gate, grad_retained = [], []
    for h, r in enumerate(retained):
        cols = slice(h * r.shape[1], (h + 1) * r.shape[1])
        g, gm = gate[:, cols], grad_mixed[:, cols]
        sigma = jax.nn.sigmoid(g)
        hat, scale = normed(r)
        grad_gate.append((gm * hat * (sigma + g * sigma * (1.0 - sigma))).astype(BF))
        grad_retained.append(norm_back(gm * g * sigma, hat, scale).astype(BF))
    return jnp.concatenate(grad_gate, axis=1), grad_retained


def retention_back(heads, parts, state, grad_retained, grad_state):
    inner, entry, leave = parts[0], parts[1], parts[2]
    grads = []
    for h, (q, k, v) in enumerate(heads):
        gr = grad_retained[h]
        scores = (dot_nt(q, k) * inner[h]).astype(BF)
        pulls = (dot_nt(gr, v) * inner[h]).astype(BF)
        gs, st = grad_state[h].astype(BF), state[h].astype(BF)
        gq = dot_nn(pulls, k) + entry[h] * dot_nt(gr, st)
        gk = dot_tn(pulls, q) + leave[h] * dot_nt(v, gs)
        gv = dot_tn(scores, gr) + leave[h] * dot_nn(k, gs)
        grads.append((gq.astype(BF), gk.astype(BF), gv.astype(BF)))
    return grads


def vmem():
    return pl.BlockSpec(memory_space=pltpu.VMEM)


def anywhere():
    return pl.BlockSpec(memory_space=pl.ANY)


def greet(plane=False, line=False, cores=False, pair=False, across=False, whole=False, every=False):
    barrier = pltpu.get_barrier_semaphore()
    chip, core, z = (lax.axis_index(a) for a in AXES)
    others = []
    if plane:
        others += [{"chip": chip ^ 1}, {"chip": chip ^ 2}]
    if cores:
        others.append({"core": 1 - core})
    if pair:
        others.append({"uly": z ^ 1})
    if across:
        others.append({"uly": z ^ 2})
    if whole:
        others += [{"uly": z ^ k} for k in range(1, 4)]
    if every:
        others += [{"chip": chip ^ (p % 4), "core": core ^ (p // 4)} for p in range(1, 8)]
    for to in others:
        pl.semaphore_signal(barrier, inc=1, device_id=to, device_id_type=MESH)
    count = len(others)
    if line:
        last = lax.axis_size("uly") - 1

        @pl.when(z > 0)
        def _():
            pl.semaphore_signal(barrier, inc=1, device_id={"uly": z - 1}, device_id_type=MESH)

        @pl.when(z < last)
        def _():
            pl.semaphore_signal(barrier, inc=1, device_id={"uly": z + 1}, device_id_type=MESH)

        count = count + jnp.where(z > 0, 1, 0) + jnp.where(z < last, 1, 0)
    pl.semaphore_wait(barrier, count)


class PlaneGather:
    def __init__(self, own, at, x_first, send, recv, cores=True):
        chip, core = lax.axis_index("chip"), lax.axis_index("core")
        x, y, other = {"chip": chip ^ 1}, {"chip": chip ^ 2}, {"core": 1 - core}

        def copy(i, src, place, to):
            return pltpu.make_async_remote_copy(
                src_ref=src,
                dst_ref=at(place),
                send_sem=send.at[i],
                recv_sem=recv.at[i],
                device_id=to,
                device_id_type=MESH,
            )

        self.x_first = x_first
        self.copies = [
            copy(0, own, 1, x),
            copy(1, own, 2, y),
            copy(2, at(1), 3, y) if x_first else copy(2, at(2), 3, x),
        ]
        self.cores = cores
        if cores:
            self.copies += [
                copy(3, own, 4, other),
                copy(4, at(1), 5, other),
                copy(5, at(2), 6, other),
                copy(6, at(3), 7, other),
            ]

    def start(self):
        for i in (0, 1) if self.x_first else (1, 0):
            self.copies[i].start()
        if self.cores:
            self.copies[3].start()

    def near(self):
        first = 0 if self.x_first else 1
        self.copies[first].wait_recv()
        self.copies[2].start()
        if self.cores:
            self.copies[4 + first].start()

    def far(self):
        second = 1 if self.x_first else 0
        self.copies[second].wait_recv()
        if self.cores:
            self.copies[4 + second].start()

    def corner(self):
        self.copies[2].wait_recv()
        if self.cores:
            self.copies[6].start()

    def finish(self):
        for c in self.copies[3:]:
            c.wait_recv()
        for c in self.copies:
            c.wait_send()


class LineGather:
    def __init__(self, slots, send, recv):
        self.z = lax.axis_index("uly")
        self.last = lax.axis_size("uly") - 1
        self.slots, self.send, self.recv = slots, send, recv

    def copy(self, right, d):
        z, last = self.z, self.last
        at = jnp.maximum(z - d, 0) if right else jnp.minimum(z + d, last)
        to = jnp.minimum(z + 1, last) if right else jnp.maximum(z - 1, 0)
        way = 0 if right else 1
        return pltpu.make_async_remote_copy(
            src_ref=self.slots.at[at],
            dst_ref=self.slots.at[at],
            send_sem=self.send.at[way, d],
            recv_sem=self.recv.at[way, d],
            device_id={"uly": to},
            device_id_type=MESH,
        )

    def pass_on(self, d):
        z, last = self.z, self.last

        @pl.when((z - d >= 0) & (z < last))
        def _():
            self.copy(True, d).start()

        @pl.when((z + d <= last) & (z > 0))
        def _():
            self.copy(False, d).start()

    def take(self, d, then):
        z, last = self.z, self.last

        @pl.when(z - d >= 0)
        def _():
            self.copy(True, d - 1).wait_recv()

        @pl.when(z + d <= last)
        def _():
            self.copy(False, d - 1).wait_recv()

        if d < last:
            self.pass_on(d)
        self.each(d, then)

    def each(self, d, then):
        z, last = self.z, self.last

        @pl.when(z - d >= 0)
        def _():
            then(jnp.maximum(z - d, 0))

        @pl.when(z + d <= last)
        def _():
            then(jnp.minimum(z + d, last))

    def finish(self):
        z, last = self.z, self.last
        for d in range(last):

            @pl.when((z - d >= 0) & (z < last))
            def _():
                self.copy(True, d).wait_send()

            @pl.when((z + d <= last) & (z > 0))
            def _():
                self.copy(False, d).wait_send()


class LineReduce:
    def __init__(self, make, out, held, came, send, recv):
        self.z = lax.axis_index("uly")
        self.last = lax.axis_size("uly") - 1
        self.make, self.out, self.held, self.came = make, out, held, came
        self.send, self.recv = send, recv

    def copy(self, right, d):
        z, last = self.z, self.last
        way = 0 if right else 1
        to = jnp.minimum(z + 1, last) if right else jnp.maximum(z - 1, 0)
        return pltpu.make_async_remote_copy(
            src_ref=self.held.at[self.place(right, d)],
            dst_ref=self.came.at[way, d - 1],
            send_sem=self.send.at[way, d - 1],
            recv_sem=self.recv.at[way, d - 1],
            device_id={"uly": to},
            device_id_type=MESH,
        )

    def place(self, right, d):
        return d - 1 if right else self.last - d

    def step(self, d):
        z, last = self.z, self.last
        for right in (True, False):
            way = 0 if right else 1
            held = self.held.at[self.place(right, d)]
            valid = (z + d <= last) if right else (z - d >= 0)
            more = (z > 0) if right else (z < last)
            to = jnp.minimum(z + d, last) if right else jnp.maximum(z - d, 0)

            @pl.when(valid)
            def _():
                self.make(to, held)

                if d < last:

                    @pl.when(more)
                    def _():
                        self.copy(right, d + 1).wait_recv()
                        held[...] = (held[...].astype(F32) + self.came[way, d].astype(F32)).astype(
                            BF
                        )

                self.copy(right, d).start()

    def own(self):
        self.make(self.z, self.out)

    def close(self):
        z, last = self.z, self.last

        @pl.when(z > 0)
        def _():
            self.copy(True, 1).wait_recv()
            self.out[...] += self.came[0, 0].astype(F32)

        @pl.when(z < last)
        def _():
            self.copy(False, 1).wait_recv()
            self.out[...] += self.came[1, 0].astype(F32)

        for d in range(1, last + 1):

            @pl.when(z + d <= last)
            def _():
                self.copy(True, d).wait_send()

            @pl.when(z - d >= 0)
            def _():
                self.copy(False, d).wait_send()


def chunk_of(place, width):
    chip, core = lax.axis_index("chip"), lax.axis_index("core")
    block = (chip ^ (place % 4)) * 2 + (core ^ (place // 4))
    return pl.ds(pl.multiple_of(block * width, width), width)


def chip_chunk(k, width):
    return pl.ds(pl.multiple_of((lax.axis_index("chip") ^ k) * width, width), width)


def chip_order(place, width):
    core = lax.axis_index("core")
    return pl.ds(pl.multiple_of((place % 4) * (2 * width) + (core ^ (place // 4)) * width, width), width)


def front_kernel(
    io,
    rates_ref,
    lengths_ref,
    tok_ref,
    dout_ref,
    gain_ref,
    q_hbm,
    k_hbm,
    v_hbm,
    g_hbm,
    out_hbm,
    up_hbm,
    down_hbm,
    one_ref,
    first_ref,
    high_ref,
    gate_ref,
    w_first_hbm,
    w_second_hbm,
    w_out_hbm,
    gains_ref,
    up_own_hbm,
    down_own_hbm,
    mixed_ref,
    kept_ref,
    state_ref,
    douts_ref,
    slots,
    wa,
    wb,
    gains,
    psend,
    precv,
    zsend,
    zrecv,
    fsend,
    frecv,
    dsend,
    drecv,
    lsem,
    stage_out,
    stage_up,
    stage_down,
    *state_refs,
):
    core, z = lax.axis_index("core"), lax.axis_index("uly")
    rows = tok_ref.shape[0] // 2
    width = tok_ref.shape[1]
    piece = width // 8
    qk, high = q_hbm.shape[1], high_ref.shape[2]
    gains[0] = jnp.zeros_like(gains[0])
    gains[0, 0:2, :] = gain_ref[...]
    line = LineGather(slots, zsend, zrecv)
    slots[z] = tok_ref[...]
    greet(every=True, line=True, across=True)
    chip = lax.axis_index("chip")
    small = [
        pltpu.make_async_remote_copy(
            src_ref=gains.at[0],
            dst_ref=gains.at[p],
            send_sem=psend.at[0, p - 1],
            recv_sem=precv.at[0, p - 1],
            device_id={"chip": chip ^ (p % 4), "core": core ^ (p // 4)},
            device_id_type=MESH,
        )
        for p in range(1, 8)
    ]
    for c in small:
        c.start()
    line.pass_on(0)
    own = pl.ds(0, piece)
    local = [
        pltpu.make_async_copy(src, dst, lsem.at[i])
        for i, (src, dst) in enumerate(
            (
                (q_hbm, wa.at[own, pl.ds(0, qk)]),
                (k_hbm, wa.at[own, pl.ds(qk, qk)]),
                (v_hbm.at[:, pl.ds(0, high)], wa.at[own, pl.ds(2 * qk, high)]),
                (v_hbm.at[:, pl.ds(high, high)], wb.at[own, pl.ds(0, high)]),
                (g_hbm, wb.at[own, pl.ds(high, g_hbm.shape[1])]),
                (out_hbm, stage_out),
            )
        )
    ]
    for c in local:
        c.start()
    items = [None]
    for i, w in enumerate((wa, wb)):
        items.append(
            PlaneGather(
                w.at[own],
                lambda p, w=w: w.at[pl.ds(p * piece, piece)],
                i == 0,
                psend.at[1 + i],
                precv.at[1 + i],
            )
        )
    half = out_hbm.shape[0] // 2
    for i in range(2):
        part = pl.ds(i * half, half)
        items.append(
            PlaneGather(
                out_hbm.at[part],
                lambda p, part=part: w_out_hbm.at[part, pl.ds(p * piece, piece)],
                i == 0,
                psend.at[3 + i],
                precv.at[3 + i],
            )
        )
    units, cols = up_hbm.shape[1] // 2, down_hbm.shape[1]
    first_half = pl.ds(0, units)
    mine, theirs = (pl.ds(pl.multiple_of(c * units, units), units) for c in (core, 1 - core))
    here = pl.ds(pl.multiple_of(core * cols, cols), cols)

    def remote(i, src, dst, to):
        return pltpu.make_async_remote_copy(
            src_ref=src,
            dst_ref=dst,
            send_sem=fsend.at[i],
            recv_sem=frecv.at[i],
            device_id=to,
            device_id_type=MESH,
        )

    stage = [
        local[5],
        pltpu.make_async_copy(up_hbm.at[:, mine], stage_up, lsem.at[6]),
        pltpu.make_async_copy(down_hbm.at[mine], stage_down, lsem.at[7]),
    ]
    cut = [
        pltpu.make_async_copy(stage_out, w_out_hbm.at[:, own], lsem.at[10]),
        pltpu.make_async_copy(stage_up, up_own_hbm.at[here, first_half], lsem.at[11]),
        pltpu.make_async_copy(stage_down, down_own_hbm.at[first_half, here], lsem.at[12]),
    ]
    give = [
        remote(0, up_hbm.at[:, theirs], up_own_hbm.at[here, first_half], {"core": 1 - core}),
        remote(1, down_hbm.at[theirs], down_own_hbm.at[first_half, here], {"core": 1 - core}),
    ]
    first_wide, second_wide = up_own_hbm.at[:, first_half], up_own_hbm.at[:, pl.ds(units, units)]
    first_tall, second_tall = down_own_hbm.at[first_half], down_own_hbm.at[pl.ds(units, units)]
    away = [
        remote(2, first_wide, second_wide, {"uly": z ^ 2}),
        remote(3, first_tall, second_tall, {"uly": z ^ 2}),
    ]
    own_rows = 2 * rows

    def rows_to(i, src, dst, to):
        return pltpu.make_async_remote_copy(
            src_ref=douts_ref.at[pl.ds(src * own_rows, own_rows)],
            dst_ref=douts_ref.at[pl.ds(dst * own_rows, own_rows)],
            send_sem=dsend.at[i],
            recv_sem=drecv.at[i],
            device_id=to,
            device_id_type=MESH,
        )

    send_rows = [
        rows_to(0, 0, 2, {"uly": z ^ 1}),
        rows_to(1, 0, 1, {"core": 1 - core}),
        rows_to(2, 2, 3, {"core": 1 - core}),
    ]
    for c in stage[1:]:
        c.start()
    for c in local[:5]:
        c.wait()
    for item in items[1:3]:
        item.start()
    for c in give:
        c.start()
    for c in small:
        c.wait()
    gains_ref[...] = jnp.zeros_like(gains_ref)
    for p in range(8):
        gains_ref[0:1, chunk_of(p, piece)] = gains[p, 0:1, :]
        gains_ref[1:2, chip_order(p, piece)] = gains[p, 1:2, :]

    def normalize(slot):
        step = 32
        for m in range(2):

            @pl.loop(0, rows // step)
            def _(i):
                at = pl.multiple_of(i * step, step)
                v = slots[slot, pl.ds(m * rows + at, step), :].astype(F32)
                mean = jnp.mean(v, axis=-1, keepdims=True)
                center = v - mean
                scale = lax.rsqrt(jnp.mean(center * center, axis=-1, keepdims=True) + EPSILON)
                to = pl.ds(pl.multiple_of(slot * rows + at, step), step)
                for p in range(8):
                    src = slots[slot, pl.ds(m * rows + at, step), chunk_of(p, piece)].astype(F32)
                    one_ref[m, to, pl.ds(p * piece, piece)] = (
                        (src - mean) * scale * gains[p, 0:1, :]
                    ).astype(BF)

    for c in stage:
        c.wait()
    for c in cut:
        c.start()
    for k in range(4):
        douts_ref[0:own_rows, k * 2 * piece : (k + 1) * 2 * piece] = dout_ref[
            :, chip_chunk(k, 2 * piece)
        ]
    at_end = (z == 0) | (z == line.last)
    inside = (z > 0) & (z < line.last)
    normalize(z)
    line.take(1, normalize)

    @pl.when(at_end)
    def _():
        send_rows[0].start()

    for item in items[1:3]:
        item.near()
    for item in items[1:3]:
        item.far()
    for item in items[3:]:
        item.start()
    line.take(2, normalize)
    for c in cut:
        c.wait()
    for c in give:
        c.wait()

    @pl.when(at_end)
    def _():
        for c in away:
            c.start()

    @pl.when(inside)
    def _():
        send_rows[0].start()

    for item in items[1:3]:
        item.corner()
    for item in items[1:3]:
        item.finish()
    outs = [
        pltpu.make_async_copy(wa, w_first_hbm, lsem.at[8]),
        pltpu.make_async_copy(wb, w_second_hbm, lsem.at[9]),
    ]
    for c in outs:
        c.start()
    tile = 512

    def multiply(slot):
        at = pl.ds(pl.multiple_of(slot * rows, rows), rows)
        x = jnp.concatenate([one_ref[0, at, :], one_ref[1, at, :]], axis=0)

        def tiles(w, start, to_ref):
            @pl.loop(0, to_ref.shape[2] // tile)
            def _(n):
                cols = pl.ds(pl.multiple_of(n * tile, tile), tile)
                from_ = pl.ds(pl.multiple_of(start + n * tile, tile), tile)
                r = jnp.dot(x, w[:, from_], preferred_element_type=F32).astype(to_ref.dtype)
                for m in range(2):
                    to_ref[m, at, cols] = r[m * rows : (m + 1) * rows]

        tiles(wa, 0, first_ref)
        tiles(wb, 0, high_ref)
        tiles(wb, high, gate_ref)

    multiply(z)
    line.each(1, multiply)
    for item in items[3:]:
        item.near()
    for item in items[3:]:
        item.far()
    line.each(2, multiply)

    def both_steps(slot):
        normalize(slot)
        multiply(slot)

    line.take(3, both_steps)

    @pl.when(inside)
    def _():
        for c in away:
            c.wait_recv()
        for c in away:
            c.start()

    io.done("one", "first", "high", "gate")
    for item in items[3:]:
        item.corner()
    for item in items[3:]:
        item.finish()
    line.finish()
    retain_part(
        io,
        rates_ref,
        lengths_ref,
        first_ref,
        high_ref,
        gate_ref,
        mixed_ref,
        kept_ref,
        state_ref,
        douts_ref,
        send_rows,
        *state_refs,
    )
    for c in outs:
        c.wait()

    @pl.when(at_end)
    def _():
        for c in away:
            c.wait_recv()

    for c in away:
        c.wait_send()


def add_rows_kernel(
    io,
    x_ref,
    w_ref,
    tok_ref,
    up_hbm,
    down_hbm,
    out_ref,
    ups_hbm,
    downs_hbm,
    held,
    came,
    send,
    recv,
    psend,
    precv,
    lsem,
    stage_up,
    stage_down,
):
    rows = out_ref.shape[0] // 2
    width = out_ref.shape[1] // 8
    greet(plane=True, line=True)
    part = up_hbm.shape[0]

    def up_at(p):
        return ups_hbm.at[pl.ds(p * part, part)]

    def down_at(p):
        return downs_hbm.at[:, pl.ds(p * part, part)]

    items = [
        PlaneGather(up_hbm, up_at, True, psend.at[0], precv.at[0], False),
        PlaneGather(down_hbm, down_at, False, psend.at[1], precv.at[1], False),
    ]
    stage = [
        pltpu.make_async_copy(up_hbm, stage_up, lsem.at[2]),
        pltpu.make_async_copy(down_hbm, stage_down, lsem.at[3]),
    ]
    local = [
        pltpu.make_async_copy(stage_up, up_at(0), lsem.at[0]),
        pltpu.make_async_copy(stage_down, down_at(0), lsem.at[1]),
    ]

    def make(a, to):
        at = pl.ds(pl.multiple_of(a * rows, rows), rows)
        x = jnp.concatenate([x_ref[0, at, :], x_ref[1, at, :]], axis=0)

        @pl.loop(0, 8)
        def _(p):
            cols = w_ref[:, pl.ds(pl.multiple_of(p * width, width), width)]
            to[:, chip_order(p, width)] = jnp.dot(x, cols, preferred_element_type=F32).astype(
                to.dtype
            )

    line = LineReduce(make, out_ref, held, came, send, recv)
    for item in items:
        item.start()
    io.ready("x", "w")
    line.step(3)
    io.start(1)
    for c in stage:
        c.start()
    line.step(2)
    for c in stage:
        c.wait()
    for c in local:
        c.start()
    for item in items:
        item.near()
    for item in items:
        item.far()
    line.step(1)
    line.own()
    line.close()
    io.ready("tokens")
    for k in range(4):
        cols = pl.ds(k * 2 * width, 2 * width)
        out_ref[:, cols] += tok_ref[:, chip_chunk(k, 2 * width)].astype(F32)
    for item in items:
        item.corner()
    for item in items:
        item.finish()
    for c in local:
        c.wait()


def fan_out_kernel(
    io,
    rows_ref,
    w_ref,
    mixed_ref,
    up_hbm,
    down_hbm,
    grad_ref,
    part_ref,
    up_ref,
    down_ref,
    slots,
    ordered,
    total,
    near_up,
    near_down,
    came_up,
    came_down,
    send,
    recv,
    psend,
    precv,
    lsem,
):
    z = lax.axis_index("uly")
    rows = rows_ref.shape[0] // 2
    width = rows_ref.shape[1] // 8
    greet(plane=True, line=True)
    line = LineGather(slots, send, recv)
    slots[z] = rows_ref[...]
    line.pass_on(0)
    local = [
        pltpu.make_async_copy(up_hbm, near_up, lsem.at[0]),
        pltpu.make_async_copy(down_hbm, near_down, lsem.at[1]),
    ]
    for c in local:
        c.start()
    groups = [
        PlaneReduce(None, near_up, came_up, True, psend.at[0], precv.at[0]),
        PlaneReduce(None, near_down, came_down, False, psend.at[1], precv.at[1]),
    ]
    for c in local:
        c.wait()
    for g in groups:
        g.start_first()

    def multiply(slot):
        at = pl.ds(pl.multiple_of(slot * rows, rows), rows)
        for p in range(8):
            ordered[:, p * width : (p + 1) * width] = slots[slot, :, chip_order(p, width)]
        tile = 256

        @pl.loop(0, w_ref.shape[0] // tile)
        def _(n):
            part = pl.ds(pl.multiple_of(n * tile, tile), tile)
            product = dot_nt(ordered[...], w_ref[part, :])
            for m in range(2):
                grad_ref[m, at, part] = product[m * rows : (m + 1) * rows]

        mixed = jnp.concatenate([mixed_ref[0, at, :], mixed_ref[1, at, :]], axis=0)

        @pl.loop(0, 8)
        def _(p):
            cols = pl.ds(pl.multiple_of(p * width, width), width)
            total[p] += dot_tn(ordered[:, cols], mixed)

    total[...] = jnp.zeros_like(total)
    io.ready("w", "mixed")
    multiply(z)
    line.take(1, multiply)
    for g in groups:
        g.first_sums(0)
    line.take(2, multiply)
    for g in groups:
        g.first_sums(1)
    line.take(3, multiply)
    io.done("grad")
    half = part_ref.shape[3]
    for i in range(2):
        part_ref[i] = total[:, :, i * half : (i + 1) * half].astype(BF)
    io.done("part")
    groups[0].finish(up_ref)
    groups[1].finish(down_ref)
    line.finish()


def feed_kernel(
    io,
    hid_ref,
    douts_ref,
    gain_ref,
    ups_ref,
    downs_ref,
    keep_ref,
    give_ref,
    grad_ref,
    rows_ref,
    gain_grad_ref,
    up_grad_ref,
    down_grad_ref,
    two,
    act,
    gu,
    sums,
    held,
    came,
    send,
    recv,
):
    core, z = lax.axis_index("core"), lax.axis_index("uly")
    rows, width = hid_ref.shape
    hidden = ups_ref.shape[1]
    other, pair = {"core": 1 - core}, {"uly": z ^ 1}
    greet(cores=True, pair=True)

    half = rows // 2

    def group(g, part=None):
        return pl.ds(g * rows, rows) if part is None else pl.ds(g * rows + part * half, half)

    def copy(i, src, dst, to):
        return pltpu.make_async_remote_copy(
            src_ref=src,
            dst_ref=dst,
            send_sem=send.at[i],
            recv_sem=recv.at[i],
            device_id=to,
            device_id_type=MESH,
        )

    parts = [pl.ds(part * half, half) for part in range(2)]
    to_pair = [copy(p, two.at[group(0, p)], two.at[group(2, p)], pair) for p in range(2)]
    through = [copy(2 + p, two.at[group(2, p)], two.at[group(3, p)], other) for p in range(2)]
    to_other = copy(4, two.at[group(0)], two.at[group(1)], other)
    step = 32
    io.ready("hid")
    io.start(1)
    for part in range(2):

        @pl.loop(0, half // step)
        def _(i):
            at = pl.ds(pl.multiple_of(part * half + i * step, step), step)
            hat, _scale = normed(hid_ref[at, :])
            two[at, :] = (hat * gain_ref[1:2, :]).astype(BF)

        to_pair[part].start()
    to_other.start()

    def work(g, part=None):
        at = group(g, part)
        to = slice(None) if part is None else parts[part]
        tile = 256

        @pl.loop(0, hidden // tile)
        def _(n):
            cols = pl.ds(pl.multiple_of(n * tile, tile), tile)
            upward = jnp.dot(two[at, :], ups_ref[:, cols], preferred_element_type=F32)
            value, slope = gelu_pair(upward)
            act[at, cols] = value.astype(BF)
            pulled = dot_nt(douts_ref[at, :], downs_ref[cols, :])
            gu[at, cols] = (pulled * slope).astype(BF)

        tile = 512

        @pl.loop(0, width // tile)
        def _(n):
            cols = pl.ds(pl.multiple_of(n * tile, tile), tile)
            back = dot_nt(gu[at, :], ups_ref[cols, :])
            down = jnp.dot(act[at, :], downs_ref[:, cols], preferred_element_type=F32)
            if g == 0:
                sums[0, :, cols] = back
                sums[1, :, cols] = down
            else:
                held[g - 1, 0, to, cols] = back.astype(BF)
                held[g - 1, 1, to, cols] = down.astype(BF)

    own_back = [copy(5 + i, held.at[0, i], came.at[3 * i], other) for i in range(2)]
    pair_back = [
        [
            copy(7 + 2 * p + i, held.at[2, i, parts[p]], came.at[1 + 3 * i, parts[p]], other)
            for i in range(2)
        ]
        for p in range(2)
    ]
    last = [copy(11 + p, held.at[1, 0, parts[p]], came.at[2, parts[p]], pair) for p in range(2)]

    io.ready("ups", "downs", "douts")
    work(0)
    to_other.wait_recv()
    work(1)
    for c in own_back:
        c.start()
    for p in range(2):
        to_pair[p].wait_recv()
        through[p].start()
        work(2, p)
        through[p].wait_recv()
        work(3, p)
        for c in pair_back[p]:
            c.start()
        for i in range(2):
            pair_back[p][i].wait_recv()

            @pl.loop(0, half // step)
            def _(r):
                at = pl.ds(pl.multiple_of(p * half + r * step, step), step)
                held[1, i, at, :] = (
                    held[1, i, at, :].astype(F32) + came[1 + 3 * i, at, :].astype(F32)
                ).astype(BF)

            if i == 0:
                last[p].start()
    give_ref[...] = held[1, 1]
    io.done("give")
    tile = 512

    @pl.loop(0, width // tile)
    def _(n):
        cols = pl.ds(pl.multiple_of(n * tile, tile), tile)
        up_grad_ref[n] = dot_tn(two[:, cols], gu[...], BF)
        down_grad_ref[n] = dot_tn(act[...], douts_ref[:, cols], BF)

    io.done("up", "down")
    for c in own_back + last:
        c.wait_recv()
    gain_grad_ref[...] = jnp.zeros_like(gain_grad_ref)

    @pl.loop(0, rows // step)
    def _(r):
        at = pl.ds(pl.multiple_of(r * step, step), step)
        back = sums[0, at, :] + came[0, at, :].astype(F32) + came[2, at, :].astype(F32)
        hat, scale = normed(hid_ref[at, :])
        gain_grad_ref[...] += jnp.sum(back * hat, axis=0, keepdims=True)
        grad = douts_ref[at, :].astype(F32) + norm_back(back * gain_ref[1:2, :], hat, scale)
        grad_ref[at, :] = grad
        rows_ref[at, :] = grad.astype(BF)
        keep_ref[at, :] = hid_ref[at, :] + sums[1, at, :] + came[3, at, :].astype(F32)

    for c in to_pair + through + own_back + pair_back[0] + pair_back[1] + last + [to_other]:
        c.wait_send()


class PlaneReduce:
    def __init__(self, far, near, came, x_first, send, recv):
        chip, core = lax.axis_index("chip"), lax.axis_index("core")
        x, y, other = {"chip": chip ^ 1}, {"chip": chip ^ 2}, {"core": 1 - core}
        self.near, self.came, self.x_first = near, came, x_first
        self.waited = ()

        def copy(i, src, to):
            return pltpu.make_async_remote_copy(
                src_ref=src,
                dst_ref=came.at[i],
                send_sem=send.at[i],
                recv_sem=recv.at[i],
                device_id=to,
                device_id_type=MESH,
            )

        self.away = (1, 3) if x_first else (2, 3)
        self.stay = (0, 2) if x_first else (0, 1)
        one, two = (x, y) if x_first else (y, x)
        self.cores = 4 if far else 0
        self.copies = [copy(i, far(4 + i), other) for i in range(self.cores)]
        self.copies += [copy(self.cores + i, near.at[self.away[i]], one) for i in range(2)]
        self.copies.append(copy(self.cores + 2, near.at[self.stay[1]], two))

    def start(self):
        for i in (3, self.away[0], self.stay[1], 0):
            self.copies[i].start()

    def add(self, place, i):
        step = 64

        @pl.loop(0, self.near.shape[1] // step)
        def _(r):
            at = pl.ds(pl.multiple_of(r * step, step), step)
            self.near[place, at, :] = (
                self.near[place, at, :].astype(F32) + self.came[i, at, :].astype(F32)
            ).astype(BF)

    def core_sums(self):
        for i in (1, 0):
            p = self.away[i]
            self.copies[p].wait_recv()
            self.add(p, p)
            self.copies[4 + i].start()
        for p in (self.stay[1], self.stay[0]):
            self.copies[p].wait_recv()
            self.add(p, p)

    def start_first(self):
        for i in (1, 0):
            self.copies[self.cores + i].start()

    def first_sums(self, step):
        i = 1 - step
        self.copies[self.cores + i].wait_recv()
        self.add(self.stay[i], self.cores + i)
        if i == 1:
            self.copies[self.cores + 2].start()

    def finish(self, out_ref):
        self.copies[self.cores + 2].wait_recv()
        self.add(self.stay[0], self.cores + 2)
        out_ref[...] = self.near[0]
        for i, c in enumerate(self.copies):
            if i not in self.waited:
                c.wait_send()


def far_slot(i, x_first):
    return ((3, 1, 2, 0) if x_first else (3, 2, 1, 0)).index(i) % 2


def close_rows_kernel(
    io,
    xa_ref,
    xb_ref,
    wa_ref,
    wb_ref,
    one_ref,
    tok_ref,
    hid_ref,
    gain_ref,
    gain_two_ref,
    out_ref,
    sum_a_ref,
    sum_b_ref,
    gains_ref,
    held,
    came,
    near_a,
    near_b,
    far_a,
    far_b,
    came_a,
    came_b,
    small,
    small_came,
    small_line,
    send,
    recv,
    psend,
    precv,
    ssend,
    srecv,
):
    chip, core, z = (lax.axis_index(a) for a in AXES)
    rows = out_ref.shape[0] // 2
    length = one_ref.shape[0] // 2
    width = out_ref.shape[1] // 8
    greet(every=True, whole=True)

    def make(a, to):
        at = [
            pl.ds(pl.multiple_of(m * length + a * rows, rows), rows) for m in range(2)
        ]
        xa = jnp.concatenate([xa_ref[i, :] for i in at], axis=0)
        xb = jnp.concatenate([xb_ref[i, :] for i in at], axis=0)

        @pl.loop(0, 8)
        def _(p):
            part = pl.ds(pl.multiple_of(p * width, width), width)
            r = dot_nt(xa, wa_ref[part, :]) + dot_nt(xb, wb_ref[part, :])
            to[:, chunk_of(p, width)] = r.astype(to.dtype)
            ones = jnp.concatenate([one_ref[i, part] for i in at], axis=0)
            small[p, 0:1, :] += jnp.sum(r * ones.astype(F32), axis=0, keepdims=True)

    small[...] = jnp.zeros_like(small)
    line = LineReduce(make, out_ref, held, came, send, recv)
    sets = []
    for i, (x_ref, near, far, got, x_first) in enumerate(
        (
            (xa_ref, near_a, far_a, came_a, True),
            (xb_ref, near_b, far_b, came_b, False),
        )
    ):
        group = PlaneReduce(
            lambda p, far=far, x=x_first: far.at[far_slot(p - 4, x)],
            near,
            got,
            x_first,
            psend.at[i],
            precv.at[i],
        )
        group.waited = tuple((3, group.away[0]))
        sets.append((group, x_ref, near, far, got))

    tile = 512

    def product(x_ref, place, to, more=None):
        @pl.loop(0, x_ref.shape[1] // tile)
        def _(n):
            cols = pl.ds(pl.multiple_of(n * tile, tile), tile)
            r = dot_tn(one_ref[:, place * width : (place + 1) * width], x_ref[:, cols])
            if more is not None:
                r = r + more[:, cols].astype(F32)
            to[:, cols] = r.astype(BF)

    io.ready("xa", "xb", "wa", "wb", "one")
    io.start(1)
    line.step(3)
    for n in range(4):
        for group, x_ref, near, far, got in sets:
            order = (3, group.away[0], group.stay[1], 0)
            if n >= 2:
                group.copies[order[n - 2]].wait_send()
            product(x_ref, 4 + order[n], far.at[n % 2])
            group.copies[order[n]].start()

    def add_near(n):
        for group, x_ref, near, far, got in sets:
            i = (3, group.away[0], group.stay[1], 0)[n]
            group.copies[i].wait_recv()
            product(x_ref, i, near.at[i], got.at[i])
            if n < 2:
                group.copies[4 + (1 - n)].start()

    add_near(0)
    add_near(1)
    line.step(2)
    add_near(2)
    add_near(3)
    line.step(1)
    line.own()
    for p in range(8):
        small[p, 0:1, :] = small[p, 0:1, :] / gain_ref[0:1, chunk_of(p, width)]
        small[p, 1:2, :] = gain_two_ref[:, chip_order(p, width)]

    def pass_small(i, src, dst, to):
        return pltpu.make_async_remote_copy(
            src_ref=src,
            dst_ref=dst,
            send_sem=ssend.at[i],
            recv_sem=srecv.at[i],
            device_id=to,
            device_id_type=MESH,
        )

    sent = [
        pass_small(
            p - 1,
            small.at[p],
            small_came.at[p],
            {"chip": chip ^ (p % 4), "core": core ^ (p // 4)},
        )
        for p in range(1, 8)
    ]
    for c in sent:
        c.start()
    for group, *_ in sets:
        group.first_sums(0)
    for group, *_ in sets:
        group.first_sums(1)
    total = small[0]
    for p in range(1, 8):
        sent[p - 1].wait_recv()
        total = total + small_came[p]
    small_line[0] = total
    last = [
        pass_small(6 + k, small_line.at[0], small_line.at[k], {"uly": z ^ k}) for k in range(1, 4)
    ]
    for c in last:
        c.start()
    io.ready("tokens", "hid")
    line.close()
    step = 32

    @pl.loop(0, 2 * rows // step)
    def _(r):
        at = pl.ds(pl.multiple_of(r * step, step), step)
        hat, scale = normed(tok_ref[at, :].astype(F32))
        out_ref[at, :] = norm_back(out_ref[at, :] * gain_ref[0:1, :], hat, scale)
        for k in range(4):
            out_ref[at, chip_chunk(k, 2 * width)] += hid_ref[
                at, k * 2 * width : (k + 1) * 2 * width
            ]

    for (group, *_), out in zip(sets, (sum_a_ref, sum_b_ref)):
        group.finish(out)
    for k in range(1, 4):
        last[k - 1].wait_recv()
        total = total + small_line[k]
    gains_ref[...] = total
    for c in sent + last:
        c.wait_send()


class StateExchange:
    def __init__(self, weights, own, sib, chips, mine, came, final, send, recv):
        self.core = lax.axis_index("core")
        self.weights, self.own, self.sib, self.chips = weights, own, sib, chips
        self.mine, self.came, self.final = mine, came, final

        def copy(i, src, dst):
            return pltpu.make_async_remote_copy(
                src_ref=src,
                dst_ref=dst,
                send_sem=send.at[2, i],
                recv_sem=recv.at[2, i],
                device_id={"core": 1 - self.core},
                device_id_type=MESH,
            )

        self.first = copy(0, own, sib)
        self.second = copy(1, mine, came)
        self.items = [
            PlaneGather(
                chips.at[0, h], lambda p, h=h: chips.at[p, h], h == 0, send.at[h], recv.at[h], False
            )
            for h in range(2)
        ]

    def start(self):
        self.first.start()

    def join(self):
        self.first.wait_recv()
        m = self.core
        for h in range(2):
            mine, other = self.weights.joined(m, h)
            self.chips[0, h] = (
                mine * self.own[m, h].astype(F32) + other * self.sib[m, h].astype(F32)
            ).astype(BF)
            self.items[h].start()

    def near(self):
        for item in self.items:
            item.near()

    def far(self):
        for item in self.items:
            item.far()

    def settle(self):
        for item in self.items:
            item.corner()
        m = self.core
        for h in range(2):
            total = self.weights.chip(m, h, 1) * self.chips[1, h].astype(F32)
            for k in (2, 3):
                total = total + self.weights.chip(m, h, k) * self.chips[k, h].astype(F32)
            self.mine[h] = total.astype(BF)
        self.second.start()
        self.last(m, self.mine)
        self.second.wait_recv()
        self.last(1 - m, self.came)

    def last(self, m, chip_state):
        for h in range(2):
            whole, other = self.weights.final(m, h)
            self.final[m, h] = (
                whole * chip_state[h].astype(F32) + other * self.sib[m, h].astype(F32)
            ).astype(BF)

    def finish(self):
        self.first.wait_send()
        self.second.wait_send()
        for item in self.items:
            item.finish()


def state_scratch(shape):
    half = shape[1:]
    return [
        pltpu.VMEM(shape, BF),
        pltpu.VMEM(shape, BF),
        pltpu.VMEM((4, *half), BF),
        pltpu.VMEM(half, BF),
        pltpu.VMEM(half, BF),
        sems(3, 3),
        sems(3, 3),
    ]


class Places:
    def __init__(self, lengths_ref, m, length):
        self.length = length
        self.base = (lax.axis_index("chip") * 2 + lax.axis_index("core")) * length
        self.bounds = []
        total = 0
        for n in range(lengths_ref.shape[1]):
            self.bounds.append(total)
            total = total + lengths_ref[m, n]

    def segment(self, at):
        found = jnp.zeros_like(at)
        for b in self.bounds:
            found = found + jnp.where(self.base + at >= b, 1, 0)
        return found

    def table(self, rate, start, count, across):
        shape = (count, self.length)
        rows = start + lax.broadcasted_iota(jnp.int32, shape, 0)
        cols = lax.broadcasted_iota(jnp.int32, shape, 1)
        off = cols - rows if across else rows - cols
        seg_rows = self.segment(start + lax.broadcasted_iota(jnp.int32, (count, 1), 0))
        seg_cols = self.segment(lax.broadcasted_iota(jnp.int32, (1, self.length), 1))
        far = jnp.maximum(off, 0).astype(F32)
        return jnp.where((off >= 0) & (seg_rows == seg_cols), jnp.exp(-rate * far), 0.0)

    def entry(self, rate, start, count):
        at = start + lax.broadcasted_iota(jnp.int32, (count, 1), 0)
        same = self.segment(at) == self.segment(jnp.full((1, 1), -1, jnp.int32))
        return jnp.where(same, jnp.exp(-rate * (at + 1).astype(F32)), 0.0)

    def leave(self, rate, start, count):
        at = start + lax.broadcasted_iota(jnp.int32, (count, 1), 0)
        end = jnp.full((1, 1), self.length - 1, jnp.int32)
        same = self.segment(at) == self.segment(end)
        return jnp.where(same, jnp.exp(-rate * (self.length - 1 - at).astype(F32)), 0.0)


def rate_of(rates_ref, h):
    return rates_ref[lax.axis_index("uly") * 2 + h]


class StateWeights:
    def __init__(self, rates_ref, lengths_ref, length, back):
        self.rates, self.lengths, self.length, self.back = rates_ref, lengths_ref, length, back
        self.chip_at, self.core = lax.axis_index("chip"), lax.axis_index("core")

    def end(self, m, block):
        at = jnp.full((1, 1), (block + 1) * self.length - 1, jnp.int32)
        found = jnp.zeros_like(at)
        total = 0
        for n in range(self.lengths.shape[1]):
            found = found + jnp.where(at >= total, 1, 0)
            total = total + self.lengths[m, n]
        return found

    def decay(self, h, count):
        far = jnp.full((1, 1), count * self.length, jnp.int32).astype(F32)
        return jnp.exp(-rate_of(self.rates, h) * far)

    def through(self, m, h, block):
        same = self.end(m, block) == self.end(m, block - 1)
        return jnp.where(same, self.decay(h, 1), 0.0)

    def pick(self, first, second):
        return jnp.where(jnp.full((1, 1), self.core, jnp.int32) == 0, first, second)

    def joined(self, m, h):
        one = jnp.ones((1, 1), F32)
        if self.back:
            even = self.through(m, h, 2 * self.chip_at)
            return self.pick(one, even), self.pick(even, one)
        odd = self.through(m, h, 2 * self.chip_at + 1)
        return self.pick(odd, one), self.pick(one, odd)

    def final(self, m, h):
        one, zero = jnp.ones((1, 1), F32), jnp.zeros((1, 1), F32)
        if self.back:
            return self.pick(self.through(m, h, 2 * self.chip_at + 1), one), self.pick(one, zero)
        return self.pick(one, self.through(m, h, 2 * self.chip_at)), self.pick(zero, one)

    def chip(self, m, h, k):
        here, there = self.chip_at, self.chip_at ^ k
        low, high = (here, there) if self.back else (there, here)
        before = jnp.full((1, 1), low, jnp.int32) < jnp.full((1, 1), high, jnp.int32)
        same = self.end(m, 2 * low + 1) == self.end(m, 2 * high - 1)
        return jnp.where(before & same, self.decay(h, 2 * jnp.maximum(high - 1 - low, 0)), 0.0)


ROWS = 128


def retain_part(
    io,
    rates_ref,
    lengths_ref,
    a_ref,
    high_ref,
    gate_ref,
    mixed_ref,
    kept_ref,
    state_ref,
    douts_ref,
    send_rows,
    own,
    sib,
    chips,
    mine,
    came,
    send,
    recv,
):
    _, length, vd = high_ref.shape
    qk = (a_ref.shape[2] - vd) // 2
    hd = qk // 2
    weights = StateWeights(rates_ref, lengths_ref, length, False)
    states = StateExchange(weights, own, sib, chips, mine, came, state_ref, send, recv)
    to_pair, to_other, through = send_rows

    def values(m, h):
        return high_ref[m] if h else a_ref[m, :, 2 * qk :]

    def keys(m, h):
        return a_ref[m, :, qk + h * hd : qk + (h + 1) * hd]

    for h in range(2):

        @pl.loop(0, 2)
        def _(m):
            leave = Places(lengths_ref, m, length).leave(rate_of(rates_ref, h), 0, length)
            k = (keys(m, h).astype(F32) * leave).astype(BF)
            own[m, h] = dot_tn(k, values(m, h), BF)

    states.start()
    parts = length // ROWS

    def local(h):
        @pl.loop(0, 2 * parts)
        def _(i):
            m, r = i // parts, i % parts
            at = pl.ds(pl.multiple_of(r * ROWS, ROWS), ROWS)
            table = Places(lengths_ref, m, length).table(rate_of(rates_ref, h), r * ROWS, ROWS, False)
            q = a_ref[m, at, h * hd : (h + 1) * hd]
            scores = (dot_nt(q, keys(m, h)) * table).astype(BF)
            kept_ref[m, at, h * vd : (h + 1) * vd] = jnp.dot(
                scores, values(m, h), preferred_element_type=F32
            )

    states.join()
    to_other.start()
    local(0)
    states.near()
    local(1)
    states.far()
    states.settle()
    for h in range(2):

        @pl.loop(0, 2 * parts)
        def _(i):
            m, r = i // parts, i % parts
            at = pl.ds(pl.multiple_of(r * ROWS, ROWS), ROWS)
            cols = slice(h * vd, (h + 1) * vd)
            entry = Places(lengths_ref, m, length).entry(rate_of(rates_ref, h), r * ROWS, ROWS)
            q = a_ref[m, at, h * hd : (h + 1) * hd]
            kept = kept_ref[m, at, cols] + entry * jnp.dot(
                q, state_ref[m, h], preferred_element_type=F32
            )
            kept_ref[m, at, cols] = kept
            g = gate_ref[m, at, cols]
            mixed_ref[m, at, cols] = (g * sigmoid(g) * normed(kept)[0]).astype(BF)

    io.done("mixed", "kept")
    states.finish()
    to_pair.wait_recv()
    through.start()
    to_other.wait_recv()
    through.wait_recv()
    io.done("douts")
    for c in send_rows:
        c.wait_send()


def sigmoid(v):
    return 0.5 * jnp.tanh(0.5 * v) + 0.5


def retain_back_kernel(
    io,
    rates_ref,
    lengths_ref,
    a_ref,
    high_ref,
    gate_ref,
    kept_ref,
    grad_ref,
    state_ref,
    part_hbm,
    keep_ref,
    give_hbm,
    up_sum_ref,
    down_sum_ref,
    xa_ref,
    xb_ref,
    sum_ref,
    out_ref,
    up_ref,
    down_ref,
    pulled,
    grad_k,
    grad_v,
    final,
    own,
    sib,
    chips,
    mine,
    came,
    send,
    recv,
    near,
    got,
    psend,
    precv,
    lsem,
    came_rows,
    rsend,
    rrecv,
    came_up,
    came_down,
    swap_up,
    swap_down,
    came_swap_up,
    came_swap_down,
    fsend,
    frecv,
):
    _, length, vd = high_ref.shape
    qk = (a_ref.shape[2] - vd) // 2
    hd = qk // 2
    greet(plane=True, cores=True, pair=True, across=True)
    core, z = lax.axis_index("core"), lax.axis_index("uly")

    def feed_copy(i, src, dst, to):
        return pltpu.make_async_remote_copy(
            src_ref=src,
            dst_ref=dst,
            send_sem=fsend.at[i],
            recv_sem=frecv.at[i],
            device_id=to,
            device_id_type=MESH,
        )

    units = came_up.shape[1]
    across = [
        feed_copy(0, up_sum_ref.at[:, pl.ds(units, units)], came_up, {"uly": z ^ 2}),
        feed_copy(1, down_sum_ref.at[pl.ds(units, units)], came_down, {"uly": z ^ 2}),
    ]
    swaps = [
        feed_copy(2, swap_up, came_swap_up, {"core": 1 - core}),
        feed_copy(3, swap_down, came_swap_down, {"core": 1 - core}),
    ]
    io.ready("up", "down")
    for c in across:
        c.start()
    give = pltpu.make_async_remote_copy(
        src_ref=give_hbm,
        dst_ref=came_rows,
        send_sem=rsend,
        recv_sem=rrecv,
        device_id={"uly": lax.axis_index("uly") ^ 1},
        device_id_type=MESH,
    )
    give.start()
    groups = [
        PlaneReduce(
            lambda p, i=i: part_hbm.at[i, p],
            near.at[i],
            got.at[i],
            i == 0,
            psend.at[i],
            precv.at[i],
        )
        for i in range(2)
    ]
    local = [
        pltpu.make_async_copy(part_hbm.at[i, pl.ds(0, 4)], near.at[i], lsem.at[i]) for i in range(2)
    ]
    for c in local:
        c.start()
    for group in groups:
        group.start()
    io.ready("gate", "kept", "grad")
    io.start(1)
    weights = StateWeights(rates_ref, lengths_ref, length, True)
    states = StateExchange(weights, own, sib, chips, mine, came, final, send, recv)
    parts = length // ROWS

    def values(m, h, at=slice(None)):
        return high_ref[m, at, :] if h else a_ref[m, at, 2 * qk :]

    def keys(m, h, at=slice(None)):
        return a_ref[m, at, qk + h * hd : qk + (h + 1) * hd]

    def queries(m, h, at=slice(None)):
        return a_ref[m, at, h * hd : (h + 1) * hd]

    for h in range(2):
        cols = slice(h * vd, (h + 1) * vd)

        @pl.loop(0, 2 * parts)
        def _(i):
            m, r = i // parts, i % parts
            at = pl.ds(pl.multiple_of(r * ROWS, ROWS), ROWS)
            g, gm = gate_ref[m, at, cols], grad_ref[m, at, cols]
            sigma = sigmoid(g)
            hat, scale = normed(kept_ref[m, at, cols])
            xb_ref[m, at, vd + h * vd : vd + (h + 1) * vd] = (
                gm * hat * (sigma + g * sigma * (1.0 - sigma))
            ).astype(BF)
            pulled[m, at, cols] = norm_back(gm * g * sigma, hat, scale).astype(BF)

        if h == 0:
            io.ready("a", "high", "state")

        @pl.loop(0, 2)
        def _(m):
            entry = Places(lengths_ref, m, length).entry(rate_of(rates_ref, h), 0, length)
            q = (queries(m, h).astype(F32) * entry).astype(BF)
            own[m, h] = dot_tn(q, pulled[m, :, cols], BF)

    states.start()

    def local_q(h):
        cols = slice(h * vd, (h + 1) * vd)

        @pl.loop(0, 2 * parts)
        def _(i):
            m, r = i // parts, i % parts
            at = pl.ds(pl.multiple_of(r * ROWS, ROWS), ROWS)
            places = Places(lengths_ref, m, length)
            table = places.table(rate_of(rates_ref, h), r * ROWS, ROWS, False)
            gr = pulled[m, at, cols]
            p = (dot_nt(gr, values(m, h)) * table).astype(BF)
            entry = places.entry(rate_of(rates_ref, h), r * ROWS, ROWS)
            xa_ref[m, at, h * hd : (h + 1) * hd] = (
                jnp.dot(p, keys(m, h), preferred_element_type=F32)
                + entry * dot_nt(gr, state_ref[m, h])
            ).astype(BF)

    def local_kv(h):
        cols = slice(h * vd, (h + 1) * vd)

        @pl.loop(0, 2 * parts)
        def _(i):
            m, r = i // parts, i % parts
            at = pl.ds(pl.multiple_of(r * ROWS, ROWS), ROWS)
            table = Places(lengths_ref, m, length).table(rate_of(rates_ref, h), r * ROWS, ROWS, True)
            p = (dot_nt(values(m, h, at), pulled[m, :, cols]) * table).astype(BF)
            scores = (dot_nt(keys(m, h, at), queries(m, h)) * table).astype(BF)
            grad_k[m, at, h * hd : (h + 1) * hd] = jnp.dot(
                p, queries(m, h), preferred_element_type=F32
            )
            grad_v[m, at, cols] = jnp.dot(
                scores, pulled[m, :, cols], preferred_element_type=F32
            )

    states.join()
    local_q(0)
    states.near()
    states.far()
    for c in local:
        c.wait()
    for group in groups:
        group.core_sums()
    local_q(1)
    states.settle()
    local_kv(0)
    for group in groups:
        group.first_sums(0)
    for group in groups:
        group.first_sums(1)
    local_kv(1)
    for h in range(2):

        @pl.loop(0, 2 * parts)
        def _(i):
            m, r = i // parts, i % parts
            at = pl.ds(pl.multiple_of(r * ROWS, ROWS), ROWS)
            leave = Places(lengths_ref, m, length).leave(rate_of(rates_ref, h), r * ROWS, ROWS)
            xa_ref[m, at, qk + h * hd : qk + (h + 1) * hd] = (
                grad_k[m, at, h * hd : (h + 1) * hd]
                + leave * dot_nt(values(m, h, at), final[m, h])
            ).astype(BF)
            gv = (
                grad_v[m, at, h * vd : (h + 1) * vd]
                + leave * jnp.dot(keys(m, h, at), final[m, h], preferred_element_type=F32)
            ).astype(BF)
            if h:
                xb_ref[m, at, :vd] = gv
            else:
                xa_ref[m, at, 2 * qk :] = gv

    io.done("xa", "xb")
    states.finish()
    give.wait()
    io.ready("keep")
    quarter = keep_ref.shape[1] // 4
    for k in range(4):
        cols = slice(k * quarter, (k + 1) * quarter)
        out_ref[:, chip_chunk(k, quarter)] = (
            keep_ref[:, cols] + came_rows[:, cols].astype(F32)
        ).astype(BF)
    for i, group in enumerate(groups):
        group.finish(sum_ref.at[i])
    rows, cols = up_ref.shape[0], down_ref.shape[1]

    def mine(size, own):
        return pl.ds(pl.multiple_of((core if own else 1 - core) * size, size), size)

    for c in across:
        c.wait()
    kept_units = slice(0, units)

    def up_total(own):
        at = mine(rows, own)
        return up_sum_ref[at, kept_units].astype(F32) + came_up[at, :].astype(F32)

    def down_total(own):
        at = mine(cols, own)
        return down_sum_ref[kept_units, at].astype(F32) + came_down[:, at].astype(F32)

    swap_up[...] = up_total(False).astype(BF)
    swap_down[...] = down_total(False).astype(BF)
    for c in swaps:
        c.start()
    up_ref[:, mine(units, True)] = up_total(True)
    down_ref[mine(units, True), :] = down_total(True)
    for c in swaps:
        c.wait()
    up_ref[:, mine(units, False)] = came_swap_up[...].astype(F32)
    down_ref[mine(units, False), :] = came_swap_down[...].astype(F32)


def sems(*shape):
    return pltpu.SemaphoreType.DMA(shape)


def like(shape, kind):
    return jax.ShapeDtypeStruct(shape, kind)


class Late:
    def __init__(self, name, order=0):
        self.name, self.order = name, order


class Early:
    def __init__(self, name):
        self.name = name


class Moves:
    def __init__(self, loads, stores):
        self.loads, self.stores = loads, stores
        self.waited, self.begun = set(), set()

    def start(self, order):
        for copy, at in self.loads.values():
            if at == order:
                copy.start()

    def ready(self, *names):
        for name in names:
            self.loads[name][0].wait()
            self.waited.add(name)

    def done(self, *names):
        for name in names:
            self.stores[name].start()
            self.begun.add(name)

    def finish(self):
        self.done(*[n for n in self.stores if n not in self.begun])
        self.ready(*[n for n in self.loads if n not in self.waited])
        for copy in self.stores.values():
            copy.wait()


def call(kernel, number, ins, outs, scratch, flops, *args):
    moved = sum(a.size * a.dtype.itemsize for a in args)
    late = [i for i, spec in enumerate(ins) if isinstance(spec, Late)]
    early = [i for i, out in enumerate(outs) if isinstance(out[2], Early)]

    def whole(*refs):
        refs = list(refs)
        in_refs, refs = refs[: len(ins)], refs[len(ins) :]
        out_refs, refs = refs[: len(outs)], refs[len(outs) :]
        own, refs = refs[: len(scratch)], refs[len(scratch) :]
        load_sem, store_sem = refs[-2:]
        loads, stores = {}, {}
        for n, i in enumerate(late):
            copy = pltpu.make_async_copy(in_refs[i], refs[n], load_sem.at[n])
            loads[ins[i].name] = (copy, ins[i].order)
            in_refs[i] = refs[n]
        for n, i in enumerate(early):
            ref = refs[len(late) + n]
            stores[outs[i][2].name] = pltpu.make_async_copy(ref, out_refs[i], store_sem.at[n])
            out_refs[i] = ref
        io = Moves(loads, stores)
        io.start(0)
        kernel(io, *in_refs, *out_refs, *own)
        io.finish()

    extra = [pltpu.VMEM(args[i].shape, args[i].dtype) for i in late]
    extra += [pltpu.VMEM(outs[i][0], outs[i][1]) for i in early]
    return pl.pallas_call(
        whole,
        out_shape=[like(shape, kind) for shape, kind, _ in outs],
        in_specs=[anywhere() if i in late else spec for i, spec in enumerate(ins)],
        out_specs=[anywhere() if i in early else out[2] for i, out in enumerate(outs)],
        scratch_shapes=list(scratch)
        + extra
        + [sems(max(len(late), 1)), sems(max(len(early), 1))],
        compiler_params=pltpu.CompilerParams(
            collective_id=number, has_side_effects=True, vmem_limit_bytes=VMEM_LIMIT
        ),
        cost_estimate=pl.CostEstimate(flops=flops, bytes_accessed=moved, transcendentals=0),
    )(*args)


def smem():
    return pl.BlockSpec(memory_space=pltpu.SMEM)


def settle_kernel(
    block_in, input_in, first_in, second_in, out_in, up_in, down_in, *outs
):
    block, inputs, query, key, value, gate, output, up, down = outs
    qk, half = query.shape[1], out_in.shape[2]
    high = value.shape[1] // 2
    block[...] = block_in[...]
    inputs[...] = input_in[...]
    query[...] = first_in[:, :qk].astype(F32)
    key[...] = first_in[:, qk : 2 * qk].astype(F32)
    value[:, :high] = first_in[:, 2 * qk :].astype(F32)
    value[:, high:] = second_in[:, :high].astype(F32)
    gate[...] = second_in[:, high:].astype(F32)
    for i in range(2):
        output[i * half : (i + 1) * half, :] = out_in[i].astype(F32).T
    up[...] = up_in[...]
    down[...] = down_in[...]


def settle(block_out, input_grad, first_sum, second_sum, out_sum, up_grad, down_grad, qk):
    piece = first_sum.shape[0]
    high = first_sum.shape[1] - 2 * qk
    args = (block_out, input_grad, first_sum, second_sum, out_sum, up_grad, down_grad)
    shapes = [
        (block_out.shape, BF),
        (input_grad.shape, F32),
        ((piece, qk), F32),
        ((piece, qk), F32),
        ((piece, 2 * high), F32),
        ((piece, second_sum.shape[1] - high), F32),
        ((2 * out_sum.shape[2], piece), F32),
        (up_grad.shape, F32),
        (down_grad.shape, F32),
    ]
    return pl.pallas_call(
        settle_kernel,
        out_shape=[like(s, t) for s, t in shapes],
        in_specs=[vmem()] * len(args),
        out_specs=[vmem()] * len(shapes),
        compiler_params=pltpu.CompilerParams(vmem_limit_bytes=VMEM_LIMIT),
    )(*args)


def retain_back(
    rates, lengths, a, high, gate, kept, grad_mixed, state, part, keep, give, up_sum, down_sum
):
    units = up_sum.shape[1] // 2
    rows, cols = up_sum.shape[0] // 2, down_sum.shape[1] // 2
    micro, length, vd = high.shape
    hd = (a.shape[2] - vd) // 4
    return call(
        retain_back_kernel,
        6,
        [smem()] * 2
        + [Late("a", 1), Late("high", 1), Late("gate"), Late("kept"), Late("grad"), Late("state", 1)]
        + [anywhere(), Late("keep", 1), anywhere(), Late("up"), Late("down")],
        [
            ((micro, length, a.shape[2]), BF, Early("xa")),
            ((micro, length, 3 * vd), BF, Early("xb")),
            ((2, *part.shape[2:]), BF, vmem()),
            (give.shape, BF, vmem()),
            ((rows, 2 * units), F32, vmem()),
            ((2 * units, cols), F32, vmem()),
        ],
        [
            pltpu.VMEM((micro, length, 2 * vd), BF),
            pltpu.VMEM((micro, length, 2 * hd), F32),
            pltpu.VMEM((micro, length, 2 * vd), F32),
            pltpu.VMEM(state.shape, BF),
        ]
        + state_scratch(state.shape)
        + [
            pltpu.VMEM((2, 4, *part.shape[2:]), BF),
            pltpu.VMEM((2, 7, *part.shape[2:]), BF),
            sems(2, 7),
            sems(2, 7),
            sems(2),
            pltpu.VMEM(give.shape, BF),
            pltpu.SemaphoreType.DMA,
            pltpu.SemaphoreType.DMA,
            pltpu.VMEM((2 * rows, units), BF),
            pltpu.VMEM((units, 2 * cols), BF),
            pltpu.VMEM((rows, units), BF),
            pltpu.VMEM((units, cols), BF),
            pltpu.VMEM((rows, units), BF),
            pltpu.VMEM((units, cols), BF),
            sems(4),
            sems(4),
        ],
        12 * micro * length * length * (hd + vd),
        rates,
        lengths,
        a,
        high,
        gate,
        kept,
        grad_mixed,
        state,
        part,
        keep,
        give,
        up_sum,
        down_sum,
    )


def front(rates, lengths, tokens, out_grad, gains, weights, out_weight, up_weight, down_weight):
    micro, rows, width = tokens.shape
    count = lax.axis_size("uly")
    query, key, value, gate = weights
    high = value.shape[1] // 2
    if not is_cube():
        first = jnp.concatenate([query, key, value[:, :high]], axis=1)
        second = jnp.concatenate([value[:, high:], gate], axis=1)
        full = lax.all_gather(jnp.stack(gains), BLK, axis=1, tiled=True)
        w_first = lax.all_gather(first, BLK, axis=0, tiled=True)
        w_second = lax.all_gather(second, BLK, axis=0, tiled=True)
        w_out = lax.all_gather(out_weight, BLK, axis=1, tiled=True)
        one = (normed(spread(tokens).astype(F32))[0] * full[0].astype(F32)).astype(BF)
        a, v_high = dot_nn(one, w_first, BF), dot_nn(one, w_second[:, :high], BF)
        gate_rows = dot_nn(one, w_second[:, high:])
        heads_here = rates.shape[0] // count
        own_rates = lax.dynamic_slice_in_dim(
            rates, lax.axis_index("uly") * heads_here, heads_here
        )
        mixed, kept = plain_forward(own_rates, lengths, a, v_high, gate_rows)
        return (
            one,
            a,
            v_high,
            gate_rows,
            w_first,
            w_second,
            w_out,
            full.astype(F32),
            up_weight,
            down_weight,
            mixed,
            kept,
            None,
            None,
        )
    wide = count * rows
    own = micro * rows
    piece = width // 8
    na, nb, no = 2 * query.shape[1] + high, high + gate.shape[1], out_weight.shape[0]
    units = up_weight.shape[1]
    state = (micro, 2, query.shape[1] // 2, high)
    return call(
        front_kernel,
        0,
        [smem()] * 2 + [vmem()] * 3 + [anywhere()] * 7,
        [
            ((micro, wide, width), BF, Early("one")),
            ((micro, wide, na), BF, Early("first")),
            ((micro, wide, high), BF, Early("high")),
            ((micro, wide, nb - high), F32, Early("gate")),
            ((width, na), BF, anywhere()),
            ((width, nb), BF, anywhere()),
            ((no, width), BF, anywhere()),
            ((8, width), F32, vmem()),
            ((2 * piece, units), BF, anywhere()),
            ((units, 2 * piece), BF, anywhere()),
            ((micro, wide, 2 * high), BF, Early("mixed")),
            ((micro, wide, 2 * high), F32, Early("kept")),
            (state, BF, vmem()),
            ((4 * own, width), BF, Early("douts")),
        ],
        [
            pltpu.VMEM((count, own, width), BF),
            pltpu.VMEM((width, na), BF),
            pltpu.VMEM((width, nb), BF),
            pltpu.VMEM((8, 8, piece), F32),
            sems(5, 7),
            sems(5, 7),
            sems(2, count - 1),
            sems(2, count - 1),
            sems(4),
            sems(4),
            sems(3),
            sems(3),
            sems(13),
            pltpu.VMEM(out_weight.shape, BF),
            pltpu.VMEM((up_weight.shape[0], units // 2), BF),
            pltpu.VMEM((units // 2, down_weight.shape[1]), BF),
        ]
        + state_scratch(state),
        2 * micro * wide * width * (na + nb),
        rates,
        lengths,
        tokens.reshape(own, width),
        out_grad.reshape(own, width),
        jnp.stack(gains).astype(F32),
        query,
        key,
        value,
        gate,
        out_weight,
        up_weight,
        down_weight,
    )


def line_scratch(count, rows, width):
    return [
        pltpu.VMEM((count - 1, rows, width), BF),
        pltpu.VMEM((2, count - 1, rows, width), BF),
    ]


def add_rows(mixed, w_out, tokens, up, down):
    micro, wide, hidden = mixed.shape
    count = lax.axis_size("uly")
    rows = wide // count
    width = w_out.shape[1]
    units = up.shape[1]
    out = call(
        add_rows_kernel,
        1,
        [Late("x"), Late("w"), Late("tokens", 1)] + [anywhere()] * 2,
        [
            ((micro * rows, width), F32, vmem()),
            ((width, units), BF, anywhere()),
            ((units, width), BF, anywhere()),
        ],
        line_scratch(count, micro * rows, width)
        + [sems(2, count - 1)] * 2
        + [sems(2, 3), sems(2, 3), sems(4), pltpu.VMEM(up.shape, BF), pltpu.VMEM(down.shape, BF)],
        2 * micro * wide * hidden * width,
        mixed,
        w_out,
        tokens,
        up,
        down,
    )
    return out


def fan_out(rows_bf, w_out, mixed, up_grad, down_grad):
    own, width = rows_bf.shape
    micro, rows = 2, own // 2
    count = lax.axis_size("uly")
    hidden = w_out.shape[0]
    up_shape, down_shape = up_grad.shape[1:], down_grad.shape[1:]
    return call(
        fan_out_kernel,
        2,
        [vmem(), Late("w"), Late("mixed")] + [anywhere()] * 2,
        [
            ((micro, count * rows, hidden), F32, Early("grad")),
            ((2, 8, width // 8, hidden // 2), BF, Early("part")),
            (up_shape, BF, vmem()),
            (down_shape, BF, vmem()),
        ],
        [
            pltpu.VMEM((count, own, width), BF),
            pltpu.VMEM((own, width), BF),
            pltpu.VMEM((8, width // 8, hidden), F32),
            pltpu.VMEM((4, *up_shape), BF),
            pltpu.VMEM((4, *down_shape), BF),
            pltpu.VMEM((3, *up_shape), BF),
            pltpu.VMEM((3, *down_shape), BF),
            sems(2, count - 1),
            sems(2, count - 1),
            sems(2, 3),
            sems(2, 3),
            sems(2),
        ],
        4 * micro * count * rows * hidden * width,
        rows_bf,
        w_out,
        mixed,
        up_grad,
        down_grad,
    )


def feed_all(hidden, douts, gain, ups, downs):
    own, width = hidden.shape
    units = ups.shape[1]
    return call(
        feed_kernel,
        4,
        [Late("hid"), Late("douts", 1), vmem(), Late("ups", 1), Late("downs", 1)],
        [
            ((own, width), F32, vmem()),
            ((own, width), BF, Early("give")),
            ((own, width), F32, vmem()),
            ((own, width), BF, vmem()),
            ((1, width), F32, vmem()),
            ((4, width // 4, units), BF, Early("up")),
            ((4, units, width // 4), BF, Early("down")),
        ],
        [
            pltpu.VMEM((4 * own, width), BF),
            pltpu.VMEM((4 * own, units), BF),
            pltpu.VMEM((4 * own, units), BF),
            pltpu.VMEM((2, own, width), F32),
            pltpu.VMEM((3, 2, own, width), BF),
            pltpu.VMEM((5, own, width), BF),
            sems(13),
            sems(13),
        ],
        2 * 6 * 4 * own * units * width,
        hidden,
        douts,
        gain,
        ups,
        downs,
    )


def middle(tokens, out_grad, douts, gains, mixed, w_out, up_weight, down_weight):
    micro, rows, width = tokens.shape
    own = micro * rows
    if not is_cube():
        gain_two = gains[1]
        hidden = tokens.astype(F32) + collect(
            jnp.stack([dot_nn(mixed[m], w_out) for m in range(micro)])
        )
        pair = feed_weights(up_weight, down_weight)
        hat, scale = normed(hidden)
        two = (hat * gain_two).astype(BF)
        flat_two, flat_out = two.reshape(own, width), out_grad.reshape(own, width)
        two_both = jnp.concatenate([flat_two, swap(flat_two, 1)], axis=0)
        out_both = jnp.concatenate([flat_out, swap(flat_out, 1)], axis=0)
        down_rows, grad_two, up_part, down_part = feed(two_both, out_both, pair)
        grad_two = grad_two[:own] + swap(grad_two[own:].astype(BF), 1).astype(F32)
        down_rows = down_rows[:own] + swap(down_rows[own:].astype(BF), 1).astype(F32)
        up_grad, down_grad = feed_reduce(up_part, down_part)
        block_out = (hidden + down_rows.reshape(micro, rows, width)).astype(BF)
        grad_two = grad_two.reshape(micro, rows, width)
        gain_part = jnp.sum(grad_two * hat, axis=(0, 1))
        grad_hidden = out_grad.astype(F32) + norm_back(grad_two * gain_two, hat, scale)
        wide_att = spread(grad_hidden.astype(BF))
        grad_mixed = jnp.stack([dot_nt(wide_att[m], w_out) for m in range(micro)])
        part = dot_tn(
            mixed.reshape(-1, mixed.shape[2]), wide_att.reshape(-1, wide_att.shape[2]), BF
        )
        return block_out, up_grad, down_grad, gain_part, grad_hidden, grad_mixed, part
    hidden, ups, downs = add_rows(mixed, w_out, tokens.reshape(own, width), up_weight, down_weight)
    keep, give, grad_hidden, rows_bf, gain_part, up_part, down_part = feed_all(
        hidden, douts, gains, ups, downs
    )
    grad_mixed, part, up_sum, down_sum = fan_out(rows_bf, w_out, mixed, up_part, down_part)
    return (
        (keep, give),
        up_sum,
        down_sum,
        gain_part,
        grad_hidden,
        grad_mixed,
        part,
    )


def close_rows(xa, xb, w_first, w_second, one, tokens, grad_hidden, gains, gain_two):
    micro, wide, na = xa.shape
    nb = xb.shape[2]
    width = w_first.shape[0]
    flat_a, flat_b = xa.reshape(micro * wide, na), xb.reshape(micro * wide, nb)
    flat_one = one.reshape(micro * wide, width)
    if not is_cube():
        partial = jnp.stack(
            [dot_nt(xa[m], w_first) + dot_nt(xb[m], w_second) for m in range(micro)]
        )
        grad_one = collect(partial)
        hat, scale = normed(tokens.astype(F32))
        both_gains = jnp.stack([jnp.sum(grad_one * hat, axis=(0, 1)), gain_two])
        total = lax.psum_scatter(both_gains, BLK, scatter_dimension=1, tiled=True)
        return (
            grad_hidden + norm_back(grad_one * gains[0], hat, scale),
            lax.psum_scatter(dot_tn(flat_one, flat_a, BF), BLK, scatter_dimension=0, tiled=True),
            lax.psum_scatter(dot_tn(flat_one, flat_b, BF), BLK, scatter_dimension=0, tiled=True),
            lax.psum(total, "uly"),
        )
    count = lax.axis_size("uly")
    rows = wide // count
    piece = width // 8
    out = call(
        close_rows_kernel,
        3,
        [Late("xa"), Late("xb"), Late("wa"), Late("wb"), Late("one"), Late("tokens", 1)]
        + [Late("hid", 1), vmem(), vmem()],
        [
            ((micro * rows, width), F32, vmem()),
            ((piece, na), BF, vmem()),
            ((piece, nb), BF, vmem()),
            ((8, piece), F32, vmem()),
        ],
        line_scratch(count, micro * rows, width)
        + [
            pltpu.VMEM((4, piece, na), BF),
            pltpu.VMEM((4, piece, nb), BF),
            pltpu.VMEM((2, piece, na), BF),
            pltpu.VMEM((2, piece, nb), BF),
            pltpu.VMEM((7, piece, na), BF),
            pltpu.VMEM((7, piece, nb), BF),
            pltpu.VMEM((8, 8, piece), F32),
            pltpu.VMEM((8, 8, piece), F32),
            pltpu.VMEM((4, 8, piece), F32),
            sems(2, count - 1),
            sems(2, count - 1),
            sems(2, 7),
            sems(2, 7),
            sems(10),
            sems(10),
        ],
        4 * micro * wide * width * (na + nb),
        flat_a,
        flat_b,
        w_first,
        w_second,
        flat_one,
        tokens.reshape(micro * rows, width),
        grad_hidden,
        gains,
        gain_two,
    )
    return out


def feed(norm_two, out_rows, pair):
    chips, count, _, rows, hidden = pair.shape
    up = pair[:, :, 0].transpose(0, 2, 1, 3).reshape(chips * rows, count * hidden)
    down_t = pair[:, :, 1].transpose(0, 2, 1, 3).reshape(chips * rows, count * hidden)
    upward = dot_nn(norm_two, up)
    act, slope = gelu_pair(upward)
    act = act.astype(BF)
    grad_act = dot_nn(out_rows, down_t)
    grad_up = (grad_act * slope).astype(BF)

    def by_owner(grad):
        return grad.reshape(chips, rows, count, hidden).transpose(0, 2, 1, 3)

    return (
        dot_nt(act, down_t),
        dot_nt(grad_up, up),
        by_owner(dot_tn(norm_two, grad_up, BF)),
        by_owner(dot_tn(out_rows, act, BF)),
    )


def plain_forward(rates, lengths, a, v_high, gate):
    micro, length = a.shape[:2]
    heads_here = rates.shape[0]
    cut_v = v_high.shape[2]
    qk = (a.shape[2] - cut_v) // 2
    hd, vd = qk // heads_here, 2 * cut_v // heads_here
    sets, parts, states = [], [], []
    for m in range(micro):
        values = jnp.concatenate([a[m, :, 2 * qk :], v_high[m]], axis=1)
        heads = [
            (
                a[m, :, h * hd : (h + 1) * hd],
                a[m, :, qk + h * hd : qk + (h + 1) * hd],
                values[:, h * vd : (h + 1) * vd],
            )
            for h in range(heads_here)
        ]
        part = decay_parts(rates, lengths[m], length)
        states.append(retention_state(heads, part[2]))
        sets.append(heads)
        parts.append(part)

    all_states = exchange(states)
    state_in, retained, mixed = [], [], []
    for m in range(micro):
        state = state_sum(parts[m][3], all_states[m])
        kept = retention(sets[m], parts[m], state)
        state_in.append(state)
        retained.append(kept)
        mixed.append(mix(gate[m], kept))
    mixed = jnp.stack(mixed)
    return mixed, (sets, parts, state_in, retained)


def plain_backward(gate, kept, grad_mixed):
    sets, parts, state_in, retained = kept
    micro, cut_v = len(sets), gate.shape[2] // 2
    grad_gates, grad_rets, grad_states = [], [], []
    for m in range(micro):
        gg, gr = mix_back(gate[m], retained[m], grad_mixed[m])
        grad_gates.append(gg)
        grad_rets.append(gr)
        grad_states.append(
            jnp.stack(
                [
                    dot_tn((q.astype(F32) * parts[m][1][h]).astype(BF), gr[h], BF)
                    for h, (q, k, v) in enumerate(sets[m])
                ]
            )
        )
    all_back = exchange(grad_states)
    xa, xb = [], []
    for m in range(micro):
        back = state_sum(parts[m][4], all_back[m])
        grads = retention_back(sets[m], parts[m], state_in[m], grad_rets[m], back)
        gq = jnp.concatenate([g[0] for g in grads], axis=1)
        gk = jnp.concatenate([g[1] for g in grads], axis=1)
        gv = jnp.concatenate([g[2] for g in grads], axis=1)
        xa.append(jnp.concatenate([gq, gk, gv[:, :cut_v]], axis=1))
        xb.append(jnp.concatenate([gv[:, cut_v:], grad_gates[m]], axis=1))
    xa, xb = jnp.stack(xa), jnp.stack(xb)
    return xa, xb


def body(
    tokens,
    retain_gain,
    query_weight,
    key_weight,
    value_weight,
    gate_matrix,
    output_weight,
    feed_gain,
    up_weight,
    down_weight,
    decay_rate,
    lengths,
    out_grad,
):
    micro, rows, width = tokens.shape
    qk = query_weight.shape[1]
    cut_v = value_weight.shape[1] // 2

    (
        one,
        a,
        v_high,
        gate,
        w_first,
        w_second,
        w_out,
        gains,
        up,
        down,
        mixed,
        kept,
        state,
        douts,
    ) = front(
        decay_rate,
        lengths,
        tokens,
        out_grad,
        (retain_gain, feed_gain),
        (query_weight, key_weight, value_weight, gate_matrix),
        output_weight,
        up_weight,
        down_weight,
    )
    block_out, up_grad, down_grad, gain_two, grad_hidden, grad_mixed, part = middle(
        tokens, out_grad, douts, gains, mixed, w_out, up, down
    )

    if is_cube():
        xa, xb, out_sum, block_out, up_grad, down_grad = retain_back(
            decay_rate,
            lengths,
            a,
            v_high,
            gate,
            kept,
            grad_mixed,
            state,
            part,
            *block_out,
            up_grad,
            down_grad,
        )
    else:
        xa, xb = plain_backward(gate, kept, grad_mixed)
        out_sum = lax.psum_scatter(part, BLK, scatter_dimension=1, tiled=True)

    input_grad, first_sum, second_sum, gain_sums = close_rows(
        xa, xb, w_first, w_second, one, tokens, grad_hidden, gains, gain_two
    )
    if is_cube():
        block_out, input_grad, query, key, value, gates, output, up_grad, down_grad = settle(
            block_out, input_grad, first_sum, second_sum, out_sum, up_grad, down_grad, qk
        )
        block_out = block_out.reshape(tokens.shape)
        input_grad = input_grad.reshape(tokens.shape)
    else:
        first_sum, second_sum = first_sum.astype(F32), second_sum.astype(F32)
        query, key = first_sum[:, :qk], first_sum[:, qk : 2 * qk]
        value = jnp.concatenate([first_sum[:, 2 * qk :], second_sum[:, :cut_v]], axis=1)
        gates, output = second_sum[:, cut_v:], out_sum.astype(F32)
    return (
        block_out,
        input_grad,
        gain_sums[0],
        query,
        key,
        value,
        gates,
        output,
        gain_sums[1],
        up_grad,
        down_grad,
    )


def solution(mesh):
    blocks, count = mesh.devices.shape
    split = Mesh(mesh.devices.reshape(blocks // 2, 2, count), AXES)
    rows = P(None, AXES, None)
    gain, wide, tall = P(BLK), P(BLK, "uly"), P("uly", BLK)
    return jax.shard_map(
        body,
        mesh=split,
        in_specs=(rows, gain, wide, wide, wide, wide, tall, gain, wide, tall, P(), P(), rows),
        out_specs=(rows, rows, gain, wide, wide, wide, wide, tall, gain, wide, tall),
        check_vma=False,
    )
```
